128 devices in a mesh: grp: 2 (over core), dp: 64 (over x, y, z).
Axes of the slice: x: 4, y: 4, z: 4, core: 2. Of those that a mesh axis runs over, the one named last changes fastest.
Arguments:
- tokens: bfloat16 [2, 64, 576, 768], P('grp', 'dp'), may hold values from -6 to 6
- cotangent: bfloat16 [2, 64, 576, 768], P('grp', 'dp'), may hold values from -6 to 6
- counts: int32 [2, 64, 2], P('grp', 'dp'), may hold values from 0 to 576, as said below
- patch_row: int32 [2, 64, 576], P('grp', 'dp'), may hold values from 0 to 23, as said below
- patch_col: int32 [2, 64, 576], P('grp', 'dp'), may hold values from 0 to 23, as said below
- w_qkv: float32 [768, 2304], P('dp'), may hold values from -0.21650635 to 0.21650635
- w_proj: float32 [768, 768], P('dp'), may hold values from -4 to 4
- w_fc1: float32 [768, 3072], P('dp'), may hold values from -0.21875 to 0.21875
- w_fc2: float32 [3072, 768], P('dp'), may hold values from -0.109375 to 0.109375
- vectors: float32 [14, 768], P(None, 'dp')
- m_qkv: float32 [768, 2304], P('dp'), may hold values from -0.00061035156 to 0.00061035156
- v_qkv: float32 [768, 2304], P('dp'), may hold values from 8.182106e-09 to 3.244628e-08
- m_proj: float32 [768, 768], P('dp'), may hold values from -6.1035156e-05 to 6.1035156e-05
- v_proj: float32 [768, 768], P('dp'), may hold values from 9.02853e-11 to 3.5267697e-10
- m_fc1: float32 [768, 3072], P('dp'), may hold values from -3.8146973e-05 to 3.8146973e-05
- v_fc1: float32 [768, 3072], P('dp'), may hold values from 3.808911e-11 to 1.4953504e-10
- m_fc2: float32 [3072, 768], P('dp'), may hold values from -7.6293945e-05 to 7.6293945e-05
- v_fc2: float32 [3072, 768], P('dp'), may hold values from 1.4107078e-10 to 5.5017607e-10
- m_vectors: float32 [14, 768], P(None, 'dp'), may hold values from -0.0024414062 to 0.0024414062
- v_vectors: float32 [14, 768], P(None, 'dp'), may hold values from 1.1849946e-07 to 4.796407e-07
Outputs:
- mixed_out: bfloat16 [2, 64, 576, 768], P('grp', 'dp')
- grad_tokens: float32 [2, 64, 576, 768], P('grp', 'dp')
- grad_norm: float32 [], replicated
- qkv_new: float32 [768, 2304], P('dp')
- qkv_first: float32 [768, 2304], P('dp')
- qkv_second: float32 [768, 2304], P('dp')
- proj_new: float32 [768, 768], P('dp')
- proj_first: float32 [768, 768], P('dp')
- proj_second: float32 [768, 768], P('dp')
- fc1_new: float32 [768, 3072], P('dp')
- fc1_first: float32 [768, 3072], P('dp')
- fc1_second: float32 [768, 3072], P('dp')
- fc2_new: float32 [3072, 768], P('dp')
- fc2_first: float32 [3072, 768], P('dp')
- fc2_second: float32 [3072, 768], P('dp')
- vectors_new: float32 [14, 768], P(None, 'dp')
- vectors_first: float32 [14, 768], P(None, 'dp')
- vectors_second: float32 [14, 768], P(None, 'dp')
- bias_proj_grad: float32 [768], P('dp')
The draws below stay inside these ranges and needn't reach their ends.
Inputs may be any that keep to these rules, and one draw needn't show every extreme that they name: counts[0, f, i] is the number of kept patches of image i of a first-group frame, 98 to 196; counts[1, f, 0] that of the one image of a second-group frame, 288 to 576; counts[1, f, 1] is 0. Kept patches fill their image's first slots. `patch_row`: the kept patches of one image sit at distinct grid positions (rows below 14 in the first group, 24 in the second); other slots hold any position. `patch_col`: column of the same positions.
All inputs are finite; a program needn't handle non-finite values.
Results may differ from the reference program's by a relative error of at most 0.023.
The reference program's roundings to bfloat16 on the way count: a program that leaves them out, or rounds other values in their place, can miss the bound.
Values may be sent and summed in bfloat16 or wider, within the bound.
No kernel may reach another device: no remote copies, remote signals or barrier semaphores. Data moves between devices by JAX's collectives and lax.ppermute only.
A program may use at most 192 MiB of HBM per device.

```python
import math
import jax
import jax.numpy as jnp
from jax import lax

D = 768
H = 12
HD = 64
FF = 3072
GA = 14
GB = 24
STEP = 10
A = 196
S = 576
GROUP_FRAMES = 64
VR = 14
PARAMS = 7088640


def patch_grid(key):
    key_small, key_large = jax.random.split(key)
    small_keys = jax.random.split(key_small, GROUP_FRAMES * 2)
    small_perm = jax.vmap(lambda single: jax.random.permutation(single, A))(small_keys)
    small_cells = jnp.pad(small_perm.reshape(GROUP_FRAMES, 2 * A), ((0, 0), (0, S - 2 * A)))
    large_keys = jax.random.split(key_large, GROUP_FRAMES)
    large_cells = jax.vmap(lambda single: jax.random.permutation(single, S))(large_keys)
    rows_all = jnp.stack([small_cells // GA, large_cells // GB]).astype(jnp.int32)
    cols_all = jnp.stack([small_cells % GA, large_cells % GB]).astype(jnp.int32)
    return (rows_all, cols_all)


def draw_patch_row(key, part):
    return patch_grid(key)[0]


def draw_patch_col(key, part):
    return patch_grid(key)[1]


def draw_counts(key, part):
    key = jax.random.fold_in(key, 7)
    key_a, key_b, key_c, key_d = jax.random.split(key, 4)
    small_counts = jax.random.randint(key_a, (GROUP_FRAMES, 2), A // 2, A + 1)
    small_full = jax.random.randint(key_b, (), 0, GROUP_FRAMES)
    small_counts = small_counts.at[small_full, 0].set(A)
    large_counts = jax.random.randint(key_c, (GROUP_FRAMES,), S // 2, S + 1)
    large_full = jax.random.randint(key_d, (), 0, GROUP_FRAMES)
    large_counts = large_counts.at[large_full].set(S)
    large_pair = jnp.stack([large_counts, jnp.zeros_like(large_counts)], axis=1)
    return jnp.stack([small_counts, large_pair]).astype(jnp.int32)


def draw_vectors(key, part):
    key = jax.random.fold_in(key, 13)
    key_a, key_b, key_c, key_d = jax.random.split(key, 4)
    position = jnp.arange(D, dtype=jnp.float32) / (D - 1)
    rising = 0.6 + 1.2 * position
    spread = 0.3 * jax.random.normal(key_a, (VR, D), jnp.float32)
    jitter = jax.random.uniform(key_b, (VR, D), jnp.float32, 0.85, 1.15)
    magnitude = jnp.exp(jax.random.uniform(key_c, (D,), jnp.float32, jnp.log(0.05), 0.0))
    signs = jnp.where(jax.random.bernoulli(key_d, 0.5, (D,)), 1.0, -1.0)
    row_ids = jnp.arange(VR)[:, None]
    gains = rising[None, :] * jitter
    values = jnp.where((row_ids == 0) | (row_ids == 2), gains, spread)
    values = jnp.where(row_ids == 9, (magnitude * signs)[None, :], values)
    return values.astype(jnp.float32)


def draw_cotangent(key, part):
    key = jax.random.fold_in(key, 21)
    key_a, key_b = jax.random.split(key)
    full_shape = (2, GROUP_FRAMES, S, D)
    noise = jnp.clip(jax.random.normal(key_a, full_shape, jnp.float32), -5.5, 5.5)
    common = jnp.clip(jax.random.normal(key_b, (D,), jnp.float32), -4.0, 4.0)
    share = 0.012
    return (noise + share * common).astype(jnp.bfloat16)


def draw_w_qkv(key, part):
    key = jax.random.fold_in(key, 29)
    key_a, key_b = jax.random.split(key)
    entries = jnp.clip(jax.random.normal(key_a, (D, 3 * D), jnp.float32), -4.0, 4.0)
    column_part = jnp.clip(jax.random.normal(key_b, (3 * D,), jnp.float32), -3.0, 3.0)
    return ((entries + 0.3 * column_part[None, :]) * D ** (-0.5)).astype(jnp.float32)


def block_levels(own_key, dims, cuts, low, largest):
    factor_of = 1.0
    for dim, shards_of in cuts:
        heights = jax.random.uniform(jax.random.fold_in(jax.random.fold_in(own_key, 6), dim), (shards_of,), jnp.float32, low / len(cuts), largest / len(cuts))
        factor_of = factor_of * jnp.repeat(jnp.exp(heights), dims[dim] // shards_of).reshape((-1,) + (1,) * (len(dims) - 1 - dim))
    return factor_of


def gaussian(own_key, dims, width, limit, cuts=(), kind=jnp.bfloat16):
    factor_of = block_levels(own_key, dims, cuts, -0.22, 0.18) if cuts else 1.0
    result = jax.random.normal(own_key, dims, jnp.float32) * width * factor_of
    return jnp.minimum(jnp.maximum(result, -limit), limit).astype(kind)


def setup_inputs(seed: int = 0) -> dict:
    seeds = jax.random.split(jax.random.key(seed), 21)
    tokens = gaussian(seeds[0], (2, GROUP_FRAMES, S, D), 1.0, 6.0, ((0, 2), (1, 64)))
    cotangent = draw_cotangent(jax.random.fold_in(seeds[20], 71), 0)
    counts = draw_counts(jax.random.fold_in(seeds[20], 71), 0)
    patch_row = draw_patch_row(jax.random.fold_in(seeds[20], 71), 0)
    patch_col = draw_patch_col(jax.random.fold_in(seeds[20], 71), 0)
    w_qkv = draw_w_qkv(jax.random.fold_in(seeds[20], 71), 0)
    w_proj = gaussian(seeds[6], (D, D), (max(1, 2 * D // S)) ** -0.5, 4.0, ((0, 64),), jnp.float32)
    w_fc1 = gaussian(seeds[7], (D, FF), D ** -0.5, 0.21875, ((0, 64),), jnp.float32)
    w_fc2 = gaussian(seeds[8], (FF, D), FF ** -0.5, 0.109375, ((0, 64),), jnp.float32)
    vectors = draw_vectors(jax.random.fold_in(seeds[20], 71), 0)
    m_qkv = gaussian(seeds[10], (D, 3 * D), (0.105 * PARAMS ** -0.5), 0.00061035156, ((0, 64),), jnp.float32)
    v_qkv = jnp.clip(jnp.exp(math.log(3.2446280329168076e-08) - 1.3776363 * jax.random.uniform(seeds[11], (D, 3 * D), jnp.float32) ** block_levels(seeds[11], (D, 3 * D), ((0, 64),), -0.2, 0.2)), 8.182105659670924e-09, 3.2446280329168076e-08)
    m_proj = gaussian(seeds[12], (D, D), (0.011 * PARAMS ** -0.5), 6.103515625e-05, ((0, 64),), jnp.float32)
    v_proj = jnp.clip(jnp.exp(math.log(3.526769709605304e-10) - 1.3625779 * jax.random.uniform(seeds[13], (D, D), jnp.float32) ** block_levels(seeds[13], (D, D), ((0, 64),), -0.2, 0.2)), 9.028530006949254e-11, 3.526769709605304e-10)
    m_fc1 = gaussian(seeds[14], (D, FF), (0.0072 * PARAMS ** -0.5), 3.814697265625e-05, ((0, 64),), jnp.float32)
    v_fc1 = jnp.clip(jnp.exp(math.log(1.4953503713055483e-10) - 1.36760227 * jax.random.uniform(seeds[15], (D, FF), jnp.float32) ** block_levels(seeds[15], (D, FF), ((0, 64),), -0.2, 0.2)), 3.8089111725758684e-11, 1.4953503713055483e-10)
    m_fc2 = gaussian(seeds[16], (FF, D), (0.0138 * PARAMS ** -0.5), 7.62939453125e-05, ((0, 64),), jnp.float32)
    v_fc2 = jnp.clip(jnp.exp(math.log(5.501760713677584e-10) - 1.3609766 * jax.random.uniform(seeds[17], (FF, D), jnp.float32) ** block_levels(seeds[17], (FF, D), ((0, 64),), -0.2, 0.2)), 1.4107078005753948e-10, 5.501760713677584e-10)
    m_vectors = gaussian(seeds[18], (VR, D), (0.44 * PARAMS ** -0.5), 0.0024414062, ((1, 64),), jnp.float32)
    v_vectors = jnp.clip(jnp.exp(math.log(4.7964067562134e-07) - 1.39812885 * jax.random.uniform(seeds[19], (VR, D), jnp.float32) ** block_levels(seeds[19], (VR, D), ((1, 64),), -0.2, 0.2)), 1.1849945735775691e-07, 4.7964067562134e-07)
    return {"tokens": tokens, "cotangent": cotangent, "counts": counts, "patch_row": patch_row, "patch_col": patch_col, "w_qkv": w_qkv, "w_proj": w_proj, "w_fc1": w_fc1, "w_fc2": w_fc2, "vectors": vectors, "m_qkv": m_qkv, "v_qkv": v_qkv, "m_proj": m_proj, "v_proj": v_proj, "m_fc1": m_fc1, "v_fc1": v_fc1, "m_fc2": m_fc2, "v_fc2": v_fc2, "m_vectors": m_vectors, "v_vectors": v_vectors}


@jax.custom_vjp
def low(v):
    return lax.optimization_barrier(v.astype(jnp.bfloat16)).astype(jnp.float32)

@jax.custom_vjp
def low_back(v):
    return v

def low_keep(v):
    return (low(v), None)

def low_pass(kept, grad):
    return (grad,)

def back_keep(v):
    return (v, None)

def back_low(kept, grad):
    return (low(grad),)
low.defvjp(low_keep, low_pass)
low_back.defvjp(back_keep, back_low)
EPS_NORM = 1e-06
BETA_ONE = 0.9
BETA_TWO = 0.95
ADAM_EPS = 1e-08
DECAY_RATE = 0.05
RATE_VECTOR = 0.8
CLIP_LIMIT = 1.0
HIGH = lax.Precision.HIGHEST

def layer_norm(inputs, gain_vec, shift_vec):
    mean_val = lax.optimization_barrier(jnp.mean(inputs, axis=-1, keepdims=True))
    centred = inputs - mean_val
    variance = lax.optimization_barrier(jnp.mean(centred * centred, axis=-1, keepdims=True))
    return centred * lax.rsqrt(variance + EPS_NORM) * gain_vec + shift_vec

def slot_layout(group_id, counts_pair):
    slot_ids = jnp.arange(S, dtype=jnp.int32)
    image_id = jnp.where(group_id == 0, slot_ids // A, 0).astype(jnp.int32)
    offset = jnp.where(group_id == 0, slot_ids - image_id * A, slot_ids)
    kept_len = jnp.where(image_id == 0, counts_pair[0], counts_pair[1])
    usable = (image_id < 2) & (offset < kept_len)
    return (usable, image_id)

def rotate_pair(values, cosine, sine_val):
    half_dim = values.shape[-1] // 2
    first_half = values[..., :half_dim]
    second_half = values[..., half_dim:]
    return jnp.concatenate([first_half * cosine - second_half * sine_val, first_half * sine_val + second_half * cosine], axis=-1)

def frame_forward(copies, entry_item):
    wqkv_copy, wproj_copy, wfc1_copy, wfc2_copy, vec_copy = copies
    inputs, row_pos, col_pos, group_id, counts_pair = entry_item
    usable, image_id = slot_layout(group_id, counts_pair)
    same_img = (image_id[:, None] == image_id[None, :]) & usable[:, None] & usable[None, :]
    allowed = same_img | jnp.eye(S, dtype=bool)
    hidden_one = low(layer_norm(inputs, vec_copy[0], vec_copy[1]))
    qkv_bias = jnp.concatenate([vec_copy[4], vec_copy[5], vec_copy[6]])
    qkv_proj = low_back(jnp.dot(hidden_one, wqkv_copy, precision=HIGH) + qkv_bias)
    query = qkv_proj[:, :D].reshape(S, H, HD)
    key_rows = qkv_proj[:, D:2 * D].reshape(S, H, HD)
    value_rows = qkv_proj[:, 2 * D:].reshape(S, H, HD)
    freq_col = vec_copy[9, :D // 2].reshape(H, HD // 2)
    freq_row = vec_copy[9, D // 2:].reshape(H, HD // 2)
    angles = col_pos.astype(jnp.float32)[:, None, None] * freq_col[None] + row_pos.astype(jnp.float32)[:, None, None] * freq_row[None]
    cosine = jnp.cos(angles)
    sine_val = jnp.sin(angles)
    query_rot = low(rotate_pair(query, cosine, sine_val))
    key_rot = low(rotate_pair(key_rows, cosine, sine_val))
    value_low = low(value_rows)
    scores = low_back(jnp.einsum('shd,thd->hst', query_rot, key_rot, precision=HIGH) * HD ** (-0.5))
    scores = jnp.where(allowed[None], scores, -1e+30)
    row_max = lax.optimization_barrier(jnp.max(scores, axis=-1, keepdims=True))
    exponent = jnp.exp(scores - row_max)
    attn_prob = low(exponent / lax.optimization_barrier(jnp.sum(exponent, axis=-1, keepdims=True)))
    mixed = jnp.einsum('hst,thd->shd', attn_prob, value_low, precision=HIGH).reshape(S, D)
    mixed = low(low_back(mixed))
    branch = low_back(jnp.dot(mixed, wproj_copy, precision=HIGH) + vec_copy[7])
    after_attn = inputs + branch
    hidden_two = low(layer_norm(after_attn, vec_copy[2], vec_copy[3]))
    up_bias = vec_copy[10:].reshape(FF)
    up_proj = low_back(jnp.dot(hidden_two, wfc1_copy, precision=HIGH) + up_bias)
    activated = low(jax.nn.gelu(up_proj))
    mlp_out = low_back(jnp.dot(activated, wfc2_copy, precision=HIGH) + vec_copy[8])
    return after_attn + mlp_out

def adam_update(master, gradient, first_old, second_old, clip_factor, rate, decay):
    clipped = gradient * clip_factor
    first_new = BETA_ONE * first_old + (1.0 - BETA_ONE) * clipped
    second_new = BETA_TWO * second_old + (1.0 - BETA_TWO) * clipped * clipped
    first_hat = first_new / (1.0 - BETA_ONE ** STEP)
    second_hat = second_new / (1.0 - BETA_TWO ** STEP)
    master_new = master - rate * (first_hat / (jnp.sqrt(second_hat) + ADAM_EPS) + decay * master)
    return (master_new, first_new, second_new)

def reference(tokens, cotangent, counts, patch_row, patch_col, w_qkv, w_proj, w_fc1, w_fc2, vectors, m_qkv, v_qkv, m_proj, v_proj, m_fc1, v_fc1, m_fc2, v_fc2, m_vectors, v_vectors):
    frame_total = 2 * GROUP_FRAMES
    group_ids = jnp.repeat(jnp.arange(2, dtype=jnp.int32), GROUP_FRAMES)
    flat_inputs = tokens.reshape(frame_total, S, D).astype(jnp.float32)
    flat_counts = counts.reshape(frame_total, 2)
    flat_rows = patch_row.reshape(frame_total, S)
    flat_cols = patch_col.reshape(frame_total, S)
    masters = (w_qkv, w_proj, w_fc1, w_fc2, vectors)
    checked = jax.checkpoint(frame_forward)

    def forward(params, inputs):
        copies = tuple((low(param) for param in params))
        return lax.map(lambda entry_item: checked(copies, entry_item), (inputs, flat_rows, flat_cols, group_ids, flat_counts))
    outputs, pullback = jax.vjp(forward, masters, flat_inputs)
    usable_all = jax.vmap(slot_layout)(group_ids, flat_counts)[0]
    grad_seed = cotangent.reshape(frame_total, S, D).astype(jnp.float32) * usable_all[..., None].astype(jnp.float32)
    grad_params, grad_inputs = pullback(grad_seed)
    squares = sum((jnp.sum(piece * piece) for piece in grad_params))
    grad_norm = jnp.sqrt(squares)
    clip_factor = jnp.minimum(1.0, CLIP_LIMIT / (grad_norm + 1e-06))
    firsts = (m_qkv, m_proj, m_fc1, m_fc2, m_vectors)
    seconds = (v_qkv, v_proj, v_fc1, v_fc2, v_vectors)
    step_rates = (D ** (-0.5), max(1, 2 * D // S) ** (-0.5), D ** (-0.5), FF ** (-0.5), RATE_VECTOR)
    results = []
    for index_num in range(5):
        decay = 0.0 if index_num == 4 else DECAY_RATE
        results.append(adam_update(masters[index_num], grad_params[index_num], firsts[index_num], seconds[index_num], clip_factor, step_rates[index_num], decay))
    bias_proj_grad = grad_params[4][7] * clip_factor
    mixed_out = outputs.reshape(2, GROUP_FRAMES, S, D).astype(jnp.bfloat16)
    grad_tokens = grad_inputs.reshape(2, GROUP_FRAMES, S, D)
    return (mixed_out, grad_tokens, grad_norm, results[0][0], results[0][1], results[0][2], results[1][0], results[1][1], results[1][2], results[2][0], results[2][1], results[2][2], results[3][0], results[3][1], results[3][2], results[4][0], results[4][1], results[4][2], bias_proj_grad)
```

```python
import functools

import jax
import jax.numpy as jnp
from jax import lax
from jax.experimental import pallas as pl
from jax.experimental.pallas import tpu as pltpu
from jax.sharding import PartitionSpec as P

D = 768
H = 12
HD = 64
FF = 3072
STEP = 10
A = 196
S = 576

CORES = 2
HC = H // CORES
DC = D // CORES
FC = FF // CORES
PAIRS = HC // 2
T = CORES * S

WIN = 208
WINDOWS = (0, 192)

EPS_NORM = 1e-06
BETA_ONE = 0.9
BETA_TWO = 0.95
ADAM_EPS = 1e-08
DECAY_RATE = 0.05
RATE_VECTOR = 0.8
CLIP_LIMIT = 1.0
NEG = -1e30

bf16 = jnp.bfloat16
f32 = jnp.float32
VMEM_LIMIT = 56 * 1024 * 1024


def params(**kw):
    return pltpu.CompilerParams(vmem_limit_bytes=VMEM_LIMIT, **kw)


def cost(flops, bytes_accessed, transcendentals=0):
    return pl.CostEstimate(
        flops=int(flops), bytes_accessed=int(bytes_accessed), transcendentals=int(transcendentals)
    )


def dot(a, b):
    return jnp.dot(a, b, preferred_element_type=f32)


def dot_t(a, b):
    return lax.dot_general(a, b, (((1,), (1,)), ((), ())), preferred_element_type=f32)


def t_dot(a, b):
    return lax.dot_general(a, b, (((0,), (0,)), ((), ())), preferred_element_type=f32)


def stats(z):
    mean_val = jnp.mean(z, axis=-1, keepdims=True)
    centred = z - mean_val
    variance = jnp.mean(centred * centred, axis=-1, keepdims=True)
    inv_std = lax.rsqrt(variance + EPS_NORM)
    return centred * inv_std, inv_std


def norm_back(grad, normed, inv_std, gain):
    e = grad * gain
    return inv_std * (
        e
        - jnp.mean(e, axis=-1, keepdims=True)
        - normed * jnp.mean(e * normed, axis=-1, keepdims=True)
    )


def swap_halves(u):
    lanes = u.shape[1]
    lane = lax.broadcasted_iota(jnp.int32, u.shape, 1)
    up = pltpu.roll(u, lanes - HD // 2, 1)
    down = pltpu.roll(u, HD // 2, 1)
    return jnp.where((lane & (HD - 1)) < HD // 2, up, down)


def qkv_kernel(h_ref, w_ref, b_ref, cos_ref, sin_ref, q_ref, k_ref, v_ref):
    cosine = cos_ref[...]
    sine = sin_ref[...]
    acc = dot(h_ref[...], w_ref[...]) + b_ref[...]
    q = acc[:, :DC]
    k = acc[:, DC : 2 * DC]
    q_ref[...] = ((q * cosine + swap_halves(q) * sine) * HD ** (-0.5)).astype(bf16)
    k_ref[...] = (k * cosine + swap_halves(k) * sine).astype(bf16)
    v_ref[...] = acc[:, 2 * DC :].astype(bf16)


def qkv_call(h1, w, bias, cosine, sine):
    rows = 288
    tile = lambda n: pl.BlockSpec((rows, n), lambda i: (i, 0))
    whole = lambda a: pl.BlockSpec(a.shape, lambda i: (0,) * a.ndim)
    return pl.pallas_call(
        qkv_kernel,
        grid=(T // rows,),
        in_specs=[tile(D), whole(w), whole(bias), tile(DC), tile(DC)],
        out_specs=[tile(DC)] * 3,
        out_shape=[jax.ShapeDtypeStruct((T, DC), bf16)] * 3,
        compiler_params=params(),
        cost_estimate=cost(2 * T * D * 3 * DC, T * D * 2 + D * 3 * DC * 2 + T * DC * 14),
    )(h1, w, bias, cosine, sine)


def softmax_head(q, k, v, mine, bias):
    s = dot_t(jnp.where(mine, q, jnp.zeros_like(q)), k) + bias
    e = jnp.exp(s - jnp.max(s, axis=-1, keepdims=True))
    p = e * (1.0 / jnp.sum(e, axis=-1, keepdims=True))
    return p


def attn_fwd_kernel(
    core_ref, q0, k0, v0, q1, k1, v1, use0, use1, bias0, bias1, own0, o0_ref, o1_ref, p0_ref, p1_ref
):
    lane = lax.broadcasted_iota(jnp.int32, (1, 2 * HD), 1)
    low = lane < HD
    q, k, v = q1[0], k1[0], v1[0]
    mixes = []
    for head, mine in ((0, low), (1, ~low)):
        p = softmax_head(q, k, v, mine, bias1[...]).astype(bf16)
        p1_ref[head] = p
        mixes.append(dot(p, v))
    mix = jnp.where(low, mixes[0], mixes[1])
    o1_ref[0] = jnp.where(use1[...] > 0, mix, v.astype(f32)).astype(bf16)
    o0_ref[0] = v0[0]
    for win, base in enumerate(WINDOWS):
        q, k, v = (r[0, base : base + WIN, :] for r in (q0, k0, v0))
        own = own0[win]
        mixes = []
        for head, mine in ((0, low), (1, ~low)):
            p = softmax_head(q, k, v, mine, bias0[win])
            p = (p * own).astype(bf16)
            p0_ref[head, win] = p
            mixes.append(dot(p, v))
        mix = jnp.where(low, mixes[0], mixes[1])
        use = (own * use0[base : base + WIN, :]) > 0
        before = o0_ref[0, base : base + WIN, :].astype(f32)
        o0_ref[0, base : base + WIN, :] = jnp.where(use, mix, before).astype(bf16)


def attn_fwd_call(core, q, k, v, masks):
    use0, use1, bias0, bias1, own0 = masks
    block = lambda g: pl.BlockSpec((1, S, 2 * HD), lambda p, c: (g ^ c[0], 0, p))
    whole = lambda a: pl.BlockSpec(a.shape, lambda p, c: (0,) * a.ndim)
    q, k, v = (a.reshape(CORES, S, DC) for a in (q, k, v))
    return pl.pallas_call(
        attn_fwd_kernel,
        grid_spec=pltpu.PrefetchScalarGridSpec(
            num_scalar_prefetch=1,
            grid=(PAIRS,),
            in_specs=[block(0)] * 3 + [block(1)] * 3 + [whole(a) for a in masks],
            out_specs=[
                pl.BlockSpec((1, S, 2 * HD), lambda p, c: (0, 0, p)),
                pl.BlockSpec((1, S, 2 * HD), lambda p, c: (0, 0, p)),
                pl.BlockSpec((2, 2, WIN, WIN), lambda p, c: (p, 0, 0, 0)),
                pl.BlockSpec((2, S, S), lambda p, c: (p, 0, 0)),
            ],
        ),
        out_shape=[
            jax.ShapeDtypeStruct((1, S, DC), bf16),
            jax.ShapeDtypeStruct((1, S, DC), bf16),
            jax.ShapeDtypeStruct((HC, 2, WIN, WIN), bf16),
            jax.ShapeDtypeStruct((HC, S, S), bf16),
        ],
        compiler_params=params(),
        cost_estimate=cost(4 * HC * (S * S + 2 * WIN * WIN) * 128, 12e6, HC * S * S),
    )(core, q, k, v, q, k, v, *masks)


def proj_kernel(core_ref, mix_ref, x_ref, w_ref, v_ref, after_ref, h2_ref):
    branch = dot(mix_ref[...], w_ref[...])
    after = x_ref[...].astype(f32) + (branch + v_ref[7:8, :])
    after_ref[...] = after
    normed, _ = stats(after)
    h2_ref[...] = (normed * v_ref[2:3, :] + v_ref[3:4, :]).astype(bf16)


def proj_call(core, mix, x, w, vec):
    rows = 288
    tile = lambda n: pl.BlockSpec((rows, n), lambda i, c: (i, 0))
    whole = lambda a: pl.BlockSpec(a.shape, lambda i, c: (0,) * a.ndim)
    return pl.pallas_call(
        proj_kernel,
        grid_spec=pltpu.PrefetchScalarGridSpec(
            num_scalar_prefetch=1,
            grid=(T // rows,),
            in_specs=[tile(D), tile(D), whole(w), whole(vec)],
            out_specs=[tile(D), tile(D)],
        ),
        out_shape=[jax.ShapeDtypeStruct((T, D), f32), jax.ShapeDtypeStruct((T, D), bf16)],
        compiler_params=params(),
        cost_estimate=cost(2 * T * D * D, T * D * 10 + D * D * 2),
    )(core, mix, x, w, vec)


FT = 384
MT = 192
K0 = (2.0 / 3.141592653589793) ** 0.5


def mlp_kernel(
    h2_ref, gy_ref, w1_ref, w2_ref, b1_ref, mlp_ref, gh2_ref, gh2b_ref, gw1_ref, gw2_ref, gb1_ref, act_s, gup_s
):
    step = pl.program_id(0)
    first = step == 0
    w1 = w1_ref[...]
    w2 = w2_ref[...]
    bias = b1_ref[...]

    @pl.when(first)
    def _():
        mlp_ref[...] = jnp.zeros_like(mlp_ref)
        gh2_ref[...] = jnp.zeros_like(gh2_ref)

    def rows(i, total):
        at = pl.ds(pl.multiple_of(i * MT, MT), MT)
        gy = gy_ref[at, :]
        up = dot(h2_ref[at, :], w1) + bias
        sq = up * up
        th = jnp.tanh(K0 * (up + 0.044715 * (sq * up)))
        half = 0.5 * (1.0 + th)
        act = (up * half).astype(bf16)
        slope = half + 0.5 * up * (1.0 - th * th) * (K0 * (1.0 + 3 * 0.044715 * sq))
        gup = (dot_t(gy, w2) * slope).astype(bf16)
        act_s[at, :] = act
        gup_s[at, :] = gup
        mlp_ref[at, :] += dot(act, w2)
        gh2_ref[at, :] += dot_t(gup, w1)
        return total + jnp.sum(gup.astype(f32), axis=0, keepdims=True)

    gb1_ref[...] = lax.fori_loop(0, T // MT, rows, jnp.zeros((1, FT), f32))
    gw2_ref[...] = t_dot(act_s[...], gy_ref[...]).astype(bf16)
    gw1_ref[...] = t_dot(h2_ref[...], gup_s[...]).astype(bf16)

    @pl.when(step == FC // FT - 1)
    def _():
        gh2b_ref[...] = gh2_ref[...].astype(bf16)


def mlp_call(h2, gy, w1, w2, b1):
    whole = lambda a: pl.BlockSpec(a.shape, lambda i: (0,) * a.ndim)
    keep = pl.BlockSpec((T, D), lambda i: (0, 0))
    return pl.pallas_call(
        mlp_kernel,
        grid=(FC // FT,),
        in_specs=[
            whole(h2),
            whole(gy),
            pl.BlockSpec((D, FT), lambda i: (0, i)),
            pl.BlockSpec((FT, D), lambda i: (i, 0)),
            pl.BlockSpec((1, FT), lambda i: (0, i)),
        ],
        out_specs=[
            keep,
            keep,
            keep,
            pl.BlockSpec((D, FT), lambda i: (0, i)),
            pl.BlockSpec((FT, D), lambda i: (i, 0)),
            pl.BlockSpec((1, FT), lambda i: (0, i)),
        ],
        out_shape=[
            jax.ShapeDtypeStruct((T, D), f32),
            jax.ShapeDtypeStruct((T, D), f32),
            jax.ShapeDtypeStruct((T, D), bf16),
            jax.ShapeDtypeStruct((D, FC), bf16),
            jax.ShapeDtypeStruct((FC, D), bf16),
            jax.ShapeDtypeStruct((1, FC), f32),
        ],
        scratch_shapes=[pltpu.VMEM((T, FT), bf16), pltpu.VMEM((T, FT), bf16)],
        compiler_params=params(),
        cost_estimate=cost(12 * T * D * FC, 30e6, T * FC),
    )(h2, gy, w1, w2, b1)


def mid_kernel(core_ref, after_ref, gy_ref, gh2_ref, other_ref, v_ref, ga_ref, gab_ref, sums_ref):
    i = pl.program_id(0)
    normed, inv_std = stats(after_ref[...])
    gh2 = gh2_ref[...] + other_ref[...].astype(f32)
    gy = gy_ref[...].astype(f32)
    ga = gy + norm_back(gh2, normed, inv_std, v_ref[2:3, :])
    gab = ga.astype(bf16)
    ga_ref[...] = ga
    gab_ref[...] = gab

    @pl.when(i == 0)
    def _():
        sums_ref[...] = jnp.zeros_like(sums_ref)

    @pl.when(i < S // 288)
    def _():
        sums_ref[0:1, :] += jnp.sum(gh2 * normed, axis=0, keepdims=True)
        sums_ref[1:2, :] += jnp.sum(gh2, axis=0, keepdims=True)
        sums_ref[2:3, :] += jnp.sum(gab.astype(f32), axis=0, keepdims=True)
        sums_ref[3:4, :] += jnp.sum(gy, axis=0, keepdims=True)


def mid_call(core, after, gy, gh2, other, vec):
    rows = 288
    half = S // rows
    tile = lambda n: pl.BlockSpec((rows, n), lambda i, c: (i, 0))
    flipped = pl.BlockSpec((rows, D), lambda i, c: ((i + half) % (2 * half), 0))
    whole = lambda a: pl.BlockSpec(a.shape, lambda i, c: (0,) * a.ndim)
    return pl.pallas_call(
        mid_kernel,
        grid_spec=pltpu.PrefetchScalarGridSpec(
            num_scalar_prefetch=1,
            grid=(T // rows,),
            in_specs=[tile(D), tile(D), tile(D), flipped, whole(vec)],
            out_specs=[tile(D), tile(D), pl.BlockSpec((8, D), lambda i, c: (0, 0))],
        ),
        out_shape=[
            jax.ShapeDtypeStruct((T, D), f32),
            jax.ShapeDtypeStruct((T, D), bf16),
            jax.ShapeDtypeStruct((8, D), f32),
        ],
        compiler_params=params(),
        cost_estimate=cost(30 * T * D, T * D * 18),
    )(core, after, gy, gh2, other, vec)


def proj_back_kernel(core_ref, ga_ref, cols_ref, mix_ref, w_ref, gmix_ref, gw_ref):
    gmix_ref[...] = dot_t(ga_ref[...], w_ref[...]).astype(bf16)
    gw_ref[...] = t_dot(mix_ref[...], cols_ref[...]).astype(bf16)


def proj_back_call(core, ga, mix, w):
    whole = lambda a: pl.BlockSpec(a.shape, lambda i, c: (0,) * a.ndim)
    return pl.pallas_call(
        proj_back_kernel,
        grid_spec=pltpu.PrefetchScalarGridSpec(
            num_scalar_prefetch=1,
            grid=(1,),
            in_specs=[
                whole(ga),
                pl.BlockSpec((T, DC), lambda i, c: (0, c[0])),
                whole(mix),
                pl.BlockSpec((DC, D), lambda i, c: (c[0], 0)),
            ],
            out_specs=[
                pl.BlockSpec((T, DC), lambda i, c: (0, 0)),
                pl.BlockSpec((D, DC), lambda i, c: (0, 0)),
            ],
        ),
        out_shape=[jax.ShapeDtypeStruct((T, DC), bf16), jax.ShapeDtypeStruct((D, DC), bf16)],
        compiler_params=params(),
        cost_estimate=cost(4 * T * D * DC, T * D * 6 + D * D * 2),
    )(core, ga, ga, mix, w)


def back_head(q_t, k, v, do, do_t, delta, p, mine, head):
    gp = dot_t(jnp.where(mine, do, jnp.zeros_like(do)), v)
    gs = (p.astype(f32) * (gp - delta)).astype(bf16)
    at = slice(head * HD, (head + 1) * HD)
    return dot(gs, k), dot(q_t[at, :], gs), dot(do_t[at, :], p)


def deltas(do, o, low):
    prod = do.astype(f32) * o.astype(f32)
    d0 = jnp.sum(jnp.where(low, prod, 0.0), axis=-1, keepdims=True)
    d1 = jnp.sum(jnp.where(low, 0.0, prod), axis=-1, keepdims=True)
    return d0, d1


def attn_bwd_kernel(
    core_ref,
    q0, k0, v0, do0, o0, p0, cos0, sin0, pos0,
    q1, k1, v1, do1, o1, p1, cos1, sin1, pos1,
    h1t_ref, w_ref,
    gw_ref, gh_ref, sums_ref,
    gq_s, gk_s, gv_s, gqkv_s,
):
    lane = lax.broadcasted_iota(jnp.int32, (1, 2 * HD), 1)
    low = lane < HD
    pair = pl.program_id(0)

    def finish(frame, q, k, cos_ref, sin_ref, pos_ref):
        cosine, sine = cos_ref[0], sin_ref[0]
        gq = gq_s[...] * HD ** (-0.5)
        gk = gk_s[...]
        sq, sk = swap_halves(gq), swap_halves(gk)
        turn = (q.astype(f32) * HD**0.5) * sq + k.astype(f32) * sk
        gq = (gq * cosine - sq * sine).astype(bf16)
        gk = (gk * cosine - sk * sine).astype(bf16)
        gv = gv_s[...].astype(bf16)
        gqkv_s[frame, :, : 2 * HD] = gq
        gqkv_s[frame, :, 2 * HD : 4 * HD] = gk
        gqkv_s[frame, :, 4 * HD :] = gv
        pos = pos_ref[0]
        col = jnp.sum(turn * pos[:, 0:1], axis=0, keepdims=True)
        row = jnp.sum(turn * pos[:, 1:2], axis=0, keepdims=True)
        bias = [jnp.sum(g.astype(f32), axis=0, keepdims=True) for g in (gq, gk, gv)]
        return jnp.concatenate([col, row] + bias, axis=0)

    q, k, v, do = q1[0], k1[0], v1[0], do1[0]
    d = deltas(do, o1[0], low)
    q_t, do_t = q.astype(f32).T.astype(bf16), do.astype(f32).T.astype(bf16)
    out = [
        back_head(q_t, k, v, do, do_t, d[head], p1[head], mine, head)
        for head, mine in ((0, low), (1, ~low))
    ]
    gq_s[...] = jnp.where(low, out[0][0], out[1][0])
    gk_s[...] = jnp.concatenate([out[0][1], out[1][1]], axis=0).T
    gv_s[...] = jnp.concatenate([out[0][2], out[1][2]], axis=0).T
    sums1 = finish(1, q, k, cos1, sin1, pos1)
    gq_s[...] = jnp.zeros_like(gq_s)
    gk_s[...] = jnp.zeros_like(gk_s)
    gv_s[...] = jnp.zeros_like(gv_s)
    for win, base in enumerate(WINDOWS):
        at = pl.ds(base, WIN)
        q, k, v, do, o = (r[0, at, :] for r in (q0, k0, v0, do0, o0))
        d = deltas(do, o, low)
        q_t, do_t = q.astype(f32).T.astype(bf16), do.astype(f32).T.astype(bf16)
        out = [
            back_head(q_t, k, v, do, do_t, d[head], p0[head, win], mine, head)
            for head, mine in ((0, low), (1, ~low))
        ]
        gq_s[at, :] += jnp.where(low, out[0][0], out[1][0])
        gk_s[at, :] += jnp.concatenate([out[0][1], out[1][1]], axis=0).T
        gv_s[at, :] += jnp.concatenate([out[0][2], out[1][2]], axis=0).T
    sums0 = finish(0, q0[0], k0[0], cos0, sin0, pos0)
    sums_ref[0, 0:5, :] = sums0 + sums1
    sums_ref[0, 5:8, :] = jnp.zeros((3, 2 * HD), f32)

    @pl.when(pair == 0)
    def _():
        gh_ref[...] = jnp.zeros_like(gh_ref)

    gw = jnp.zeros((D, 6 * HD), f32)
    for frame in range(CORES):
        rel = frame ^ core_ref[0]
        g = gqkv_s[frame]
        gw += dot(h1t_ref[rel], g)
        gh_ref[rel] += dot_t(g, w_ref[0])
    gw_ref[0] = gw.astype(bf16)


def attn_bwd_call(core, q, k, v, do, o0, o1, p0, p1, cosine, sine, pos, h1t, w):
    q, k, v, do, cosine, sine = (a.reshape(CORES, S, DC) for a in (q, k, v, do, cosine, sine))
    block = lambda g: pl.BlockSpec((1, S, 2 * HD), lambda p, c: (g ^ c[0], 0, p))
    own = pl.BlockSpec((1, S, 2 * HD), lambda p, c: (0, 0, p))
    at = lambda g: pl.BlockSpec((1, S, 2), lambda p, c: (g ^ c[0], 0, 0))
    whole = lambda a: pl.BlockSpec(a.shape, lambda p, c: (0,) * a.ndim)
    return pl.pallas_call(
        attn_bwd_kernel,
        grid_spec=pltpu.PrefetchScalarGridSpec(
            num_scalar_prefetch=1,
            grid=(PAIRS,),
            in_specs=[block(0)] * 4
            + [own, pl.BlockSpec((2, 2, WIN, WIN), lambda p, c: (p, 0, 0, 0))]
            + [block(0)] * 2
            + [at(0)]
            + [block(1)] * 4
            + [own, pl.BlockSpec((2, S, S), lambda p, c: (p, 0, 0))]
            + [block(1)] * 2
            + [at(1)]
            + [whole(h1t), pl.BlockSpec((1, D, 6 * HD), lambda p, c: (p, 0, 0))],
            out_specs=[
                pl.BlockSpec((1, D, 6 * HD), lambda p, c: (p, 0, 0)),
                pl.BlockSpec((CORES, S, D), lambda p, c: (0, 0, 0)),
                pl.BlockSpec((1, 8, 2 * HD), lambda p, c: (p, 0, 0)),
            ],
            scratch_shapes=[pltpu.VMEM((S, 2 * HD), f32)] * 3 + [pltpu.VMEM((CORES, S, 6 * HD), bf16)],
        ),
        out_shape=[
            jax.ShapeDtypeStruct((PAIRS, D, 6 * HD), bf16),
            jax.ShapeDtypeStruct((CORES, S, D), f32),
            jax.ShapeDtypeStruct((PAIRS, 8, 2 * HD), f32),
        ],
        compiler_params=params(),
        cost_estimate=cost(10 * HC * S * S * 128 + 4 * T * D * 3 * DC, 30e6),
    )(
        core,
        q, k, v, do, o0, p0, cosine, sine, pos,
        q, k, v, do, o1, p1, cosine, sine, pos,
        h1t, w,
    )


def last_kernel(x_ref, ga_ref, gh_ref, other_ref, v_ref, gt_ref, sums_ref):
    normed, inv_std = stats(x_ref[...].astype(f32))
    gh = gh_ref[...] + other_ref[...]
    gt_ref[...] = ga_ref[...] + norm_back(gh, normed, inv_std, v_ref[0:1, :])

    @pl.when(pl.program_id(0) == 0)
    def _():
        sums_ref[...] = jnp.zeros_like(sums_ref)

    sums_ref[0:1, :] += jnp.sum(gh * normed, axis=0, keepdims=True)
    sums_ref[1:2, :] += jnp.sum(gh, axis=0, keepdims=True)


def last_call(x, ga, gh, other, vec):
    rows = 288
    tile = lambda n: pl.BlockSpec((rows, n), lambda i: (i, 0))
    return pl.pallas_call(
        last_kernel,
        grid=(S // rows,),
        in_specs=[tile(D)] * 4 + [pl.BlockSpec(vec.shape, lambda i: (0, 0))],
        out_specs=[tile(D), pl.BlockSpec((8, D), lambda i: (0, 0))],
        out_shape=[jax.ShapeDtypeStruct((S, D), f32), jax.ShapeDtypeStruct((8, D), f32)],
        compiler_params=params(),
        cost_estimate=cost(25 * S * D, S * D * 14),
    )(x, ga, gh, other, vec)


def adam_update(master, gradient, first_old, second_old, clip_factor, rate, decay):
    clipped = gradient * clip_factor
    first_new = BETA_ONE * first_old + (1.0 - BETA_ONE) * clipped
    second_new = BETA_TWO * second_old + (1.0 - BETA_TWO) * clipped * clipped
    first_hat = first_new / (1.0 - BETA_ONE**STEP)
    second_hat = second_new / (1.0 - BETA_TWO**STEP)
    master_new = master - rate * (first_hat / (jnp.sqrt(second_hat) + ADAM_EPS) + decay * master)
    return (master_new, first_new, second_new)


RATES = (D ** (-0.5), max(1, 2 * D // S) ** (-0.5), D ** (-0.5), FF ** (-0.5), RATE_VECTOR)


def local(
    chips,
    tokens,
    cotangent,
    counts,
    patch_row,
    patch_col,
    w_qkv,
    w_proj,
    w_fc1,
    w_fc2,
    vectors,
    m_qkv,
    v_qkv,
    m_proj,
    v_proj,
    m_fc1,
    v_fc1,
    m_fc2,
    v_fc2,
    m_vectors,
    v_vectors,
):
    core = lax.axis_index("grp")
    core_arr = core.astype(jnp.int32).reshape(1)
    first_core = core == 0
    kr = D // chips
    fr = FC // chips
    vr = vectors.shape[0]

    def swap(a):
        return lax.ppermute(a, "grp", [(0, 1), (1, 0)])

    def gather(share):
        return lax.all_to_all(jnp.broadcast_to(share[None], (chips,) + share.shape), "dp", 0, 0)

    def scatter_sum(whole):
        return jnp.sum(lax.all_to_all(whole, "dp", 0, 0).astype(f32), axis=0)

    def halves(a):
        n = a.shape[-1] // 2
        return jnp.where(first_core, a[..., :n], a[..., n:])

    vec_b = gather(vectors.astype(bf16))
    vec = vec_b.transpose(1, 0, 2).reshape(vr, D).astype(f32)
    qkv_b = w_qkv.astype(bf16)
    parts = [halves(qkv_b[:, i * D : (i + 1) * D]) for i in range(3)]
    share_qkv = jnp.concatenate(parts, axis=1)
    full_qkv = gather(share_qkv).reshape(D, 3 * DC)
    full_proj = gather(w_proj.astype(bf16)).reshape(D, D)
    fc1_b = w_fc1.astype(bf16).reshape(kr, chips, CORES, fr)
    share_fc1 = jnp.where(first_core, fc1_b[:, :, 0], fc1_b[:, :, 1]).reshape(kr, FC)
    full_fc1 = gather(share_fc1).reshape(D, FC)
    fc2_b = w_fc2.astype(bf16)
    share_fc2 = jnp.where(first_core, fc2_b[:fr], fc2_b[fr:])
    full_fc2 = gather(share_fc2).reshape(FC, D)

    x_own = tokens.reshape(S, D)
    cot_own = cotangent.reshape(S, D)
    ints = jnp.concatenate(
        [patch_row.reshape(1, S), patch_col.reshape(1, S), jnp.pad(counts.reshape(1, 2), ((0, 0), (0, S - 2)))]
    )
    ints = jnp.stack([ints, swap(ints)])
    x_all = jnp.concatenate([x_own, swap(x_own)])
    counts_own, counts_other = ints[0, 2, :2], ints[1, 2, :2]
    counts0 = jnp.where(first_core, counts_own, counts_other)
    counts1 = jnp.where(first_core, counts_other, counts_own)
    slot = jnp.arange(S, dtype=jnp.int32)
    image = slot // A
    kept = jnp.where(image == 0, counts0[0], counts0[1])
    usable0 = (image < 2) & (slot - A * image < kept)
    usable1 = slot < counts1[0]
    usable = jnp.where(
        first_core, jnp.stack([usable0, usable1]), jnp.stack([usable1, usable0])
    )
    use0 = usable0.astype(f32)[:, None]
    use1 = usable1.astype(f32)[:, None]
    bias1 = jnp.where(usable1, 0.0, NEG).astype(f32)[None]
    bias0, own0 = [], []
    for win, base in enumerate(WINDOWS):
        inside = image[base : base + WIN] == win
        bias0.append(jnp.where(usable0[base : base + WIN] & inside, 0.0, NEG).astype(f32)[None])
        own0.append(inside.astype(f32)[:, None])
    bias0, own0 = jnp.stack(bias0), jnp.stack(own0)
    masks = (use0, use1, bias0, bias1, own0)
    cot_all = jnp.concatenate([cot_own, swap(cot_own)])
    gy = jnp.where(usable.reshape(T, 1), cot_all, jnp.zeros_like(cot_all))

    pos = jnp.stack([ints[:, 1], ints[:, 0]], axis=-1).astype(f32)

    def my_freq(a):
        a = halves(a).reshape(HC, 1, HD // 2)
        return jnp.broadcast_to(a, (HC, 2, HD // 2)).reshape(1, DC)

    flat = pos.reshape(T, 2)
    angle = flat[:, 0:1] * my_freq(vec[9, : D // 2]) + flat[:, 1:2] * my_freq(vec[9, D // 2 :])
    sign = jnp.where((jnp.arange(DC) & (HD - 1)) < HD // 2, -1.0, 1.0).astype(f32)[None]
    cosine = jnp.cos(angle)
    sine = jnp.sin(angle) * sign
    normed, _ = stats(x_all.astype(f32))
    h1 = (normed * vec[0:1] + vec[1:2]).astype(bf16)
    h1t = h1.reshape(CORES, S, D).transpose(0, 2, 1)
    bias_qkv = jnp.concatenate([halves(vec[4 + i : 5 + i]) for i in range(3)], axis=1)

    q, k, v = qkv_call(h1, full_qkv, bias_qkv, cosine, sine)
    o0, o1, p0, p1 = attn_fwd_call(core_arr, q, k, v, masks)
    mix_mine = jnp.concatenate([jnp.where(first_core, o0, o1), jnp.where(first_core, o1, o0)]).reshape(T, DC)
    mix_other = swap(mix_mine)
    mix_other = jnp.concatenate([mix_other[S:], mix_other[:S]])
    mix = jnp.concatenate(
        [jnp.where(first_core, mix_mine, mix_other), jnp.where(first_core, mix_other, mix_mine)], axis=1
    )
    after, h2 = proj_call(core_arr, mix, x_all, full_proj, vec)
    b1 = vec[10:].reshape(chips, CORES, fr)
    b1 = jnp.where(first_core, b1[:, 0], b1[:, 1]).reshape(1, FC)
    mlp, gh2, gh2b, gw1, gw2, gb1 = mlp_call(h2, gy, full_fc1, full_fc2, b1)
    mixed = (after[:S] + (mlp[:S] + swap(mlp[S:]) + vec[8:9])).astype(bf16)

    other_gh2 = swap(gh2b)
    ga, gab, sums_mid = mid_call(core_arr, after, gy, gh2, other_gh2, vec)
    gmix, gwp = proj_back_call(core_arr, gab, mix, full_proj)
    w_pairs = full_qkv.reshape(D, 3, PAIRS, 2 * HD).transpose(2, 0, 1, 3).reshape(PAIRS, D, 6 * HD)
    gwq, gh1, sums_att = attn_bwd_call(
        core_arr, q, k, v, gmix, o0, o1, p0, p1, cosine, sine, pos, h1t, w_pairs
    )
    other_gh1 = swap(gh1[1])
    gt, sums_last = last_call(x_own, ga[:S], gh1[0], other_gh1, vec)

    g_fc2 = scatter_sum(gw2.reshape(chips, fr, D))
    g_fc1 = scatter_sum(gw1.reshape(chips, kr, FC))
    g_proj = scatter_sum(gwp.reshape(chips, kr, DC))
    g_qkv = [scatter_sum(gwq[p].reshape(chips, kr, 6 * HD)) for p in range(PAIRS)]
    g_qkv = jnp.stack(g_qkv, axis=1).reshape(kr, PAIRS, 3, 2 * HD).transpose(0, 2, 1, 3).reshape(kr, 3 * DC)

    def place(a, axis=-1):
        zero = jnp.zeros_like(a)
        return jnp.concatenate([jnp.where(first_core, a, zero), jnp.where(first_core, zero, a)], axis=axis)

    sums_att = sums_att.transpose(1, 0, 2).reshape(8, DC)
    turn = (sums_att[:2] * -sign).reshape(2, HC, 2, HD // 2).sum(axis=2).reshape(2, DC // 2)
    freq = place(turn).reshape(1, D)
    bias_sums = place(sums_att[2:5])
    gb1 = gb1.reshape(chips, 1, fr)
    gb1 = place(gb1, axis=1).reshape(vr - 10, D)
    g_vec = jnp.concatenate(
        [sums_last[0:2], sums_mid[0:2], bias_sums, sums_mid[2:4], freq, gb1], axis=0
    )
    g_vec = scatter_sum(g_vec.reshape(vr, chips, D // chips).transpose(1, 0, 2))

    def pieces(a):
        b = swap(a)
        return jnp.where(first_core, a, b), jnp.where(first_core, b, a)

    qkv_a, qkv_b = pieces(g_qkv)
    g_qkv = jnp.stack([qkv_a.reshape(kr, 3, DC), qkv_b.reshape(kr, 3, DC)], axis=2).reshape(kr, 3 * D)
    g_proj = jnp.concatenate(pieces(g_proj), axis=1)
    fc1_a, fc1_b = pieces(g_fc1)
    g_fc1 = jnp.stack([fc1_a.reshape(kr, chips, fr), fc1_b.reshape(kr, chips, fr)], axis=2).reshape(kr, FF)
    g_fc2 = jnp.concatenate(pieces(g_fc2), axis=0)
    g_vec = g_vec + swap(g_vec)

    shards = (g_qkv, g_proj, g_fc1, g_fc2, g_vec)
    squares = sum(jnp.sum(g * g) for g in shards)
    total = jnp.sum(gather(jnp.full((8, 128), squares, f32))[:, 0, 0])
    grad_norm = jnp.sqrt(total)
    clip_factor = jnp.minimum(1.0, CLIP_LIMIT / (grad_norm + 1e-06))
    masters = (w_qkv, w_proj, w_fc1, w_fc2, vectors)
    firsts = (m_qkv, m_proj, m_fc1, m_fc2, m_vectors)
    seconds = (v_qkv, v_proj, v_fc1, v_fc2, v_vectors)
    updates = []
    for i in range(5):
        updates.extend(
            adam_update(
                masters[i], shards[i], firsts[i], seconds[i], clip_factor, RATES[i], 0.0 if i == 4 else DECAY_RATE
            )
        )
    return (mixed.reshape(1, 1, S, D), gt.reshape(1, 1, S, D), grad_norm, *updates, g_vec[7] * clip_factor)


def solution(mesh):
    frame = P("grp", "dp", None, None)
    ints = P("grp", "dp", None)
    rows = P("dp", None)
    cols = P(None, "dp")
    return jax.shard_map(
        functools.partial(local, mesh.shape["dp"]),
        mesh=mesh,
        in_specs=(frame, frame, ints, ints, ints, rows, rows, rows, rows, cols) + (rows,) * 8 + (cols,) * 2,
        out_specs=(frame, frame, P()) + (rows,) * 12 + (cols,) * 3 + (P("dp"),),
        check_vma=False,
    )
```

```python
import jax
import jax.numpy as jnp
from jax import lax
from jax.experimental import pallas as pl
from jax.experimental.pallas import tpu as pltpu
from jax.sharding import PartitionSpec as P

D = 768
H = 12
HD = 64
FF = 3072
STEP = 10
A = 196
S = 576

CORES = 2
HC = H // CORES
DC = D // CORES
FC = FF // CORES
PAIRS = HC // 2
T = CORES * S

WIN = 208
WINDOWS = (0, 192)

EPS_NORM = 1e-06
BETA_ONE = 0.9
BETA_TWO = 0.95
ADAM_EPS = 1e-08
DECAY_RATE = 0.05
RATE_VECTOR = 0.8
CLIP_LIMIT = 1.0
NEG = -1e30

bf16 = jnp.bfloat16
f32 = jnp.float32
VMEM_LIMIT = 56 * 1024 * 1024


SIDE = 4
CHIPS = SIDE**3
PLANE = SIDE * SIDE
KR = D // CHIPS
FR = FC // CHIPS
BLOCK = SIDE * KR
QUARTER = PLANE * KR
BOTH = ("grp", "dp")


def device(core, x, y, z):
    return ((core * SIDE + x) * SIDE + y) * SIDE + z


def lines():
    r = range(SIDE)
    return [[device(0, a, g, z) for a in r] for g in r for z in r] + [
        [device(1, g, a, z) for a in r] for g in r for z in r
    ]


def planes():
    r = range(SIDE)
    return [[device(0, a, g, z) for g in r for z in r] for a in r] + [
        [device(1, g, a, z) for g in r for z in r] for a in r
    ]


def shift(value, d):
    pairs = [(group[i], group[(i + d) % SIDE]) for group in lines() for i in range(SIDE)]
    return lax.ppermute(value, BOTH, pairs)


def plane_swap(value):
    return lax.all_to_all(value, BOTH, 0, 0, axis_index_groups=planes())


def natural(core, a, g):
    return jnp.where(core == 0, SIDE * a + g, SIDE * g + a)


def lay_out(place_ref, pieces, full_ref):
    core, me = place_ref[0], place_ref[1]
    for d, piece in enumerate(pieces):
        a = (me + SIDE - d) & (SIDE - 1)
        for g in range(SIDE):
            at = pl.multiple_of(natural(core, a, g) * BLOCK, BLOCK)
            full_ref[pl.ds(at, BLOCK), :] = piece[g * BLOCK : (g + 1) * BLOCK, :]


def usable_rows(place_ref, group, rows, base=0):
    slot = lax.broadcasted_iota(jnp.int32, (rows, 1), 0) + base
    first = ((slot < A) & (slot < place_ref[2])) | ((slot >= A) & (slot < 2 * A) & (slot - A < place_ref[3]))
    first = first.astype(f32)
    second = (slot < place_ref[4]).astype(f32)
    if isinstance(group, int):
        return second if group else first
    return jnp.where(group == 0, first, second)


def own_rows(win):
    row = lax.broadcasted_iota(jnp.int32, (WIN, 1), 0) + (WINDOWS[win] - win * A)
    return ((row >= 0) & (row < A)).astype(f32)


def key_bias(place_ref, win=None):
    if win is None:
        key = lax.broadcasted_iota(jnp.int32, (1, S), 1)
        return jnp.where(key < place_ref[4], 0.0, NEG)
    key = lax.broadcasted_iota(jnp.int32, (1, WIN), 1) + (WINDOWS[win] - win * A)
    return jnp.where((key >= 0) & (key < place_ref[2 + win]), 0.0, NEG)


def exact_dot(a, b):
    high = a.astype(bf16)
    rest = a - high.astype(f32)
    mid = rest.astype(bf16)
    low = (rest - mid.astype(f32)).astype(bf16)
    b = b.astype(bf16)
    return dot(high, b) + dot(mid, b) + dot(low, b)


def spots(core, shape, full, part):
    l = lax.broadcasted_iota(jnp.int32, shape, full)
    m = lax.broadcasted_iota(jnp.int32, shape, part)
    q = (m * 2731) >> 16
    return l == m + FR * (q + core)


def spots_t(core):
    return spots(core, (DC, D), 1, 0)


def params(**kw):
    return pltpu.CompilerParams(vmem_limit_bytes=VMEM_LIMIT, **kw)


def cost(flops, bytes_accessed, transcendentals=0):
    return pl.CostEstimate(
        flops=int(flops), bytes_accessed=int(bytes_accessed), transcendentals=int(transcendentals)
    )


def dot(a, b):
    return jnp.dot(a, b, preferred_element_type=f32)


def dot_t(a, b):
    return lax.dot_general(a, b, (((1,), (1,)), ((), ())), preferred_element_type=f32)


def t_dot(a, b):
    return lax.dot_general(a, b, (((0,), (0,)), ((), ())), preferred_element_type=f32)


def stats(z):
    mean_val = jnp.mean(z, axis=-1, keepdims=True)
    centred = z - mean_val
    variance = jnp.mean(centred * centred, axis=-1, keepdims=True)
    inv_std = lax.rsqrt(variance + EPS_NORM)
    return centred * inv_std, inv_std


def norm_back(grad, normed, inv_std, gain):
    e = grad * gain
    return inv_std * (
        e
        - jnp.mean(e, axis=-1, keepdims=True)
        - normed * jnp.mean(e * normed, axis=-1, keepdims=True)
    )


def swap_halves(u):
    lanes = u.shape[1]
    lane = lax.broadcasted_iota(jnp.int32, u.shape, 1)
    up = pltpu.roll(u, lanes - HD // 2, 1)
    down = pltpu.roll(u, HD // 2, 1)
    return jnp.where((lane & (HD - 1)) < HD // 2, up, down)


TURN = 1.5707963267948966


def sin_cos(a):
    k = jnp.floor(a * (1.0 / TURN) + 0.5)
    r = ((a - k * 1.5703125) - k * 4.837512969970703125e-4) - k * 7.54978995489188216e-8
    z = r * r
    s = ((-1.9515295891e-4 * z + 8.3321608736e-3) * z - 1.6666654611e-1) * z * r + r
    c = ((2.443315711809948e-5 * z - 1.388731625493765e-3) * z + 4.166664568298827e-2) * z * z - 0.5 * z + 1.0
    quarter = k.astype(jnp.int32)
    odd = (quarter & 1) == 1
    sine = jnp.where(odd, c, s)
    cosine = jnp.where(odd, s, c)
    sine = jnp.where((quarter & 2) == 0, sine, -sine)
    cosine = jnp.where(((quarter + 1) & 2) == 0, cosine, -cosine)
    return sine, cosine


def pre_kernel(
    place_ref, x_ref, xo_ref, c_ref, co_ref, ints_ref, v0, v1, v2, v3,
    vec_ref, h_ref, ht_ref, cos_ref, sin_ref, gy_ref, b1_ref, pos_ref,
    full_s, rows_s,
):
    i = pl.program_id(0)
    core = place_ref[0]

    @pl.when(i == 0)
    def _():
        lay_out(place_ref, (v0, v1, v2, v3), full_s)
        rows_s[...] = full_s[...].astype(f32).T[:16, :]
        vec_ref[...] = rows_s[...]
        units = dot(rows_s[8:16, :].astype(bf16), spots(core, (D, DC), 0, 1).astype(bf16))
        for r in range(FC // DC):
            b1_ref[:, r * DC : (r + 1) * DC] = units[2 + r : 3 + r, :]

    mine = i == 0
    normed, _ = stats(jnp.where(mine, x_ref[...], xo_ref[...]).astype(f32))
    h = normed * rows_s[0:1, :] + rows_s[1:2, :]
    h_ref[...] = h.astype(bf16)
    ht_ref[0] = h.T.astype(bf16)
    keep = usable_rows(place_ref, i ^ core, S)
    gy_ref[...] = (jnp.where(mine, c_ref[...], co_ref[...]).astype(f32) * keep).astype(bf16)
    src = lax.broadcasted_iota(jnp.int32, (D, DC), 0)
    dst = lax.broadcasted_iota(jnp.int32, (D, DC), 1)
    want = core * (DC // 2) + (dst // HD) * (HD // 2) + (dst & (HD // 2 - 1))
    freqs = rows_s[8:16, :].astype(bf16)
    col = dot(freqs, (src == want).astype(bf16))[1:2, :]
    row = dot(freqs, (src == want + D // 2).astype(bf16))[1:2, :]
    pos = ints_ref[0].astype(f32).T
    pos_ref[0] = pos
    angle = pos[:, 1:2] * col + pos[:, 0:1] * row
    lane = lax.broadcasted_iota(jnp.int32, (1, DC), 1)
    sign = jnp.where((lane & (HD - 1)) < HD // 2, -1.0, 1.0)
    small = jnp.max(jnp.abs(angle)) < 8000.0

    @pl.when(small)
    def _():
        sine, cosine = sin_cos(angle)
        cos_ref[...] = cosine
        sin_ref[...] = sine * sign

    @pl.when(jnp.logical_not(small))
    def _():
        cos_ref[...] = jnp.cos(angle)
        sin_ref[...] = jnp.sin(angle) * sign


def pre_call(place, x, xo, c, co, ints, pieces):
    tile = lambda n: pl.BlockSpec((S, n), lambda i, c: (i, 0))
    whole = lambda a: pl.BlockSpec(a.shape, lambda i, c: (0,) * a.ndim)
    return pl.pallas_call(
        pre_kernel,
        grid_spec=pltpu.PrefetchScalarGridSpec(
            num_scalar_prefetch=1,
            grid=(CORES,),
            in_specs=[whole(a) for a in (x, xo, c, co)]
            + [pl.BlockSpec((1, 8, S), lambda i, c: (i, 0, 0))]
            + [whole(a) for a in pieces],
            out_specs=[
                pl.BlockSpec((16, D), lambda i, c: (0, 0)),
                tile(D),
                pl.BlockSpec((1, D, S), lambda i, c: (i, 0, 0)),
                tile(DC),
                tile(DC),
                tile(D),
                pl.BlockSpec((1, FC), lambda i, c: (0, 0)),
                pl.BlockSpec((1, S, 8), lambda i, c: (i, 0, 0)),
            ],
            scratch_shapes=[pltpu.VMEM((D, 128), bf16), pltpu.VMEM((16, D), f32)],
        ),
        out_shape=[
            jax.ShapeDtypeStruct((16, D), f32),
            jax.ShapeDtypeStruct((T, D), bf16),
            jax.ShapeDtypeStruct((CORES, D, S), bf16),
            jax.ShapeDtypeStruct((T, DC), f32),
            jax.ShapeDtypeStruct((T, DC), f32),
            jax.ShapeDtypeStruct((T, D), bf16),
            jax.ShapeDtypeStruct((1, FC), f32),
            jax.ShapeDtypeStruct((CORES, S, 8), f32),
        ],
        compiler_params=params(),
        cost_estimate=cost(T * (20 * D + 40 * DC), T * (D * 10 + DC * 8)),
    )(place, x, xo, c, co, ints, *pieces)


def qkv_kernel(place_ref, h_ref, w0, w1, w2, w3, v_ref, cos_ref, sin_ref, q_out, k_out, v_out, w_s):
    @pl.when(pl.program_id(0) == 0)
    def _():
        lay_out(place_ref, (w0, w1, w2, w3), w_s)

    cosine = cos_ref[...]
    sine = sin_ref[...]
    at = pl.ds(pl.multiple_of(place_ref[0] * DC, DC), DC)
    acc = dot(h_ref[...], w_s[...])
    part = lambda i: jnp.concatenate([acc[:, (3 * p + i) * 128 : (3 * p + i + 1) * 128] for p in range(PAIRS)], axis=1)
    q = part(0) + v_ref[4:5, at]
    k = part(1) + v_ref[5:6, at]
    q_out[...] = ((q * cosine + swap_halves(q) * sine) * HD ** (-0.5)).astype(bf16)
    k_out[...] = (k * cosine + swap_halves(k) * sine).astype(bf16)
    v_out[...] = (part(2) + v_ref[6:7, at]).astype(bf16)


def qkv_call(place, h1, pieces, vec, cosine, sine):
    rows = 288
    tile = lambda n: pl.BlockSpec((rows, n), lambda i, c: (i, 0))
    whole = lambda a: pl.BlockSpec(a.shape, lambda i, c: (0,) * a.ndim)
    return pl.pallas_call(
        qkv_kernel,
        grid_spec=pltpu.PrefetchScalarGridSpec(
            num_scalar_prefetch=1,
            grid=(T // rows,),
            in_specs=[tile(D)] + [whole(a) for a in pieces] + [whole(vec), tile(DC), tile(DC)],
            out_specs=[tile(DC)] * 3,
            scratch_shapes=[pltpu.VMEM((D, 3 * DC), bf16)],
        ),
        out_shape=[jax.ShapeDtypeStruct((T, DC), bf16)] * 3,
        compiler_params=params(),
        cost_estimate=cost(2 * T * D * 3 * DC, T * D * 2 + D * 3 * DC * 2 + T * DC * 14),
    )(place, h1, *pieces, vec, cosine, sine)


def softmax_head(q, k, v, mine, bias):
    s = dot_t(jnp.where(mine, q, jnp.zeros_like(q)), k) + bias
    e = jnp.exp(s - jnp.max(s, axis=-1, keepdims=True))
    p = e * (1.0 / jnp.sum(e, axis=-1, keepdims=True))
    return p


def attn_fwd_kernel(
    place_ref, q0, k0, v0, q1, k1, v1, o_ref, p0_ref, p1_ref
):
    lane = lax.broadcasted_iota(jnp.int32, (1, 2 * HD), 1)
    low = lane < HD
    q, k, v = q1[0], k1[0], v1[0]
    mixes = []
    bias = key_bias(place_ref)
    for head, mine in ((0, low), (1, ~low)):
        p = softmax_head(q, k, v, mine, bias).astype(bf16)
        p1_ref[head] = p
        mixes.append(dot(p, v))
    mix = jnp.where(low, mixes[0], mixes[1])
    o_ref[1] = jnp.where(usable_rows(place_ref, 1, S) > 0, mix, v.astype(f32)).astype(bf16)
    o_ref[0] = v0[0]
    for win, base in enumerate(WINDOWS):
        q, k, v = (r[0, base : base + WIN, :] for r in (q0, k0, v0))
        own = own_rows(win)
        bias = key_bias(place_ref, win)
        mixes = []
        for head, mine in ((0, low), (1, ~low)):
            p = softmax_head(q, k, v, mine, bias)
            p = (p * own).astype(bf16)
            p0_ref[head, win] = p
            mixes.append(dot(p, v))
        mix = jnp.where(low, mixes[0], mixes[1])
        use = (own * usable_rows(place_ref, 0, WIN, base)) > 0
        before = o_ref[0, base : base + WIN, :].astype(f32)
        o_ref[0, base : base + WIN, :] = jnp.where(use, mix, before).astype(bf16)


def attn_fwd_call(place, q, k, v):
    block = lambda g: pl.BlockSpec((1, S, 2 * HD), lambda p, c: (g ^ c[0], 0, p))
    q, k, v = (a.reshape(CORES, S, DC) for a in (q, k, v))
    return pl.pallas_call(
        attn_fwd_kernel,
        grid_spec=pltpu.PrefetchScalarGridSpec(
            num_scalar_prefetch=1,
            grid=(PAIRS,),
            in_specs=[block(0)] * 3 + [block(1)] * 3,
            out_specs=[
                pl.BlockSpec((CORES, S, 2 * HD), lambda p, c: (0, 0, p)),
                pl.BlockSpec((2, 2, WIN, WIN), lambda p, c: (p, 0, 0, 0)),
                pl.BlockSpec((2, S, S), lambda p, c: (p, 0, 0)),
            ],
        ),
        out_shape=[
            jax.ShapeDtypeStruct((CORES, S, DC), bf16),
            jax.ShapeDtypeStruct((HC, 2, WIN, WIN), bf16),
            jax.ShapeDtypeStruct((HC, S, S), bf16),
        ],
        compiler_params=params(),
        cost_estimate=cost(4 * HC * (S * S + 2 * WIN * WIN) * 128, 12e6, HC * S * S),
    )(place, q, k, v, q, k, v)


def proj_kernel(place_ref, mine_ref, other_ref, x_ref, xo_ref, w0, w1, w2, w3, v_ref, after_ref, h2_ref, w_s):
    @pl.when(pl.program_id(0) == 0)
    def _():
        lay_out(place_ref, (w0, w1, w2, w3), w_s)

    core = place_ref[0]
    at = lambda c: pl.ds(pl.multiple_of(c * DC, DC), DC)
    branch = dot(mine_ref[0], w_s[at(core), :]) + dot(other_ref[0], w_s[at(1 - core), :])
    x = jnp.where(pl.program_id(0) < pl.num_programs(0) // CORES, x_ref[...], xo_ref[...])
    after = x.astype(f32) + (branch + v_ref[7:8, :])
    after_ref[...] = after
    normed, _ = stats(after)
    h2_ref[...] = (normed * v_ref[2:3, :] + v_ref[3:4, :]).astype(bf16)


def proj_call(place, mine, other, x, xo, pieces, vec):
    rows = 288
    half = S // rows
    tile = lambda n: pl.BlockSpec((rows, n), lambda i, c: (i, 0))
    whole = lambda a: pl.BlockSpec(a.shape, lambda i, c: (0,) * a.ndim)
    return pl.pallas_call(
        proj_kernel,
        grid_spec=pltpu.PrefetchScalarGridSpec(
            num_scalar_prefetch=1,
            grid=(T // rows,),
            in_specs=[
                pl.BlockSpec((1, rows, DC), lambda i, c: ((i // half) ^ c[0], i % half, 0)),
                pl.BlockSpec((1, rows, DC), lambda i, c: ((i // half) ^ c[0], i % half, 0)),
                pl.BlockSpec((rows, D), lambda i, c: (jnp.minimum(i, half - 1), 0)),
                pl.BlockSpec((rows, D), lambda i, c: (jnp.maximum(i - half, 0), 0)),
            ]
            + [whole(a) for a in pieces]
            + [whole(vec)],
            out_specs=[tile(D), tile(D)],
            scratch_shapes=[pltpu.VMEM((D, D), bf16)],
        ),
        out_shape=[jax.ShapeDtypeStruct((T, D), f32), jax.ShapeDtypeStruct((T, D), bf16)],
        compiler_params=params(),
        cost_estimate=cost(2 * T * D * D, T * D * 10 + D * D * 2),
    )(place, mine, other, x, xo, *pieces, vec)


K0 = (2.0 / 3.141592653589793) ** 0.5
FT = 768


def gelu_slope(u):
    sq = u * u
    th = jnp.tanh(u * (K0 + (K0 * 0.044715) * sq))
    half = 0.5 + 0.5 * th
    return u * half, half + (u * (half - half * half)) * (2 * K0 + (6 * K0 * 0.044715) * sq)


def mlp_kernel(
    place_ref, h2_ref, gy_ref, w10, w11, w12, w13, w2_ref, b1_ref, mlp_ref, mlpo_ref, gh2b_ref, act_ref, gup_ref, gb1_ref, w1_s
):
    i = pl.program_id(0)

    @pl.when(i == 0)
    def _():
        lay_out(place_ref, (w10, w11, w12, w13), w1_s)
        gb1_ref[...] = jnp.zeros_like(gb1_ref)

    for f in range(FC // FT):
        c = slice(f * FT, (f + 1) * FT)
        act, slope = gelu_slope(dot(h2_ref[...], w1_s[:, c]) + b1_ref[:, c])
        act_ref[:, c] = act.astype(bf16)
        gup = (dot_t(gy_ref[...], w2_ref[c, :]) * slope).astype(bf16)
        gup_ref[:, c] = gup
        gb1_ref[:, c] += jnp.sum(gup.astype(f32), axis=0, keepdims=True)
    gh2b_ref[...] = dot_t(gup_ref[...], w1_s[...]).astype(bf16)
    mlp = dot(act_ref[...], w2_ref[...])
    half = pl.num_programs(0) // CORES

    @pl.when(i < half)
    def _():
        mlp_ref[...] = mlp

    @pl.when(i >= half)
    def _():
        mlpo_ref[...] = mlp


def mlp_call(place, h2, gy, pieces, w2, b1):
    rows = 288
    half = S // rows
    tile = lambda n: pl.BlockSpec((rows, n), lambda i, c: (i, 0))
    whole = lambda a: pl.BlockSpec(a.shape, lambda i, c: (0,) * a.ndim)
    return pl.pallas_call(
        mlp_kernel,
        grid_spec=pltpu.PrefetchScalarGridSpec(
            num_scalar_prefetch=1,
            grid=(T // rows,),
            in_specs=[tile(D), tile(D)]
            + [whole(a) for a in pieces]
            + [whole(w2), whole(b1)],
            out_specs=[
                pl.BlockSpec((rows, D), lambda i, c: (jnp.minimum(i, half - 1), 0)),
                pl.BlockSpec((rows, D), lambda i, c: (jnp.maximum(i - half, 0), 0)),
                tile(D),
                tile(FC),
                tile(FC),
                pl.BlockSpec((1, FC), lambda i, c: (0, 0)),
            ],
            scratch_shapes=[pltpu.VMEM((D, FC), bf16)],
        ),
        out_shape=[
            jax.ShapeDtypeStruct((S, D), f32),
            jax.ShapeDtypeStruct((S, D), f32),
            jax.ShapeDtypeStruct((T, D), bf16),
            jax.ShapeDtypeStruct((T, FC), bf16),
            jax.ShapeDtypeStruct((T, FC), bf16),
            jax.ShapeDtypeStruct((1, FC), f32),
        ],
        compiler_params=params(),
        cost_estimate=cost(8 * T * D * FC, 30e6, T * FC),
    )(place, h2, gy, *pieces, w2, b1)


def by_line(place_ref, value, block, out_ref):
    core = place_ref[0]
    for n in range(PLANE):
        to = jnp.where(core == 0, n, (n % SIDE) * SIDE + n // SIDE)
        out_ref[pl.ds(pl.multiple_of(to * block, block), block), :] = value[n * block : (n + 1) * block, :].astype(bf16)


def fc_grad_kernel(place_ref, h2_ref, gup_ref, act_ref, gy_ref, gw1_ref, gw2_ref):
    by_line(place_ref, t_dot(act_ref[...], gy_ref[...]), SIDE * FR, gw2_ref)
    by_line(place_ref, t_dot(h2_ref[...], gup_ref[...]), BLOCK, gw1_ref)


def fc_grad_call(place, h2, gup, act, gy):
    whole = lambda a: pl.BlockSpec(a.shape, lambda i, c: (0, 0))
    return pl.pallas_call(
        fc_grad_kernel,
        grid_spec=pltpu.PrefetchScalarGridSpec(
            num_scalar_prefetch=1,
            grid=(2,),
            in_specs=[
                whole(h2),
                pl.BlockSpec((T, FC // 2), lambda i, c: (0, i)),
                whole(act),
                pl.BlockSpec((T, DC), lambda i, c: (0, i)),
            ],
            out_specs=[
                pl.BlockSpec((D, FC // 2), lambda i, c: (0, i)),
                pl.BlockSpec((FC, DC), lambda i, c: (0, i)),
            ],
        ),
        out_shape=[jax.ShapeDtypeStruct((D, FC), bf16), jax.ShapeDtypeStruct((FC, D), bf16)],
        compiler_params=params(),
        cost_estimate=cost(4 * T * D * FC, T * (D + FC) * 4 + D * FC * 4),
    )(place, h2, gup, act, gy)


def mid_kernel(place_ref, after_ref, gy_ref, gh2_ref, other_ref, v_ref, ga_ref, gab_ref, sums_ref):
    i = pl.program_id(0)
    normed, inv_std = stats(after_ref[...])
    gh2 = gh2_ref[...].astype(f32) + other_ref[...].astype(f32)
    gy = gy_ref[...].astype(f32)
    ga = gy + norm_back(gh2, normed, inv_std, v_ref[2:3, :])
    gab = ga.astype(bf16)
    gab_ref[...] = gab

    @pl.when(i == 0)
    def _():
        sums_ref[...] = jnp.zeros_like(sums_ref)

    @pl.when(i < pl.num_programs(0) // CORES)
    def _():
        ga_ref[...] = ga
        sums_ref[0:1, :] += jnp.sum(gh2 * normed, axis=0, keepdims=True)
        sums_ref[1:2, :] += jnp.sum(gh2, axis=0, keepdims=True)
        sums_ref[2:3, :] += jnp.sum(gab.astype(f32), axis=0, keepdims=True)
        sums_ref[3:4, :] += jnp.sum(gy, axis=0, keepdims=True)


def mid_call(place, after, gy, gh2, other, vec):
    rows = 288
    half = S // rows
    tile = lambda n: pl.BlockSpec((rows, n), lambda i, c: (i, 0))
    flipped = pl.BlockSpec((rows, D), lambda i, c: ((i + half) % (2 * half), 0))
    whole = lambda a: pl.BlockSpec(a.shape, lambda i, c: (0,) * a.ndim)
    return pl.pallas_call(
        mid_kernel,
        grid_spec=pltpu.PrefetchScalarGridSpec(
            num_scalar_prefetch=1,
            grid=(T // rows,),
            in_specs=[tile(D), tile(D), tile(D), flipped, whole(vec)],
            out_specs=[
                pl.BlockSpec((rows, D), lambda i, c: (jnp.minimum(i, half - 1), 0)),
                tile(D),
                pl.BlockSpec((8, D), lambda i, c: (0, 0)),
            ],
        ),
        out_shape=[
            jax.ShapeDtypeStruct((S, D), f32),
            jax.ShapeDtypeStruct((T, D), bf16),
            jax.ShapeDtypeStruct((8, D), f32),
        ],
        compiler_params=params(),
        cost_estimate=cost(30 * T * D, T * D * 14),
    )(place, after, gy, gh2, other, vec)


def back_head(q_t, k, v, do, do_t, delta, p, mine, head):
    gp = dot_t(jnp.where(mine, do, jnp.zeros_like(do)), v)
    gs = (p.astype(f32) * (gp - delta)).astype(bf16)
    at = slice(head * HD, (head + 1) * HD)
    return dot(gs, k), dot(q_t[at, :], gs), dot(do_t[at, :], p)


def deltas(do, o, low):
    prod = do.astype(f32) * o.astype(f32)
    d0 = jnp.sum(jnp.where(low, prod, 0.0), axis=-1, keepdims=True)
    d1 = jnp.sum(jnp.where(low, 0.0, prod), axis=-1, keepdims=True)
    return d0, d1


def attn_bwd_kernel(
    place_ref,
    q0, k0, v0, o0, p0, cos0, sin0, pos0,
    q1, k1, v1, o1, p1, cos1, sin1, pos1,
    h1t_ref, ga_ref, cols_ref, mine_ref, other_ref, w0, w1, w2, w3, y0, y1, y2, y3,
    gw0, gw1, gw2, gw3, gh_ref, gho_ref, sums_ref,
    gq_s, gk_s, gv_s, gqkv_s, w_s, gw_s, y_s, do_s,
):
    lane = lax.broadcasted_iota(jnp.int32, (1, 2 * HD), 1)
    low = lane < HD
    pair = pl.program_id(0)
    core = place_ref[0]

    @pl.when(pair == 0)
    def _():
        lay_out(place_ref, (y0, y1, y2, y3), y_s)

    wy = y_s[pl.ds(pl.multiple_of(core * DC + pair * 2 * HD, 2 * HD), 2 * HD), :]
    for frame in range(CORES):
        do_s[frame] = dot_t(ga_ref[frame], wy).astype(bf16)

    def finish(frame, q, k, cos_ref, sin_ref, pos_ref):
        cosine, sine = cos_ref[0], sin_ref[0]
        gq = gq_s[...] * HD ** (-0.5)
        gk = gk_s[...]
        sq, sk = swap_halves(gq), swap_halves(gk)
        turn = (q.astype(f32) * HD**0.5) * sq + k.astype(f32) * sk
        gq = (gq * cosine - sq * sine).astype(bf16)
        gk = (gk * cosine - sk * sine).astype(bf16)
        gv = gv_s[...].astype(bf16)
        gqkv_s[frame, :, : 2 * HD] = gq
        gqkv_s[frame, :, 2 * HD : 4 * HD] = gk
        gqkv_s[frame, :, 4 * HD :] = gv
        pos = pos_ref[0]
        col = jnp.sum(turn * pos[:, 1:2], axis=0, keepdims=True)
        row = jnp.sum(turn * pos[:, 0:1], axis=0, keepdims=True)
        bias = [jnp.sum(g.astype(f32), axis=0, keepdims=True) for g in (gq, gk, gv)]
        return jnp.concatenate([col, row] + bias, axis=0)

    q, k, v, do = q1[0], k1[0], v1[0], do_s[1 ^ core]
    d = deltas(do, o1[0], low)
    q_t, do_t = q.astype(f32).T.astype(bf16), do.astype(f32).T.astype(bf16)
    out = [
        back_head(q_t, k, v, do, do_t, d[head], p1[head], mine, head)
        for head, mine in ((0, low), (1, ~low))
    ]
    gq_s[...] = jnp.where(low, out[0][0], out[1][0])
    gk_s[...] = jnp.concatenate([out[0][1], out[1][1]], axis=0).T
    gv_s[...] = jnp.concatenate([out[0][2], out[1][2]], axis=0).T
    sums1 = finish(1, q, k, cos1, sin1, pos1)
    gq_s[...] = jnp.zeros_like(gq_s)
    gk_s[...] = jnp.zeros_like(gk_s)
    gv_s[...] = jnp.zeros_like(gv_s)
    for win, base in enumerate(WINDOWS):
        at = pl.ds(base, WIN)
        q, k, v, o = (r[0, at, :] for r in (q0, k0, v0, o0))
        do = do_s[core, at, :]
        d = deltas(do, o, low)
        q_t, do_t = q.astype(f32).T.astype(bf16), do.astype(f32).T.astype(bf16)
        out = [
            back_head(q_t, k, v, do, do_t, d[head], p0[head, win], mine, head)
            for head, mine in ((0, low), (1, ~low))
        ]
        gq_s[at, :] += jnp.where(low, out[0][0], out[1][0])
        gk_s[at, :] += jnp.concatenate([out[0][1], out[1][1]], axis=0).T
        gv_s[at, :] += jnp.concatenate([out[0][2], out[1][2]], axis=0).T
    sums0 = finish(0, q0[0], k0[0], cos0, sin0, pos0)
    sums_ref[0, 0:5, :] = sums0 + sums1
    sums_ref[0, 5:8, :] = jnp.zeros((3, 2 * HD), f32)

    lay_out(place_ref, (w0, w1, w2, w3), w_s)
    gw = jnp.zeros((D, 6 * HD), f32)
    gw_mine = jnp.zeros((2 * HD, DC), f32)
    gw_other = jnp.zeros((2 * HD, DC), f32)
    for frame, out in ((0, gh_ref), (1, gho_ref)):
        g = gqkv_s[frame ^ core]
        gw += dot(h1t_ref[frame], g)
        gh = dot_t(g, w_s[...])

        @pl.when(pair == 0)
        def _(out=out, gh=gh):
            out[...] = gh

        @pl.when(pair > 0)
        def _(out=out, gh=gh):
            out[...] += gh

        cols = cols_ref[frame].astype(f32).T.astype(bf16)
        gw_mine += dot(cols, mine_ref[frame ^ core])
        gw_other += dot(cols, other_ref[frame ^ core])
    gw_s[:, : 6 * HD] = gw.astype(bf16)
    at = lambda c: pl.ds(pl.multiple_of(c * DC, DC), DC)
    gw_s[at(core), 6 * HD :] = gw_mine.T.astype(bf16)
    gw_s[at(1 - core), 6 * HD :] = gw_other.T.astype(bf16)
    for d, out in enumerate((gw0, gw1, gw2, gw3)):
        a = (place_ref[1] + d) & (SIDE - 1)
        for g in range(SIDE):
            at = pl.multiple_of(natural(core, a, g) * BLOCK, BLOCK)
            out[g * BLOCK : (g + 1) * BLOCK, :] = gw_s[pl.ds(at, BLOCK), :]


def attn_bwd_call(place, q, k, v, ga, mine, other, p0, p1, cosine, sine, pos, h1t, pieces, proj_pieces):
    q, k, v, cosine, sine = (a.reshape(CORES, S, DC) for a in (q, k, v, cosine, sine))
    ga = ga.reshape(CORES, S, D)
    block = lambda g: pl.BlockSpec((1, S, 2 * HD), lambda p, c: (g ^ c[0], 0, p))
    own = lambda g: pl.BlockSpec((1, S, 2 * HD), lambda p, c: (g, 0, p))
    quarter = pl.BlockSpec((QUARTER, 6 * HD), lambda p, c: (0, p))
    grads = pl.BlockSpec((QUARTER, 8 * HD), lambda p, c: (0, p))
    at = lambda g: pl.BlockSpec((1, S, 8), lambda p, c: (g ^ c[0], 0, 0))
    whole = lambda a: pl.BlockSpec(a.shape, lambda p, c: (0,) * a.ndim)
    return pl.pallas_call(
        attn_bwd_kernel,
        grid_spec=pltpu.PrefetchScalarGridSpec(
            num_scalar_prefetch=1,
            grid=(PAIRS,),
            in_specs=[block(0)] * 3
            + [own(0), pl.BlockSpec((2, 2, WIN, WIN), lambda p, c: (p, 0, 0, 0))]
            + [block(0)] * 2
            + [at(0)]
            + [block(1)] * 3
            + [own(1), pl.BlockSpec((2, S, S), lambda p, c: (p, 0, 0))]
            + [block(1)] * 2
            + [at(1)]
            + [whole(h1t), whole(ga), pl.BlockSpec((CORES, S, 2 * HD), lambda p, c: (0, 0, PAIRS * c[0] + p))]
            + [whole(mine), whole(other)]
            + [quarter] * 4
            + [whole(a) for a in proj_pieces],
            out_specs=[grads] * 4
            + [
                pl.BlockSpec((S, D), lambda p, c: (0, 0)),
                pl.BlockSpec((S, D), lambda p, c: (0, 0)),
                pl.BlockSpec((1, 8, 2 * HD), lambda p, c: (p, 0, 0)),
            ],
            scratch_shapes=[pltpu.VMEM((S, 2 * HD), f32)] * 3
            + [pltpu.VMEM((CORES, S, 6 * HD), bf16)]
            + [pltpu.VMEM((D, 6 * HD), bf16), pltpu.VMEM((D, 8 * HD), bf16)]
            + [pltpu.VMEM((D, D), bf16), pltpu.VMEM((CORES, S, 2 * HD), bf16)],
        ),
        out_shape=[
            *[jax.ShapeDtypeStruct((QUARTER, 4 * DC), bf16)] * 4,
            jax.ShapeDtypeStruct((S, D), f32),
            jax.ShapeDtypeStruct((S, D), f32),
            jax.ShapeDtypeStruct((PAIRS, 8, 2 * HD), f32),
        ],
        compiler_params=params(),
        cost_estimate=cost(10 * HC * S * S * 128 + 4 * T * D * 4 * DC, 36e6),
    )(
        place,
        q, k, v, mine, p0, cosine, sine, pos,
        q, k, v, mine, p1, cosine, sine, pos,
        h1t, ga, ga, mine, other, *pieces, *proj_pieces,
    )


def last_kernel(x_ref, ga_ref, gh_ref, other_ref, after_ref, mlp_ref, mlpo_ref, v_ref, gt_ref, out_ref):
    normed, inv_std = stats(x_ref[...].astype(f32))
    gt_ref[...] = ga_ref[...] + norm_back(gh_ref[...] + other_ref[...], normed, inv_std, v_ref[0:1, :])
    out_ref[...] = (after_ref[...] + (mlp_ref[...] + mlpo_ref[...] + v_ref[8:9, :])).astype(bf16)


def last_call(x, ga, gh, other, after, mlp, mlp_other, vec):
    rows = 288
    tile = lambda n: pl.BlockSpec((rows, n), lambda i: (i, 0))
    return pl.pallas_call(
        last_kernel,
        grid=(S // rows,),
        in_specs=[tile(D)] * 7 + [pl.BlockSpec(vec.shape, lambda i: (0, 0))],
        out_specs=[tile(D), tile(D)],
        out_shape=[jax.ShapeDtypeStruct((S, D), f32), jax.ShapeDtypeStruct((S, D), bf16)],
        compiler_params=params(),
        cost_estimate=cost(30 * S * D, S * D * 28),
    )(x, ga, gh, other, after, mlp, mlp_other, vec)


def vec_kernel(place_ref, x_ref, xo_ref, gh_ref, gho_ref, mid_ref, att_ref, gb1_ref, o0, o1, o2, o3, rows_s, full_s):
    core, me = place_ref[0], place_ref[1]
    rows_s[...] = jnp.zeros_like(rows_s)
    for x, gh in ((x_ref, gh_ref), (xo_ref, gho_ref)):
        normed, _ = stats(x[...].astype(f32))
        g = gh[...]
        rows_s[0:1, :] += jnp.sum(g * normed, axis=0, keepdims=True)
        rows_s[1:2, :] += jnp.sum(g, axis=0, keepdims=True)
    rows_s[2:4, :] = mid_ref[0:2, :]
    rows_s[7:9, :] = mid_ref[2:4, :]
    att = jnp.concatenate([att_ref[p] for p in range(PAIRS)], axis=1)
    rows_s[4:7, pl.ds(pl.multiple_of(core * DC, DC), DC)] = att[2:5, :]
    src = lax.broadcasted_iota(jnp.int32, (DC, D), 0)
    dst = lax.broadcasted_iota(jnp.int32, (DC, D), 1)
    want = core * (DC // 2) + (src // HD) * (HD // 2) + (src & (HD // 2 - 1))
    lane = lax.broadcasted_iota(jnp.int32, (1, DC), 1)
    turn = jnp.where((lane & (HD - 1)) < HD // 2, att, -att)
    rows_s[9:10, :] = (
        exact_dot(turn, dst == want)[0:1, :] + exact_dot(turn, dst == want + D // 2)[1:2, :]
    )
    gb1 = jnp.concatenate([gb1_ref[:, r * DC : (r + 1) * DC] for r in range(FC // DC)] * 2, axis=0)
    rows_s[10:14, :] = exact_dot(gb1, spots_t(core))[:4, :]
    full_s[...] = rows_s[...].T
    for d, out in enumerate((o0, o1, o2, o3)):
        a = (me + d) & (SIDE - 1)
        for g in range(SIDE):
            at = pl.multiple_of(natural(core, a, g) * BLOCK, BLOCK)
            out[g * BLOCK : (g + 1) * BLOCK, :] = full_s[pl.ds(at, BLOCK), :]


def vec_call(place, x, xo, gh, gho, mid, att, gb1):
    whole = lambda a: pl.BlockSpec(a.shape, lambda i, c: (0,) * a.ndim)
    return pl.pallas_call(
        vec_kernel,
        grid_spec=pltpu.PrefetchScalarGridSpec(
            num_scalar_prefetch=1,
            grid=(1,),
            in_specs=[whole(a) for a in (x, xo, gh, gho, mid, att, gb1)],
            out_specs=[pl.BlockSpec((QUARTER, 128), lambda i, c: (0, 0))] * 4,
            scratch_shapes=[pltpu.VMEM((128, D), f32), pltpu.VMEM((D, 128), f32)],
        ),
        out_shape=[jax.ShapeDtypeStruct((QUARTER, 128), f32)] * 4,
        compiler_params=params(),
        cost_estimate=cost(20 * T * D, T * D * 6),
    )(place, x, xo, gh, gho, mid, att, gb1)


PACK = 4 * DC + 128 + 2 * FC


def pack_kernel(q0, q1, q2, q3, v0, v1, v2, v3, f1_ref, f2_ref, out_ref):
    qs = q0[...].astype(f32) + q1[...].astype(f32) + q2[...].astype(f32) + q3[...].astype(f32)
    vs = v0[...] + v1[...] + v2[...] + v3[...]
    f1 = f1_ref[...].astype(f32)
    f2 = f2_ref[...].astype(f32)
    for n in range(PLANE):
        at = slice(n * KR, (n + 1) * KR)
        out_ref[n, :, : 4 * DC] = qs[at, :].astype(bf16)
        out_ref[n, :, 4 * DC : 4 * DC + 128] = vs[at, :].astype(bf16)
        out_ref[n, :, 4 * DC + 128 : 4 * DC + 128 + FC] = f1[at, :].astype(bf16)
        for h in range(2):
            to = 4 * DC + 128 + FC + h * D
            out_ref[n, :, to : to + D] = f2[(2 * n + h) * KR : (2 * n + h + 1) * KR, :].astype(bf16)


def pack_call(qs, vs, f1, f2):
    return pl.pallas_call(
        pack_kernel,
        out_shape=jax.ShapeDtypeStruct((PLANE, KR, PACK), bf16),
        compiler_params=params(),
        cost_estimate=cost(QUARTER * PACK * 4, QUARTER * PACK * 8),
    )(*qs, *vs, f1, f2)


def sum_kernel(in_ref, out_ref):
    total = in_ref[0].astype(f32)
    for n in range(1, PLANE):
        total += in_ref[n].astype(f32)
    out_ref[...] = total


def sum_call(packed):
    return pl.pallas_call(
        sum_kernel,
        out_shape=jax.ShapeDtypeStruct((KR, PACK), f32),
        compiler_params=params(),
        cost_estimate=cost(QUARTER * PACK, QUARTER * PACK * 2),
    )(packed)


RATES = (D ** (-0.5), max(1, 2 * D // S) ** (-0.5), D ** (-0.5), FF ** (-0.5), RATE_VECTOR)


def adam_kernel(place_ref, norm_ref, mine_ref, other_ref, *refs):
    masters, firsts, seconds = refs[0:5], refs[5:10], refs[10:15]
    outs = refs[15:30]
    norm_out, bias_out = refs[30:32]
    core = place_ref[0]
    mine, other = mine_ref[...], other_ref[...]
    g0 = jnp.where(core == 0, mine, other)
    g1 = jnp.where(core == 0, other, mine)
    total = jnp.sum(jnp.sum(norm_ref[...], axis=0)[0:1, 0:1], axis=(0, 1), keepdims=True)
    grad_norm = jnp.sqrt(total)
    norm_out[...] = jnp.broadcast_to(grad_norm, norm_out.shape)
    clip = jnp.minimum(1.0, CLIP_LIMIT / (grad_norm + 1e-06))

    def update(i, at, grad):
        clipped = grad * clip
        master = masters[i][at]
        first = BETA_ONE * firsts[i][at] + (1.0 - BETA_ONE) * clipped
        second = BETA_TWO * seconds[i][at] + (1.0 - BETA_TWO) * clipped * clipped
        first_hat = first / (1.0 - BETA_ONE**STEP)
        second_hat = second / (1.0 - BETA_TWO**STEP)
        decay = 0.0 if i == 4 else DECAY_RATE
        outs[3 * i][at] = master - RATES[i] * (first_hat / (jnp.sqrt(second_hat) + ADAM_EPS) + decay * master)
        outs[3 * i + 1][at] = first
        outs[3 * i + 2][at] = second

    rows = slice(None)
    for c, g in ((0, g0), (1, g1)):
        for p in range(PAIRS):
            for i in range(3):
                col = i * D + c * DC + p * 128
                update(0, (rows, slice(col, col + 128)), g[:, (4 * p + i) * 128 : (4 * p + i + 1) * 128])
            col = c * DC + p * 128
            update(1, (rows, slice(col, col + 128)), g[:, (4 * p + 3) * 128 : (4 * p + 4) * 128])
        base = 4 * DC + 128 + FC
        for h in range(2):
            row = c * FR + h * KR
            update(3, (slice(row, row + KR), rows), g[:, base + h * D : base + (h + 1) * D])
    base = 4 * DC + 128
    for r in range(FC // DC):
        at = slice(base + r * DC, base + (r + 1) * DC)
        part = exact_dot(g0[:, at], spots_t(0)) + exact_dot(g1[:, at], spots_t(1))
        update(2, (rows, slice(r * D, (r + 1) * D)), part)
    vec = (g0 + g1)[:, 4 * DC : 4 * DC + 128]
    vec = jnp.concatenate([vec, jnp.zeros((16 - KR, 128), f32)], axis=0).T[:16, :KR]
    update(4, (rows, rows), vec[: masters[4].shape[0], :])
    bias_out[...] = vec[7:8, :] * clip


def adam_call(place, norm, mine, other, masters, firsts, seconds):
    whole = lambda a: pl.BlockSpec(a.shape, lambda i, c: (0,) * len(a.shape))
    args = [norm, mine, other, *masters, *firsts, *seconds]
    shapes = [jax.ShapeDtypeStruct(m.shape, f32) for m in masters for _ in range(3)]
    shapes += [jax.ShapeDtypeStruct((1, 128), f32), jax.ShapeDtypeStruct((1, KR), f32)]
    return pl.pallas_call(
        adam_kernel,
        grid_spec=pltpu.PrefetchScalarGridSpec(
            num_scalar_prefetch=1,
            grid=(1,),
            in_specs=[whole(a) for a in args],
            out_specs=[whole(a) for a in shapes],
        ),
        out_shape=shapes,
        compiler_params=params(),
        cost_estimate=cost(20 * KR * FF * 3, 3e6),
    )(place, *args)


def local(
    tokens,
    cotangent,
    counts,
    patch_row,
    patch_col,
    w_qkv,
    w_proj,
    w_fc1,
    w_fc2,
    vectors,
    m_qkv,
    v_qkv,
    m_proj,
    v_proj,
    m_fc1,
    v_fc1,
    m_fc2,
    v_fc2,
    m_vectors,
    v_vectors,
):
    core = lax.axis_index("grp")
    chip = lax.axis_index("dp")
    first_core = core == 0
    along = jnp.where(first_core, chip // PLANE, (chip // SIDE) % SIDE)
    vr = vectors.shape[0]

    def swap(a):
        return lax.ppermute(a, "grp", [(0, 1), (1, 0)])

    def halves(a):
        n = a.shape[-1] // 2
        return jnp.where(first_core, a[..., :n], a[..., n:])

    def over_plane(share):
        got = plane_swap(jnp.broadcast_to(share[None], (PLANE,) + share.shape))
        return got.reshape(PLANE * share.shape[0], share.shape[1])

    def along_line(quarter):
        return [quarter] + [shift(quarter, d) for d in range(1, SIDE)]

    def line_sum(whole):
        return lax.psum_scatter(whole, BOTH, scatter_dimension=0, axis_index_groups=lines(), tiled=True)

    fc2_b = w_fc2.astype(bf16)
    full_fc2 = lax.all_gather(jnp.where(first_core, fc2_b[:FR], fc2_b[FR:]), "dp", axis=0, tiled=True)
    qkv_b = w_qkv.astype(bf16)
    parts = [halves(qkv_b[:, i * D : (i + 1) * D]) for i in range(3)]
    by_pair = [parts[i][:, p * 128 : (p + 1) * 128] for p in range(PAIRS) for i in range(3)]
    vec_t = jnp.pad(vectors.astype(bf16).T, ((0, 0), (0, 128 - vr)))
    quarter = over_plane(jnp.concatenate(by_pair + [vec_t], axis=1))
    vec_pieces = along_line(quarter[:, 3 * DC :])
    qkv_pieces = along_line(quarter[:, : 3 * DC])
    fc1_b = w_fc1.astype(bf16).reshape(KR, CHIPS, CORES, FR)
    share_fc1 = jnp.where(first_core, fc1_b[:, :, 0], fc1_b[:, :, 1]).reshape(KR, FC)
    share = jnp.concatenate([share_fc1, w_proj.astype(bf16)], axis=1)
    share, vec_pieces = lax.optimization_barrier((share, vec_pieces))
    quarter = over_plane(share)
    proj_pieces = along_line(quarter[:, FC:])
    fc1_pieces = along_line(quarter[:, :FC])

    x_own = tokens.reshape(S, D)
    cot_own = cotangent.reshape(S, D)
    x_other, cot_other = swap(x_own), swap(cot_own)
    ints = jnp.concatenate(
        [
            patch_row.reshape(1, S),
            patch_col.reshape(1, S),
            jnp.pad(counts.reshape(1, 2), ((0, 0), (0, S - 2))),
            jnp.zeros((5, S), jnp.int32),
        ]
    )
    ints = jnp.stack([ints, swap(ints)])
    counts0 = jnp.where(first_core, ints[0, 2, :2], ints[1, 2, :2])
    counts1 = jnp.where(first_core, ints[1, 2, :1], ints[0, 2, :1])
    place = jnp.concatenate([jnp.stack([core, along]).astype(jnp.int32), counts0, counts1])

    vec, h1, h1t, cosine, sine, gy, b1, pos = pre_call(place, x_own, x_other, cot_own, cot_other, ints, vec_pieces)
    q, k, v = qkv_call(place, h1, qkv_pieces, vec, cosine, sine)
    mine, p0, p1 = attn_fwd_call(place, q, k, v)
    other = swap(mine)
    after, h2 = proj_call(place, mine, other, x_own, x_other, proj_pieces, vec)
    mlp, mlp_part, gh2, act, gup, gb1 = mlp_call(place, h2, gy, fc1_pieces, full_fc2, b1)
    mlp_other = swap(mlp_part)
    other_gh2 = swap(gh2)

    gw1, gw2 = fc_grad_call(place, h2, gup, act, gy)
    sum_fc2 = line_sum(gw2)
    sum_fc1 = line_sum(gw1)
    ga, gab, sums_mid = mid_call(place, after, gy, gh2, other_gh2, vec)
    *gw, gh1, gh1_part, sums_att = attn_bwd_call(
        place, q, k, v, gab, mine, other, p0, p1, cosine, sine, pos, h1t, qkv_pieces, proj_pieces
    )
    gh1_other = swap(gh1_part)

    sums_qkv = [gw[0]] + [shift(gw[d], d) for d in range(1, SIDE)]
    vec_parts = vec_call(place, x_own, x_other, gh1, gh1_part, sums_mid, sums_att, gb1)
    sums_vec = [vec_parts[0]] + [shift(vec_parts[d], d) for d in range(1, SIDE)]
    grads = sum_call(plane_swap(pack_call(sums_qkv, sums_vec, sum_fc1, sum_fc2)))
    gt, mixed = last_call(x_own, ga, gh1, gh1_other, after, mlp, mlp_other, vec)

    grads_other = swap(grads)
    is_vec = (jnp.arange(PACK) >= 4 * DC) & (jnp.arange(PACK) < 4 * DC + 128)
    squares = jnp.where(
        is_vec, (grads + grads_other) * (grads + grads_other), grads * grads + grads_other * grads_other
    )
    squares = jnp.sum(squares)
    norms = lax.all_to_all(jnp.full((CHIPS, 8, 128), squares, f32), "dp", 0, 0)
    *updates, grad_norm, bias_proj_grad = adam_call(
        place,
        norms,
        grads,
        grads_other,
        (w_qkv, w_proj, w_fc1, w_fc2, vectors),
        (m_qkv, m_proj, m_fc1, m_fc2, m_vectors),
        (v_qkv, v_proj, v_fc1, v_fc2, v_vectors),
    )
    return (
        mixed.reshape(1, 1, S, D),
        gt.reshape(1, 1, S, D),
        grad_norm[0, 0],
        *updates,
        bias_proj_grad.reshape(KR),
    )


def solution(mesh):
    frame = P("grp", "dp", None, None)
    ints = P("grp", "dp", None)
    rows = P("dp", None)
    cols = P(None, "dp")
    return jax.shard_map(
        local,
        mesh=mesh,
        in_specs=(frame, frame, ints, ints, ints, rows, rows, rows, rows, cols) + (rows,) * 8 + (cols,) * 2,
        out_specs=(frame, frame, P()) + (rows,) * 12 + (cols,) * 3 + (P("dp"),),
        check_vma=False,
    )
```

```python
import jax
import jax.numpy as jnp
from jax import lax
from jax.experimental import pallas as pl
from jax.experimental.pallas import tpu as pltpu
from jax.sharding import PartitionSpec as P

D = 768
H = 12
HD = 64
FF = 3072
STEP = 10
A = 196
S = 576

CORES = 2
HC = H // CORES
DC = D // CORES
FC = FF // CORES
PAIRS = HC // 2
T = CORES * S

WIN = 208
WINDOWS = (0, 192)

EPS_NORM = 1e-06
BETA_ONE = 0.9
BETA_TWO = 0.95
ADAM_EPS = 1e-08
DECAY_RATE = 0.05
RATE_VECTOR = 0.8
CLIP_LIMIT = 1.0
NEG = -1e30

bf16 = jnp.bfloat16
f32 = jnp.float32
VMEM_LIMIT = 56 * 1024 * 1024


SIDE = 4
CHIPS = SIDE**3
PLANE = SIDE * SIDE
KR = D // CHIPS
FR = FC // CHIPS
BLOCK = SIDE * KR
QUARTER = PLANE * KR
BOTH = ("grp", "dp")


def device(core, x, y, z):
    return ((core * SIDE + x) * SIDE + y) * SIDE + z


def lines():
    r = range(SIDE)
    return [[device(0, a, g, z) for a in r] for g in r for z in r] + [
        [device(1, g, a, z) for a in r] for g in r for z in r
    ]


def planes():
    r = range(SIDE)
    return [[device(0, a, g, z) for g in r for z in r] for a in r] + [
        [device(1, g, a, z) for g in r for z in r] for a in r
    ]


def shift(value, d):
    pairs = [(group[i], group[(i + d) % SIDE]) for group in lines() for i in range(SIDE)]
    return lax.ppermute(value, BOTH, pairs)


def plane_swap(value):
    return lax.all_to_all(value, BOTH, 0, 0, axis_index_groups=planes())


def natural(core, a, g):
    return jnp.where(core == 0, SIDE * a + g, SIDE * g + a)


def lay_out(place_ref, pieces, full_ref):
    core, me = place_ref[0], place_ref[1]
    for d, piece in enumerate(pieces):
        a = (me + SIDE - d) & (SIDE - 1)
        for g in range(SIDE):
            at = pl.multiple_of(natural(core, a, g) * BLOCK, BLOCK)
            full_ref[pl.ds(at, BLOCK), :] = piece[g * BLOCK : (g + 1) * BLOCK, :]


def usable_rows(place_ref, group, rows, base=0):
    slot = lax.broadcasted_iota(jnp.int32, (rows, 1), 0) + base
    first = ((slot < A) & (slot < place_ref[2])) | ((slot >= A) & (slot < 2 * A) & (slot - A < place_ref[3]))
    first = first.astype(f32)
    second = (slot < place_ref[4]).astype(f32)
    if isinstance(group, int):
        return second if group else first
    return jnp.where(group == 0, first, second)


def own_rows(win):
    row = lax.broadcasted_iota(jnp.int32, (WIN, 1), 0) + (WINDOWS[win] - win * A)
    return ((row >= 0) & (row < A)).astype(f32)


def key_bias(place_ref, win=None):
    if win is None:
        key = lax.broadcasted_iota(jnp.int32, (1, S), 1)
        return jnp.where(key < place_ref[4], 0.0, NEG)
    key = lax.broadcasted_iota(jnp.int32, (1, WIN), 1) + (WINDOWS[win] - win * A)
    return jnp.where((key >= 0) & (key < place_ref[2 + win]), 0.0, NEG)


def exact_dot(a, b):
    high = a.astype(bf16)
    rest = a - high.astype(f32)
    mid = rest.astype(bf16)
    low = (rest - mid.astype(f32)).astype(bf16)
    b = b.astype(bf16)
    return dot(high, b) + dot(mid, b) + dot(low, b)


def spots(core, shape, full, part):
    l = lax.broadcasted_iota(jnp.int32, shape, full)
    m = lax.broadcasted_iota(jnp.int32, shape, part)
    q = (m * 2731) >> 16
    return l == m + FR * (q + core)


def spots_t(core):
    return spots(core, (DC, D), 1, 0)


def params(**kw):
    return pltpu.CompilerParams(vmem_limit_bytes=VMEM_LIMIT, **kw)


def cost(flops, bytes_accessed, transcendentals=0):
    return pl.CostEstimate(
        flops=int(flops), bytes_accessed=int(bytes_accessed), transcendentals=int(transcendentals)
    )


def dot(a, b):
    return jnp.dot(a, b, preferred_element_type=f32)


def dot_t(a, b):
    return lax.dot_general(a, b, (((1,), (1,)), ((), ())), preferred_element_type=f32)


def t_dot(a, b):
    return lax.dot_general(a, b, (((0,), (0,)), ((), ())), preferred_element_type=f32)


def stats(z):
    mean_val = jnp.mean(z, axis=-1, keepdims=True)
    centred = z - mean_val
    variance = jnp.mean(centred * centred, axis=-1, keepdims=True)
    inv_std = lax.rsqrt(variance + EPS_NORM)
    return centred * inv_std, inv_std


def norm_back(grad, normed, inv_std, gain):
    e = grad * gain
    return inv_std * (
        e
        - jnp.mean(e, axis=-1, keepdims=True)
        - normed * jnp.mean(e * normed, axis=-1, keepdims=True)
    )


def swap_halves(u):
    lanes = u.shape[1]
    lane = lax.broadcasted_iota(jnp.int32, u.shape, 1)
    up = pltpu.roll(u, lanes - HD // 2, 1)
    down = pltpu.roll(u, HD // 2, 1)
    return jnp.where((lane & (HD - 1)) < HD // 2, up, down)


TURN = 1.5707963267948966


def sin_cos(a):
    k = jnp.floor(a * (1.0 / TURN) + 0.5)
    r = ((a - k * 1.5703125) - k * 4.837512969970703125e-4) - k * 7.54978995489188216e-8
    z = r * r
    s = ((-1.9515295891e-4 * z + 8.3321608736e-3) * z - 1.6666654611e-1) * z * r + r
    c = ((2.443315711809948e-5 * z - 1.388731625493765e-3) * z + 4.166664568298827e-2) * z * z - 0.5 * z + 1.0
    quarter = k.astype(jnp.int32)
    odd = (quarter & 1) == 1
    sine = jnp.where(odd, c, s)
    cosine = jnp.where(odd, s, c)
    sine = jnp.where((quarter & 2) == 0, sine, -sine)
    cosine = jnp.where(((quarter + 1) & 2) == 0, cosine, -cosine)
    return sine, cosine


def pre_kernel(
    place_ref, x_ref, xo_ref, ints_ref, v0, v1, v2, v3,
    vec_ref, h_ref, ht_ref, cos_ref, sin_ref, b1_ref, pos_ref,
    full_s, rows_s,
):
    i = pl.program_id(0)
    core = place_ref[0]

    @pl.when(i == 0)
    def _():
        lay_out(place_ref, (v0, v1, v2, v3), full_s)
        rows_s[...] = full_s[...].astype(f32).T[:16, :]
        vec_ref[...] = rows_s[...]
        units = dot(rows_s[8:16, :].astype(bf16), spots(core, (D, DC), 0, 1).astype(bf16))
        for r in range(FC // DC):
            b1_ref[:, r * DC : (r + 1) * DC] = units[2 + r : 3 + r, :]

    mine = i == 0
    normed, _ = stats(jnp.where(mine, x_ref[...], xo_ref[...]).astype(f32))
    h = normed * rows_s[0:1, :] + rows_s[1:2, :]
    h_ref[...] = h.astype(bf16)
    ht_ref[0] = h.T.astype(bf16)
    src = lax.broadcasted_iota(jnp.int32, (D, DC), 0)
    dst = lax.broadcasted_iota(jnp.int32, (D, DC), 1)
    want = core * (DC // 2) + (dst // HD) * (HD // 2) + (dst & (HD // 2 - 1))
    freqs = rows_s[8:16, :].astype(bf16)
    col = dot(freqs, (src == want).astype(bf16))[1:2, :]
    row = dot(freqs, (src == want + D // 2).astype(bf16))[1:2, :]
    pos = ints_ref[0].astype(f32).T
    pos_ref[0] = pos
    angle = pos[:, 1:2] * col + pos[:, 0:1] * row
    lane = lax.broadcasted_iota(jnp.int32, (1, DC), 1)
    sign = jnp.where((lane & (HD - 1)) < HD // 2, -1.0, 1.0)
    small = jnp.max(jnp.abs(angle)) < 8000.0

    @pl.when(small)
    def _():
        sine, cosine = sin_cos(angle)
        cos_ref[...] = cosine
        sin_ref[...] = sine * sign

    @pl.when(jnp.logical_not(small))
    def _():
        cos_ref[...] = jnp.cos(angle)
        sin_ref[...] = jnp.sin(angle) * sign


def gy_kernel(place_ref, c_ref, co_ref, gy_ref):
    i = pl.program_id(0)
    keep = usable_rows(place_ref, i ^ place_ref[0], S)
    gy_ref[...] = (jnp.where(i == 0, c_ref[...], co_ref[...]).astype(f32) * keep).astype(bf16)


def gy_call(place, c, co):
    whole = pl.BlockSpec((S, D), lambda i, c: (0, 0))
    return pl.pallas_call(
        gy_kernel,
        grid_spec=pltpu.PrefetchScalarGridSpec(
            num_scalar_prefetch=1,
            grid=(CORES,),
            in_specs=[whole, whole],
            out_specs=pl.BlockSpec((S, D), lambda i, c: (i, 0)),
        ),
        out_shape=jax.ShapeDtypeStruct((T, D), bf16),
        compiler_params=params(),
        cost_estimate=cost(4 * T * D, T * D * 4),
    )(place, c, co)


def pre_call(place, x, xo, ints, pieces):
    tile = lambda n: pl.BlockSpec((S, n), lambda i, c: (i, 0))
    whole = lambda a: pl.BlockSpec(a.shape, lambda i, c: (0,) * a.ndim)
    return pl.pallas_call(
        pre_kernel,
        grid_spec=pltpu.PrefetchScalarGridSpec(
            num_scalar_prefetch=1,
            grid=(CORES,),
            in_specs=[whole(a) for a in (x, xo)]
            + [pl.BlockSpec((1, 8, S), lambda i, c: (i, 0, 0))]
            + [whole(a) for a in pieces],
            out_specs=[
                pl.BlockSpec((16, D), lambda i, c: (0, 0)),
                tile(D),
                pl.BlockSpec((1, D, S), lambda i, c: (i, 0, 0)),
                tile(DC),
                tile(DC),
                pl.BlockSpec((1, FC), lambda i, c: (0, 0)),
                pl.BlockSpec((1, S, 8), lambda i, c: (i, 0, 0)),
            ],
            scratch_shapes=[pltpu.VMEM((D, 128), bf16), pltpu.VMEM((16, D), f32)],
        ),
        out_shape=[
            jax.ShapeDtypeStruct((16, D), f32),
            jax.ShapeDtypeStruct((T, D), bf16),
            jax.ShapeDtypeStruct((CORES, D, S), bf16),
            jax.ShapeDtypeStruct((T, DC), f32),
            jax.ShapeDtypeStruct((T, DC), f32),
            jax.ShapeDtypeStruct((1, FC), f32),
            jax.ShapeDtypeStruct((CORES, S, 8), f32),
        ],
        compiler_params=params(),
        cost_estimate=cost(T * (20 * D + 40 * DC), T * (D * 10 + DC * 8)),
    )(place, x, xo, ints, *pieces)


def qkv_kernel(place_ref, h_ref, w0, w1, w2, w3, v_ref, cos_ref, sin_ref, q_out, k_out, v_out, w_s):
    @pl.when(pl.program_id(0) == 0)
    def _():
        lay_out(place_ref, (w0, w1, w2, w3), w_s)

    cosine = cos_ref[...]
    sine = sin_ref[...]
    at = pl.ds(pl.multiple_of(place_ref[0] * DC, DC), DC)
    acc = dot(h_ref[...], w_s[...])
    part = lambda i: jnp.concatenate([acc[:, (3 * p + i) * 128 : (3 * p + i + 1) * 128] for p in range(PAIRS)], axis=1)
    q = part(0) + v_ref[4:5, at]
    k = part(1) + v_ref[5:6, at]
    q_out[...] = ((q * cosine + swap_halves(q) * sine) * HD ** (-0.5)).astype(bf16)
    k_out[...] = (k * cosine + swap_halves(k) * sine).astype(bf16)
    v_out[...] = (part(2) + v_ref[6:7, at]).astype(bf16)


def qkv_call(place, h1, pieces, vec, cosine, sine):
    rows = 288
    tile = lambda n: pl.BlockSpec((rows, n), lambda i, c: (i, 0))
    whole = lambda a: pl.BlockSpec(a.shape, lambda i, c: (0,) * a.ndim)
    return pl.pallas_call(
        qkv_kernel,
        grid_spec=pltpu.PrefetchScalarGridSpec(
            num_scalar_prefetch=1,
            grid=(T // rows,),
            in_specs=[tile(D)] + [whole(a) for a in pieces] + [whole(vec), tile(DC), tile(DC)],
            out_specs=[tile(DC)] * 3,
            scratch_shapes=[pltpu.VMEM((D, 3 * DC), bf16)],
        ),
        out_shape=[jax.ShapeDtypeStruct((T, DC), bf16)] * 3,
        compiler_params=params(),
        cost_estimate=cost(2 * T * D * 3 * DC, T * D * 2 + D * 3 * DC * 2 + T * DC * 14),
    )(place, h1, *pieces, vec, cosine, sine)


def softmax_head(q, k, v, mine, bias):
    s = dot_t(jnp.where(mine, q, jnp.zeros_like(q)), k) + bias
    e = jnp.exp(s - jnp.max(s, axis=-1, keepdims=True))
    p = e * (1.0 / jnp.sum(e, axis=-1, keepdims=True))
    return p


def attn_fwd_kernel(
    place_ref, q0, k0, v0, q1, k1, v1, o_ref, p0_ref, p1_ref
):
    lane = lax.broadcasted_iota(jnp.int32, (1, 2 * HD), 1)
    low = lane < HD
    q, k, v = q1[0], k1[0], v1[0]
    mixes = []
    bias = key_bias(place_ref)
    for head, mine in ((0, low), (1, ~low)):
        p = softmax_head(q, k, v, mine, bias).astype(bf16)
        p1_ref[head] = p
        mixes.append(dot(p, v))
    mix = jnp.where(low, mixes[0], mixes[1])
    o_ref[1] = jnp.where(usable_rows(place_ref, 1, S) > 0, mix, v.astype(f32)).astype(bf16)
    o_ref[0] = v0[0]
    for win, base in enumerate(WINDOWS):
        q, k, v = (r[0, base : base + WIN, :] for r in (q0, k0, v0))
        own = own_rows(win)
        bias = key_bias(place_ref, win)
        mixes = []
        for head, mine in ((0, low), (1, ~low)):
            p = softmax_head(q, k, v, mine, bias)
            p = (p * own).astype(bf16)
            p0_ref[head, win] = p
            mixes.append(dot(p, v))
        mix = jnp.where(low, mixes[0], mixes[1])
        use = (own * usable_rows(place_ref, 0, WIN, base)) > 0
        before = o_ref[0, base : base + WIN, :].astype(f32)
        o_ref[0, base : base + WIN, :] = jnp.where(use, mix, before).astype(bf16)


def attn_fwd_call(place, q, k, v):
    block = lambda g: pl.BlockSpec((1, S, 2 * HD), lambda p, c: (g ^ c[0], 0, p))
    q, k, v = (a.reshape(CORES, S, DC) for a in (q, k, v))
    return pl.pallas_call(
        attn_fwd_kernel,
        grid_spec=pltpu.PrefetchScalarGridSpec(
            num_scalar_prefetch=1,
            grid=(PAIRS,),
            in_specs=[block(0)] * 3 + [block(1)] * 3,
            out_specs=[
                pl.BlockSpec((CORES, S, 2 * HD), lambda p, c: (0, 0, p)),
                pl.BlockSpec((2, 2, WIN, WIN), lambda p, c: (p, 0, 0, 0)),
                pl.BlockSpec((2, S, S), lambda p, c: (p, 0, 0)),
            ],
        ),
        out_shape=[
            jax.ShapeDtypeStruct((CORES, S, DC), bf16),
            jax.ShapeDtypeStruct((HC, 2, WIN, WIN), bf16),
            jax.ShapeDtypeStruct((HC, S, S), bf16),
        ],
        compiler_params=params(),
        cost_estimate=cost(4 * HC * (S * S + 2 * WIN * WIN) * 128, 12e6, HC * S * S),
    )(place, q, k, v, q, k, v)


def proj_kernel(place_ref, mine_ref, other_ref, x_ref, xo_ref, w0, w1, w2, w3, v_ref, after_ref, h2_ref, w_s):
    @pl.when(pl.program_id(0) == 0)
    def _():
        lay_out(place_ref, (w0, w1, w2, w3), w_s)

    core = place_ref[0]
    at = lambda c: pl.ds(pl.multiple_of(c * DC, DC), DC)
    branch = dot(mine_ref[0], w_s[at(core), :]) + dot(other_ref[0], w_s[at(1 - core), :])
    x = jnp.where(pl.program_id(0) < pl.num_programs(0) // CORES, x_ref[...], xo_ref[...])
    after = x.astype(f32) + (branch + v_ref[7:8, :])
    after_ref[...] = after
    normed, _ = stats(after)
    h2_ref[...] = (normed * v_ref[2:3, :] + v_ref[3:4, :]).astype(bf16)


def proj_call(place, mine, other, x, xo, pieces, vec):
    rows = 288
    half = S // rows
    tile = lambda n: pl.BlockSpec((rows, n), lambda i, c: (i, 0))
    whole = lambda a: pl.BlockSpec(a.shape, lambda i, c: (0,) * a.ndim)
    return pl.pallas_call(
        proj_kernel,
        grid_spec=pltpu.PrefetchScalarGridSpec(
            num_scalar_prefetch=1,
            grid=(T // rows,),
            in_specs=[
                pl.BlockSpec((1, rows, DC), lambda i, c: ((i // half) ^ c[0], i % half, 0)),
                pl.BlockSpec((1, rows, DC), lambda i, c: ((i // half) ^ c[0], i % half, 0)),
                pl.BlockSpec((rows, D), lambda i, c: (jnp.minimum(i, half - 1), 0)),
                pl.BlockSpec((rows, D), lambda i, c: (jnp.maximum(i - half, 0), 0)),
            ]
            + [whole(a) for a in pieces]
            + [whole(vec)],
            out_specs=[tile(D), tile(D)],
            scratch_shapes=[pltpu.VMEM((D, D), bf16)],
        ),
        out_shape=[jax.ShapeDtypeStruct((T, D), f32), jax.ShapeDtypeStruct((T, D), bf16)],
        compiler_params=params(),
        cost_estimate=cost(2 * T * D * D, T * D * 10 + D * D * 2),
    )(place, mine, other, x, xo, *pieces, vec)


PACK = 4 * DC + 128
K0 = (2.0 / 3.141592653589793) ** 0.5
FT = 768


def gelu_slope(u):
    sq = u * u
    th = jnp.tanh(u * (K0 + (K0 * 0.044715) * sq))
    half = 0.5 + 0.5 * th
    return u * half, half + (u * (half - half * half)) * (2 * K0 + (6 * K0 * 0.044715) * sq)


def mlp_kernel(
    place_ref, h2_ref, w10, w11, w12, w13, w2_ref, b1_ref, mlp_ref, mlpo_ref, act_ref, slope_ref, w1_s
):
    i = pl.program_id(0)

    @pl.when(i == 0)
    def _():
        lay_out(place_ref, (w10, w11, w12, w13), w1_s)

    for f in range(FC // FT):
        c = slice(f * FT, (f + 1) * FT)
        act, slope = gelu_slope(dot(h2_ref[...], w1_s[:, c]) + b1_ref[:, c])
        act_ref[:, c] = act.astype(bf16)
        slope_ref[:, c] = slope.astype(bf16)
    mlp = dot(act_ref[...], w2_ref[...])
    half = pl.num_programs(0) // CORES

    @pl.when(i < half)
    def _():
        mlp_ref[...] = mlp

    @pl.when(i >= half)
    def _():
        mlpo_ref[...] = mlp


def mlp_call(place, h2, pieces, w2, b1):
    rows = 288
    half = S // rows
    tile = lambda n: pl.BlockSpec((rows, n), lambda i, c: (i, 0))
    whole = lambda a: pl.BlockSpec(a.shape, lambda i, c: (0,) * a.ndim)
    return pl.pallas_call(
        mlp_kernel,
        grid_spec=pltpu.PrefetchScalarGridSpec(
            num_scalar_prefetch=1,
            grid=(T // rows,),
            in_specs=[tile(D)] + [whole(a) for a in pieces] + [whole(w2), whole(b1)],
            out_specs=[
                pl.BlockSpec((rows, D), lambda i, c: (jnp.minimum(i, half - 1), 0)),
                pl.BlockSpec((rows, D), lambda i, c: (jnp.maximum(i - half, 0), 0)),
                tile(FC),
                tile(FC),
            ],
            scratch_shapes=[pltpu.VMEM((D, FC), bf16)],
        ),
        out_shape=[
            jax.ShapeDtypeStruct((S, D), f32),
            jax.ShapeDtypeStruct((S, D), f32),
            jax.ShapeDtypeStruct((T, FC), bf16),
            jax.ShapeDtypeStruct((T, FC), bf16),
        ],
        compiler_params=params(),
        cost_estimate=cost(4 * T * D * FC, 20e6, T * FC),
    )(place, h2, *pieces, w2, b1)


def mlp_back_kernel(place_ref, gy_ref, slope_ref, w10, w11, w12, w13, w2_ref, gh2_ref, gup_ref, gb1_ref, w1_s):
    @pl.when(pl.program_id(0) == 0)
    def _():
        lay_out(place_ref, (w10, w11, w12, w13), w1_s)
        gb1_ref[...] = jnp.zeros_like(gb1_ref)

    for f in range(FC // FT):
        c = slice(f * FT, (f + 1) * FT)
        gup = (dot_t(gy_ref[...], w2_ref[c, :]) * slope_ref[:, c].astype(f32)).astype(bf16)
        gup_ref[:, c] = gup
        gb1_ref[:, c] += jnp.sum(gup.astype(f32), axis=0, keepdims=True)
    gh2_ref[...] = dot_t(gup_ref[...], w1_s[...]).astype(bf16)


def mlp_back_call(place, gy, slope, pieces, w2):
    rows = 288
    tile = lambda n: pl.BlockSpec((rows, n), lambda i, c: (i, 0))
    whole = lambda a: pl.BlockSpec(a.shape, lambda i, c: (0,) * a.ndim)
    return pl.pallas_call(
        mlp_back_kernel,
        grid_spec=pltpu.PrefetchScalarGridSpec(
            num_scalar_prefetch=1,
            grid=(T // rows,),
            in_specs=[tile(D), tile(FC)] + [whole(a) for a in pieces] + [whole(w2)],
            out_specs=[tile(D), tile(FC), pl.BlockSpec((1, FC), lambda i, c: (0, 0))],
            scratch_shapes=[pltpu.VMEM((D, FC), bf16)],
        ),
        out_shape=[
            jax.ShapeDtypeStruct((T, D), bf16),
            jax.ShapeDtypeStruct((T, FC), bf16),
            jax.ShapeDtypeStruct((1, FC), f32),
        ],
        compiler_params=params(),
        cost_estimate=cost(4 * T * D * FC, 16e6),
    )(place, gy, slope, *pieces, w2)


def by_line(place_ref, value, block, out_ref):
    core = place_ref[0]
    for n in range(PLANE):
        to = jnp.where(core == 0, n, (n % SIDE) * SIDE + n // SIDE)
        out_ref[pl.ds(pl.multiple_of(to * block, block), block), :] = value[n * block : (n + 1) * block, :].astype(bf16)


def fc1_grad_kernel(place_ref, h2_ref, gup_ref, out_ref):
    by_line(place_ref, t_dot(h2_ref[...], gup_ref[...]), BLOCK, out_ref)


def fc1_grad_call(place, h2, gup):
    return pl.pallas_call(
        fc1_grad_kernel,
        grid_spec=pltpu.PrefetchScalarGridSpec(
            num_scalar_prefetch=1,
            grid=(FC // FT,),
            in_specs=[pl.BlockSpec((T, D), lambda i, c: (0, 0)), pl.BlockSpec((T, FT), lambda i, c: (0, i))],
            out_specs=pl.BlockSpec((D, FT), lambda i, c: (0, i)),
        ),
        out_shape=jax.ShapeDtypeStruct((D, FC), bf16),
        compiler_params=params(),
        cost_estimate=cost(2 * T * D * FC, T * (D + FC) * 2 + D * FC * 2),
    )(place, h2, gup)


def fc2_grad_kernel(place_ref, act_ref, gy_ref, out_ref):
    by_line(place_ref, t_dot(act_ref[...], gy_ref[...]), SIDE * FR, out_ref)


def fc2_grad_call(place, act, gy):
    return pl.pallas_call(
        fc2_grad_kernel,
        grid_spec=pltpu.PrefetchScalarGridSpec(
            num_scalar_prefetch=1,
            grid=(D // DC,),
            in_specs=[pl.BlockSpec((T, FC), lambda i, c: (0, 0)), pl.BlockSpec((T, DC), lambda i, c: (0, i))],
            out_specs=pl.BlockSpec((FC, DC), lambda i, c: (0, i)),
        ),
        out_shape=jax.ShapeDtypeStruct((FC, D), bf16),
        compiler_params=params(),
        cost_estimate=cost(2 * T * D * FC, T * (D + FC) * 2 + D * FC * 2),
    )(place, act, gy)


def mid_kernel(place_ref, after_ref, gy_ref, gh2_ref, other_ref, v_ref, ga_ref, gab_ref, sums_ref):
    i = pl.program_id(0)
    normed, inv_std = stats(after_ref[...])
    gh2 = gh2_ref[...].astype(f32) + other_ref[...].astype(f32)
    gy = gy_ref[...].astype(f32)
    ga = gy + norm_back(gh2, normed, inv_std, v_ref[2:3, :])
    gab = ga.astype(bf16)
    gab_ref[...] = gab

    @pl.when(i == 0)
    def _():
        sums_ref[...] = jnp.zeros_like(sums_ref)

    @pl.when(i < pl.num_programs(0) // CORES)
    def _():
        ga_ref[...] = ga
        sums_ref[0:1, :] += jnp.sum(gh2 * normed, axis=0, keepdims=True)
        sums_ref[1:2, :] += jnp.sum(gh2, axis=0, keepdims=True)
        sums_ref[2:3, :] += jnp.sum(gab.astype(f32), axis=0, keepdims=True)
        sums_ref[3:4, :] += jnp.sum(gy, axis=0, keepdims=True)


def mid_call(place, after, gy, gh2, other, vec):
    rows = 288
    half = S // rows
    tile = lambda n: pl.BlockSpec((rows, n), lambda i, c: (i, 0))
    flipped = pl.BlockSpec((rows, D), lambda i, c: ((i + half) % (2 * half), 0))
    whole = lambda a: pl.BlockSpec(a.shape, lambda i, c: (0,) * a.ndim)
    return pl.pallas_call(
        mid_kernel,
        grid_spec=pltpu.PrefetchScalarGridSpec(
            num_scalar_prefetch=1,
            grid=(T // rows,),
            in_specs=[tile(D), tile(D), tile(D), flipped, whole(vec)],
            out_specs=[
                pl.BlockSpec((rows, D), lambda i, c: (jnp.minimum(i, half - 1), 0)),
                tile(D),
                pl.BlockSpec((8, D), lambda i, c: (0, 0)),
            ],
        ),
        out_shape=[
            jax.ShapeDtypeStruct((S, D), f32),
            jax.ShapeDtypeStruct((T, D), bf16),
            jax.ShapeDtypeStruct((8, D), f32),
        ],
        compiler_params=params(),
        cost_estimate=cost(30 * T * D, T * D * 14),
    )(place, after, gy, gh2, other, vec)


def back_head(q_t, k, v, do, do_t, delta, p, mine, head):
    gp = dot_t(jnp.where(mine, do, jnp.zeros_like(do)), v)
    gs = (p.astype(f32) * (gp - delta)).astype(bf16)
    at = slice(head * HD, (head + 1) * HD)
    return dot(gs, k), dot(q_t[at, :], gs), dot(do_t[at, :], p)


def deltas(do, o, low):
    prod = do.astype(f32) * o.astype(f32)
    d0 = jnp.sum(jnp.where(low, prod, 0.0), axis=-1, keepdims=True)
    d1 = jnp.sum(jnp.where(low, 0.0, prod), axis=-1, keepdims=True)
    return d0, d1


def vec_sums(place_ref, x_ref, xo_ref, gh_ref, gho_ref, mid_ref, att_ref, gb1_ref, rows_s):
    core = place_ref[0]
    rows_s[...] = jnp.zeros_like(rows_s)
    for x, gh in ((x_ref, gh_ref), (xo_ref, gho_ref)):
        normed, _ = stats(x[...].astype(f32))
        g = gh[...]
        rows_s[0:1, :] += jnp.sum(g * normed, axis=0, keepdims=True)
        rows_s[1:2, :] += jnp.sum(g, axis=0, keepdims=True)
    rows_s[2:4, :] = mid_ref[0:2, :]
    rows_s[7:9, :] = mid_ref[2:4, :]
    att = jnp.concatenate([att_ref[p] for p in range(PAIRS)], axis=1)
    rows_s[4:7, pl.ds(pl.multiple_of(core * DC, DC), DC)] = att[2:5, :]
    src = lax.broadcasted_iota(jnp.int32, (DC, D), 0)
    dst = lax.broadcasted_iota(jnp.int32, (DC, D), 1)
    want = core * (DC // 2) + (src // HD) * (HD // 2) + (src & (HD // 2 - 1))
    lane = lax.broadcasted_iota(jnp.int32, (1, DC), 1)
    turn = jnp.where((lane & (HD - 1)) < HD // 2, att, -att)
    rows_s[9:10, :] = (
        exact_dot(turn, dst == want)[0:1, :] + exact_dot(turn, dst == want + D // 2)[1:2, :]
    )
    gb1 = jnp.concatenate([gb1_ref[:, r * DC : (r + 1) * DC] for r in range(FC // DC)] * 2, axis=0)
    rows_s[10:14, :] = exact_dot(gb1, spots_t(core))[:4, :]


def attn_bwd_kernel(
    place_ref,
    q0, k0, v0, o0, p0, cos0, sin0, pos0,
    q1, k1, v1, o1, p1, cos1, sin1, pos1,
    h1t_ref, ga_ref, cols_ref, mine_ref, other_ref, w0, w1, w2, w3, y0, y1, y2, y3,
    x_ref, xo_ref, mid_ref, gb1_ref,
    gw0, gw1, gw2, gw3, gh_ref, gho_ref,
    gq_s, gk_s, gv_s, gqkv_s, w_s, gw_s, y_s, do_s, att_s, rows_s, full_s,
):
    lane = lax.broadcasted_iota(jnp.int32, (1, 2 * HD), 1)
    low = lane < HD
    pair = pl.program_id(0)
    core = place_ref[0]

    @pl.when(pair == 0)
    def _():
        lay_out(place_ref, (y0, y1, y2, y3), y_s)

    wy = y_s[pl.ds(pl.multiple_of(core * DC + pair * 2 * HD, 2 * HD), 2 * HD), :]
    for frame in range(CORES):
        do_s[frame] = dot_t(ga_ref[frame], wy).astype(bf16)

    def finish(frame, q, k, cos_ref, sin_ref, pos_ref):
        cosine, sine = cos_ref[0], sin_ref[0]
        gq = gq_s[...] * HD ** (-0.5)
        gk = gk_s[...]
        sq, sk = swap_halves(gq), swap_halves(gk)
        turn = (q.astype(f32) * HD**0.5) * sq + k.astype(f32) * sk
        gq = (gq * cosine - sq * sine).astype(bf16)
        gk = (gk * cosine - sk * sine).astype(bf16)
        gv = gv_s[...].astype(bf16)
        gqkv_s[frame, :, : 2 * HD] = gq
        gqkv_s[frame, :, 2 * HD : 4 * HD] = gk
        gqkv_s[frame, :, 4 * HD :] = gv
        pos = pos_ref[0]
        col = jnp.sum(turn * pos[:, 1:2], axis=0, keepdims=True)
        row = jnp.sum(turn * pos[:, 0:1], axis=0, keepdims=True)
        bias = [jnp.sum(g.astype(f32), axis=0, keepdims=True) for g in (gq, gk, gv)]
        return jnp.concatenate([col, row] + bias, axis=0)

    q, k, v, do = q1[0], k1[0], v1[0], do_s[1 ^ core]
    d = deltas(do, o1[0], low)
    q_t, do_t = q.astype(f32).T.astype(bf16), do.astype(f32).T.astype(bf16)
    out = [
        back_head(q_t, k, v, do, do_t, d[head], p1[head], mine, head)
        for head, mine in ((0, low), (1, ~low))
    ]
    gq_s[...] = jnp.where(low, out[0][0], out[1][0])
    gk_s[...] = jnp.concatenate([out[0][1], out[1][1]], axis=0).T
    gv_s[...] = jnp.concatenate([out[0][2], out[1][2]], axis=0).T
    sums1 = finish(1, q, k, cos1, sin1, pos1)
    gq_s[...] = jnp.zeros_like(gq_s)
    gk_s[...] = jnp.zeros_like(gk_s)
    gv_s[...] = jnp.zeros_like(gv_s)
    for win, base in enumerate(WINDOWS):
        at = pl.ds(base, WIN)
        q, k, v, o = (r[0, at, :] for r in (q0, k0, v0, o0))
        do = do_s[core, at, :]
        d = deltas(do, o, low)
        q_t, do_t = q.astype(f32).T.astype(bf16), do.astype(f32).T.astype(bf16)
        out = [
            back_head(q_t, k, v, do, do_t, d[head], p0[head, win], mine, head)
            for head, mine in ((0, low), (1, ~low))
        ]
        gq_s[at, :] += jnp.where(low, out[0][0], out[1][0])
        gk_s[at, :] += jnp.concatenate([out[0][1], out[1][1]], axis=0).T
        gv_s[at, :] += jnp.concatenate([out[0][2], out[1][2]], axis=0).T
    sums0 = finish(0, q0[0], k0[0], cos0, sin0, pos0)
    att_s[pair, 0:5, :] = sums0 + sums1

    lay_out(place_ref, (w0, w1, w2, w3), w_s)
    gw = jnp.zeros((D, 6 * HD), f32)
    gw_mine = jnp.zeros((2 * HD, DC), f32)
    gw_other = jnp.zeros((2 * HD, DC), f32)
    for frame, out in ((0, gh_ref), (1, gho_ref)):
        g = gqkv_s[frame ^ core]
        gw += dot(h1t_ref[frame], g)
        gh = dot_t(g, w_s[...])

        @pl.when(pair == 0)
        def _(out=out, gh=gh):
            out[...] = gh

        @pl.when(pair > 0)
        def _(out=out, gh=gh):
            out[...] += gh

        cols = cols_ref[frame].astype(f32).T.astype(bf16)
        gw_mine += dot(cols, mine_ref[frame ^ core])
        gw_other += dot(cols, other_ref[frame ^ core])
    gw_s[:, : 6 * HD] = gw.astype(bf16)
    at = lambda c: pl.ds(pl.multiple_of(c * DC, DC), DC)
    gw_s[at(core), 6 * HD :] = gw_mine.T.astype(bf16)
    gw_s[at(1 - core), 6 * HD :] = gw_other.T.astype(bf16)
    to = pl.ds(pl.multiple_of(pair * 8 * HD, 8 * HD), 8 * HD)
    for d, out in enumerate((gw0, gw1, gw2, gw3)):
        a = (place_ref[1] + d) & (SIDE - 1)
        for g in range(SIDE):
            at = pl.multiple_of(natural(core, a, g) * BLOCK, BLOCK)
            out[g * BLOCK : (g + 1) * BLOCK, to] = gw_s[pl.ds(at, BLOCK), :]

    @pl.when(pair == PAIRS - 1)
    def _():
        vec_sums(place_ref, x_ref, xo_ref, gh_ref, gho_ref, mid_ref, att_s, gb1_ref, rows_s)
        full_s[...] = rows_s[...].T.astype(bf16)
        for d, out in enumerate((gw0, gw1, gw2, gw3)):
            a = (place_ref[1] + d) & (SIDE - 1)
            for g in range(SIDE):
                at = pl.multiple_of(natural(core, a, g) * BLOCK, BLOCK)
                out[g * BLOCK : (g + 1) * BLOCK, 4 * DC :] = full_s[pl.ds(at, BLOCK), :]


def attn_bwd_call(
    place, q, k, v, ga, mine, other, p0, p1, cosine, sine, pos, h1t, pieces, proj_pieces, x, xo, mid, gb1
):
    q, k, v, cosine, sine = (a.reshape(CORES, S, DC) for a in (q, k, v, cosine, sine))
    ga = ga.reshape(CORES, S, D)
    block = lambda g: pl.BlockSpec((1, S, 2 * HD), lambda p, c: (g ^ c[0], 0, p))
    own = lambda g: pl.BlockSpec((1, S, 2 * HD), lambda p, c: (g, 0, p))
    quarter = pl.BlockSpec((QUARTER, 6 * HD), lambda p, c: (0, p))
    keep = lambda *n: pl.BlockSpec(n, lambda p, c: (0,) * len(n))
    at = lambda g: pl.BlockSpec((1, S, 8), lambda p, c: (g ^ c[0], 0, 0))
    whole = lambda a: pl.BlockSpec(a.shape, lambda p, c: (0,) * a.ndim)
    return pl.pallas_call(
        attn_bwd_kernel,
        grid_spec=pltpu.PrefetchScalarGridSpec(
            num_scalar_prefetch=1,
            grid=(PAIRS,),
            in_specs=[block(0)] * 3
            + [own(0), pl.BlockSpec((2, 2, WIN, WIN), lambda p, c: (p, 0, 0, 0))]
            + [block(0)] * 2
            + [at(0)]
            + [block(1)] * 3
            + [own(1), pl.BlockSpec((2, S, S), lambda p, c: (p, 0, 0))]
            + [block(1)] * 2
            + [at(1)]
            + [whole(h1t), whole(ga), pl.BlockSpec((CORES, S, 2 * HD), lambda p, c: (0, 0, PAIRS * c[0] + p))]
            + [whole(mine), whole(other)]
            + [quarter] * 4
            + [whole(a) for a in proj_pieces]
            + [whole(a) for a in (x, xo, mid, gb1)],
            out_specs=[keep(QUARTER, PACK)] * 4 + [keep(S, D)] * 2,
            scratch_shapes=[pltpu.VMEM((S, 2 * HD), f32)] * 3
            + [pltpu.VMEM((CORES, S, 6 * HD), bf16)]
            + [pltpu.VMEM((D, 6 * HD), bf16), pltpu.VMEM((D, 8 * HD), bf16)]
            + [pltpu.VMEM((D, D), bf16), pltpu.VMEM((CORES, S, 2 * HD), bf16)]
            + [pltpu.VMEM((PAIRS, 8, 2 * HD), f32), pltpu.VMEM((128, D), f32), pltpu.VMEM((D, 128), bf16)],
        ),
        out_shape=[
            *[jax.ShapeDtypeStruct((QUARTER, PACK), bf16)] * 4,
            jax.ShapeDtypeStruct((S, D), f32),
            jax.ShapeDtypeStruct((S, D), f32),
        ],
        compiler_params=params(),
        cost_estimate=cost(10 * HC * S * S * 128 + 4 * T * D * 4 * DC, 36e6),
    )(
        place,
        q, k, v, mine, p0, cosine, sine, pos,
        q, k, v, mine, p1, cosine, sine, pos,
        h1t, ga, ga, mine, other, *pieces, *proj_pieces, x, xo, mid, gb1,
    )


def last_kernel(x_ref, ga_ref, gh_ref, other_ref, after_ref, mlp_ref, mlpo_ref, v_ref, gt_ref, out_ref):
    normed, inv_std = stats(x_ref[...].astype(f32))
    gt_ref[...] = ga_ref[...] + norm_back(gh_ref[...] + other_ref[...], normed, inv_std, v_ref[0:1, :])
    out_ref[...] = (after_ref[...] + (mlp_ref[...] + mlpo_ref[...] + v_ref[8:9, :])).astype(bf16)


def last_call(x, ga, gh, other, after, mlp, mlp_other, vec):
    rows = 288
    tile = lambda n: pl.BlockSpec((rows, n), lambda i: (i, 0))
    return pl.pallas_call(
        last_kernel,
        grid=(S // rows,),
        in_specs=[tile(D)] * 7 + [pl.BlockSpec(vec.shape, lambda i: (0, 0))],
        out_specs=[tile(D), tile(D)],
        out_shape=[jax.ShapeDtypeStruct((S, D), f32), jax.ShapeDtypeStruct((S, D), bf16)],
        compiler_params=params(),
        cost_estimate=cost(30 * S * D, S * D * 28),
    )(x, ga, gh, other, after, mlp, mlp_other, vec)


def pack_kernel(q0, q1, q2, q3, out_ref):
    total = q0[...].astype(f32) + q1[...].astype(f32) + q2[...].astype(f32) + q3[...].astype(f32)
    for n in range(PLANE):
        out_ref[n] = total[n * KR : (n + 1) * KR, :].astype(bf16)


def pack_call(parts):
    return pl.pallas_call(
        pack_kernel,
        out_shape=jax.ShapeDtypeStruct((PLANE, KR, PACK), bf16),
        compiler_params=params(),
        cost_estimate=cost(QUARTER * PACK * 4, QUARTER * PACK * 10),
    )(*parts)


def sum_kernel(in_ref, out_ref):
    total = in_ref[0].astype(f32)
    for n in range(1, PLANE):
        total += in_ref[n].astype(f32)
    out_ref[...] = total


def sum_call(packed):
    return pl.pallas_call(
        sum_kernel,
        out_shape=jax.ShapeDtypeStruct(packed.shape[1:], f32),
        compiler_params=params(),
        cost_estimate=cost(packed.size, packed.size * 2),
    )(packed)


def fc_kernel(place_ref, f1_ref, f1o_ref, f2_ref, f2o_ref, g1_ref, g2_ref, sq_ref):
    first = place_ref[0] == 0
    a, b = f1_ref[...], f1o_ref[...]
    a, b = jnp.where(first, a, b), jnp.where(first, b, a)
    for r in range(FC // DC):
        at = slice(r * DC, (r + 1) * DC)
        g1_ref[:, r * D : (r + 1) * D] = exact_dot(a[:, at], spots_t(0)) + exact_dot(b[:, at], spots_t(1))
    c, d = f2_ref[...], f2o_ref[...]
    g2_ref[:FR, :] = jnp.where(first, c, d)
    g2_ref[FR:, :] = jnp.where(first, d, c)
    total = jnp.sum(a * a + b * b, axis=(0, 1), keepdims=True) + jnp.sum(c * c + d * d, axis=(0, 1), keepdims=True)
    sq_ref[...] = jnp.broadcast_to(total, sq_ref.shape)


def fc_call(place, f1, f1o, f2, f2o):
    whole = lambda a: pl.BlockSpec(a.shape, lambda i, c: (0,) * len(a.shape))
    args = (f1, f1o, f2, f2o)
    shapes = [jax.ShapeDtypeStruct(s, f32) for s in ((KR, FF), (2 * FR, D), (8, 128))]
    return pl.pallas_call(
        fc_kernel,
        grid_spec=pltpu.PrefetchScalarGridSpec(
            num_scalar_prefetch=1,
            grid=(1,),
            in_specs=[whole(a) for a in args],
            out_specs=[whole(a) for a in shapes],
        ),
        out_shape=shapes,
        compiler_params=params(),
        cost_estimate=cost(6 * KR * DC * D * 8, 1e6),
    )(place, *args)


def norm_kernel(g_ref, o_ref, sq_ref, out_ref):
    g, o = g_ref[...], o_ref[...]
    cut = 4 * DC
    part = jnp.sum(g[:, :cut] * g[:, :cut] + o[:, :cut] * o[:, :cut], axis=(0, 1), keepdims=True)
    both = g[:, cut:] + o[:, cut:]
    part += jnp.sum(both * both, axis=(0, 1), keepdims=True)
    out_ref[...] = jnp.broadcast_to((part + sq_ref[0:1, 0:1])[None], out_ref.shape)


def norm_call(g, o, squares):
    return pl.pallas_call(
        norm_kernel,
        out_shape=jax.ShapeDtypeStruct((CHIPS, 8, 128), f32),
        compiler_params=params(),
        cost_estimate=cost(4 * KR * PACK, 1e6),
    )(g, o, squares)


RATES = (D ** (-0.5), max(1, 2 * D // S) ** (-0.5), D ** (-0.5), FF ** (-0.5), RATE_VECTOR)


def adam_kernel(place_ref, norm_ref, mine_ref, other_ref, g1_ref, g2_ref, *refs):
    masters, firsts, seconds = refs[0:5], refs[5:10], refs[10:15]
    outs = refs[15:30]
    norm_out, bias_out = refs[30:32]
    core = place_ref[0]
    mine, other = mine_ref[...], other_ref[...]
    g0 = jnp.where(core == 0, mine, other)
    g1 = jnp.where(core == 0, other, mine)
    total = jnp.sum(jnp.sum(norm_ref[...], axis=0)[0:1, 0:1], axis=(0, 1), keepdims=True)
    grad_norm = jnp.sqrt(total)
    norm_out[...] = jnp.broadcast_to(grad_norm, norm_out.shape)
    clip = jnp.minimum(1.0, CLIP_LIMIT / (grad_norm + 1e-06))

    def update(i, at, grad):
        clipped = grad * clip
        master = masters[i][at]
        first = BETA_ONE * firsts[i][at] + (1.0 - BETA_ONE) * clipped
        second = BETA_TWO * seconds[i][at] + (1.0 - BETA_TWO) * clipped * clipped
        first_hat = first / (1.0 - BETA_ONE**STEP)
        second_hat = second / (1.0 - BETA_TWO**STEP)
        decay = 0.0 if i == 4 else DECAY_RATE
        outs[3 * i][at] = master - RATES[i] * (first_hat / (jnp.sqrt(second_hat) + ADAM_EPS) + decay * master)
        outs[3 * i + 1][at] = first
        outs[3 * i + 2][at] = second

    rows = slice(None)
    for c, g in ((0, g0), (1, g1)):
        for p in range(PAIRS):
            for i in range(3):
                col = i * D + c * DC + p * 128
                update(0, (rows, slice(col, col + 128)), g[:, (4 * p + i) * 128 : (4 * p + i + 1) * 128])
            col = c * DC + p * 128
            update(1, (rows, slice(col, col + 128)), g[:, (4 * p + 3) * 128 : (4 * p + 4) * 128])
    update(2, (rows, rows), g1_ref[...])
    update(3, (rows, rows), g2_ref[...])
    vec = (g0 + g1)[:, 4 * DC : 4 * DC + 128]
    vec = jnp.concatenate([vec, jnp.zeros((16 - KR, 128), f32)], axis=0).T[:16, :KR]
    update(4, (rows, rows), vec[: masters[4].shape[0], :])
    bias_out[...] = vec[7:8, :] * clip


def adam_call(place, norm, mine, other, g1, g2, masters, firsts, seconds):
    whole = lambda a: pl.BlockSpec(a.shape, lambda i, c: (0,) * len(a.shape))
    args = [norm, mine, other, g1, g2, *masters, *firsts, *seconds]
    shapes = [jax.ShapeDtypeStruct(m.shape, f32) for m in masters for _ in range(3)]
    shapes += [jax.ShapeDtypeStruct((1, 128), f32), jax.ShapeDtypeStruct((1, KR), f32)]
    return pl.pallas_call(
        adam_kernel,
        grid_spec=pltpu.PrefetchScalarGridSpec(
            num_scalar_prefetch=1,
            grid=(1,),
            in_specs=[whole(a) for a in args],
            out_specs=[whole(a) for a in shapes],
        ),
        out_shape=shapes,
        compiler_params=params(),
        cost_estimate=cost(20 * KR * FF * 3, 3e6),
    )(place, *args)


def local(
    tokens,
    cotangent,
    counts,
    patch_row,
    patch_col,
    w_qkv,
    w_proj,
    w_fc1,
    w_fc2,
    vectors,
    m_qkv,
    v_qkv,
    m_proj,
    v_proj,
    m_fc1,
    v_fc1,
    m_fc2,
    v_fc2,
    m_vectors,
    v_vectors,
):
    core = lax.axis_index("grp")
    chip = lax.axis_index("dp")
    first_core = core == 0
    along = jnp.where(first_core, chip // PLANE, (chip // SIDE) % SIDE)
    vr = vectors.shape[0]

    def swap(a):
        return lax.ppermute(a, "grp", [(0, 1), (1, 0)])

    def halves(a):
        n = a.shape[-1] // 2
        return jnp.where(first_core, a[..., :n], a[..., n:])

    def over_plane(share):
        got = plane_swap(jnp.broadcast_to(share[None], (PLANE,) + share.shape))
        return got.reshape(PLANE * share.shape[0], share.shape[1])

    def along_line(quarter):
        return [quarter] + [shift(quarter, d) for d in range(1, SIDE)]

    def line_sum(whole):
        return lax.psum_scatter(whole, BOTH, scatter_dimension=0, axis_index_groups=lines(), tiled=True)

    fc2_b = w_fc2.astype(bf16)
    full_fc2 = lax.all_gather(jnp.where(first_core, fc2_b[:FR], fc2_b[FR:]), "dp", axis=0, tiled=True)
    qkv_b = w_qkv.astype(bf16)
    parts = [halves(qkv_b[:, i * D : (i + 1) * D]) for i in range(3)]
    by_pair = [parts[i][:, p * 128 : (p + 1) * 128] for p in range(PAIRS) for i in range(3)]
    vec_t = jnp.pad(vectors.astype(bf16).T, ((0, 0), (0, 128 - vr)))
    fc1_b = w_fc1.astype(bf16).reshape(KR, CHIPS, CORES, FR)
    share_fc1 = jnp.where(first_core, fc1_b[:, :, 0], fc1_b[:, :, 1]).reshape(KR, FC)
    quarter = over_plane(jnp.concatenate(by_pair + [vec_t, w_proj.astype(bf16), share_fc1], axis=1))
    cut = 3 * DC
    qkv_pieces = along_line(quarter[:, :cut])
    vec_pieces = along_line(quarter[:, cut : cut + 128])
    quarter, vec_pieces = lax.optimization_barrier((quarter, vec_pieces))
    proj_pieces = along_line(quarter[:, cut + 128 : cut + 128 + D])
    fc1_pieces = along_line(quarter[:, cut + 128 + D :])

    x_own = tokens.reshape(S, D)
    cot_own = cotangent.reshape(S, D)
    x_other, cot_other = swap(x_own), swap(cot_own)
    ints = jnp.concatenate(
        [
            patch_row.reshape(1, S),
            patch_col.reshape(1, S),
            jnp.pad(counts.reshape(1, 2), ((0, 0), (0, S - 2))),
            jnp.zeros((5, S), jnp.int32),
        ]
    )
    ints = jnp.stack([ints, swap(ints)])
    counts0 = jnp.where(first_core, ints[0, 2, :2], ints[1, 2, :2])
    counts1 = jnp.where(first_core, ints[1, 2, :1], ints[0, 2, :1])
    place = jnp.concatenate([jnp.stack([core, along]).astype(jnp.int32), counts0, counts1])

    gy = gy_call(place, cot_own, cot_other)
    vec, h1, h1t, cosine, sine, b1, pos = pre_call(place, x_own, x_other, ints, vec_pieces)
    q, k, v = qkv_call(place, h1, qkv_pieces, vec, cosine, sine)
    mine, p0, p1 = attn_fwd_call(place, q, k, v)
    other = swap(mine)
    after, h2 = proj_call(place, mine, other, x_own, x_other, proj_pieces, vec)
    mlp, mlp_part, act, slope = mlp_call(place, h2, fc1_pieces, full_fc2, b1)
    mlp_other = swap(mlp_part)

    sum_fc2 = line_sum(fc2_grad_call(place, act, gy))
    gh2, gup, gb1 = mlp_back_call(place, gy, slope, fc1_pieces, full_fc2)
    other_gh2 = swap(gh2)
    sum_fc1 = line_sum(fc1_grad_call(place, h2, gup))
    ga, gab, sums_mid = mid_call(place, after, gy, gh2, other_gh2, vec)
    gab, sum_fc2 = lax.optimization_barrier((gab, sum_fc2))
    got_fc2 = plane_swap(sum_fc2.reshape(PLANE, FR, D))
    *gw, gh1, gh1_part = attn_bwd_call(
        place, q, k, v, gab, mine, other, p0, p1, cosine, sine, pos, h1t, qkv_pieces, proj_pieces,
        x_own, x_other, sums_mid, gb1,
    )
    gh1_other = swap(gh1_part)
    got_fc1 = plane_swap(sum_fc1.reshape(PLANE, KR, FC))

    parts = [gw[0]] + [shift(gw[d], d) for d in range(1, SIDE)]
    g_fc2, g_fc1 = sum_call(got_fc2), sum_call(got_fc1)
    g1, g2, squares = fc_call(place, g_fc1, swap(g_fc1), g_fc2, swap(g_fc2))
    grads = sum_call(plane_swap(pack_call(parts)))
    gt, mixed = last_call(x_own, ga, gh1, gh1_other, after, mlp, mlp_other, vec)

    grads_other = swap(grads)
    norms = lax.all_to_all(norm_call(grads, grads_other, squares), "dp", 0, 0)
    *updates, grad_norm, bias_proj_grad = adam_call(
        place,
        norms,
        grads,
        grads_other,
        g1,
        g2,
        (w_qkv, w_proj, w_fc1, w_fc2, vectors),
        (m_qkv, m_proj, m_fc1, m_fc2, m_vectors),
        (v_qkv, v_proj, v_fc1, v_fc2, v_vectors),
    )
    return (
        mixed.reshape(1, 1, S, D),
        gt.reshape(1, 1, S, D),
        grad_norm[0, 0],
        *updates,
        bias_proj_grad.reshape(KR),
    )


def solution(mesh):
    frame = P("grp", "dp", None, None)
    ints = P("grp", "dp", None)
    rows = P("dp", None)
    cols = P(None, "dp")
    return jax.shard_map(
        local,
        mesh=mesh,
        in_specs=(frame, frame, ints, ints, ints, rows, rows, rows, rows, cols) + (rows,) * 8 + (cols,) * 2,
        out_specs=(frame, frame, P()) + (rows,) * 12 + (cols,) * 3 + (P("dp"),),
        check_vma=False,
    )
```

```python
import jax
import jax.numpy as jnp
from jax import lax
from jax.experimental import pallas as pl
from jax.experimental.pallas import tpu as pltpu
from jax.sharding import PartitionSpec as P

D = 768
H = 12
HD = 64
FF = 3072
STEP = 10
A = 196
S = 576

CORES = 2
HC = H // CORES
DC = D // CORES
FC = FF // CORES
PAIRS = HC // 2
T = CORES * S

WIN = 208
WINDOWS = (0, 192)

EPS_NORM = 1e-06
BETA_ONE = 0.9
BETA_TWO = 0.95
ADAM_EPS = 1e-08
DECAY_RATE = 0.05
RATE_VECTOR = 0.8
CLIP_LIMIT = 1.0
NEG = -1e30

bf16 = jnp.bfloat16
f32 = jnp.float32
VMEM_LIMIT = 56 * 1024 * 1024


SIDE = 4
CHIPS = SIDE**3
PLANE = SIDE * SIDE
KR = D // CHIPS
FR = FC // CHIPS
BLOCK = SIDE * KR
QUARTER = PLANE * KR
BOTH = ("grp", "dp")


def device(core, x, y, z):
    return ((core * SIDE + x) * SIDE + y) * SIDE + z


def lines():
    r = range(SIDE)
    return [[device(0, a, g, z) for a in r] for g in r for z in r] + [
        [device(1, g, a, z) for a in r] for g in r for z in r
    ]


def planes():
    r = range(SIDE)
    return [[device(0, a, g, z) for g in r for z in r] for a in r] + [
        [device(1, g, a, z) for g in r for z in r] for a in r
    ]


def shift(value, d):
    pairs = [(group[i], group[(i + d) % SIDE]) for group in lines() for i in range(SIDE)]
    return lax.ppermute(value, BOTH, pairs)


def plane_swap(value):
    return lax.all_to_all(value, BOTH, 0, 0, axis_index_groups=planes())


def natural(core, a, g):
    return jnp.where(core == 0, SIDE * a + g, SIDE * g + a)


def lay_out(place_ref, pieces, full_ref):
    core, me = place_ref[0], place_ref[1]
    for d, piece in enumerate(pieces):
        a = (me + SIDE - d) & (SIDE - 1)
        for g in range(SIDE):
            at = pl.multiple_of(natural(core, a, g) * BLOCK, BLOCK)
            full_ref[pl.ds(at, BLOCK), :] = piece[g * BLOCK : (g + 1) * BLOCK, :]


def usable_rows(place_ref, group, rows, base=0):
    slot = lax.broadcasted_iota(jnp.int32, (rows, 1), 0) + base
    first = ((slot < A) & (slot < place_ref[2])) | ((slot >= A) & (slot < 2 * A) & (slot - A < place_ref[3]))
    first = first.astype(f32)
    second = (slot < place_ref[4]).astype(f32)
    if isinstance(group, int):
        return second if group else first
    return jnp.where(group == 0, first, second)


def own_rows(win):
    row = lax.broadcasted_iota(jnp.int32, (WIN, 1), 0) + (WINDOWS[win] - win * A)
    return ((row >= 0) & (row < A)).astype(f32)


def key_bias(place_ref, win=None):
    if win is None:
        key = lax.broadcasted_iota(jnp.int32, (1, S), 1)
        return jnp.where(key < place_ref[4], 0.0, NEG)
    key = lax.broadcasted_iota(jnp.int32, (1, WIN), 1) + (WINDOWS[win] - win * A)
    return jnp.where((key >= 0) & (key < place_ref[2 + win]), 0.0, NEG)


def exact_dot(a, b):
    high = a.astype(bf16)
    rest = a - high.astype(f32)
    mid = rest.astype(bf16)
    low = (rest - mid.astype(f32)).astype(bf16)
    b = b.astype(bf16)
    return dot(high, b) + dot(mid, b) + dot(low, b)


def spots(core, shape, full, part):
    l = lax.broadcasted_iota(jnp.int32, shape, full)
    m = lax.broadcasted_iota(jnp.int32, shape, part)
    q = (m * 2731) >> 16
    return l == m + FR * (q + core)


def spots_t(core):
    return spots(core, (DC, D), 1, 0)


def params(**kw):
    return pltpu.CompilerParams(vmem_limit_bytes=VMEM_LIMIT, **kw)


def cost(flops, bytes_accessed, transcendentals=0):
    return pl.CostEstimate(
        flops=int(flops), bytes_accessed=int(bytes_accessed), transcendentals=int(transcendentals)
    )


def dot(a, b):
    return jnp.dot(a, b, preferred_element_type=f32)


def dot_t(a, b):
    return lax.dot_general(a, b, (((1,), (1,)), ((), ())), preferred_element_type=f32)


def t_dot(a, b):
    return lax.dot_general(a, b, (((0,), (0,)), ((), ())), preferred_element_type=f32)


def stats(z):
    mean_val = jnp.mean(z, axis=-1, keepdims=True)
    centred = z - mean_val
    variance = jnp.mean(centred * centred, axis=-1, keepdims=True)
    inv_std = lax.rsqrt(variance + EPS_NORM)
    return centred * inv_std, inv_std


def norm_back(grad, normed, inv_std, gain):
    e = grad * gain
    return inv_std * (
        e
        - jnp.mean(e, axis=-1, keepdims=True)
        - normed * jnp.mean(e * normed, axis=-1, keepdims=True)
    )


def swap_halves(u):
    lanes = u.shape[1]
    lane = lax.broadcasted_iota(jnp.int32, u.shape, 1)
    up = pltpu.roll(u, lanes - HD // 2, 1)
    down = pltpu.roll(u, HD // 2, 1)
    return jnp.where((lane & (HD - 1)) < HD // 2, up, down)


TURN = 1.5707963267948966


def sin_cos(a):
    k = jnp.floor(a * (1.0 / TURN) + 0.5)
    r = ((a - k * 1.5703125) - k * 4.837512969970703125e-4) - k * 7.54978995489188216e-8
    z = r * r
    s = ((-1.9515295891e-4 * z + 8.3321608736e-3) * z - 1.6666654611e-1) * z * r + r
    c = ((2.443315711809948e-5 * z - 1.388731625493765e-3) * z + 4.166664568298827e-2) * z * z - 0.5 * z + 1.0
    quarter = k.astype(jnp.int32)
    odd = (quarter & 1) == 1
    sine = jnp.where(odd, c, s)
    cosine = jnp.where(odd, s, c)
    sine = jnp.where((quarter & 2) == 0, sine, -sine)
    cosine = jnp.where(((quarter + 1) & 2) == 0, cosine, -cosine)
    return sine, cosine


def pre_kernel(
    place_ref, x_ref, xo_ref, ints_ref, v0, v1, v2, v3,
    vec_ref, h_ref, ht_ref, cos_ref, sin_ref, b1_ref, pos_ref,
    full_s, rows_s,
):
    i = pl.program_id(0)
    core = place_ref[0]

    @pl.when(i == 0)
    def _():
        lay_out(place_ref, (v0, v1, v2, v3), full_s)
        rows_s[...] = full_s[...].astype(f32).T[:16, :]
        vec_ref[...] = rows_s[...]
        units = dot(rows_s[8:16, :].astype(bf16), spots(core, (D, DC), 0, 1).astype(bf16))
        for r in range(FC // DC):
            b1_ref[:, r * DC : (r + 1) * DC] = units[2 + r : 3 + r, :]

    mine = i == 0
    normed, _ = stats(jnp.where(mine, x_ref[...], xo_ref[...]).astype(f32))
    h = normed * rows_s[0:1, :] + rows_s[1:2, :]
    h_ref[...] = h.astype(bf16)
    ht_ref[0] = h.T.astype(bf16)
    src = lax.broadcasted_iota(jnp.int32, (D, DC), 0)
    dst = lax.broadcasted_iota(jnp.int32, (D, DC), 1)
    want = core * (DC // 2) + (dst // HD) * (HD // 2) + (dst & (HD // 2 - 1))
    freqs = rows_s[8:16, :].astype(bf16)
    col = dot(freqs, (src == want).astype(bf16))[1:2, :]
    row = dot(freqs, (src == want + D // 2).astype(bf16))[1:2, :]
    pos = ints_ref[0].astype(f32).T
    pos_ref[0] = pos
    angle = pos[:, 1:2] * col + pos[:, 0:1] * row
    lane = lax.broadcasted_iota(jnp.int32, (1, DC), 1)
    sign = jnp.where((lane & (HD - 1)) < HD // 2, -1.0, 1.0)
    small = jnp.max(jnp.abs(angle)) < 8000.0

    @pl.when(small)
    def _():
        sine, cosine = sin_cos(angle)
        cos_ref[...] = cosine
        sin_ref[...] = sine * sign

    @pl.when(jnp.logical_not(small))
    def _():
        cos_ref[...] = jnp.cos(angle)
        sin_ref[...] = jnp.sin(angle) * sign


def gy_kernel(place_ref, c_ref, co_ref, gy_ref):
    i = pl.program_id(0)
    keep = usable_rows(place_ref, i ^ place_ref[0], S)
    gy_ref[...] = (jnp.where(i == 0, c_ref[...], co_ref[...]).astype(f32) * keep).astype(bf16)


def gy_call(place, c, co):
    whole = pl.BlockSpec((S, D), lambda i, c: (0, 0))
    return pl.pallas_call(
        gy_kernel,
        grid_spec=pltpu.PrefetchScalarGridSpec(
            num_scalar_prefetch=1,
            grid=(CORES,),
            in_specs=[whole, whole],
            out_specs=pl.BlockSpec((S, D), lambda i, c: (i, 0)),
        ),
        out_shape=jax.ShapeDtypeStruct((T, D), bf16),
        compiler_params=params(),
        cost_estimate=cost(4 * T * D, T * D * 4),
    )(place, c, co)


def pre_call(place, x, xo, ints, pieces):
    tile = lambda n: pl.BlockSpec((S, n), lambda i, c: (i, 0))
    whole = lambda a: pl.BlockSpec(a.shape, lambda i, c: (0,) * a.ndim)
    return pl.pallas_call(
        pre_kernel,
        grid_spec=pltpu.PrefetchScalarGridSpec(
            num_scalar_prefetch=1,
            grid=(CORES,),
            in_specs=[whole(a) for a in (x, xo)]
            + [pl.BlockSpec((1, 8, S), lambda i, c: (i, 0, 0))]
            + [whole(a) for a in pieces],
            out_specs=[
                pl.BlockSpec((16, D), lambda i, c: (0, 0)),
                tile(D),
                pl.BlockSpec((1, D, S), lambda i, c: (i, 0, 0)),
                tile(DC),
                tile(DC),
                pl.BlockSpec((1, FC), lambda i, c: (0, 0)),
                pl.BlockSpec((1, S, 8), lambda i, c: (i, 0, 0)),
            ],
            scratch_shapes=[pltpu.VMEM((D, 128), bf16), pltpu.VMEM((16, D), f32)],
        ),
        out_shape=[
            jax.ShapeDtypeStruct((16, D), f32),
            jax.ShapeDtypeStruct((T, D), bf16),
            jax.ShapeDtypeStruct((CORES, D, S), bf16),
            jax.ShapeDtypeStruct((T, DC), f32),
            jax.ShapeDtypeStruct((T, DC), f32),
            jax.ShapeDtypeStruct((1, FC), f32),
            jax.ShapeDtypeStruct((CORES, S, 8), f32),
        ],
        compiler_params=params(),
        cost_estimate=cost(T * (20 * D + 40 * DC), T * (D * 10 + DC * 8)),
    )(place, x, xo, ints, *pieces)


def qkv_kernel(place_ref, h_ref, w0, w1, w2, w3, v_ref, cos_ref, sin_ref, q_out, k_out, v_out, w_s):
    @pl.when(pl.program_id(0) == 0)
    def _():
        lay_out(place_ref, (w0, w1, w2, w3), w_s)

    cosine = cos_ref[...]
    sine = sin_ref[...]
    at = pl.ds(pl.multiple_of(place_ref[0] * DC, DC), DC)
    acc = dot(h_ref[...], w_s[...])
    part = lambda i: jnp.concatenate([acc[:, (3 * p + i) * 128 : (3 * p + i + 1) * 128] for p in range(PAIRS)], axis=1)
    q = part(0) + v_ref[4:5, at]
    k = part(1) + v_ref[5:6, at]
    q_out[...] = ((q * cosine + swap_halves(q) * sine) * HD ** (-0.5)).astype(bf16)
    k_out[...] = (k * cosine + swap_halves(k) * sine).astype(bf16)
    v_out[...] = (part(2) + v_ref[6:7, at]).astype(bf16)


def qkv_call(place, h1, pieces, vec, cosine, sine):
    rows = 288
    tile = lambda n: pl.BlockSpec((rows, n), lambda i, c: (i, 0))
    whole = lambda a: pl.BlockSpec(a.shape, lambda i, c: (0,) * a.ndim)
    return pl.pallas_call(
        qkv_kernel,
        grid_spec=pltpu.PrefetchScalarGridSpec(
            num_scalar_prefetch=1,
            grid=(T // rows,),
            in_specs=[tile(D)] + [whole(a) for a in pieces] + [whole(vec), tile(DC), tile(DC)],
            out_specs=[tile(DC)] * 3,
            scratch_shapes=[pltpu.VMEM((D, 3 * DC), bf16)],
        ),
        out_shape=[jax.ShapeDtypeStruct((T, DC), bf16)] * 3,
        compiler_params=params(),
        cost_estimate=cost(2 * T * D * 3 * DC, T * D * 2 + D * 3 * DC * 2 + T * DC * 14),
    )(place, h1, *pieces, vec, cosine, sine)


def softmax_head(q, k, v, mine, bias):
    s = dot_t(jnp.where(mine, q, jnp.zeros_like(q)), k) + bias
    e = jnp.exp(s - jnp.max(s, axis=-1, keepdims=True))
    p = e * (1.0 / jnp.sum(e, axis=-1, keepdims=True))
    return p


def attn_fwd_kernel(
    place_ref, q0, k0, v0, q1, k1, v1, o_ref, p0_ref, p1_ref
):
    lane = lax.broadcasted_iota(jnp.int32, (1, 2 * HD), 1)
    low = lane < HD
    q, k, v = q1[0], k1[0], v1[0]
    mixes = []
    bias = key_bias(place_ref)
    for head, mine in ((0, low), (1, ~low)):
        p = softmax_head(q, k, v, mine, bias).astype(bf16)
        p1_ref[head] = p
        mixes.append(dot(p, v))
    mix = jnp.where(low, mixes[0], mixes[1])
    o_ref[1] = jnp.where(usable_rows(place_ref, 1, S) > 0, mix, v.astype(f32)).astype(bf16)
    o_ref[0] = v0[0]
    for win, base in enumerate(WINDOWS):
        q, k, v = (r[0, base : base + WIN, :] for r in (q0, k0, v0))
        own = own_rows(win)
        bias = key_bias(place_ref, win)
        mixes = []
        for head, mine in ((0, low), (1, ~low)):
            p = softmax_head(q, k, v, mine, bias)
            p = (p * own).astype(bf16)
            p0_ref[head, win] = p
            mixes.append(dot(p, v))
        mix = jnp.where(low, mixes[0], mixes[1])
        use = (own * usable_rows(place_ref, 0, WIN, base)) > 0
        before = o_ref[0, base : base + WIN, :].astype(f32)
        o_ref[0, base : base + WIN, :] = jnp.where(use, mix, before).astype(bf16)


def attn_fwd_call(place, q, k, v):
    block = lambda g: pl.BlockSpec((1, S, 2 * HD), lambda p, c: (g ^ c[0], 0, p))
    q, k, v = (a.reshape(CORES, S, DC) for a in (q, k, v))
    return pl.pallas_call(
        attn_fwd_kernel,
        grid_spec=pltpu.PrefetchScalarGridSpec(
            num_scalar_prefetch=1,
            grid=(PAIRS,),
            in_specs=[block(0)] * 3 + [block(1)] * 3,
            out_specs=[
                pl.BlockSpec((CORES, S, 2 * HD), lambda p, c: (0, 0, p)),
                pl.BlockSpec((2, 2, WIN, WIN), lambda p, c: (p, 0, 0, 0)),
                pl.BlockSpec((2, S, S), lambda p, c: (p, 0, 0)),
            ],
        ),
        out_shape=[
            jax.ShapeDtypeStruct((CORES, S, DC), bf16),
            jax.ShapeDtypeStruct((HC, 2, WIN, WIN), bf16),
            jax.ShapeDtypeStruct((HC, S, S), bf16),
        ],
        compiler_params=params(),
        cost_estimate=cost(4 * HC * (S * S + 2 * WIN * WIN) * 128, 12e6, HC * S * S),
    )(place, q, k, v, q, k, v)


def proj_kernel(place_ref, mine_ref, other_ref, x_ref, xo_ref, w0, w1, w2, w3, v_ref, after_ref, h2_ref, w_s):
    @pl.when(pl.program_id(0) == 0)
    def _():
        lay_out(place_ref, (w0, w1, w2, w3), w_s)

    core = place_ref[0]
    at = lambda c: pl.ds(pl.multiple_of(c * DC, DC), DC)
    branch = dot(mine_ref[0], w_s[at(core), :]) + dot(other_ref[0], w_s[at(1 - core), :])
    x = jnp.where(pl.program_id(0) < pl.num_programs(0) // CORES, x_ref[...], xo_ref[...])
    after = x.astype(f32) + (branch + v_ref[7:8, :])
    after_ref[...] = after
    normed, _ = stats(after)
    h2_ref[...] = (normed * v_ref[2:3, :] + v_ref[3:4, :]).astype(bf16)


def proj_call(place, mine, other, x, xo, pieces, vec):
    rows = 288
    half = S // rows
    tile = lambda n: pl.BlockSpec((rows, n), lambda i, c: (i, 0))
    whole = lambda a: pl.BlockSpec(a.shape, lambda i, c: (0,) * a.ndim)
    return pl.pallas_call(
        proj_kernel,
        grid_spec=pltpu.PrefetchScalarGridSpec(
            num_scalar_prefetch=1,
            grid=(T // rows,),
            in_specs=[
                pl.BlockSpec((1, rows, DC), lambda i, c: ((i // half) ^ c[0], i % half, 0)),
                pl.BlockSpec((1, rows, DC), lambda i, c: ((i // half) ^ c[0], i % half, 0)),
                pl.BlockSpec((rows, D), lambda i, c: (jnp.minimum(i, half - 1), 0)),
                pl.BlockSpec((rows, D), lambda i, c: (jnp.maximum(i - half, 0), 0)),
            ]
            + [whole(a) for a in pieces]
            + [whole(vec)],
            out_specs=[tile(D), tile(D)],
            scratch_shapes=[pltpu.VMEM((D, D), bf16)],
        ),
        out_shape=[jax.ShapeDtypeStruct((T, D), f32), jax.ShapeDtypeStruct((T, D), bf16)],
        compiler_params=params(),
        cost_estimate=cost(2 * T * D * D, T * D * 10 + D * D * 2),
    )(place, mine, other, x, xo, *pieces, vec)


PACK = 4 * DC + 128
K0 = (2.0 / 3.141592653589793) ** 0.5
FT = 768


def gelu_slope(u):
    sq = u * u
    th = jnp.tanh(u * (K0 + (K0 * 0.044715) * sq))
    half = 0.5 + 0.5 * th
    return u * half, half + (u * (half - half * half)) * (2 * K0 + (6 * K0 * 0.044715) * sq)


def mlp_kernel(
    place_ref, h2_ref, gy_ref, w10, w11, w12, w13, w2_ref, b1_ref, mlp_ref, mlpo_ref, gh2b_ref, act_ref, gup_ref, gb1_ref, w1_s
):
    i = pl.program_id(0)

    @pl.when(i == 0)
    def _():
        lay_out(place_ref, (w10, w11, w12, w13), w1_s)
        gb1_ref[...] = jnp.zeros_like(gb1_ref)

    for f in range(FC // FT):
        c = slice(f * FT, (f + 1) * FT)
        act, slope = gelu_slope(dot(h2_ref[...], w1_s[:, c]) + b1_ref[:, c])
        act_ref[:, c] = act.astype(bf16)
        gup = (dot_t(gy_ref[...], w2_ref[c, :]) * slope).astype(bf16)
        gup_ref[:, c] = gup
        gb1_ref[:, c] += jnp.sum(gup.astype(f32), axis=0, keepdims=True)
    gh2b_ref[...] = dot_t(gup_ref[...], w1_s[...]).astype(bf16)
    mlp = dot(act_ref[...], w2_ref[...])
    half = pl.num_programs(0) // CORES

    @pl.when(i < half)
    def _():
        mlp_ref[...] = mlp

    @pl.when(i >= half)
    def _():
        mlpo_ref[...] = mlp


def mlp_call(place, h2, gy, pieces, w2, b1):
    rows = 288
    half = S // rows
    tile = lambda n: pl.BlockSpec((rows, n), lambda i, c: (i, 0))
    whole = lambda a: pl.BlockSpec(a.shape, lambda i, c: (0,) * a.ndim)
    return pl.pallas_call(
        mlp_kernel,
        grid_spec=pltpu.PrefetchScalarGridSpec(
            num_scalar_prefetch=1,
            grid=(T // rows,),
            in_specs=[tile(D), tile(D)]
            + [whole(a) for a in pieces]
            + [whole(w2), whole(b1)],
            out_specs=[
                pl.BlockSpec((rows, D), lambda i, c: (jnp.minimum(i, half - 1), 0)),
                pl.BlockSpec((rows, D), lambda i, c: (jnp.maximum(i - half, 0), 0)),
                tile(D),
                tile(FC),
                tile(FC),
                pl.BlockSpec((1, FC), lambda i, c: (0, 0)),
            ],
            scratch_shapes=[pltpu.VMEM((D, FC), bf16)],
        ),
        out_shape=[
            jax.ShapeDtypeStruct((S, D), f32),
            jax.ShapeDtypeStruct((S, D), f32),
            jax.ShapeDtypeStruct((T, D), bf16),
            jax.ShapeDtypeStruct((T, FC), bf16),
            jax.ShapeDtypeStruct((T, FC), bf16),
            jax.ShapeDtypeStruct((1, FC), f32),
        ],
        compiler_params=params(),
        cost_estimate=cost(8 * T * D * FC, 30e6, T * FC),
    )(place, h2, gy, *pieces, w2, b1)


def by_line(place_ref, value, block, out_ref):
    core = place_ref[0]
    for n in range(PLANE):
        to = jnp.where(core == 0, n, (n % SIDE) * SIDE + n // SIDE)
        out_ref[pl.ds(pl.multiple_of(to * block, block), block), :] = value[n * block : (n + 1) * block, :].astype(bf16)


def fc_grad_kernel(place_ref, h2_ref, gup_ref, act_ref, gy_ref, gw1_ref, gw2_ref):
    by_line(place_ref, t_dot(act_ref[...], gy_ref[...]), SIDE * FR, gw2_ref)
    by_line(place_ref, t_dot(h2_ref[...], gup_ref[...]), BLOCK, gw1_ref)


def fc_grad_call(place, h2, gup, act, gy):
    whole = lambda a: pl.BlockSpec(a.shape, lambda i, c: (0, 0))
    return pl.pallas_call(
        fc_grad_kernel,
        grid_spec=pltpu.PrefetchScalarGridSpec(
            num_scalar_prefetch=1,
            grid=(2,),
            in_specs=[
                whole(h2),
                pl.BlockSpec((T, FC // 2), lambda i, c: (0, i)),
                whole(act),
                pl.BlockSpec((T, DC), lambda i, c: (0, i)),
            ],
            out_specs=[
                pl.BlockSpec((D, FC // 2), lambda i, c: (0, i)),
                pl.BlockSpec((FC, DC), lambda i, c: (0, i)),
            ],
        ),
        out_shape=[jax.ShapeDtypeStruct((D, FC), bf16), jax.ShapeDtypeStruct((FC, D), bf16)],
        compiler_params=params(),
        cost_estimate=cost(4 * T * D * FC, T * (D + FC) * 4 + D * FC * 4),
    )(place, h2, gup, act, gy)


def mid_kernel(place_ref, after_ref, gy_ref, gh2_ref, other_ref, v_ref, ga_ref, gab_ref, sums_ref):
    i = pl.program_id(0)
    normed, inv_std = stats(after_ref[...])
    gh2 = gh2_ref[...].astype(f32) + other_ref[...].astype(f32)
    gy = gy_ref[...].astype(f32)
    ga = gy + norm_back(gh2, normed, inv_std, v_ref[2:3, :])
    gab = ga.astype(bf16)
    gab_ref[...] = gab

    @pl.when(i == 0)
    def _():
        sums_ref[...] = jnp.zeros_like(sums_ref)

    @pl.when(i < pl.num_programs(0) // CORES)
    def _():
        ga_ref[...] = ga
        sums_ref[0:1, :] += jnp.sum(gh2 * normed, axis=0, keepdims=True)
        sums_ref[1:2, :] += jnp.sum(gh2, axis=0, keepdims=True)
        sums_ref[2:3, :] += jnp.sum(gab.astype(f32), axis=0, keepdims=True)
        sums_ref[3:4, :] += jnp.sum(gy, axis=0, keepdims=True)


def mid_call(place, after, gy, gh2, other, vec):
    rows = 288
    half = S // rows
    tile = lambda n: pl.BlockSpec((rows, n), lambda i, c: (i, 0))
    flipped = pl.BlockSpec((rows, D), lambda i, c: ((i + half) % (2 * half), 0))
    whole = lambda a: pl.BlockSpec(a.shape, lambda i, c: (0,) * a.ndim)
    return pl.pallas_call(
        mid_kernel,
        grid_spec=pltpu.PrefetchScalarGridSpec(
            num_scalar_prefetch=1,
            grid=(T // rows,),
            in_specs=[tile(D), tile(D), tile(D), flipped, whole(vec)],
            out_specs=[
                pl.BlockSpec((rows, D), lambda i, c: (jnp.minimum(i, half - 1), 0)),
                tile(D),
                pl.BlockSpec((8, D), lambda i, c: (0, 0)),
            ],
        ),
        out_shape=[
            jax.ShapeDtypeStruct((S, D), f32),
            jax.ShapeDtypeStruct((T, D), bf16),
            jax.ShapeDtypeStruct((8, D), f32),
        ],
        compiler_params=params(),
        cost_estimate=cost(30 * T * D, T * D * 14),
    )(place, after, gy, gh2, other, vec)


def back_head(q_t, k, v, do, do_t, delta, p, mine, head):
    gp = dot_t(jnp.where(mine, do, jnp.zeros_like(do)), v)
    gs = (p.astype(f32) * (gp - delta)).astype(bf16)
    at = slice(head * HD, (head + 1) * HD)
    return dot(gs, k), dot(q_t[at, :], gs), dot(do_t[at, :], p)


def deltas(do, o, low):
    prod = do.astype(f32) * o.astype(f32)
    d0 = jnp.sum(jnp.where(low, prod, 0.0), axis=-1, keepdims=True)
    d1 = jnp.sum(jnp.where(low, 0.0, prod), axis=-1, keepdims=True)
    return d0, d1


def vec_sums(place_ref, x_ref, xo_ref, gh_ref, gho_ref, mid_ref, att_ref, gb1_ref, rows_s):
    core = place_ref[0]
    rows_s[...] = jnp.zeros_like(rows_s)
    for x, gh in ((x_ref, gh_ref), (xo_ref, gho_ref)):
        normed, _ = stats(x[...].astype(f32))
        g = gh[...]
        rows_s[0:1, :] += jnp.sum(g * normed, axis=0, keepdims=True)
        rows_s[1:2, :] += jnp.sum(g, axis=0, keepdims=True)
    rows_s[2:4, :] = mid_ref[0:2, :]
    rows_s[7:9, :] = mid_ref[2:4, :]
    att = jnp.concatenate([att_ref[p] for p in range(PAIRS)], axis=1)
    rows_s[4:7, pl.ds(pl.multiple_of(core * DC, DC), DC)] = att[2:5, :]
    src = lax.broadcasted_iota(jnp.int32, (DC, D), 0)
    dst = lax.broadcasted_iota(jnp.int32, (DC, D), 1)
    want = core * (DC // 2) + (src // HD) * (HD // 2) + (src & (HD // 2 - 1))
    lane = lax.broadcasted_iota(jnp.int32, (1, DC), 1)
    turn = jnp.where((lane & (HD - 1)) < HD // 2, att, -att)
    rows_s[9:10, :] = (
        exact_dot(turn, dst == want)[0:1, :] + exact_dot(turn, dst == want + D // 2)[1:2, :]
    )
    gb1 = jnp.concatenate([gb1_ref[:, r * DC : (r + 1) * DC] for r in range(FC // DC)] * 2, axis=0)
    rows_s[10:14, :] = exact_dot(gb1, spots_t(core))[:4, :]


def attn_bwd_kernel(
    place_ref,
    q0, k0, v0, o0, p0, cos0, sin0, pos0,
    q1, k1, v1, o1, p1, cos1, sin1, pos1,
    h1t_ref, ga_ref, cols_ref, mine_ref, other_ref, w0, w1, w2, w3, y0, y1, y2, y3,
    x_ref, xo_ref, mid_ref, gb1_ref,
    gw0, gw1, gw2, gw3, gh_ref, gho_ref,
    gq_s, gk_s, gv_s, gqkv_s, w_s, gw_s, y_s, do_s, att_s, rows_s, full_s,
):
    lane = lax.broadcasted_iota(jnp.int32, (1, 2 * HD), 1)
    low = lane < HD
    pair = pl.program_id(0)
    core = place_ref[0]

    @pl.when(pair == 0)
    def _():
        lay_out(place_ref, (y0, y1, y2, y3), y_s)

    wy = y_s[pl.ds(pl.multiple_of(core * DC + pair * 2 * HD, 2 * HD), 2 * HD), :]
    for frame in range(CORES):
        do_s[frame] = dot_t(ga_ref[frame], wy).astype(bf16)

    def finish(frame, q, k, cos_ref, sin_ref, pos_ref):
        cosine, sine = cos_ref[0], sin_ref[0]
        gq = gq_s[...] * HD ** (-0.5)
        gk = gk_s[...]
        sq, sk = swap_halves(gq), swap_halves(gk)
        turn = (q.astype(f32) * HD**0.5) * sq + k.astype(f32) * sk
        gq = (gq * cosine - sq * sine).astype(bf16)
        gk = (gk * cosine - sk * sine).astype(bf16)
        gv = gv_s[...].astype(bf16)
        gqkv_s[frame, :, : 2 * HD] = gq
        gqkv_s[frame, :, 2 * HD : 4 * HD] = gk
        gqkv_s[frame, :, 4 * HD :] = gv
        pos = pos_ref[0]
        col = jnp.sum(turn * pos[:, 1:2], axis=0, keepdims=True)
        row = jnp.sum(turn * pos[:, 0:1], axis=0, keepdims=True)
        bias = [jnp.sum(g.astype(f32), axis=0, keepdims=True) for g in (gq, gk, gv)]
        return jnp.concatenate([col, row] + bias, axis=0)

    q, k, v, do = q1[0], k1[0], v1[0], do_s[1 ^ core]
    d = deltas(do, o1[0], low)
    q_t, do_t = q.astype(f32).T.astype(bf16), do.astype(f32).T.astype(bf16)
    out = [
        back_head(q_t, k, v, do, do_t, d[head], p1[head], mine, head)
        for head, mine in ((0, low), (1, ~low))
    ]
    gq_s[...] = jnp.where(low, out[0][0], out[1][0])
    gk_s[...] = jnp.concatenate([out[0][1], out[1][1]], axis=0).T
    gv_s[...] = jnp.concatenate([out[0][2], out[1][2]], axis=0).T
    sums1 = finish(1, q, k, cos1, sin1, pos1)
    gq_s[...] = jnp.zeros_like(gq_s)
    gk_s[...] = jnp.zeros_like(gk_s)
    gv_s[...] = jnp.zeros_like(gv_s)
    for win, base in enumerate(WINDOWS):
        at = pl.ds(base, WIN)
        q, k, v, o = (r[0, at, :] for r in (q0, k0, v0, o0))
        do = do_s[core, at, :]
        d = deltas(do, o, low)
        q_t, do_t = q.astype(f32).T.astype(bf16), do.astype(f32).T.astype(bf16)
        out = [
            back_head(q_t, k, v, do, do_t, d[head], p0[head, win], mine, head)
            for head, mine in ((0, low), (1, ~low))
        ]
        gq_s[at, :] += jnp.where(low, out[0][0], out[1][0])
        gk_s[at, :] += jnp.concatenate([out[0][1], out[1][1]], axis=0).T
        gv_s[at, :] += jnp.concatenate([out[0][2], out[1][2]], axis=0).T
    sums0 = finish(0, q0[0], k0[0], cos0, sin0, pos0)
    att_s[pair, 0:5, :] = sums0 + sums1

    lay_out(place_ref, (w0, w1, w2, w3), w_s)
    gw = jnp.zeros((D, 6 * HD), f32)
    gw_mine = jnp.zeros((2 * HD, DC), f32)
    gw_other = jnp.zeros((2 * HD, DC), f32)
    for frame, out in ((0, gh_ref), (1, gho_ref)):
        g = gqkv_s[frame ^ core]
        gw += dot(h1t_ref[frame], g)
        gh = dot_t(g, w_s[...])

        @pl.when(pair == 0)
        def _(out=out, gh=gh):
            out[...] = gh

        @pl.when(pair > 0)
        def _(out=out, gh=gh):
            out[...] += gh

        cols = cols_ref[frame].astype(f32).T.astype(bf16)
        gw_mine += dot(cols, mine_ref[frame ^ core])
        gw_other += dot(cols, other_ref[frame ^ core])
    gw_s[:, : 6 * HD] = gw.astype(bf16)
    at = lambda c: pl.ds(pl.multiple_of(c * DC, DC), DC)
    gw_s[at(core), 6 * HD :] = gw_mine.T.astype(bf16)
    gw_s[at(1 - core), 6 * HD :] = gw_other.T.astype(bf16)
    to = pl.ds(pl.multiple_of(pair * 8 * HD, 8 * HD), 8 * HD)
    for d, out in enumerate((gw0, gw1, gw2, gw3)):
        a = (place_ref[1] + d) & (SIDE - 1)
        for g in range(SIDE):
            at = pl.multiple_of(natural(core, a, g) * BLOCK, BLOCK)
            out[g * BLOCK : (g + 1) * BLOCK, to] = gw_s[pl.ds(at, BLOCK), :]

    @pl.when(pair == PAIRS - 1)
    def _():
        vec_sums(place_ref, x_ref, xo_ref, gh_ref, gho_ref, mid_ref, att_s, gb1_ref, rows_s)
        full_s[...] = rows_s[...].T.astype(bf16)
        for d, out in enumerate((gw0, gw1, gw2, gw3)):
            a = (place_ref[1] + d) & (SIDE - 1)
            for g in range(SIDE):
                at = pl.multiple_of(natural(core, a, g) * BLOCK, BLOCK)
                out[g * BLOCK : (g + 1) * BLOCK, 4 * DC :] = full_s[pl.ds(at, BLOCK), :]


def attn_bwd_call(
    place, q, k, v, ga, mine, other, p0, p1, cosine, sine, pos, h1t, pieces, proj_pieces, x, xo, mid, gb1
):
    q, k, v, cosine, sine = (a.reshape(CORES, S, DC) for a in (q, k, v, cosine, sine))
    ga = ga.reshape(CORES, S, D)
    block = lambda g: pl.BlockSpec((1, S, 2 * HD), lambda p, c: (g ^ c[0], 0, p))
    own = lambda g: pl.BlockSpec((1, S, 2 * HD), lambda p, c: (g, 0, p))
    quarter = pl.BlockSpec((QUARTER, 6 * HD), lambda p, c: (0, p))
    keep = lambda *n: pl.BlockSpec(n, lambda p, c: (0,) * len(n))
    at = lambda g: pl.BlockSpec((1, S, 8), lambda p, c: (g ^ c[0], 0, 0))
    whole = lambda a: pl.BlockSpec(a.shape, lambda p, c: (0,) * a.ndim)
    return pl.pallas_call(
        attn_bwd_kernel,
        grid_spec=pltpu.PrefetchScalarGridSpec(
            num_scalar_prefetch=1,
            grid=(PAIRS,),
            in_specs=[block(0)] * 3
            + [own(0), pl.BlockSpec((2, 2, WIN, WIN), lambda p, c: (p, 0, 0, 0))]
            + [block(0)] * 2
            + [at(0)]
            + [block(1)] * 3
            + [own(1), pl.BlockSpec((2, S, S), lambda p, c: (p, 0, 0))]
            + [block(1)] * 2
            + [at(1)]
            + [whole(h1t), whole(ga), pl.BlockSpec((CORES, S, 2 * HD), lambda p, c: (0, 0, PAIRS * c[0] + p))]
            + [whole(mine), whole(other)]
            + [quarter] * 4
            + [whole(a) for a in proj_pieces]
            + [whole(a) for a in (x, xo, mid, gb1)],
            out_specs=[keep(QUARTER, PACK)] * 4 + [keep(S, D)] * 2,
            scratch_shapes=[pltpu.VMEM((S, 2 * HD), f32)] * 3
            + [pltpu.VMEM((CORES, S, 6 * HD), bf16)]
            + [pltpu.VMEM((D, 6 * HD), bf16), pltpu.VMEM((D, 8 * HD), bf16)]
            + [pltpu.VMEM((D, D), bf16), pltpu.VMEM((CORES, S, 2 * HD), bf16)]
            + [pltpu.VMEM((PAIRS, 8, 2 * HD), f32), pltpu.VMEM((128, D), f32), pltpu.VMEM((D, 128), bf16)],
        ),
        out_shape=[
            *[jax.ShapeDtypeStruct((QUARTER, PACK), bf16)] * 4,
            jax.ShapeDtypeStruct((S, D), f32),
            jax.ShapeDtypeStruct((S, D), f32),
        ],
        compiler_params=params(),
        cost_estimate=cost(10 * HC * S * S * 128 + 4 * T * D * 4 * DC, 36e6),
    )(
        place,
        q, k, v, mine, p0, cosine, sine, pos,
        q, k, v, mine, p1, cosine, sine, pos,
        h1t, ga, ga, mine, other, *pieces, *proj_pieces, x, xo, mid, gb1,
    )


def last_kernel(x_ref, ga_ref, gh_ref, other_ref, after_ref, mlp_ref, mlpo_ref, v_ref, gt_ref, out_ref):
    normed, inv_std = stats(x_ref[...].astype(f32))
    gt_ref[...] = ga_ref[...] + norm_back(gh_ref[...] + other_ref[...], normed, inv_std, v_ref[0:1, :])
    out_ref[...] = (after_ref[...] + (mlp_ref[...] + mlpo_ref[...] + v_ref[8:9, :])).astype(bf16)


def last_call(x, ga, gh, other, after, mlp, mlp_other, vec):
    rows = 288
    tile = lambda n: pl.BlockSpec((rows, n), lambda i: (i, 0))
    return pl.pallas_call(
        last_kernel,
        grid=(S // rows,),
        in_specs=[tile(D)] * 7 + [pl.BlockSpec(vec.shape, lambda i: (0, 0))],
        out_specs=[tile(D), tile(D)],
        out_shape=[jax.ShapeDtypeStruct((S, D), f32), jax.ShapeDtypeStruct((S, D), bf16)],
        compiler_params=params(),
        cost_estimate=cost(30 * S * D, S * D * 28),
    )(x, ga, gh, other, after, mlp, mlp_other, vec)


WIDE = PACK + FC


def pack_kernel(q0, q1, q2, q3, f_ref, out_ref):
    total = q0[...].astype(f32) + q1[...].astype(f32) + q2[...].astype(f32) + q3[...].astype(f32)
    fc1 = f_ref[...].astype(f32)
    for n in range(PLANE):
        at = slice(n * KR, (n + 1) * KR)
        out_ref[n, :, :PACK] = total[at, :].astype(bf16)
        out_ref[n, :, PACK:] = fc1[at, :].astype(bf16)


def pack_call(parts, fc1):
    return pl.pallas_call(
        pack_kernel,
        out_shape=jax.ShapeDtypeStruct((PLANE, KR, WIDE), bf16),
        compiler_params=params(),
        cost_estimate=cost(QUARTER * PACK * 4, QUARTER * PACK * 10),
    )(*parts, fc1)


def sum_kernel(in_ref, out_ref):
    total = in_ref[0].astype(f32)
    for n in range(1, PLANE):
        total += in_ref[n].astype(f32)
    out_ref[...] = total


def sum_call(packed):
    return pl.pallas_call(
        sum_kernel,
        out_shape=jax.ShapeDtypeStruct(packed.shape[1:], f32),
        compiler_params=params(),
        cost_estimate=cost(packed.size, packed.size * 2),
    )(packed)


def fc2_kernel(place_ref, mine_ref, other_ref, out_ref, sq_ref):
    first = place_ref[0] == 0
    a, b = mine_ref[...], other_ref[...]
    out_ref[:FR, :] = jnp.where(first, a, b)
    out_ref[FR:, :] = jnp.where(first, b, a)
    total = jnp.sum(a * a + b * b, axis=(0, 1), keepdims=True)
    sq_ref[...] = jnp.broadcast_to(total, sq_ref.shape)


def fc2_call(place, mine, other):
    whole = lambda a: pl.BlockSpec(a.shape, lambda i, c: (0,) * len(a.shape))
    shapes = [jax.ShapeDtypeStruct(s, f32) for s in ((2 * FR, D), (8, 128))]
    return pl.pallas_call(
        fc2_kernel,
        grid_spec=pltpu.PrefetchScalarGridSpec(
            num_scalar_prefetch=1,
            grid=(1,),
            in_specs=[whole(mine), whole(other)],
            out_specs=[whole(a) for a in shapes],
        ),
        out_shape=shapes,
        compiler_params=params(),
        cost_estimate=cost(6 * FR * D, FR * D * 16),
    )(place, mine, other)


def norm_kernel(g_ref, o_ref, sq_ref, out_ref):
    g, o = g_ref[...], o_ref[...]
    part = jnp.sum(g * g + o * o, axis=(0, 1), keepdims=True)
    cross = g[:, 4 * DC : PACK] * o[:, 4 * DC : PACK]
    part += 2.0 * jnp.sum(cross, axis=(0, 1), keepdims=True)
    out_ref[...] = jnp.broadcast_to((part + sq_ref[0:1, 0:1])[None], out_ref.shape)


def norm_call(g, o, squares):
    return pl.pallas_call(
        norm_kernel,
        out_shape=jax.ShapeDtypeStruct((CHIPS, 8, 128), f32),
        compiler_params=params(),
        cost_estimate=cost(4 * KR * PACK, 1e6),
    )(g, o, squares)


RATES = (D ** (-0.5), max(1, 2 * D // S) ** (-0.5), D ** (-0.5), FF ** (-0.5), RATE_VECTOR)


def adam_kernel(place_ref, norm_ref, mine_ref, other_ref, g2_ref, *refs):
    masters, firsts, seconds = refs[0:5], refs[5:10], refs[10:15]
    outs = refs[15:30]
    norm_out, bias_out = refs[30:32]
    core = place_ref[0]
    mine, other = mine_ref[...], other_ref[...]
    g0 = jnp.where(core == 0, mine, other)
    g1 = jnp.where(core == 0, other, mine)
    total = jnp.sum(jnp.sum(norm_ref[...], axis=0)[0:1, 0:1], axis=(0, 1), keepdims=True)
    grad_norm = jnp.sqrt(total)
    norm_out[...] = jnp.broadcast_to(grad_norm, norm_out.shape)
    clip = jnp.minimum(1.0, CLIP_LIMIT / (grad_norm + 1e-06))

    def update(i, at, grad):
        clipped = grad * clip
        master = masters[i][at]
        first = BETA_ONE * firsts[i][at] + (1.0 - BETA_ONE) * clipped
        second = BETA_TWO * seconds[i][at] + (1.0 - BETA_TWO) * clipped * clipped
        first_hat = first / (1.0 - BETA_ONE**STEP)
        second_hat = second / (1.0 - BETA_TWO**STEP)
        decay = 0.0 if i == 4 else DECAY_RATE
        outs[3 * i][at] = master - RATES[i] * (first_hat / (jnp.sqrt(second_hat) + ADAM_EPS) + decay * master)
        outs[3 * i + 1][at] = first
        outs[3 * i + 2][at] = second

    rows = slice(None)
    for c, g in ((0, g0), (1, g1)):
        for p in range(PAIRS):
            for i in range(3):
                col = i * D + c * DC + p * 128
                update(0, (rows, slice(col, col + 128)), g[:, (4 * p + i) * 128 : (4 * p + i + 1) * 128])
            col = c * DC + p * 128
            update(1, (rows, slice(col, col + 128)), g[:, (4 * p + 3) * 128 : (4 * p + 4) * 128])
    for r in range(FC // DC):
        at = slice(PACK + r * DC, PACK + (r + 1) * DC)
        part = exact_dot(g0[:, at], spots_t(0)) + exact_dot(g1[:, at], spots_t(1))
        update(2, (rows, slice(r * D, (r + 1) * D)), part)
    update(3, (rows, rows), g2_ref[...])
    vec = (g0 + g1)[:, 4 * DC : 4 * DC + 128]
    vec = jnp.concatenate([vec, jnp.zeros((16 - KR, 128), f32)], axis=0).T[:16, :KR]
    update(4, (rows, rows), vec[: masters[4].shape[0], :])
    bias_out[...] = vec[7:8, :] * clip


def adam_call(place, norm, mine, other, g2, masters, firsts, seconds):
    whole = lambda a: pl.BlockSpec(a.shape, lambda i, c: (0,) * len(a.shape))
    args = [norm, mine, other, g2, *masters, *firsts, *seconds]
    shapes = [jax.ShapeDtypeStruct(m.shape, f32) for m in masters for _ in range(3)]
    shapes += [jax.ShapeDtypeStruct((1, 128), f32), jax.ShapeDtypeStruct((1, KR), f32)]
    return pl.pallas_call(
        adam_kernel,
        grid_spec=pltpu.PrefetchScalarGridSpec(
            num_scalar_prefetch=1,
            grid=(1,),
            in_specs=[whole(a) for a in args],
            out_specs=[whole(a) for a in shapes],
        ),
        out_shape=shapes,
        compiler_params=params(),
        cost_estimate=cost(20 * KR * FF * 3, 3e6),
    )(place, *args)


def local(
    tokens,
    cotangent,
    counts,
    patch_row,
    patch_col,
    w_qkv,
    w_proj,
    w_fc1,
    w_fc2,
    vectors,
    m_qkv,
    v_qkv,
    m_proj,
    v_proj,
    m_fc1,
    v_fc1,
    m_fc2,
    v_fc2,
    m_vectors,
    v_vectors,
):
    core = lax.axis_index("grp")
    chip = lax.axis_index("dp")
    first_core = core == 0
    along = jnp.where(first_core, chip // PLANE, (chip // SIDE) % SIDE)
    vr = vectors.shape[0]

    def swap(a):
        return lax.ppermute(a, "grp", [(0, 1), (1, 0)])

    def halves(a):
        n = a.shape[-1] // 2
        return jnp.where(first_core, a[..., :n], a[..., n:])

    def over_plane(share):
        got = plane_swap(jnp.broadcast_to(share[None], (PLANE,) + share.shape))
        return got.reshape(PLANE * share.shape[0], share.shape[1])

    def along_line(quarter):
        return [quarter] + [shift(quarter, d) for d in range(1, SIDE)]

    def line_sum(whole):
        return lax.psum_scatter(whole, BOTH, scatter_dimension=0, axis_index_groups=lines(), tiled=True)

    fc2_b = w_fc2.astype(bf16)
    full_fc2 = lax.all_gather(jnp.where(first_core, fc2_b[:FR], fc2_b[FR:]), "dp", axis=0, tiled=True)
    qkv_b = w_qkv.astype(bf16)
    parts = [halves(qkv_b[:, i * D : (i + 1) * D]) for i in range(3)]
    by_pair = [parts[i][:, p * 128 : (p + 1) * 128] for p in range(PAIRS) for i in range(3)]
    vec_t = jnp.pad(vectors.astype(bf16).T, ((0, 0), (0, 128 - vr)))
    quarter = over_plane(jnp.concatenate(by_pair + [vec_t], axis=1))
    vec_pieces = along_line(quarter[:, 3 * DC :])
    qkv_pieces = along_line(quarter[:, : 3 * DC])
    fc1_b = w_fc1.astype(bf16).reshape(KR, CHIPS, CORES, FR)
    share_fc1 = jnp.where(first_core, fc1_b[:, :, 0], fc1_b[:, :, 1]).reshape(KR, FC)
    share = jnp.concatenate([share_fc1, w_proj.astype(bf16)], axis=1)
    share, vec_pieces = lax.optimization_barrier((share, vec_pieces))
    quarter = over_plane(share)

    x_own = tokens.reshape(S, D)
    cot_own = cotangent.reshape(S, D)
    x_other, cot_other = swap(x_own), swap(cot_own)
    ints = jnp.concatenate(
        [
            patch_row.reshape(1, S),
            patch_col.reshape(1, S),
            jnp.pad(counts.reshape(1, 2), ((0, 0), (0, S - 2))),
            jnp.zeros((5, S), jnp.int32),
        ]
    )
    ints = jnp.stack([ints, swap(ints)])
    counts0 = jnp.where(first_core, ints[0, 2, :2], ints[1, 2, :2])
    counts1 = jnp.where(first_core, ints[1, 2, :1], ints[0, 2, :1])
    place = jnp.concatenate([jnp.stack([core, along]).astype(jnp.int32), counts0, counts1])

    gy = gy_call(place, cot_own, cot_other)
    gy, x_other = lax.optimization_barrier((gy, x_other))
    vec, h1, h1t, cosine, sine, b1, pos = pre_call(place, x_own, x_other, ints, vec_pieces)
    h1, quarter = lax.optimization_barrier((h1, quarter))
    proj_pieces = along_line(quarter[:, FC:])
    q, k, v = qkv_call(place, h1, qkv_pieces, vec, cosine, sine)
    q, proj_pieces = lax.optimization_barrier((q, proj_pieces))
    fc1_pieces = along_line(quarter[:, :FC])
    mine, p0, p1 = attn_fwd_call(place, q, k, v)
    other = swap(mine)
    after, h2 = proj_call(place, mine, other, x_own, x_other, proj_pieces, vec)
    mlp, mlp_part, gh2, act, gup, gb1 = mlp_call(place, h2, gy, fc1_pieces, full_fc2, b1)
    other_gh2 = swap(gh2)
    mlp_other = swap(mlp_part)

    gw1, gw2 = fc_grad_call(place, h2, gup, act, gy)
    sum_fc2 = line_sum(gw2)
    sum_fc1 = line_sum(gw1)
    ga, gab, sums_mid = mid_call(place, after, gy, gh2, other_gh2, vec)
    *gw, gh1, gh1_part = attn_bwd_call(
        place, q, k, v, gab, mine, other, p0, p1, cosine, sine, pos, h1t, qkv_pieces, proj_pieces,
        x_own, x_other, sums_mid, gb1,
    )
    gh1_other = swap(gh1_part)

    got_fc2 = plane_swap(sum_fc2.reshape(PLANE, FR, D))
    parts = [gw[0]] + [shift(gw[d], d) for d in range(1, SIDE)]
    got_fc2, sum_fc1 = lax.optimization_barrier((got_fc2, sum_fc1))
    g_fc2 = sum_call(got_fc2)
    g2, squares = fc2_call(place, g_fc2, swap(g_fc2))
    grads = sum_call(plane_swap(pack_call(parts, sum_fc1)))
    grads_other = swap(grads)
    squares = norm_call(grads, grads_other, squares)
    squares, gh1 = lax.optimization_barrier((squares, gh1))
    norms = lax.all_to_all(squares, "dp", 0, 0)
    gt, mixed = last_call(x_own, ga, gh1, gh1_other, after, mlp, mlp_other, vec)
    norms, gt, mixed = lax.optimization_barrier((norms, gt, mixed))
    *updates, grad_norm, bias_proj_grad = adam_call(
        place,
        norms,
        grads,
        grads_other,
        g2,
        (w_qkv, w_proj, w_fc1, w_fc2, vectors),
        (m_qkv, m_proj, m_fc1, m_fc2, m_vectors),
        (v_qkv, v_proj, v_fc1, v_fc2, v_vectors),
    )
    return (
        mixed.reshape(1, 1, S, D),
        gt.reshape(1, 1, S, D),
        grad_norm[0, 0],
        *updates,
        bias_proj_grad.reshape(KR),
    )


def solution(mesh):
    frame = P("grp", "dp", None, None)
    ints = P("grp", "dp", None)
    rows = P("dp", None)
    cols = P(None, "dp")
    return jax.shard_map(
        local,
        mesh=mesh,
        in_specs=(frame, frame, ints, ints, ints, rows, rows, rows, rows, cols) + (rows,) * 8 + (cols,) * 2,
        out_specs=(frame, frame, P()) + (rows,) * 12 + (cols,) * 3 + (P("dp"),),
        check_vma=False,
    )
```

```python
import functools

import jax
import jax.numpy as jnp
from jax import lax
from jax.experimental import pallas as pl
from jax.experimental.pallas import tpu as pltpu
from jax.sharding import PartitionSpec as P

D = 768
H = 12
HD = 64
FF = 3072
STEP = 10
A = 196
S = 576

CORES = 2
HC = H // CORES
DC = D // CORES
FC = FF // CORES
PAIRS = HC // 2
T = CORES * S

WIN = 208
WINDOWS = (0, 192)

EPS_NORM = 1e-06
BETA_ONE = 0.9
BETA_TWO = 0.95
ADAM_EPS = 1e-08
DECAY_RATE = 0.05
RATE_VECTOR = 0.8
CLIP_LIMIT = 1.0
NEG = -1e30

bf16 = jnp.bfloat16
f32 = jnp.float32
VMEM_LIMIT = 56 * 1024 * 1024


SIDE = 4
CHIPS = SIDE**3
PLANE = SIDE * SIDE
KR = D // CHIPS
FR = FC // CHIPS
BLOCK = SIDE * KR
QUARTER = PLANE * KR
BOTH = ("grp", "dp")


def device(core, x, y, z):
    return ((core * SIDE + x) * SIDE + y) * SIDE + z


def lines():
    r = range(SIDE)
    return [[device(0, a, g, z) for a in r] for g in r for z in r] + [
        [device(1, g, a, z) for a in r] for g in r for z in r
    ]


def planes():
    r = range(SIDE)
    return [[device(0, a, g, z) for g in r for z in r] for a in r] + [
        [device(1, g, a, z) for g in r for z in r] for a in r
    ]


def shift(value, d):
    pairs = [(group[i], group[(i + d) % SIDE]) for group in lines() for i in range(SIDE)]
    return lax.ppermute(value, BOTH, pairs)


def plane_swap(value):
    return lax.all_to_all(value, BOTH, 0, 0, axis_index_groups=planes())


def natural(core, a, g):
    return jnp.where(core == 0, SIDE * a + g, SIDE * g + a)


def lay_out(place_ref, pieces, full_ref):
    core, me = place_ref[0], place_ref[1]
    for d, piece in enumerate(pieces):
        a = (me + SIDE - d) & (SIDE - 1)
        for g in range(SIDE):
            at = pl.multiple_of(natural(core, a, g) * BLOCK, BLOCK)
            full_ref[pl.ds(at, BLOCK), :] = piece[g * BLOCK : (g + 1) * BLOCK, :]


def usable_rows(place_ref, group, rows, base=0):
    slot = lax.broadcasted_iota(jnp.int32, (rows, 1), 0) + base
    first = ((slot < A) & (slot < place_ref[2])) | ((slot >= A) & (slot < 2 * A) & (slot - A < place_ref[3]))
    first = first.astype(f32)
    second = (slot < place_ref[4]).astype(f32)
    if isinstance(group, int):
        return second if group else first
    return jnp.where(group == 0, first, second)


def own_rows(win):
    row = lax.broadcasted_iota(jnp.int32, (WIN, 1), 0) + (WINDOWS[win] - win * A)
    return ((row >= 0) & (row < A)).astype(f32)


def key_bias(place_ref, win=None):
    if win is None:
        key = lax.broadcasted_iota(jnp.int32, (1, S), 1)
        return jnp.where(key < place_ref[4], 0.0, NEG)
    key = lax.broadcasted_iota(jnp.int32, (1, WIN), 1) + (WINDOWS[win] - win * A)
    return jnp.where((key >= 0) & (key < place_ref[2 + win]), 0.0, NEG)


def exact_dot(a, b):
    high = a.astype(bf16)
    rest = a - high.astype(f32)
    mid = rest.astype(bf16)
    low = (rest - mid.astype(f32)).astype(bf16)
    b = b.astype(bf16)
    return dot(high, b) + dot(mid, b) + dot(low, b)


def spots(core, shape, full, part):
    l = lax.broadcasted_iota(jnp.int32, shape, full)
    m = lax.broadcasted_iota(jnp.int32, shape, part)
    q = (m * 2731) >> 16
    return l == m + FR * (q + core)


def spots_t(core):
    return spots(core, (DC, D), 1, 0)


def params(**kw):
    return pltpu.CompilerParams(vmem_limit_bytes=VMEM_LIMIT, **kw)


def cost(flops, bytes_accessed, transcendentals=0):
    return pl.CostEstimate(
        flops=int(flops), bytes_accessed=int(bytes_accessed), transcendentals=int(transcendentals)
    )


def dot(a, b):
    return jnp.dot(a, b, preferred_element_type=f32)


def dot_t(a, b):
    return lax.dot_general(a, b, (((1,), (1,)), ((), ())), preferred_element_type=f32)


def t_dot(a, b):
    return lax.dot_general(a, b, (((0,), (0,)), ((), ())), preferred_element_type=f32)


def stats(z):
    mean_val = jnp.mean(z, axis=-1, keepdims=True)
    centred = z - mean_val
    variance = jnp.mean(centred * centred, axis=-1, keepdims=True)
    inv_std = lax.rsqrt(variance + EPS_NORM)
    return centred * inv_std, inv_std


def norm_back(grad, normed, inv_std, gain):
    e = grad * gain
    return inv_std * (
        e
        - jnp.mean(e, axis=-1, keepdims=True)
        - normed * jnp.mean(e * normed, axis=-1, keepdims=True)
    )


def swap_halves(u):
    lanes = u.shape[1]
    lane = lax.broadcasted_iota(jnp.int32, u.shape, 1)
    up = pltpu.roll(u, lanes - HD // 2, 1)
    down = pltpu.roll(u, HD // 2, 1)
    return jnp.where((lane & (HD - 1)) < HD // 2, up, down)


TURN = 1.5707963267948966


def sin_cos(a):
    k = jnp.floor(a * (1.0 / TURN) + 0.5)
    r = ((a - k * 1.5703125) - k * 4.837512969970703125e-4) - k * 7.54978995489188216e-8
    z = r * r
    s = ((-1.9515295891e-4 * z + 8.3321608736e-3) * z - 1.6666654611e-1) * z * r + r
    c = ((2.443315711809948e-5 * z - 1.388731625493765e-3) * z + 4.166664568298827e-2) * z * z - 0.5 * z + 1.0
    quarter = k.astype(jnp.int32)
    odd = (quarter & 1) == 1
    sine = jnp.where(odd, c, s)
    cosine = jnp.where(odd, s, c)
    sine = jnp.where((quarter & 2) == 0, sine, -sine)
    cosine = jnp.where(((quarter + 1) & 2) == 0, cosine, -cosine)
    return sine, cosine


def early_kernel(place_ref, x_ref, xo_ref, c_ref, co_ref, ints_ref, n1_ref, gy_ref, pos_ref):
    i = pl.program_id(0)
    mine = i == 0
    keep = usable_rows(place_ref, i ^ place_ref[0], S)
    gy_ref[...] = (jnp.where(mine, c_ref[...], co_ref[...]).astype(f32) * keep).astype(bf16)
    n1_ref[...] = stats(jnp.where(mine, x_ref[...], xo_ref[...]).astype(f32))[0]
    pos_ref[...] = ints_ref[0].astype(f32).T


def early_call(place, x, xo, c, co, ints):
    whole = pl.BlockSpec((S, D), lambda i, c: (0, 0))
    tile = lambda n: pl.BlockSpec((S, n), lambda i, c: (i, 0))
    return pl.pallas_call(
        early_kernel,
        grid_spec=pltpu.PrefetchScalarGridSpec(
            num_scalar_prefetch=1,
            grid=(CORES,),
            in_specs=[whole] * 4 + [pl.BlockSpec((1, 8, S), lambda i, c: (i, 0, 0))],
            out_specs=[tile(D), tile(D), tile(8)],
        ),
        out_shape=[
            jax.ShapeDtypeStruct((T, D), f32),
            jax.ShapeDtypeStruct((T, D), bf16),
            jax.ShapeDtypeStruct((T, 8), f32),
        ],
        compiler_params=params(),
        cost_estimate=cost(15 * T * D, T * D * 10),
    )(place, x, xo, c, co, ints)


def qkv_kernel(
    place_ref, n1_ref, pos_ref, w0, w1, w2, w3, v0, v1, v2, v3,
    vec_ref, ht_ref, cos_ref, sin_ref, q_out, k_out, v_out, b1_ref,
    w_s, full_s, rows_s, freq_s,
):
    core = place_ref[0]

    @pl.when(pl.program_id(0) == 0)
    def _():
        lay_out(place_ref, (w0, w1, w2, w3), w_s)
        lay_out(place_ref, (v0, v1, v2, v3), full_s)
        rows_s[...] = full_s[...].astype(f32).T[:16, :]
        vec_ref[...] = rows_s[...]
        late = rows_s[8:16, :].astype(bf16)
        units = dot(late, spots(core, (D, DC), 0, 1).astype(bf16))
        for r in range(FC // DC):
            b1_ref[:, r * DC : (r + 1) * DC] = units[2 + r : 3 + r, :]
        src = lax.broadcasted_iota(jnp.int32, (D, DC), 0)
        dst = lax.broadcasted_iota(jnp.int32, (D, DC), 1)
        want = core * (DC // 2) + (dst // HD) * (HD // 2) + (dst & (HD // 2 - 1))
        freq_s[0:8, :] = dot(late, (src == want).astype(bf16))
        freq_s[8:16, :] = dot(late, (src == want + D // 2).astype(bf16))

    h = n1_ref[...] * rows_s[0:1, :] + rows_s[1:2, :]
    ht_ref[...] = h.T.astype(bf16)
    acc = dot(h.astype(bf16), w_s[...])
    angle = pos_ref[:, 1:2] * freq_s[1:2, :] + pos_ref[:, 0:1] * freq_s[9:10, :]
    lane = lax.broadcasted_iota(jnp.int32, (1, DC), 1)
    sign = jnp.where((lane & (HD - 1)) < HD // 2, -1.0, 1.0)
    small = jnp.max(jnp.abs(angle)) < 8000.0

    @pl.when(small)
    def _():
        sine, cosine = sin_cos(angle)
        cos_ref[...] = cosine
        sin_ref[...] = sine * sign

    @pl.when(jnp.logical_not(small))
    def _():
        cos_ref[...] = jnp.cos(angle)
        sin_ref[...] = jnp.sin(angle) * sign

    cosine, sine = cos_ref[...], sin_ref[...]
    at = pl.ds(pl.multiple_of(core * DC, DC), DC)
    part = lambda i: jnp.concatenate([acc[:, (3 * p + i) * 128 : (3 * p + i + 1) * 128] for p in range(PAIRS)], axis=1)
    q = part(0) + rows_s[4:5, at]
    k = part(1) + rows_s[5:6, at]
    q_out[...] = ((q * cosine + swap_halves(q) * sine) * HD ** (-0.5)).astype(bf16)
    k_out[...] = (k * cosine + swap_halves(k) * sine).astype(bf16)
    v_out[...] = (part(2) + rows_s[6:7, at]).astype(bf16)


def qkv_call(place, n1, pos, pieces):
    rows = 384
    tile = lambda n: pl.BlockSpec((rows, n), lambda i, c: (i, 0))
    keep = lambda *n: pl.BlockSpec(n, lambda i, c: (0,) * len(n))
    return pl.pallas_call(
        qkv_kernel,
        grid_spec=pltpu.PrefetchScalarGridSpec(
            num_scalar_prefetch=1,
            grid=(T // rows,),
            in_specs=[tile(D), tile(8)]
            + [keep(QUARTER, 3 * DC)] * 4
            + [pl.BlockSpec((QUARTER, 128), lambda i, c: (0, 3 * DC // 128))] * 4,
            out_specs=[keep(16, D), pl.BlockSpec((D, rows), lambda i, c: (0, i))] + [tile(DC)] * 5 + [keep(1, FC)],
            scratch_shapes=[
                pltpu.VMEM((D, 3 * DC), bf16),
                pltpu.VMEM((D, 128), bf16),
                pltpu.VMEM((16, D), f32),
                pltpu.VMEM((16, DC), f32),
            ],
        ),
        out_shape=[
            jax.ShapeDtypeStruct((16, D), f32),
            jax.ShapeDtypeStruct((D, T), bf16),
            jax.ShapeDtypeStruct((T, DC), f32),
            jax.ShapeDtypeStruct((T, DC), f32),
            *[jax.ShapeDtypeStruct((T, DC), bf16)] * 3,
            jax.ShapeDtypeStruct((1, FC), f32),
        ],
        compiler_params=params(),
        cost_estimate=cost(2 * T * D * 3 * DC + 50 * T * DC, T * D * 6 + D * 3 * DC * 2 + T * DC * 14),
    )(place, n1, pos, *pieces, *pieces)


def softmax_head(q, k, v, mine, bias):
    s = dot_t(jnp.where(mine, q, jnp.zeros_like(q)), k) + bias
    e = jnp.exp(s - jnp.max(s, axis=-1, keepdims=True))
    p = e * (1.0 / jnp.sum(e, axis=-1, keepdims=True))
    return p


def attn_fwd_kernel(
    place_ref, q0, k0, v0, q1, k1, v1, o_ref, p0_ref, p1_ref
):
    lane = lax.broadcasted_iota(jnp.int32, (1, 2 * HD), 1)
    low = lane < HD
    q, k, v = q1[0], k1[0], v1[0]
    mixes = []
    bias = key_bias(place_ref)
    for head, mine in ((0, low), (1, ~low)):
        p = softmax_head(q, k, v, mine, bias).astype(bf16)
        p1_ref[head] = p
        mixes.append(dot(p, v))
    mix = jnp.where(low, mixes[0], mixes[1])
    o_ref[1] = jnp.where(usable_rows(place_ref, 1, S) > 0, mix, v.astype(f32)).astype(bf16)
    o_ref[0] = v0[0]
    for win, base in enumerate(WINDOWS):
        q, k, v = (r[0, base : base + WIN, :] for r in (q0, k0, v0))
        own = own_rows(win)
        bias = key_bias(place_ref, win)
        mixes = []
        for head, mine in ((0, low), (1, ~low)):
            p = softmax_head(q, k, v, mine, bias)
            p = (p * own).astype(bf16)
            p0_ref[head, win] = p
            mixes.append(dot(p, v))
        mix = jnp.where(low, mixes[0], mixes[1])
        use = (own * usable_rows(place_ref, 0, WIN, base)) > 0
        before = o_ref[0, base : base + WIN, :].astype(f32)
        o_ref[0, base : base + WIN, :] = jnp.where(use, mix, before).astype(bf16)


def attn_fwd_call(place, q, k, v):
    block = lambda g: pl.BlockSpec((1, S, 2 * HD), lambda p, c: (g ^ c[0], 0, p))
    q, k, v = (a.reshape(CORES, S, DC) for a in (q, k, v))
    return pl.pallas_call(
        attn_fwd_kernel,
        grid_spec=pltpu.PrefetchScalarGridSpec(
            num_scalar_prefetch=1,
            grid=(PAIRS,),
            in_specs=[block(0)] * 3 + [block(1)] * 3,
            out_specs=[
                pl.BlockSpec((CORES, S, 2 * HD), lambda p, c: (0, 0, p)),
                pl.BlockSpec((2, 2, WIN, WIN), lambda p, c: (p, 0, 0, 0)),
                pl.BlockSpec((2, S, S), lambda p, c: (p, 0, 0)),
            ],
        ),
        out_shape=[
            jax.ShapeDtypeStruct((CORES, S, DC), bf16),
            jax.ShapeDtypeStruct((HC, 2, WIN, WIN), bf16),
            jax.ShapeDtypeStruct((HC, S, S), bf16),
        ],
        compiler_params=params(),
        cost_estimate=cost(4 * HC * (S * S + 2 * WIN * WIN) * 128, 12e6, HC * S * S),
    )(place, q, k, v, q, k, v)


def proj_kernel(place_ref, mine_ref, other_ref, x_ref, xo_ref, w0, w1, w2, w3, v_ref, after_ref, h2_ref, w_s):
    @pl.when(pl.program_id(0) == 0)
    def _():
        lay_out(place_ref, (w0, w1, w2, w3), w_s)

    core = place_ref[0]
    at = lambda c: pl.ds(pl.multiple_of(c * DC, DC), DC)
    branch = dot(mine_ref[0], w_s[at(core), :]) + dot(other_ref[0], w_s[at(1 - core), :])
    x = jnp.where(pl.program_id(0) < pl.num_programs(0) // CORES, x_ref[...], xo_ref[...])
    after = x.astype(f32) + (branch + v_ref[7:8, :])
    after_ref[...] = after
    normed, _ = stats(after)
    h2_ref[...] = (normed * v_ref[2:3, :] + v_ref[3:4, :]).astype(bf16)


def proj_call(place, mine, other, x, xo, pieces, vec):
    rows = 288
    half = S // rows
    tile = lambda n: pl.BlockSpec((rows, n), lambda i, c: (i, 0))
    whole = lambda a: pl.BlockSpec(a.shape, lambda i, c: (0,) * a.ndim)
    return pl.pallas_call(
        proj_kernel,
        grid_spec=pltpu.PrefetchScalarGridSpec(
            num_scalar_prefetch=1,
            grid=(T // rows,),
            in_specs=[
                pl.BlockSpec((1, rows, DC), lambda i, c: ((i // half) ^ c[0], i % half, 0)),
                pl.BlockSpec((1, rows, DC), lambda i, c: ((i // half) ^ c[0], i % half, 0)),
                pl.BlockSpec((rows, D), lambda i, c: (jnp.minimum(i, half - 1), 0)),
                pl.BlockSpec((rows, D), lambda i, c: (jnp.maximum(i - half, 0), 0)),
            ]
            + [pl.BlockSpec((QUARTER, D), lambda i, c: (0, FC // D))] * 4
            + [whole(vec)],
            out_specs=[tile(D), tile(D)],
            scratch_shapes=[pltpu.VMEM((D, D), bf16)],
        ),
        out_shape=[jax.ShapeDtypeStruct((T, D), f32), jax.ShapeDtypeStruct((T, D), bf16)],
        compiler_params=params(),
        cost_estimate=cost(2 * T * D * D, T * D * 10 + D * D * 2),
    )(place, mine, other, x, xo, *pieces, vec)


PACK = 4 * DC + 128
K0 = (2.0 / 3.141592653589793) ** 0.5
FT = 768


def gelu_slope(u):
    sq = u * u
    th = jnp.tanh(u * (K0 + (K0 * 0.044715) * sq))
    half = 0.5 + 0.5 * th
    return u * half, half + (u * (half - half * half)) * (2 * K0 + (6 * K0 * 0.044715) * sq)


def mlp_kernel(
    place_ref, h2_ref, gy_ref, w10, w11, w12, w13, w2_ref, b1_ref, mlp_ref, mlpo_ref, gh2b_ref, act_ref, gup_ref, gb1_ref, w1_s
):
    i = pl.program_id(0)

    @pl.when(i == 0)
    def _():
        lay_out(place_ref, (w10, w11, w12, w13), w1_s)
        gb1_ref[...] = jnp.zeros_like(gb1_ref)

    for f in range(FC // FT):
        c = slice(f * FT, (f + 1) * FT)
        act, slope = gelu_slope(dot(h2_ref[...], w1_s[:, c]) + b1_ref[:, c])
        act_ref[:, c] = act.astype(bf16)
        gup = (dot_t(gy_ref[...], w2_ref[c, :]) * slope).astype(bf16)
        gup_ref[:, c] = gup
        gb1_ref[:, c] += jnp.sum(gup.astype(f32), axis=0, keepdims=True)
    gh2b_ref[...] = dot_t(gup_ref[...], w1_s[...]).astype(bf16)
    mlp = dot(act_ref[...], w2_ref[...])
    half = pl.num_programs(0) // CORES

    @pl.when(i < half)
    def _():
        mlp_ref[...] = mlp

    @pl.when(i >= half)
    def _():
        mlpo_ref[...] = mlp


def mlp_call(place, h2, gy, pieces, w2, b1):
    rows = 288
    half = S // rows
    tile = lambda n: pl.BlockSpec((rows, n), lambda i, c: (i, 0))
    whole = lambda a: pl.BlockSpec(a.shape, lambda i, c: (0,) * a.ndim)
    return pl.pallas_call(
        mlp_kernel,
        grid_spec=pltpu.PrefetchScalarGridSpec(
            num_scalar_prefetch=1,
            grid=(T // rows,),
            in_specs=[tile(D), tile(D)]
            + [pl.BlockSpec((QUARTER, FC), lambda i, c: (0, 0))] * 4
            + [whole(w2), whole(b1)],
            out_specs=[
                pl.BlockSpec((rows, D), lambda i, c: (jnp.minimum(i, half - 1), 0)),
                pl.BlockSpec((rows, D), lambda i, c: (jnp.maximum(i - half, 0), 0)),
                tile(D),
                tile(FC),
                tile(FC),
                pl.BlockSpec((1, FC), lambda i, c: (0, 0)),
            ],
            scratch_shapes=[pltpu.VMEM((D, FC), bf16)],
        ),
        out_shape=[
            jax.ShapeDtypeStruct((S, D), f32),
            jax.ShapeDtypeStruct((S, D), f32),
            jax.ShapeDtypeStruct((T, D), bf16),
            jax.ShapeDtypeStruct((T, FC), bf16),
            jax.ShapeDtypeStruct((T, FC), bf16),
            jax.ShapeDtypeStruct((1, FC), f32),
        ],
        compiler_params=params(),
        cost_estimate=cost(8 * T * D * FC, 30e6, T * FC),
    )(place, h2, gy, *pieces, w2, b1)


def by_line(place_ref, value, block, out_ref):
    core = place_ref[0]
    for n in range(PLANE):
        to = jnp.where(core == 0, n, (n % SIDE) * SIDE + n // SIDE)
        out_ref[pl.ds(pl.multiple_of(to * block, block), block), :] = value[n * block : (n + 1) * block, :].astype(bf16)


def fc_grad_kernel(place_ref, h2_ref, gup_ref, act_ref, gy_ref, gw1_ref, gw2_ref):
    by_line(place_ref, t_dot(act_ref[...], gy_ref[...]), SIDE * FR, gw2_ref)
    by_line(place_ref, t_dot(h2_ref[...], gup_ref[...]), BLOCK, gw1_ref)


def fc_grad_call(place, h2, gup, act, gy):
    whole = lambda a: pl.BlockSpec(a.shape, lambda i, c: (0, 0))
    return pl.pallas_call(
        fc_grad_kernel,
        grid_spec=pltpu.PrefetchScalarGridSpec(
            num_scalar_prefetch=1,
            grid=(2,),
            in_specs=[
                whole(h2),
                pl.BlockSpec((T, FC // 2), lambda i, c: (0, i)),
                whole(act),
                pl.BlockSpec((T, DC), lambda i, c: (0, i)),
            ],
            out_specs=[
                pl.BlockSpec((D, FC // 2), lambda i, c: (0, i)),
                pl.BlockSpec((FC, DC), lambda i, c: (0, i)),
            ],
        ),
        out_shape=[jax.ShapeDtypeStruct((D, FC), bf16), jax.ShapeDtypeStruct((FC, D), bf16)],
        compiler_params=params(),
        cost_estimate=cost(4 * T * D * FC, T * (D + FC) * 4 + D * FC * 4),
    )(place, h2, gup, act, gy)


def mid_kernel(place_ref, after_ref, gy_ref, gh2_ref, other_ref, v_ref, ga_ref, gab_ref, sums_ref):
    i = pl.program_id(0)
    normed, inv_std = stats(after_ref[...])
    gh2 = gh2_ref[...].astype(f32) + other_ref[...].astype(f32)
    gy = gy_ref[...].astype(f32)
    ga = gy + norm_back(gh2, normed, inv_std, v_ref[2:3, :])
    gab = ga.astype(bf16)
    gab_ref[...] = gab

    @pl.when(i == 0)
    def _():
        sums_ref[...] = jnp.zeros_like(sums_ref)

    @pl.when(i < pl.num_programs(0) // CORES)
    def _():
        ga_ref[...] = ga
        sums_ref[0:1, :] += jnp.sum(gh2 * normed, axis=0, keepdims=True)
        sums_ref[1:2, :] += jnp.sum(gh2, axis=0, keepdims=True)
        sums_ref[2:3, :] += jnp.sum(gab.astype(f32), axis=0, keepdims=True)
        sums_ref[3:4, :] += jnp.sum(gy, axis=0, keepdims=True)


def mid_call(place, after, gy, gh2, other, vec):
    rows = 288
    half = S // rows
    tile = lambda n: pl.BlockSpec((rows, n), lambda i, c: (i, 0))
    flipped = pl.BlockSpec((rows, D), lambda i, c: ((i + half) % (2 * half), 0))
    whole = lambda a: pl.BlockSpec(a.shape, lambda i, c: (0,) * a.ndim)
    return pl.pallas_call(
        mid_kernel,
        grid_spec=pltpu.PrefetchScalarGridSpec(
            num_scalar_prefetch=1,
            grid=(T // rows,),
            in_specs=[tile(D), tile(D), tile(D), flipped, whole(vec)],
            out_specs=[
                pl.BlockSpec((rows, D), lambda i, c: (jnp.minimum(i, half - 1), 0)),
                tile(D),
                pl.BlockSpec((8, D), lambda i, c: (0, 0)),
            ],
        ),
        out_shape=[
            jax.ShapeDtypeStruct((S, D), f32),
            jax.ShapeDtypeStruct((T, D), bf16),
            jax.ShapeDtypeStruct((8, D), f32),
        ],
        compiler_params=params(),
        cost_estimate=cost(30 * T * D, T * D * 14),
    )(place, after, gy, gh2, other, vec)


def back_head(q_t, k, v, do, do_t, delta, p, mine, head):
    gp = dot_t(jnp.where(mine, do, jnp.zeros_like(do)), v)
    gs = (p.astype(f32) * (gp - delta)).astype(bf16)
    at = slice(head * HD, (head + 1) * HD)
    return dot(gs, k), dot(q_t[at, :], gs), dot(do_t[at, :], p)


def deltas(do, o, low):
    prod = do.astype(f32) * o.astype(f32)
    d0 = jnp.sum(jnp.where(low, prod, 0.0), axis=-1, keepdims=True)
    d1 = jnp.sum(jnp.where(low, 0.0, prod), axis=-1, keepdims=True)
    return d0, d1


def attn_bwd_kernel(
    start,
    place_ref,
    q0, k0, v0, o0, p0, cos0, sin0, pos0,
    q1, k1, v1, o1, p1, cos1, sin1, pos1,
    h1t_ref, ga_ref, cols_ref, mine_ref, other_ref, y0, y1, y2, y3,
    gw0, gw1, gw2, gw3, gqkv_ref, sums_ref,
    gq_s, gk_s, gv_s, gw_s, y_s, do_s,
):
    lane = lax.broadcasted_iota(jnp.int32, (1, 2 * HD), 1)
    low = lane < HD
    pair = pl.program_id(0)
    core = place_ref[0]

    @pl.when(pair == 0)
    def _():
        lay_out(place_ref, (y0, y1, y2, y3), y_s)

    wy = y_s[pl.ds(pl.multiple_of(core * DC + (start + pair) * 2 * HD, 2 * HD), 2 * HD), :]
    for frame in range(CORES):
        do_s[frame] = dot_t(ga_ref[frame], wy).astype(bf16)

    def finish(frame, q, k, cos_ref, sin_ref, pos_ref):
        cosine, sine = cos_ref[0], sin_ref[0]
        gq = gq_s[...] * HD ** (-0.5)
        gk = gk_s[...]
        sq, sk = swap_halves(gq), swap_halves(gk)
        turn = (q.astype(f32) * HD**0.5) * sq + k.astype(f32) * sk
        gq = (gq * cosine - sq * sine).astype(bf16)
        gk = (gk * cosine - sk * sine).astype(bf16)
        gv = gv_s[...].astype(bf16)
        at = pl.ds(pl.multiple_of((frame ^ core) * S, S), S)
        gqkv_ref[at, : 2 * HD] = gq
        gqkv_ref[at, 2 * HD : 4 * HD] = gk
        gqkv_ref[at, 4 * HD :] = gv
        pos = pos_ref[0]
        col = jnp.sum(turn * pos[:, 1:2], axis=0, keepdims=True)
        row = jnp.sum(turn * pos[:, 0:1], axis=0, keepdims=True)
        bias = [jnp.sum(g.astype(f32), axis=0, keepdims=True) for g in (gq, gk, gv)]
        return jnp.concatenate([col, row] + bias, axis=0)

    q, k, v, do = q1[0], k1[0], v1[0], do_s[1 ^ core]
    d = deltas(do, o1[0], low)
    q_t, do_t = q.astype(f32).T.astype(bf16), do.astype(f32).T.astype(bf16)
    out = [
        back_head(q_t, k, v, do, do_t, d[head], p1[head], mine, head)
        for head, mine in ((0, low), (1, ~low))
    ]
    gq_s[...] = jnp.where(low, out[0][0], out[1][0])
    gk_s[...] = jnp.concatenate([out[0][1], out[1][1]], axis=0).T
    gv_s[...] = jnp.concatenate([out[0][2], out[1][2]], axis=0).T
    sums1 = finish(1, q, k, cos1, sin1, pos1)
    gq_s[...] = jnp.zeros_like(gq_s)
    gk_s[...] = jnp.zeros_like(gk_s)
    gv_s[...] = jnp.zeros_like(gv_s)
    for win, base in enumerate(WINDOWS):
        at = pl.ds(base, WIN)
        q, k, v, o = (r[0, at, :] for r in (q0, k0, v0, o0))
        do = do_s[core, at, :]
        d = deltas(do, o, low)
        q_t, do_t = q.astype(f32).T.astype(bf16), do.astype(f32).T.astype(bf16)
        out = [
            back_head(q_t, k, v, do, do_t, d[head], p0[head, win], mine, head)
            for head, mine in ((0, low), (1, ~low))
        ]
        gq_s[at, :] += jnp.where(low, out[0][0], out[1][0])
        gk_s[at, :] += jnp.concatenate([out[0][1], out[1][1]], axis=0).T
        gv_s[at, :] += jnp.concatenate([out[0][2], out[1][2]], axis=0).T
    sums0 = finish(0, q0[0], k0[0], cos0, sin0, pos0)
    sums_ref[0, 0:5, :] = sums0 + sums1
    sums_ref[0, 5:8, :] = jnp.zeros((3, 2 * HD), f32)

    gw_mine = jnp.zeros((2 * HD, DC), f32)
    gw_other = jnp.zeros((2 * HD, DC), f32)
    for frame in range(CORES):
        cols = cols_ref[frame].astype(f32).T.astype(bf16)
        gw_mine += dot(cols, mine_ref[frame ^ core])
        gw_other += dot(cols, other_ref[frame ^ core])
    gw_s[:, : 6 * HD] = dot(h1t_ref[...], gqkv_ref[...]).astype(bf16)
    at = lambda c: pl.ds(pl.multiple_of(c * DC, DC), DC)
    gw_s[at(core), 6 * HD :] = gw_mine.T.astype(bf16)
    gw_s[at(1 - core), 6 * HD :] = gw_other.T.astype(bf16)
    to_chips(place_ref, gw_s, (gw0, gw1, gw2, gw3))


def to_chips(place_ref, full_ref, outs):
    for d, out in enumerate(outs):
        a = (place_ref[1] + d) & (SIDE - 1)
        for g in range(SIDE):
            at = pl.multiple_of(natural(place_ref[0], a, g) * BLOCK, BLOCK)
            out[g * BLOCK : (g + 1) * BLOCK, :] = full_ref[pl.ds(at, BLOCK), :]


def attn_bwd_call(start, pairs, place, q, k, v, ga, mine, other, p0, p1, cosine, sine, pos, h1t, proj_pieces):
    q, k, v, cosine, sine, pos, ga = (a.reshape(CORES, S, -1) for a in (q, k, v, cosine, sine, pos, ga))
    block = lambda g: pl.BlockSpec((1, S, 2 * HD), lambda p, c: (g ^ c[0], 0, start + p))
    own = lambda g: pl.BlockSpec((1, S, 2 * HD), lambda p, c: (g, 0, start + p))
    at = lambda g: pl.BlockSpec((1, S, 8), lambda p, c: (g ^ c[0], 0, 0))
    whole = lambda a: pl.BlockSpec(a.shape, lambda p, c: (0,) * a.ndim)
    grads = pl.BlockSpec((QUARTER, 8 * HD), lambda p, c: (0, p))
    return pl.pallas_call(
        functools.partial(attn_bwd_kernel, start),
        grid_spec=pltpu.PrefetchScalarGridSpec(
            num_scalar_prefetch=1,
            grid=(pairs,),
            in_specs=[block(0)] * 3
            + [own(0), pl.BlockSpec((2, 2, WIN, WIN), lambda p, c: (start + p, 0, 0, 0))]
            + [block(0)] * 2
            + [at(0)]
            + [block(1)] * 3
            + [own(1), pl.BlockSpec((2, S, S), lambda p, c: (start + p, 0, 0))]
            + [block(1)] * 2
            + [at(1)]
            + [whole(h1t), whole(ga)]
            + [pl.BlockSpec((CORES, S, 2 * HD), lambda p, c: (0, 0, PAIRS * c[0] + start + p))]
            + [whole(mine), whole(other)]
            + [pl.BlockSpec((QUARTER, D), lambda p, c: (0, FC // D))] * 4,
            out_specs=[grads] * 4
            + [
                pl.BlockSpec((T, 6 * HD), lambda p, c: (0, p)),
                pl.BlockSpec((1, 8, 2 * HD), lambda p, c: (p, 0, 0)),
            ],
            scratch_shapes=[pltpu.VMEM((S, 2 * HD), f32)] * 3
            + [pltpu.VMEM((D, 8 * HD), bf16), pltpu.VMEM((D, D), bf16), pltpu.VMEM((CORES, S, 2 * HD), bf16)],
        ),
        out_shape=[
            *[jax.ShapeDtypeStruct((QUARTER, pairs * 8 * HD), bf16)] * 4,
            jax.ShapeDtypeStruct((T, pairs * 6 * HD), bf16),
            jax.ShapeDtypeStruct((pairs, 8, 2 * HD), f32),
        ],
        compiler_params=params(),
        cost_estimate=cost((10 * HC * S * S * 128 + 4 * T * D * 4 * DC) * pairs / PAIRS, 9e6 * (1 + pairs)),
    )(
        place,
        q, k, v, mine, p0, cosine, sine, pos,
        q, k, v, mine, p1, cosine, sine, pos,
        h1t, ga, ga, mine, other, *proj_pieces,
    )


def gh_kernel(
    place_ref, ga_ref, gb_ref, n1_ref, mid_ref, sa_ref, sb_ref, gb1_ref, w0, w1, w2, w3,
    gh_ref, gho_ref, o0, o1, o2, o3,
    w_s, rows_s, full_s,
):
    core = place_ref[0]
    i = pl.program_id(0)
    half = pl.num_programs(0) // CORES

    @pl.when(i == 0)
    def _():
        lay_out(place_ref, (w0, w1, w2, w3), w_s)
        rows_s[...] = jnp.zeros_like(rows_s)

    g = jnp.concatenate([ga_ref[...], gb_ref[...]], axis=1)
    gh = dot_t(g, w_s[...])

    @pl.when(i < half)
    def _():
        gh_ref[...] = gh

    @pl.when(i >= half)
    def _():
        gho_ref[...] = gh

    rows_s[0:1, :] += jnp.sum(gh * n1_ref[...], axis=0, keepdims=True)
    rows_s[1:2, :] += jnp.sum(gh, axis=0, keepdims=True)

    @pl.when(i == 2 * half - 1)
    def _():
        rows_s[2:4, :] = mid_ref[0:2, :]
        rows_s[7:9, :] = mid_ref[2:4, :]
        att = jnp.concatenate([s[p] for s in (sa_ref, sb_ref) for p in range(s.shape[0])], axis=1)
        rows_s[4:7, pl.ds(pl.multiple_of(core * DC, DC), DC)] = att[2:5, :]
        src = lax.broadcasted_iota(jnp.int32, (DC, D), 0)
        dst = lax.broadcasted_iota(jnp.int32, (DC, D), 1)
        want = core * (DC // 2) + (src // HD) * (HD // 2) + (src & (HD // 2 - 1))
        lane = lax.broadcasted_iota(jnp.int32, (1, DC), 1)
        turn = jnp.where((lane & (HD - 1)) < HD // 2, att, -att)
        rows_s[9:10, :] = exact_dot(turn, dst == want)[0:1, :] + exact_dot(turn, dst == want + D // 2)[1:2, :]
        gb1 = jnp.concatenate([gb1_ref[:, r * DC : (r + 1) * DC] for r in range(FC // DC)] * 2, axis=0)
        rows_s[10:14, :] = exact_dot(gb1, spots_t(core))[:4, :]
        full_s[...] = rows_s[...].T
        to_chips(place_ref, full_s, (o0, o1, o2, o3))


def gh_call(place, ga, gb, n1, mid, sa, sb, gb1, pieces):
    rows = 288
    half = S // rows
    tile = lambda n: pl.BlockSpec((rows, n), lambda i, c: (i, 0))
    whole = lambda a: pl.BlockSpec(a.shape, lambda i, c: (0,) * a.ndim)
    keep = lambda *n: pl.BlockSpec(n, lambda i, c: (0,) * len(n))
    return pl.pallas_call(
        gh_kernel,
        grid_spec=pltpu.PrefetchScalarGridSpec(
            num_scalar_prefetch=1,
            grid=(T // rows,),
            in_specs=[tile(ga.shape[1]), tile(gb.shape[1]), tile(D)]
            + [whole(a) for a in (mid, sa, sb, gb1)]
            + [keep(QUARTER, 3 * DC)] * 4,
            out_specs=[
                pl.BlockSpec((rows, D), lambda i, c: (jnp.minimum(i, half - 1), 0)),
                pl.BlockSpec((rows, D), lambda i, c: (jnp.maximum(i - half, 0), 0)),
            ]
            + [keep(QUARTER, 128)] * 4,
            scratch_shapes=[pltpu.VMEM((D, 3 * DC), bf16), pltpu.VMEM((128, D), f32), pltpu.VMEM((D, 128), f32)],
        ),
        out_shape=[
            jax.ShapeDtypeStruct((S, D), f32),
            jax.ShapeDtypeStruct((S, D), f32),
            *[jax.ShapeDtypeStruct((QUARTER, 128), f32)] * 4,
        ],
        compiler_params=params(),
        cost_estimate=cost(2 * T * D * 3 * DC, T * D * 12),
    )(place, ga, gb, n1, mid, sa, sb, gb1, *pieces)


def last_kernel(x_ref, ga_ref, gh_ref, other_ref, after_ref, mlp_ref, mlpo_ref, v_ref, gt_ref, out_ref):
    normed, inv_std = stats(x_ref[...].astype(f32))
    gt_ref[...] = ga_ref[...] + norm_back(gh_ref[...] + other_ref[...], normed, inv_std, v_ref[0:1, :])
    out_ref[...] = (after_ref[...] + (mlp_ref[...] + mlpo_ref[...] + v_ref[8:9, :])).astype(bf16)


def last_call(x, ga, gh, other, after, mlp, mlp_other, vec):
    rows = 288
    tile = lambda n: pl.BlockSpec((rows, n), lambda i: (i, 0))
    return pl.pallas_call(
        last_kernel,
        grid=(S // rows,),
        in_specs=[tile(D)] * 7 + [pl.BlockSpec(vec.shape, lambda i: (0, 0))],
        out_specs=[tile(D), tile(D)],
        out_shape=[jax.ShapeDtypeStruct((S, D), f32), jax.ShapeDtypeStruct((S, D), bf16)],
        compiler_params=params(),
        cost_estimate=cost(30 * S * D, S * D * 28),
    )(x, ga, gh, other, after, mlp, mlp_other, vec)


def pack_kernel(a0, a1, a2, a3, b0, b1, b2, b3, v0, v1, v2, v3, out_ref):
    def add(*refs):
        return sum(r[...].astype(f32) for r in refs)

    parts = [add(a0, a1, a2, a3), add(b0, b1, b2, b3), add(v0, v1, v2, v3)]
    to = 0
    for part in parts:
        for n in range(PLANE):
            out_ref[n, :, to : to + part.shape[1]] = part[n * KR : (n + 1) * KR, :].astype(bf16)
        to += part.shape[1]


def pack_call(*parts):
    return pl.pallas_call(
        pack_kernel,
        out_shape=jax.ShapeDtypeStruct((PLANE, KR, PACK), bf16),
        compiler_params=params(),
        cost_estimate=cost(QUARTER * PACK * 4, QUARTER * PACK * 10),
    )(*(a for part in parts for a in part))


def sum_kernel(in_ref, out_ref):
    total = in_ref[0].astype(f32)
    for n in range(1, PLANE):
        total += in_ref[n].astype(f32)
    out_ref[...] = total


def sum_call(packed):
    return pl.pallas_call(
        sum_kernel,
        out_shape=jax.ShapeDtypeStruct(packed.shape[1:], f32),
        compiler_params=params(),
        cost_estimate=cost(packed.size, packed.size * 2),
    )(packed)


def fc_kernel(place_ref, f1_ref, f1o_ref, f2_ref, f2o_ref, g1_ref, g2_ref, sq_ref):
    first = place_ref[0] == 0
    a, b = f1_ref[...], f1o_ref[...]
    a, b = jnp.where(first, a, b), jnp.where(first, b, a)
    for r in range(FC // DC):
        at = slice(r * DC, (r + 1) * DC)
        g1_ref[:, r * D : (r + 1) * D] = exact_dot(a[:, at], spots_t(0)) + exact_dot(b[:, at], spots_t(1))
    c, d = f2_ref[...], f2o_ref[...]
    g2_ref[:FR, :] = jnp.where(first, c, d)
    g2_ref[FR:, :] = jnp.where(first, d, c)
    total = jnp.sum(a * a + b * b, axis=(0, 1), keepdims=True) + jnp.sum(c * c + d * d, axis=(0, 1), keepdims=True)
    sq_ref[...] = jnp.broadcast_to(total, sq_ref.shape)


def fc_call(place, f1, f1o, f2, f2o):
    whole = lambda a: pl.BlockSpec(a.shape, lambda i, c: (0,) * len(a.shape))
    args = (f1, f1o, f2, f2o)
    shapes = [jax.ShapeDtypeStruct(s, f32) for s in ((KR, FF), (2 * FR, D), (8, 128))]
    return pl.pallas_call(
        fc_kernel,
        grid_spec=pltpu.PrefetchScalarGridSpec(
            num_scalar_prefetch=1,
            grid=(1,),
            in_specs=[whole(a) for a in args],
            out_specs=[whole(a) for a in shapes],
        ),
        out_shape=shapes,
        compiler_params=params(),
        cost_estimate=cost(6 * KR * DC * D * 8, 1e6),
    )(place, *args)


def norm_kernel(g_ref, o_ref, sq_ref, out_ref):
    g, o = g_ref[...], o_ref[...]
    part = jnp.sum(g * g + o * o, axis=(0, 1), keepdims=True)
    cross = g[:, 4 * DC : PACK] * o[:, 4 * DC : PACK]
    part += 2.0 * jnp.sum(cross, axis=(0, 1), keepdims=True)
    out_ref[...] = jnp.broadcast_to((part + sq_ref[0:1, 0:1])[None], out_ref.shape)


def norm_call(g, o, squares):
    return pl.pallas_call(
        norm_kernel,
        out_shape=jax.ShapeDtypeStruct((CHIPS, 8, 128), f32),
        compiler_params=params(),
        cost_estimate=cost(4 * KR * PACK, 1e6),
    )(g, o, squares)


RATES = (D ** (-0.5), max(1, 2 * D // S) ** (-0.5), D ** (-0.5), FF ** (-0.5), RATE_VECTOR)


def adam_kernel(place_ref, norm_ref, mine_ref, other_ref, g1_ref, g2_ref, *refs):
    masters, firsts, seconds = refs[0:5], refs[5:10], refs[10:15]
    outs = refs[15:30]
    norm_out, bias_out = refs[30:32]
    core = place_ref[0]
    mine, other = mine_ref[...], other_ref[...]
    g0 = jnp.where(core == 0, mine, other)
    g1 = jnp.where(core == 0, other, mine)
    total = jnp.sum(jnp.sum(norm_ref[...], axis=0)[0:1, 0:1], axis=(0, 1), keepdims=True)
    grad_norm = jnp.sqrt(total)
    norm_out[...] = jnp.broadcast_to(grad_norm, norm_out.shape)
    clip = jnp.minimum(1.0, CLIP_LIMIT / (grad_norm + 1e-06))

    def update(i, at, grad):
        clipped = grad * clip
        master = masters[i][at]
        first = BETA_ONE * firsts[i][at] + (1.0 - BETA_ONE) * clipped
        second = BETA_TWO * seconds[i][at] + (1.0 - BETA_TWO) * clipped * clipped
        first_hat = first / (1.0 - BETA_ONE**STEP)
        second_hat = second / (1.0 - BETA_TWO**STEP)
        decay = 0.0 if i == 4 else DECAY_RATE
        outs[3 * i][at] = master - RATES[i] * (first_hat / (jnp.sqrt(second_hat) + ADAM_EPS) + decay * master)
        outs[3 * i + 1][at] = first
        outs[3 * i + 2][at] = second

    rows = slice(None)
    for c, g in ((0, g0), (1, g1)):
        for p in range(PAIRS):
            for i in range(3):
                col = i * D + c * DC + p * 128
                update(0, (rows, slice(col, col + 128)), g[:, (4 * p + i) * 128 : (4 * p + i + 1) * 128])
            col = c * DC + p * 128
            update(1, (rows, slice(col, col + 128)), g[:, (4 * p + 3) * 128 : (4 * p + 4) * 128])
    update(2, (rows, rows), g1_ref[...])
    update(3, (rows, rows), g2_ref[...])
    vec = (g0 + g1)[:, 4 * DC : 4 * DC + 128]
    vec = jnp.concatenate([vec, jnp.zeros((16 - KR, 128), f32)], axis=0).T[:16, :KR]
    update(4, (rows, rows), vec[: masters[4].shape[0], :])
    bias_out[...] = vec[7:8, :] * clip


def adam_call(place, norm, mine, other, g1, g2, masters, firsts, seconds):
    whole = lambda a: pl.BlockSpec(a.shape, lambda i, c: (0,) * len(a.shape))
    args = [norm, mine, other, g1, g2, *masters, *firsts, *seconds]
    shapes = [jax.ShapeDtypeStruct(m.shape, f32) for m in masters for _ in range(3)]
    shapes += [jax.ShapeDtypeStruct((1, 128), f32), jax.ShapeDtypeStruct((1, KR), f32)]
    return pl.pallas_call(
        adam_kernel,
        grid_spec=pltpu.PrefetchScalarGridSpec(
            num_scalar_prefetch=1,
            grid=(1,),
            in_specs=[whole(a) for a in args],
            out_specs=[whole(a) for a in shapes],
        ),
        out_shape=shapes,
        compiler_params=params(),
        cost_estimate=cost(20 * KR * FF * 3, 3e6),
    )(place, *args)


def local(
    tokens,
    cotangent,
    counts,
    patch_row,
    patch_col,
    w_qkv,
    w_proj,
    w_fc1,
    w_fc2,
    vectors,
    m_qkv,
    v_qkv,
    m_proj,
    v_proj,
    m_fc1,
    v_fc1,
    m_fc2,
    v_fc2,
    m_vectors,
    v_vectors,
):
    core = lax.axis_index("grp")
    chip = lax.axis_index("dp")
    first_core = core == 0
    along = jnp.where(first_core, chip // PLANE, (chip // SIDE) % SIDE)
    vr = vectors.shape[0]

    def swap(a):
        return lax.ppermute(a, "grp", [(0, 1), (1, 0)])

    def halves(a):
        n = a.shape[-1] // 2
        return jnp.where(first_core, a[..., :n], a[..., n:])

    def over_plane(share):
        got = plane_swap(jnp.broadcast_to(share[None], (PLANE,) + share.shape))
        return got.reshape(PLANE * share.shape[0], share.shape[1])

    def along_line(quarter):
        return [quarter] + [shift(quarter, d) for d in range(1, SIDE)]

    def line_sum(whole):
        return lax.psum_scatter(whole, BOTH, scatter_dimension=0, axis_index_groups=lines(), tiled=True)

    fc2_b = w_fc2.astype(bf16)
    full_fc2 = lax.all_gather(jnp.where(first_core, fc2_b[:FR], fc2_b[FR:]), "dp", axis=0, tiled=True)
    qkv_b = w_qkv.astype(bf16)
    parts = [halves(qkv_b[:, i * D : (i + 1) * D]) for i in range(3)]
    by_pair = [parts[i][:, p * 128 : (p + 1) * 128] for p in range(PAIRS) for i in range(3)]
    vec_t = jnp.pad(vectors.astype(bf16).T, ((0, 0), (0, 128 - vr)))
    share_qkv = jnp.concatenate(by_pair + [vec_t], axis=1)
    fc1_b = w_fc1.astype(bf16).reshape(KR, CHIPS, CORES, FR)
    share_fc1 = jnp.where(first_core, fc1_b[:, :, 0], fc1_b[:, :, 1]).reshape(KR, FC)
    share = jnp.concatenate([share_fc1, w_proj.astype(bf16)], axis=1)

    x_own = tokens.reshape(S, D)
    cot_own = cotangent.reshape(S, D)
    x_other, cot_other = swap(x_own), swap(cot_own)
    ints = jnp.concatenate(
        [
            patch_row.reshape(1, S),
            patch_col.reshape(1, S),
            jnp.pad(counts.reshape(1, 2), ((0, 0), (0, S - 2))),
            jnp.zeros((5, S), jnp.int32),
        ]
    )
    ints = jnp.stack([ints, swap(ints)])
    counts0 = jnp.where(first_core, ints[0, 2, :2], ints[1, 2, :2])
    counts1 = jnp.where(first_core, ints[1, 2, :1], ints[0, 2, :1])
    place = jnp.concatenate([jnp.stack([core, along]).astype(jnp.int32), counts0, counts1])

    n1, gy, pos = early_call(place, x_own, x_other, cot_own, cot_other, ints)

    quarter = over_plane(share_qkv)
    quarter, n1, gy, share = lax.optimization_barrier((quarter, n1, gy, share))
    qkv_pieces = along_line(quarter)
    quarter = over_plane(share)

    vec, h1t, cosine, sine, q, k, v, b1 = qkv_call(place, n1, pos, qkv_pieces)
    q, quarter = lax.optimization_barrier((q, quarter))
    pieces = along_line(quarter)
    mine, p0, p1 = attn_fwd_call(place, q, k, v)
    mine, pieces[1], pieces[3] = lax.optimization_barrier((mine, pieces[1], pieces[3]))
    other = swap(mine)
    after, h2 = proj_call(place, mine, other, x_own, x_other, pieces, vec)
    mlp, mlp_part, gh2, act, gup, gb1 = mlp_call(place, h2, gy, pieces, full_fc2, b1)
    other_gh2 = swap(gh2)
    mlp_other = swap(mlp_part)

    gw1, gw2 = fc_grad_call(place, h2, gup, act, gy)
    sum_fc1 = line_sum(gw1)
    ga, gab, sums_mid = mid_call(place, after, gy, gh2, other_gh2, vec)
    gw2, gab = lax.optimization_barrier((gw2, gab))
    sum_fc2 = line_sum(gw2)
    back = functools.partial(
        attn_bwd_call, place=place, q=q, k=k, v=v, mine=mine, other=other, p0=p0, p1=p1,
        cosine=cosine, sine=sine, pos=pos, h1t=h1t, proj_pieces=pieces,
    )
    *gw_a, gqkv_a, sums_a = back(0, 2, ga=gab)
    gab, gqkv_a = lax.optimization_barrier((gab, gqkv_a))
    parts_a = [gw_a[0]] + [shift(gw_a[d], d) for d in range(1, SIDE)]
    *gw_b, gqkv_b, sums_b = back(2, 1, ga=gab)
    parts_b = [gw_b[0]] + [shift(gw_b[d], d) for d in range(1, SIDE)]
    gqkv_b, *parts_a = lax.optimization_barrier((gqkv_b, *parts_a))
    gh1, gh1_part, *gv = gh_call(place, gqkv_a, gqkv_b, n1, sums_mid, sums_a, sums_b, gb1, qkv_pieces)
    got_fc1 = plane_swap(sum_fc1.reshape(PLANE, KR, FC))
    gv, parts_b, got_fc1 = lax.optimization_barrier((gv, parts_b, got_fc1))
    parts_v = [gv[0]] + [shift(gv[d], d) for d in range(1, SIDE)]
    gh1_other = swap(gh1_part)

    got_fc2 = plane_swap(sum_fc2.reshape(PLANE, FR, D))
    parts_v, got_fc2 = lax.optimization_barrier((parts_v, got_fc2))
    g_fc1, g_fc2 = sum_call(got_fc1), sum_call(got_fc2)
    g1, g2, squares = fc_call(place, g_fc1, swap(g_fc1), g_fc2, swap(g_fc2))
    got = plane_swap(pack_call(parts_a, parts_b, parts_v))
    got, g1, g2, squares = lax.optimization_barrier((got, g1, g2, squares))
    grads = sum_call(got)

    grads_other = swap(grads)
    squares = norm_call(grads, grads_other, squares)
    squares, gh1 = lax.optimization_barrier((squares, gh1))
    norms = lax.all_to_all(squares, "dp", 0, 0)
    gt, mixed = last_call(x_own, ga, gh1, gh1_other, after, mlp, mlp_other, vec)
    norms, gt, mixed = lax.optimization_barrier((norms, gt, mixed))
    *updates, grad_norm, bias_proj_grad = adam_call(
        place,
        norms,
        grads,
        grads_other,
        g1,
        g2,
        (w_qkv, w_proj, w_fc1, w_fc2, vectors),
        (m_qkv, m_proj, m_fc1, m_fc2, m_vectors),
        (v_qkv, v_proj, v_fc1, v_fc2, v_vectors),
    )
    return (
        mixed.reshape(1, 1, S, D),
        gt.reshape(1, 1, S, D),
        grad_norm[0, 0],
        *updates,
        bias_proj_grad.reshape(KR),
    )


def solution(mesh):
    frame = P("grp", "dp", None, None)
    ints = P("grp", "dp", None)
    rows = P("dp", None)
    cols = P(None, "dp")
    return jax.shard_map(
        local,
        mesh=mesh,
        in_specs=(frame, frame, ints, ints, ints, rows, rows, rows, rows, cols) + (rows,) * 8 + (cols,) * 2,
        out_specs=(frame, frame, P()) + (rows,) * 12 + (cols,) * 3 + (P("dp"),),
        check_vma=False,
    )
```

```python
import jax
import jax.numpy as jnp
from jax import lax
from jax.experimental import pallas as pl
from jax.experimental.pallas import tpu as pltpu
from jax.sharding import PartitionSpec as P

D = 768
H = 12
HD = 64
FF = 3072
STEP = 10
A = 196
S = 576

CORES = 2
HC = H // CORES
DC = D // CORES
FC = FF // CORES
PAIRS = HC // 2
T = CORES * S

WIN = 208
WINDOWS = (0, 192)

EPS_NORM = 1e-06
BETA_ONE = 0.9
BETA_TWO = 0.95
ADAM_EPS = 1e-08
DECAY_RATE = 0.05
RATE_VECTOR = 0.8
CLIP_LIMIT = 1.0
NEG = -1e30

bf16 = jnp.bfloat16
f32 = jnp.float32
VMEM_LIMIT = 56 * 1024 * 1024


SIDE = 4
CHIPS = SIDE**3
PLANE = SIDE * SIDE
KR = D // CHIPS
FR = FC // CHIPS
BLOCK = SIDE * KR
QUARTER = PLANE * KR
BOTH = ("grp", "dp")


def device(core, x, y, z):
    return ((core * SIDE + x) * SIDE + y) * SIDE + z


def lines():
    r = range(SIDE)
    return [[device(0, a, g, z) for a in r] for g in r for z in r] + [
        [device(1, g, a, z) for a in r] for g in r for z in r
    ]


def planes():
    r = range(SIDE)
    return [[device(0, a, g, z) for g in r for z in r] for a in r] + [
        [device(1, g, a, z) for g in r for z in r] for a in r
    ]


def shift(value, d):
    pairs = [(group[i], group[(i + d) % SIDE]) for group in lines() for i in range(SIDE)]
    return lax.ppermute(value, BOTH, pairs)


def plane_swap(value):
    return lax.all_to_all(value, BOTH, 0, 0, axis_index_groups=planes())


def natural(core, a, g):
    return jnp.where(core == 0, SIDE * a + g, SIDE * g + a)


def lay_out(place_ref, pieces, full_ref):
    core, me = place_ref[0], place_ref[1]
    for d, piece in enumerate(pieces):
        a = (me + SIDE - d) & (SIDE - 1)
        for g in range(SIDE):
            at = pl.multiple_of(natural(core, a, g) * BLOCK, BLOCK)
            full_ref[pl.ds(at, BLOCK), :] = piece[g * BLOCK : (g + 1) * BLOCK, :]


def usable_rows(place_ref, group, rows, base=0):
    slot = lax.broadcasted_iota(jnp.int32, (rows, 1), 0) + base
    first = ((slot < A) & (slot < place_ref[2])) | ((slot >= A) & (slot < 2 * A) & (slot - A < place_ref[3]))
    first = first.astype(f32)
    second = (slot < place_ref[4]).astype(f32)
    if isinstance(group, int):
        return second if group else first
    return jnp.where(group == 0, first, second)


def own_rows(win):
    row = lax.broadcasted_iota(jnp.int32, (WIN, 1), 0) + (WINDOWS[win] - win * A)
    return ((row >= 0) & (row < A)).astype(f32)


def key_bias(place_ref, win=None):
    if win is None:
        key = lax.broadcasted_iota(jnp.int32, (1, S), 1)
        return jnp.where(key < place_ref[4], 0.0, NEG)
    key = lax.broadcasted_iota(jnp.int32, (1, WIN), 1) + (WINDOWS[win] - win * A)
    return jnp.where((key >= 0) & (key < place_ref[2 + win]), 0.0, NEG)


def exact_dot(a, b):
    high = a.astype(bf16)
    rest = a - high.astype(f32)
    mid = rest.astype(bf16)
    low = (rest - mid.astype(f32)).astype(bf16)
    b = b.astype(bf16)
    return dot(high, b) + dot(mid, b) + dot(low, b)


def spots(core, shape, full, part):
    l = lax.broadcasted_iota(jnp.int32, shape, full)
    m = lax.broadcasted_iota(jnp.int32, shape, part)
    q = (m * 2731) >> 16
    return l == m + FR * (q + core)


def spots_t(core):
    return spots(core, (DC, D), 1, 0)


def params(**kw):
    return pltpu.CompilerParams(vmem_limit_bytes=VMEM_LIMIT, **kw)


def cost(flops, bytes_accessed, transcendentals=0):
    return pl.CostEstimate(
        flops=int(flops), bytes_accessed=int(bytes_accessed), transcendentals=int(transcendentals)
    )


def dot(a, b):
    return jnp.dot(a, b, preferred_element_type=f32)


def dot_t(a, b):
    return lax.dot_general(a, b, (((1,), (1,)), ((), ())), preferred_element_type=f32)


def t_dot(a, b):
    return lax.dot_general(a, b, (((0,), (0,)), ((), ())), preferred_element_type=f32)


def stats(z):
    mean_val = jnp.mean(z, axis=-1, keepdims=True)
    centred = z - mean_val
    variance = jnp.mean(centred * centred, axis=-1, keepdims=True)
    inv_std = lax.rsqrt(variance + EPS_NORM)
    return centred * inv_std, inv_std


def norm_back(grad, normed, inv_std, gain):
    e = grad * gain
    return inv_std * (
        e
        - jnp.mean(e, axis=-1, keepdims=True)
        - normed * jnp.mean(e * normed, axis=-1, keepdims=True)
    )


def swap_halves(u):
    lanes = u.shape[1]
    lane = lax.broadcasted_iota(jnp.int32, u.shape, 1)
    up = pltpu.roll(u, lanes - HD // 2, 1)
    down = pltpu.roll(u, HD // 2, 1)
    return jnp.where((lane & (HD - 1)) < HD // 2, up, down)


TURN = 1.5707963267948966


def sin_cos(a):
    k = jnp.floor(a * (1.0 / TURN) + 0.5)
    r = ((a - k * 1.5703125) - k * 4.837512969970703125e-4) - k * 7.54978995489188216e-8
    z = r * r
    s = ((-1.9515295891e-4 * z + 8.3321608736e-3) * z - 1.6666654611e-1) * z * r + r
    c = ((2.443315711809948e-5 * z - 1.388731625493765e-3) * z + 4.166664568298827e-2) * z * z - 0.5 * z + 1.0
    quarter = k.astype(jnp.int32)
    odd = (quarter & 1) == 1
    sine = jnp.where(odd, c, s)
    cosine = jnp.where(odd, s, c)
    sine = jnp.where((quarter & 2) == 0, sine, -sine)
    cosine = jnp.where(((quarter + 1) & 2) == 0, cosine, -cosine)
    return sine, cosine


def share_kernel(place_ref, w_ref, v_ref, out_ref):
    core = place_ref[0]
    w = w_ref[...].astype(bf16)
    cols = []
    for p in range(PAIRS):
        for i in range(3):
            at = i * D + p * 128
            cols.append(jnp.where(core == 0, w[:, at : at + 128], w[:, at + DC : at + DC + 128]))
    v = jnp.concatenate([v_ref[...], jnp.zeros((128 - v_ref.shape[0], KR), f32)], axis=0)
    v = jnp.concatenate([v, jnp.zeros((128, 128 - KR), f32)], axis=1)
    cols.append(v.T[:KR, :].astype(bf16))
    share = jnp.concatenate(cols, axis=1)
    for n in range(PLANE):
        out_ref[n] = share


def share_call(place, w, vectors):
    whole = lambda a: pl.BlockSpec(a.shape, lambda i, c: (0, 0))
    return pl.pallas_call(
        share_kernel,
        grid_spec=pltpu.PrefetchScalarGridSpec(
            num_scalar_prefetch=1,
            grid=(1,),
            in_specs=[whole(w), whole(vectors)],
            out_specs=pl.BlockSpec((PLANE, KR, 3 * DC + 128), lambda i, c: (0, 0, 0)),
        ),
        out_shape=jax.ShapeDtypeStruct((PLANE, KR, 3 * DC + 128), bf16),
        compiler_params=params(),
        cost_estimate=cost(KR * D * 3, 1e6),
    )(place, w, vectors)


def gy_kernel(place_ref, c_ref, co_ref, gy_ref):
    i = pl.program_id(0)
    keep = usable_rows(place_ref, i ^ place_ref[0], S)
    gy_ref[...] = (jnp.where(i == 0, c_ref[...], co_ref[...]).astype(f32) * keep).astype(bf16)


def gy_call(place, c, co):
    whole = pl.BlockSpec((S, D), lambda i, c: (0, 0))
    return pl.pallas_call(
        gy_kernel,
        grid_spec=pltpu.PrefetchScalarGridSpec(
            num_scalar_prefetch=1,
            grid=(CORES,),
            in_specs=[whole, whole],
            out_specs=pl.BlockSpec((S, D), lambda i, c: (i, 0)),
        ),
        out_shape=jax.ShapeDtypeStruct((T, D), bf16),
        compiler_params=params(),
        cost_estimate=cost(4 * T * D, T * D * 4),
    )(place, c, co)


def qkv_kernel(
    place_ref, x_ref, xo_ref, ints_ref, w0, w1, w2, w3, v0, v1, v2, v3,
    vec_ref, ht_ref, cos_ref, sin_ref, q_out, k_out, v_out, b1_ref, pos_ref,
    w_s, full_s, rows_s, freq_s,
):
    core = place_ref[0]

    @pl.when(pl.program_id(0) == 0)
    def _():
        lay_out(place_ref, (w0, w1, w2, w3), w_s)
        lay_out(place_ref, (v0, v1, v2, v3), full_s)
        rows_s[...] = full_s[...].astype(f32).T[:16, :]
        vec_ref[...] = rows_s[...]
        late = rows_s[8:16, :].astype(bf16)
        units = dot(late, spots(core, (D, DC), 0, 1).astype(bf16))
        for r in range(FC // DC):
            b1_ref[:, r * DC : (r + 1) * DC] = units[2 + r : 3 + r, :]
        src = lax.broadcasted_iota(jnp.int32, (D, DC), 0)
        dst = lax.broadcasted_iota(jnp.int32, (D, DC), 1)
        want = core * (DC // 2) + (dst // HD) * (HD // 2) + (dst & (HD // 2 - 1))
        freq_s[0:8, :] = dot(late, (src == want).astype(bf16))
        freq_s[8:16, :] = dot(late, (src == want + D // 2).astype(bf16))

    i = pl.program_id(0)
    x = jnp.where(i < pl.num_programs(0) // CORES, x_ref[...], xo_ref[...])
    h = stats(x.astype(f32))[0] * rows_s[0:1, :] + rows_s[1:2, :]
    pos = ints_ref[...].astype(f32).T
    pos_ref[...] = pos
    ht_ref[...] = h.T.astype(bf16)
    acc = dot(h.astype(bf16), w_s[...])
    angle = pos[:, 1:2] * freq_s[1:2, :] + pos[:, 0:1] * freq_s[9:10, :]
    lane = lax.broadcasted_iota(jnp.int32, (1, DC), 1)
    sign = jnp.where((lane & (HD - 1)) < HD // 2, -1.0, 1.0)
    small = jnp.max(jnp.abs(angle)) < 8000.0

    @pl.when(small)
    def _():
        sine, cosine = sin_cos(angle)
        cos_ref[...] = cosine
        sin_ref[...] = sine * sign

    @pl.when(jnp.logical_not(small))
    def _():
        cos_ref[...] = jnp.cos(angle)
        sin_ref[...] = jnp.sin(angle) * sign

    cosine, sine = cos_ref[...], sin_ref[...]
    at = pl.ds(pl.multiple_of(core * DC, DC), DC)
    part = lambda i: jnp.concatenate([acc[:, (3 * p + i) * 128 : (3 * p + i + 1) * 128] for p in range(PAIRS)], axis=1)
    q = part(0) + rows_s[4:5, at]
    k = part(1) + rows_s[5:6, at]
    q_out[...] = ((q * cosine + swap_halves(q) * sine) * HD ** (-0.5)).astype(bf16)
    k_out[...] = (k * cosine + swap_halves(k) * sine).astype(bf16)
    v_out[...] = (part(2) + rows_s[6:7, at]).astype(bf16)


def qkv_call(place, x, xo, ints, pieces):
    rows = S
    tile = lambda n: pl.BlockSpec((rows, n), lambda i, c: (i, 0))
    keep = lambda *n: pl.BlockSpec(n, lambda i, c: (0,) * len(n))
    return pl.pallas_call(
        qkv_kernel,
        grid_spec=pltpu.PrefetchScalarGridSpec(
            num_scalar_prefetch=1,
            grid=(CORES,),
            in_specs=[keep(S, D), keep(S, D), pl.BlockSpec((None, 8, S), lambda i, c: (i, 0, 0))]
            + [keep(QUARTER, 3 * DC)] * 4
            + [pl.BlockSpec((QUARTER, 128), lambda i, c: (0, 3 * DC // 128))] * 4,
            out_specs=[keep(16, D), pl.BlockSpec((None, D, rows), lambda i, c: (i, 0, 0))]
            + [tile(DC)] * 5
            + [keep(1, FC), tile(8)],
            scratch_shapes=[
                pltpu.VMEM((D, 3 * DC), bf16),
                pltpu.VMEM((D, 128), bf16),
                pltpu.VMEM((16, D), f32),
                pltpu.VMEM((16, DC), f32),
            ],
        ),
        out_shape=[
            jax.ShapeDtypeStruct((16, D), f32),
            jax.ShapeDtypeStruct((CORES, D, S), bf16),
            jax.ShapeDtypeStruct((T, DC), f32),
            jax.ShapeDtypeStruct((T, DC), f32),
            *[jax.ShapeDtypeStruct((T, DC), bf16)] * 3,
            jax.ShapeDtypeStruct((1, FC), f32),
            jax.ShapeDtypeStruct((T, 8), f32),
        ],
        compiler_params=params(),
        cost_estimate=cost(2 * T * D * 3 * DC + 60 * T * DC, T * D * 6 + D * 3 * DC * 2 + T * DC * 14),
    )(place, x, xo, ints, *pieces, *pieces)


def softmax_head(q, k, v, mine, bias):
    s = dot_t(jnp.where(mine, q, jnp.zeros_like(q)), k) + bias
    e = jnp.exp(s - jnp.max(s, axis=-1, keepdims=True))
    p = e * (1.0 / jnp.sum(e, axis=-1, keepdims=True))
    return p


def attn_fwd_kernel(
    place_ref, q0, k0, v0, q1, k1, v1, o_ref, p0_ref, p1_ref
):
    lane = lax.broadcasted_iota(jnp.int32, (1, 2 * HD), 1)
    low = lane < HD
    q, k, v = q1[0], k1[0], v1[0]
    mixes = []
    bias = key_bias(place_ref)
    for head, mine in ((0, low), (1, ~low)):
        p = softmax_head(q, k, v, mine, bias).astype(bf16)
        p1_ref[head] = p
        mixes.append(dot(p, v))
    mix = jnp.where(low, mixes[0], mixes[1])
    o_ref[1] = jnp.where(usable_rows(place_ref, 1, S) > 0, mix, v.astype(f32)).astype(bf16)
    o_ref[0] = v0[0]
    for win, base in enumerate(WINDOWS):
        q, k, v = (r[0, base : base + WIN, :] for r in (q0, k0, v0))
        own = own_rows(win)
        bias = key_bias(place_ref, win)
        mixes = []
        for head, mine in ((0, low), (1, ~low)):
            p = softmax_head(q, k, v, mine, bias)
            p = (p * own).astype(bf16)
            p0_ref[head, win] = p
            mixes.append(dot(p, v))
        mix = jnp.where(low, mixes[0], mixes[1])
        use = (own * usable_rows(place_ref, 0, WIN, base)) > 0
        before = o_ref[0, base : base + WIN, :].astype(f32)
        o_ref[0, base : base + WIN, :] = jnp.where(use, mix, before).astype(bf16)


def attn_fwd_call(place, q, k, v):
    block = lambda g: pl.BlockSpec((1, S, 2 * HD), lambda p, c: (g ^ c[0], 0, p))
    q, k, v = (a.reshape(CORES, S, DC) for a in (q, k, v))
    return pl.pallas_call(
        attn_fwd_kernel,
        grid_spec=pltpu.PrefetchScalarGridSpec(
            num_scalar_prefetch=1,
            grid=(PAIRS,),
            in_specs=[block(0)] * 3 + [block(1)] * 3,
            out_specs=[
                pl.BlockSpec((CORES, S, 2 * HD), lambda p, c: (0, 0, p)),
                pl.BlockSpec((2, 2, WIN, WIN), lambda p, c: (p, 0, 0, 0)),
                pl.BlockSpec((2, S, S), lambda p, c: (p, 0, 0)),
            ],
        ),
        out_shape=[
            jax.ShapeDtypeStruct((CORES, S, DC), bf16),
            jax.ShapeDtypeStruct((HC, 2, WIN, WIN), bf16),
            jax.ShapeDtypeStruct((HC, S, S), bf16),
        ],
        compiler_params=params(),
        cost_estimate=cost(4 * HC * (S * S + 2 * WIN * WIN) * 128, 12e6, HC * S * S),
    )(place, q, k, v, q, k, v)


def proj_kernel(place_ref, mine_ref, other_ref, x_ref, xo_ref, w0, w1, w2, w3, v_ref, after_ref, n2_ref, r2_ref, h2_ref, w_s):
    @pl.when(pl.program_id(0) == 0)
    def _():
        lay_out(place_ref, (w0, w1, w2, w3), w_s)

    core = place_ref[0]
    at = lambda c: pl.ds(pl.multiple_of(c * DC, DC), DC)
    branch = dot(mine_ref[0], w_s[at(core), :]) + dot(other_ref[0], w_s[at(1 - core), :])
    x = jnp.where(pl.program_id(0) < pl.num_programs(0) // CORES, x_ref[...], xo_ref[...])
    after = x.astype(f32) + (branch + v_ref[7:8, :])
    normed, inv_std = stats(after)
    n2_ref[...] = normed
    r2_ref[...] = jnp.broadcast_to(inv_std, r2_ref.shape)

    @pl.when(pl.program_id(0) < pl.num_programs(0) // CORES)
    def _():
        after_ref[...] = after

    h2_ref[...] = (normed * v_ref[2:3, :] + v_ref[3:4, :]).astype(bf16)


def proj_call(place, mine, other, x, xo, pieces, vec):
    rows = 288
    half = S // rows
    tile = lambda n: pl.BlockSpec((rows, n), lambda i, c: (i, 0))
    whole = lambda a: pl.BlockSpec(a.shape, lambda i, c: (0,) * a.ndim)
    return pl.pallas_call(
        proj_kernel,
        grid_spec=pltpu.PrefetchScalarGridSpec(
            num_scalar_prefetch=1,
            grid=(T // rows,),
            in_specs=[
                pl.BlockSpec((1, rows, DC), lambda i, c: ((i // half) ^ c[0], i % half, 0)),
                pl.BlockSpec((1, rows, DC), lambda i, c: ((i // half) ^ c[0], i % half, 0)),
                pl.BlockSpec((rows, D), lambda i, c: (jnp.minimum(i, half - 1), 0)),
                pl.BlockSpec((rows, D), lambda i, c: (jnp.maximum(i - half, 0), 0)),
            ]
            + [pl.BlockSpec((QUARTER, D), lambda i, c: (0, FC // D))] * 4
            + [whole(vec)],
            out_specs=[pl.BlockSpec((rows, D), lambda i, c: (jnp.minimum(i, half - 1), 0)), tile(D), tile(8), tile(D)],
            scratch_shapes=[pltpu.VMEM((D, D), bf16)],
        ),
        out_shape=[
            jax.ShapeDtypeStruct((S, D), f32),
            jax.ShapeDtypeStruct((T, D), f32),
            jax.ShapeDtypeStruct((T, 8), f32),
            jax.ShapeDtypeStruct((T, D), bf16),
        ],
        compiler_params=params(),
        cost_estimate=cost(2 * T * D * D, T * D * 10 + D * D * 2),
    )(place, mine, other, x, xo, *pieces, vec)


PACK = 4 * DC + 128
K0 = (2.0 / 3.141592653589793) ** 0.5
FT = 768


def gelu_slope(u):
    sq = u * u
    th = jnp.tanh(u * (K0 + (K0 * 0.044715) * sq))
    half = 0.5 + 0.5 * th
    return u * half, half + (u * (half - half * half)) * (2 * K0 + (6 * K0 * 0.044715) * sq)


def mlp_kernel(
    place_ref, h2_ref, gy_ref, w10, w11, w12, w13, w2_ref, b1_ref, mlp_ref, mlpo_ref, gh2b_ref, act_ref, gup_ref, gb1_ref, w1_s
):
    i = pl.program_id(0)

    @pl.when(i == 0)
    def _():
        lay_out(place_ref, (w10, w11, w12, w13), w1_s)
        gb1_ref[...] = jnp.zeros_like(gb1_ref)

    for f in range(FC // FT):
        c = slice(f * FT, (f + 1) * FT)
        act, slope = gelu_slope(dot(h2_ref[...], w1_s[:, c]) + b1_ref[:, c])
        act_ref[:, c] = act.astype(bf16)
        gup = (dot_t(gy_ref[...], w2_ref[c, :]) * slope).astype(bf16)
        gup_ref[:, c] = gup
        gb1_ref[:, c] += jnp.sum(gup.astype(f32), axis=0, keepdims=True)
    gh2b_ref[...] = dot_t(gup_ref[...], w1_s[...]).astype(bf16)
    mlp = dot(act_ref[...], w2_ref[...])
    half = pl.num_programs(0) // CORES

    @pl.when(i < half)
    def _():
        mlp_ref[...] = mlp

    @pl.when(i >= half)
    def _():
        mlpo_ref[...] = mlp


def mlp_call(place, h2, gy, pieces, w2, b1):
    rows = 288
    half = S // rows
    tile = lambda n: pl.BlockSpec((rows, n), lambda i, c: (i, 0))
    whole = lambda a: pl.BlockSpec(a.shape, lambda i, c: (0,) * a.ndim)
    return pl.pallas_call(
        mlp_kernel,
        grid_spec=pltpu.PrefetchScalarGridSpec(
            num_scalar_prefetch=1,
            grid=(T // rows,),
            in_specs=[tile(D), tile(D)]
            + [pl.BlockSpec((QUARTER, FC), lambda i, c: (0, 0))] * 4
            + [whole(w2), whole(b1)],
            out_specs=[
                pl.BlockSpec((rows, D), lambda i, c: (jnp.minimum(i, half - 1), 0)),
                pl.BlockSpec((rows, D), lambda i, c: (jnp.maximum(i - half, 0), 0)),
                tile(D),
                tile(FC),
                tile(FC),
                pl.BlockSpec((1, FC), lambda i, c: (0, 0)),
            ],
            scratch_shapes=[pltpu.VMEM((D, FC), bf16)],
        ),
        out_shape=[
            jax.ShapeDtypeStruct((S, D), f32),
            jax.ShapeDtypeStruct((S, D), f32),
            jax.ShapeDtypeStruct((T, D), bf16),
            jax.ShapeDtypeStruct((T, FC), bf16),
            jax.ShapeDtypeStruct((T, FC), bf16),
            jax.ShapeDtypeStruct((1, FC), f32),
        ],
        compiler_params=params(),
        cost_estimate=cost(8 * T * D * FC, 30e6, T * FC),
    )(place, h2, gy, *pieces, w2, b1)


def by_line(place_ref, value, block, out_ref):
    core = place_ref[0]
    for n in range(PLANE):
        to = jnp.where(core == 0, n, (n % SIDE) * SIDE + n // SIDE)
        out_ref[pl.ds(pl.multiple_of(to * block, block), block), :] = value[n * block : (n + 1) * block, :].astype(bf16)


def fc_grad_kernel(place_ref, h2_ref, gup_ref, act_ref, gy_ref, gw1_ref, gw2_ref):
    by_line(place_ref, t_dot(act_ref[...], gy_ref[...]), SIDE * FR, gw2_ref)
    by_line(place_ref, t_dot(h2_ref[...], gup_ref[...]), BLOCK, gw1_ref)


def fc_grad_call(place, h2, gup, act, gy):
    whole = lambda a: pl.BlockSpec(a.shape, lambda i, c: (0, 0))
    return pl.pallas_call(
        fc_grad_kernel,
        grid_spec=pltpu.PrefetchScalarGridSpec(
            num_scalar_prefetch=1,
            grid=(2,),
            in_specs=[
                whole(h2),
                pl.BlockSpec((T, FC // 2), lambda i, c: (0, i)),
                whole(act),
                pl.BlockSpec((T, DC), lambda i, c: (0, i)),
            ],
            out_specs=[
                pl.BlockSpec((D, FC // 2), lambda i, c: (0, i)),
                pl.BlockSpec((FC, DC), lambda i, c: (0, i)),
            ],
        ),
        out_shape=[jax.ShapeDtypeStruct((D, FC), bf16), jax.ShapeDtypeStruct((FC, D), bf16)],
        compiler_params=params(),
        cost_estimate=cost(4 * T * D * FC, T * (D + FC) * 4 + D * FC * 4),
    )(place, h2, gup, act, gy)


def mid_kernel(place_ref, n2_ref, r2_ref, gy_ref, gh2_ref, other_ref, v_ref, ga_ref, gab_ref, sums_ref):
    i = pl.program_id(0)
    normed, inv_std = n2_ref[...], r2_ref[:, 0:1]
    gh2 = gh2_ref[...].astype(f32) + other_ref[...].astype(f32)
    gy = gy_ref[...].astype(f32)
    ga = gy + norm_back(gh2, normed, inv_std, v_ref[2:3, :])
    gab = ga.astype(bf16)
    gab_ref[...] = gab

    @pl.when(i == 0)
    def _():
        sums_ref[...] = jnp.zeros_like(sums_ref)

    @pl.when(i < pl.num_programs(0) // CORES)
    def _():
        ga_ref[...] = ga
        sums_ref[0:1, :] += jnp.sum(gh2 * normed, axis=0, keepdims=True)
        sums_ref[1:2, :] += jnp.sum(gh2, axis=0, keepdims=True)
        sums_ref[2:3, :] += jnp.sum(gab.astype(f32), axis=0, keepdims=True)
        sums_ref[3:4, :] += jnp.sum(gy, axis=0, keepdims=True)


def mid_call(place, n2, r2, gy, gh2, other, vec):
    rows = 288
    half = S // rows
    tile = lambda n: pl.BlockSpec((rows, n), lambda i, c: (i, 0))
    flipped = pl.BlockSpec((rows, D), lambda i, c: ((i + half) % (2 * half), 0))
    whole = lambda a: pl.BlockSpec(a.shape, lambda i, c: (0,) * a.ndim)
    return pl.pallas_call(
        mid_kernel,
        grid_spec=pltpu.PrefetchScalarGridSpec(
            num_scalar_prefetch=1,
            grid=(T // rows,),
            in_specs=[tile(D), tile(8), tile(D), tile(D), flipped, whole(vec)],
            out_specs=[
                pl.BlockSpec((rows, D), lambda i, c: (jnp.minimum(i, half - 1), 0)),
                tile(D),
                pl.BlockSpec((8, D), lambda i, c: (0, 0)),
            ],
        ),
        out_shape=[
            jax.ShapeDtypeStruct((S, D), f32),
            jax.ShapeDtypeStruct((T, D), bf16),
            jax.ShapeDtypeStruct((8, D), f32),
        ],
        compiler_params=params(),
        cost_estimate=cost(30 * T * D, T * D * 14),
    )(place, n2, r2, gy, gh2, other, vec)


def back_head(q_t, k, v, do, do_t, delta, p, mine, head):
    gp = dot_t(jnp.where(mine, do, jnp.zeros_like(do)), v)
    gs = (p.astype(f32) * (gp - delta)).astype(bf16)
    at = slice(head * HD, (head + 1) * HD)
    return dot(gs, k), dot(q_t[at, :], gs), dot(do_t[at, :], p)


def deltas(do, o, low):
    prod = do.astype(f32) * o.astype(f32)
    d0 = jnp.sum(jnp.where(low, prod, 0.0), axis=-1, keepdims=True)
    d1 = jnp.sum(jnp.where(low, 0.0, prod), axis=-1, keepdims=True)
    return d0, d1


def attn_bwd_kernel(
    place_ref,
    q0, k0, v0, o0, p0, cos0, sin0, pos0,
    q1, k1, v1, o1, p1, cos1, sin1, pos1,
    h1t_ref, ga_ref, cols_ref, mine_ref, other_ref, y0, y1, y2, y3, w0, w1, w2, w3,
    x_ref, xo_ref, mid_ref, gb1_ref,
    gw0, gw1, gw2, gw3, gh_ref, gho_ref,
    gq_s, gk_s, gv_s, gw_s, y_s, do_s, gqkv_s, att_s, rows_s, full_s, w_s,
):
    lane = lax.broadcasted_iota(jnp.int32, (1, 2 * HD), 1)
    low = lane < HD
    pair = pl.program_id(0)
    core = place_ref[0]

    @pl.when(pair == 0)
    def _():
        lay_out(place_ref, (y0, y1, y2, y3), y_s)

    wy = y_s[pl.ds(pl.multiple_of(core * DC + pair * 2 * HD, 2 * HD), 2 * HD), :]
    for frame in range(CORES):
        do_s[frame] = dot_t(ga_ref[frame], wy).astype(bf16)

    def finish(frame, q, k, cos_ref, sin_ref, pos_ref):
        cosine, sine = cos_ref[0], sin_ref[0]
        gq = gq_s[...] * HD ** (-0.5)
        gk = gk_s[...]
        sq, sk = swap_halves(gq), swap_halves(gk)
        turn = (q.astype(f32) * HD**0.5) * sq + k.astype(f32) * sk
        gq = (gq * cosine - sq * sine).astype(bf16)
        gk = (gk * cosine - sk * sine).astype(bf16)
        gv = gv_s[...].astype(bf16)
        for i, g in enumerate((gq, gk, gv)):
            gqkv_s[frame ^ core, :, pl.ds(pl.multiple_of(pair * 6 * HD + i * 2 * HD, 2 * HD), 2 * HD)] = g
        pos = pos_ref[0]
        col = jnp.sum(turn * pos[:, 1:2], axis=0, keepdims=True)
        row = jnp.sum(turn * pos[:, 0:1], axis=0, keepdims=True)
        bias = [jnp.sum(g.astype(f32), axis=0, keepdims=True) for g in (gq, gk, gv)]
        return jnp.concatenate([col, row] + bias, axis=0)

    q, k, v, do = q1[0], k1[0], v1[0], do_s[1 ^ core]
    d = deltas(do, o1[0], low)
    q_t, do_t = q.astype(f32).T.astype(bf16), do.astype(f32).T.astype(bf16)
    out = [
        back_head(q_t, k, v, do, do_t, d[head], p1[head], mine, head)
        for head, mine in ((0, low), (1, ~low))
    ]
    gq_s[...] = jnp.where(low, out[0][0], out[1][0])
    gk_s[...] = jnp.concatenate([out[0][1], out[1][1]], axis=0).T
    gv_s[...] = jnp.concatenate([out[0][2], out[1][2]], axis=0).T
    sums1 = finish(1, q, k, cos1, sin1, pos1)
    gq_s[...] = jnp.zeros_like(gq_s)
    gk_s[...] = jnp.zeros_like(gk_s)
    gv_s[...] = jnp.zeros_like(gv_s)
    for win, base in enumerate(WINDOWS):
        at = pl.ds(base, WIN)
        q, k, v, o = (r[0, at, :] for r in (q0, k0, v0, o0))
        do = do_s[core, at, :]
        d = deltas(do, o, low)
        q_t, do_t = q.astype(f32).T.astype(bf16), do.astype(f32).T.astype(bf16)
        out = [
            back_head(q_t, k, v, do, do_t, d[head], p0[head, win], mine, head)
            for head, mine in ((0, low), (1, ~low))
        ]
        gq_s[at, :] += jnp.where(low, out[0][0], out[1][0])
        gk_s[at, :] += jnp.concatenate([out[0][1], out[1][1]], axis=0).T
        gv_s[at, :] += jnp.concatenate([out[0][2], out[1][2]], axis=0).T
    sums0 = finish(0, q0[0], k0[0], cos0, sin0, pos0)
    att_s[pair, 0:5, :] = sums0 + sums1

    gw = jnp.zeros((D, 6 * HD), f32)
    gw_mine = jnp.zeros((2 * HD, DC), f32)
    gw_other = jnp.zeros((2 * HD, DC), f32)
    for frame in range(CORES):
        cols = cols_ref[frame].astype(f32).T.astype(bf16)
        gw_mine += dot(cols, mine_ref[frame ^ core])
        gw_other += dot(cols, other_ref[frame ^ core])
        gw += dot(h1t_ref[frame], gqkv_s[frame, :, pl.ds(pl.multiple_of(pair * 6 * HD, 6 * HD), 6 * HD)])
    gw_s[:, : 6 * HD] = gw.astype(bf16)
    at = lambda c: pl.ds(pl.multiple_of(c * DC, DC), DC)
    gw_s[at(core), 6 * HD :] = gw_mine.T.astype(bf16)
    gw_s[at(1 - core), 6 * HD :] = gw_other.T.astype(bf16)
    to_chips(place_ref, gw_s, (gw0, gw1, gw2, gw3), pl.ds(pl.multiple_of(pair * 8 * HD, 8 * HD), 8 * HD))

    @pl.when(pair == PAIRS - 1)
    def _():
        lay_out(place_ref, (w0, w1, w2, w3), w_s)
        rows_s[...] = jnp.zeros_like(rows_s)
        for frame, x, out in ((0, x_ref, gh_ref), (1, xo_ref, gho_ref)):
            for half in range(2):
                at = slice(half * (S // 2), (half + 1) * (S // 2))
                gh = dot_t(gqkv_s[frame, at, :], w_s[...])
                out[at, :] = gh
                normed, _ = stats(x[at, :].astype(f32))
                rows_s[0:1, :] += jnp.sum(gh * normed, axis=0, keepdims=True)
                rows_s[1:2, :] += jnp.sum(gh, axis=0, keepdims=True)
        rows_s[2:4, :] = mid_ref[0:2, :]
        rows_s[7:9, :] = mid_ref[2:4, :]
        att = jnp.concatenate([att_s[p] for p in range(PAIRS)], axis=1)
        rows_s[4:7, pl.ds(pl.multiple_of(core * DC, DC), DC)] = att[2:5, :]
        src = lax.broadcasted_iota(jnp.int32, (DC, D), 0)
        dst = lax.broadcasted_iota(jnp.int32, (DC, D), 1)
        want = core * (DC // 2) + (src // HD) * (HD // 2) + (src & (HD // 2 - 1))
        side = lax.broadcasted_iota(jnp.int32, (1, DC), 1)
        turn = jnp.where((side & (HD - 1)) < HD // 2, att, -att)
        rows_s[9:10, :] = exact_dot(turn, dst == want)[0:1, :] + exact_dot(turn, dst == want + D // 2)[1:2, :]
        gb1 = jnp.concatenate([gb1_ref[:, r * DC : (r + 1) * DC] for r in range(FC // DC)] * 2, axis=0)
        rows_s[10:14, :] = exact_dot(gb1, spots_t(core))[:4, :]
        full_s[...] = rows_s[...].T.astype(bf16)
        to_chips(place_ref, full_s, (gw0, gw1, gw2, gw3), slice(4 * DC, PACK))


def to_chips(place_ref, full_ref, outs, cols):
    for d, out in enumerate(outs):
        a = (place_ref[1] + d) & (SIDE - 1)
        for g in range(SIDE):
            at = pl.multiple_of(natural(place_ref[0], a, g) * BLOCK, BLOCK)
            out[g * BLOCK : (g + 1) * BLOCK, cols] = full_ref[pl.ds(at, BLOCK), :]


def attn_bwd_call(
    place, q, k, v, ga, mine, other, p0, p1, cosine, sine, pos, h1t, pieces, proj_pieces, x, xo, mid, gb1
):
    q, k, v, cosine, sine, pos, ga = (a.reshape(CORES, S, -1) for a in (q, k, v, cosine, sine, pos, ga))
    block = lambda g: pl.BlockSpec((1, S, 2 * HD), lambda p, c: (g ^ c[0], 0, p))
    own = lambda g: pl.BlockSpec((1, S, 2 * HD), lambda p, c: (g, 0, p))
    at = lambda g: pl.BlockSpec((1, S, 8), lambda p, c: (g ^ c[0], 0, 0))
    whole = lambda a: pl.BlockSpec(a.shape, lambda p, c: (0,) * a.ndim)
    keep = lambda *n: pl.BlockSpec(n, lambda p, c: (0,) * len(n))
    return pl.pallas_call(
        attn_bwd_kernel,
        grid_spec=pltpu.PrefetchScalarGridSpec(
            num_scalar_prefetch=1,
            grid=(PAIRS,),
            in_specs=[block(0)] * 3
            + [own(0), pl.BlockSpec((2, 2, WIN, WIN), lambda p, c: (p, 0, 0, 0))]
            + [block(0)] * 2
            + [at(0)]
            + [block(1)] * 3
            + [own(1), pl.BlockSpec((2, S, S), lambda p, c: (p, 0, 0))]
            + [block(1)] * 2
            + [at(1)]
            + [whole(h1t), whole(ga)]
            + [pl.BlockSpec((CORES, S, 2 * HD), lambda p, c: (0, 0, PAIRS * c[0] + p))]
            + [whole(mine), whole(other)]
            + [pl.BlockSpec((QUARTER, D), lambda p, c: (0, FC // D))] * 4
            + [keep(QUARTER, 3 * DC)] * 4
            + [whole(a) for a in (x, xo, mid, gb1)],
            out_specs=[keep(QUARTER, PACK)] * 4 + [keep(S, D)] * 2,
            scratch_shapes=[pltpu.VMEM((S, 2 * HD), f32)] * 3
            + [pltpu.VMEM((D, 8 * HD), bf16), pltpu.VMEM((D, D), bf16), pltpu.VMEM((CORES, S, 2 * HD), bf16)]
            + [pltpu.VMEM((CORES, S, 3 * DC), bf16), pltpu.VMEM((PAIRS, 8, 2 * HD), f32)]
            + [pltpu.VMEM((128, D), f32), pltpu.VMEM((D, 128), bf16), pltpu.VMEM((D, 3 * DC), bf16)],
        ),
        out_shape=[
            *[jax.ShapeDtypeStruct((QUARTER, PACK), bf16)] * 4,
            *[jax.ShapeDtypeStruct((S, D), f32)] * 2,
        ],
        compiler_params=params(),
        cost_estimate=cost(10 * HC * S * S * 128 + 4 * T * D * 4 * DC, 36e6),
    )(
        place,
        q, k, v, mine, p0, cosine, sine, pos,
        q, k, v, mine, p1, cosine, sine, pos,
        h1t, ga, ga, mine, other, *proj_pieces, *pieces, x, xo, mid, gb1,
    )


def last_kernel(x_ref, ga_ref, gh_ref, other_ref, after_ref, mlp_ref, mlpo_ref, v_ref, gt_ref, out_ref):
    normed, inv_std = stats(x_ref[...].astype(f32))
    gt_ref[...] = ga_ref[...] + norm_back(gh_ref[...] + other_ref[...], normed, inv_std, v_ref[0:1, :])
    out_ref[...] = (after_ref[...] + (mlp_ref[...] + mlpo_ref[...] + v_ref[8:9, :])).astype(bf16)


def last_call(x, ga, gh, other, after, mlp, mlp_other, vec):
    rows = 288
    tile = lambda n: pl.BlockSpec((rows, n), lambda i: (i, 0))
    return pl.pallas_call(
        last_kernel,
        grid=(S // rows,),
        in_specs=[tile(D)] * 7 + [pl.BlockSpec(vec.shape, lambda i: (0, 0))],
        out_specs=[tile(D), tile(D)],
        out_shape=[jax.ShapeDtypeStruct((S, D), f32), jax.ShapeDtypeStruct((S, D), bf16)],
        compiler_params=params(),
        cost_estimate=cost(30 * S * D, S * D * 28),
    )(x, ga, gh, other, after, mlp, mlp_other, vec)


WIDE = PACK + FC


def pack_kernel(q0, q1, q2, q3, f_ref, out_ref):
    total = q0[...].astype(f32) + q1[...].astype(f32) + q2[...].astype(f32) + q3[...].astype(f32)
    fc1 = f_ref[...].astype(f32)
    for n in range(PLANE):
        at = slice(n * KR, (n + 1) * KR)
        out_ref[n, :, :PACK] = total[at, :].astype(bf16)
        out_ref[n, :, PACK:] = fc1[at, :].astype(bf16)


def pack_call(parts, fc1):
    return pl.pallas_call(
        pack_kernel,
        out_shape=jax.ShapeDtypeStruct((PLANE, KR, WIDE), bf16),
        compiler_params=params(),
        cost_estimate=cost(QUARTER * PACK * 4, QUARTER * PACK * 10),
    )(*parts, fc1)


def sum_kernel(in_ref, out_ref):
    total = in_ref[0].astype(f32)
    for n in range(1, PLANE):
        total += in_ref[n].astype(f32)
    out_ref[...] = total


def sum_call(packed):
    return pl.pallas_call(
        sum_kernel,
        out_shape=jax.ShapeDtypeStruct(packed.shape[1:], f32),
        compiler_params=params(),
        cost_estimate=cost(packed.size, packed.size * 2),
    )(packed)


def fc2_kernel(place_ref, mine_ref, other_ref, out_ref, sq_ref):
    first = place_ref[0] == 0
    a, b = mine_ref[...], other_ref[...]
    out_ref[:FR, :] = jnp.where(first, a, b)
    out_ref[FR:, :] = jnp.where(first, b, a)
    total = jnp.sum(a * a + b * b, axis=(0, 1), keepdims=True)
    sq_ref[...] = jnp.broadcast_to(total, sq_ref.shape)


def fc2_call(place, mine, other):
    whole = lambda a: pl.BlockSpec(a.shape, lambda i, c: (0,) * len(a.shape))
    shapes = [jax.ShapeDtypeStruct(s, f32) for s in ((2 * FR, D), (8, 128))]
    return pl.pallas_call(
        fc2_kernel,
        grid_spec=pltpu.PrefetchScalarGridSpec(
            num_scalar_prefetch=1,
            grid=(1,),
            in_specs=[whole(mine), whole(other)],
            out_specs=[whole(a) for a in shapes],
        ),
        out_shape=shapes,
        compiler_params=params(),
        cost_estimate=cost(6 * FR * D, FR * D * 16),
    )(place, mine, other)


def norm_kernel(g_ref, o_ref, sq_ref, out_ref):
    g, o = g_ref[...], o_ref[...]
    part = jnp.sum(g * g + o * o, axis=(0, 1), keepdims=True)
    cross = g[:, 4 * DC : PACK] * o[:, 4 * DC : PACK]
    part += 2.0 * jnp.sum(cross, axis=(0, 1), keepdims=True)
    out_ref[...] = jnp.broadcast_to((part + sq_ref[0:1, 0:1])[None], out_ref.shape)


def norm_call(g, o, squares):
    return pl.pallas_call(
        norm_kernel,
        out_shape=jax.ShapeDtypeStruct((CHIPS, 8, 128), f32),
        compiler_params=params(),
        cost_estimate=cost(4 * KR * PACK, 1e6),
    )(g, o, squares)


RATES = (D ** (-0.5), max(1, 2 * D // S) ** (-0.5), D ** (-0.5), FF ** (-0.5), RATE_VECTOR)


def adam_kernel(place_ref, norm_ref, mine_ref, other_ref, g2_ref, *refs):
    masters, firsts, seconds = refs[0:5], refs[5:10], refs[10:15]
    outs = refs[15:30]
    norm_out, bias_out = refs[30:32]
    core = place_ref[0]
    mine, other = mine_ref[...], other_ref[...]
    g0 = jnp.where(core == 0, mine, other)
    g1 = jnp.where(core == 0, other, mine)
    total = jnp.sum(jnp.sum(norm_ref[...], axis=0)[0:1, 0:1], axis=(0, 1), keepdims=True)
    grad_norm = jnp.sqrt(total)
    norm_out[...] = jnp.broadcast_to(grad_norm, norm_out.shape)
    clip = jnp.minimum(1.0, CLIP_LIMIT / (grad_norm + 1e-06))

    def update(i, at, grad):
        clipped = grad * clip
        master = masters[i][at]
        first = BETA_ONE * firsts[i][at] + (1.0 - BETA_ONE) * clipped
        second = BETA_TWO * seconds[i][at] + (1.0 - BETA_TWO) * clipped * clipped
        first_hat = first / (1.0 - BETA_ONE**STEP)
        second_hat = second / (1.0 - BETA_TWO**STEP)
        decay = 0.0 if i == 4 else DECAY_RATE
        outs[3 * i][at] = master - RATES[i] * (first_hat / (jnp.sqrt(second_hat) + ADAM_EPS) + decay * master)
        outs[3 * i + 1][at] = first
        outs[3 * i + 2][at] = second

    rows = slice(None)
    for c, g in ((0, g0), (1, g1)):
        for p in range(PAIRS):
            for i in range(3):
                col = i * D + c * DC + p * 128
                update(0, (rows, slice(col, col + 128)), g[:, (4 * p + i) * 128 : (4 * p + i + 1) * 128])
            col = c * DC + p * 128
            update(1, (rows, slice(col, col + 128)), g[:, (4 * p + 3) * 128 : (4 * p + 4) * 128])
    for r in range(FC // DC):
        at = slice(PACK + r * DC, PACK + (r + 1) * DC)
        part = exact_dot(g0[:, at], spots_t(0)) + exact_dot(g1[:, at], spots_t(1))
        update(2, (rows, slice(r * D, (r + 1) * D)), part)
    update(3, (rows, rows), g2_ref[...])
    vec = (g0 + g1)[:, 4 * DC : 4 * DC + 128]
    vec = jnp.concatenate([vec, jnp.zeros((16 - KR, 128), f32)], axis=0).T[:16, :KR]
    update(4, (rows, rows), vec[: masters[4].shape[0], :])
    bias_out[...] = vec[7:8, :] * clip


def adam_call(place, norm, mine, other, g2, masters, firsts, seconds):
    whole = lambda a: pl.BlockSpec(a.shape, lambda i, c: (0,) * len(a.shape))
    args = [norm, mine, other, g2, *masters, *firsts, *seconds]
    shapes = [jax.ShapeDtypeStruct(m.shape, f32) for m in masters for _ in range(3)]
    shapes += [jax.ShapeDtypeStruct((1, 128), f32), jax.ShapeDtypeStruct((1, KR), f32)]
    return pl.pallas_call(
        adam_kernel,
        grid_spec=pltpu.PrefetchScalarGridSpec(
            num_scalar_prefetch=1,
            grid=(1,),
            in_specs=[whole(a) for a in args],
            out_specs=[whole(a) for a in shapes],
        ),
        out_shape=shapes,
        compiler_params=params(),
        cost_estimate=cost(20 * KR * FF * 3, 3e6),
    )(place, *args)


def local(
    tokens,
    cotangent,
    counts,
    patch_row,
    patch_col,
    w_qkv,
    w_proj,
    w_fc1,
    w_fc2,
    vectors,
    m_qkv,
    v_qkv,
    m_proj,
    v_proj,
    m_fc1,
    v_fc1,
    m_fc2,
    v_fc2,
    m_vectors,
    v_vectors,
):
    core = lax.axis_index("grp")
    chip = lax.axis_index("dp")
    first_core = core == 0
    along = jnp.where(first_core, chip // PLANE, (chip // SIDE) % SIDE)
    vr = vectors.shape[0]

    def swap(a):
        return lax.ppermute(a, "grp", [(0, 1), (1, 0)])

    def along_line(quarter):
        return [quarter] + [shift(quarter, d) for d in range(1, SIDE)]

    def line_sum(whole):
        return lax.psum_scatter(whole, BOTH, scatter_dimension=0, axis_index_groups=lines(), tiled=True)

    fc2_b = w_fc2.astype(bf16)
    share_fc2 = jnp.where(first_core, fc2_b[:FR], fc2_b[FR:])
    me = jnp.stack([core, along]).astype(jnp.int32)
    shares = share_call(me, w_qkv, vectors)
    shares, share_fc2 = lax.optimization_barrier((shares, share_fc2))
    full_fc2 = lax.all_gather(share_fc2, "dp", axis=0, tiled=True)
    quarter = plane_swap(shares).reshape(QUARTER, 3 * DC + 128)
    qkv_pieces = along_line(quarter)
    fc1_b = w_fc1.astype(bf16).reshape(KR, CHIPS, CORES, FR)
    share_fc1 = jnp.where(first_core, fc1_b[:, :, 0], fc1_b[:, :, 1]).reshape(KR, FC)
    share = jnp.concatenate([share_fc1, w_proj.astype(bf16)], axis=1)
    share = jnp.broadcast_to(share[None], (PLANE,) + share.shape)
    share, qkv_pieces[1] = lax.optimization_barrier((share, qkv_pieces[1]))
    quarter = plane_swap(share).reshape(QUARTER, FC + D)

    x_own = tokens.reshape(S, D)
    cot_own = cotangent.reshape(S, D)
    x_other, cot_other = swap(x_own), swap(cot_own)
    ints = jnp.concatenate(
        [
            patch_row.reshape(1, S),
            patch_col.reshape(1, S),
            jnp.pad(counts.reshape(1, 2), ((0, 0), (0, S - 2))),
            jnp.zeros((5, S), jnp.int32),
        ]
    )
    ints = jnp.stack([ints, swap(ints)])
    counts0 = jnp.where(first_core, ints[0, 2, :2], ints[1, 2, :2])
    counts1 = jnp.where(first_core, ints[1, 2, :1], ints[0, 2, :1])
    place = jnp.concatenate([jnp.stack([core, along]).astype(jnp.int32), counts0, counts1])

    vec, h1t, cosine, sine, q, k, v, b1, pos = qkv_call(place, x_own, x_other, ints, qkv_pieces)
    q, quarter = lax.optimization_barrier((q, quarter))
    pieces = along_line(quarter)
    mine, p0, p1 = attn_fwd_call(place, q, k, v)
    mine, pieces[1], pieces[3], cot_other = lax.optimization_barrier((mine, pieces[1], pieces[3], cot_other))
    other = swap(mine)
    gy = gy_call(place, cot_own, cot_other)
    other, gy = lax.optimization_barrier((other, gy))
    after, n2, r2, h2 = proj_call(place, mine, other, x_own, x_other, pieces, vec)
    mlp, mlp_part, gh2, act, gup, gb1 = mlp_call(place, h2, gy, pieces, full_fc2, b1)
    other_gh2 = swap(gh2)
    mlp_other = swap(mlp_part)

    gw1, gw2 = fc_grad_call(place, h2, gup, act, gy)
    gw1, gw2, other_gh2 = lax.optimization_barrier((gw1, gw2, other_gh2))
    sum_fc2 = line_sum(gw2)
    sum_fc1 = line_sum(gw1)
    ga, gab, sums_mid = mid_call(place, n2, r2, gy, gh2, other_gh2, vec)
    *gw, gh1, gh1_part = attn_bwd_call(
        place, q, k, v, gab, mine, other, p0, p1, cosine, sine, pos, h1t, qkv_pieces, pieces,
        x_own, x_other, sums_mid, gb1,
    )
    gh1_other = swap(gh1_part)

    got_fc2 = plane_swap(sum_fc2.reshape(PLANE, FR, D))
    parts = [gw[0]] + [shift(gw[d], d) for d in range(1, SIDE)]
    got_fc2, sum_fc1 = lax.optimization_barrier((got_fc2, sum_fc1))
    g_fc2 = sum_call(got_fc2)
    g2, squares = fc2_call(place, g_fc2, swap(g_fc2))
    got = plane_swap(pack_call(parts, sum_fc1))
    got, g2, squares = lax.optimization_barrier((got, g2, squares))
    grads = sum_call(got)

    grads_other = swap(grads)
    squares = norm_call(grads, grads_other, squares)
    squares, gh1 = lax.optimization_barrier((squares, gh1))
    norms = lax.all_to_all(squares, "dp", 0, 0)
    gt, mixed = last_call(x_own, ga, gh1, gh1_other, after, mlp, mlp_other, vec)
    norms, gt, mixed = lax.optimization_barrier((norms, gt, mixed))
    *updates, grad_norm, bias_proj_grad = adam_call(
        place,
        norms,
        grads,
        grads_other,
        g2,
        (w_qkv, w_proj, w_fc1, w_fc2, vectors),
        (m_qkv, m_proj, m_fc1, m_fc2, m_vectors),
        (v_qkv, v_proj, v_fc1, v_fc2, v_vectors),
    )
    return (
        mixed.reshape(1, 1, S, D),
        gt.reshape(1, 1, S, D),
        grad_norm[0, 0],
        *updates,
        bias_proj_grad.reshape(KR),
    )


def solution(mesh):
    frame = P("grp", "dp", None, None)
    ints = P("grp", "dp", None)
    rows = P("dp", None)
    cols = P(None, "dp")
    return jax.shard_map(
        local,
        mesh=mesh,
        in_specs=(frame, frame, ints, ints, ints, rows, rows, rows, rows, cols) + (rows,) * 8 + (cols,) * 2,
        out_specs=(frame, frame, P()) + (rows,) * 12 + (cols,) * 3 + (P("dp"),),
        check_vma=False,
    )
```

```python
import jax
import jax.numpy as jnp
from jax import lax
from jax.experimental import pallas as pl
from jax.experimental.pallas import tpu as pltpu
from jax.sharding import PartitionSpec as P

D = 768
H = 12
HD = 64
FF = 3072
STEP = 10
A = 196
S = 576

CORES = 2
HC = H // CORES
DC = D // CORES
FC = FF // CORES
PAIRS = HC // 2
T = CORES * S

WIN = 208
WINDOWS = (0, 192)

EPS_NORM = 1e-06
BETA_ONE = 0.9
BETA_TWO = 0.95
ADAM_EPS = 1e-08
DECAY_RATE = 0.05
RATE_VECTOR = 0.8
CLIP_LIMIT = 1.0
NEG = -1e30

bf16 = jnp.bfloat16
f32 = jnp.float32
VMEM_LIMIT = 56 * 1024 * 1024


SIDE = 4
CHIPS = SIDE**3
PLANE = SIDE * SIDE
KR = D // CHIPS
FR = FC // CHIPS
BLOCK = SIDE * KR
QUARTER = PLANE * KR
BOTH = ("grp", "dp")


def device(core, x, y, z):
    return ((core * SIDE + x) * SIDE + y) * SIDE + z


def lines():
    r = range(SIDE)
    return [[device(0, a, g, z) for a in r] for g in r for z in r] + [
        [device(1, g, a, z) for a in r] for g in r for z in r
    ]


def planes():
    r = range(SIDE)
    return [[device(0, a, g, z) for g in r for z in r] for a in r] + [
        [device(1, g, a, z) for g in r for z in r] for a in r
    ]


def shift(value, d):
    pairs = [(group[i], group[(i + d) % SIDE]) for group in lines() for i in range(SIDE)]
    return lax.ppermute(value, BOTH, pairs)


def plane_swap(value):
    return lax.all_to_all(value, BOTH, 0, 0, axis_index_groups=planes())


def natural(core, a, g):
    return jnp.where(core == 0, SIDE * a + g, SIDE * g + a)


def lay_out(place_ref, pieces, full_ref):
    core, me = place_ref[0], place_ref[1]
    for d, piece in enumerate(pieces):
        a = (me + SIDE - d) & (SIDE - 1)
        for g in range(SIDE):
            at = pl.multiple_of(natural(core, a, g) * BLOCK, BLOCK)
            full_ref[pl.ds(at, BLOCK), :] = piece[g * BLOCK : (g + 1) * BLOCK, :]


def usable_rows(place_ref, group, rows, base=0):
    slot = lax.broadcasted_iota(jnp.int32, (rows, 1), 0) + base
    first = ((slot < A) & (slot < place_ref[2])) | ((slot >= A) & (slot < 2 * A) & (slot - A < place_ref[3]))
    first = first.astype(f32)
    second = (slot < place_ref[4]).astype(f32)
    if isinstance(group, int):
        return second if group else first
    return jnp.where(group == 0, first, second)


def own_rows(win):
    row = lax.broadcasted_iota(jnp.int32, (WIN, 1), 0) + (WINDOWS[win] - win * A)
    return ((row >= 0) & (row < A)).astype(f32)


def key_bias(place_ref, win=None):
    if win is None:
        key = lax.broadcasted_iota(jnp.int32, (1, S), 1)
        return jnp.where(key < place_ref[4], 0.0, NEG)
    key = lax.broadcasted_iota(jnp.int32, (1, WIN), 1) + (WINDOWS[win] - win * A)
    return jnp.where((key >= 0) & (key < place_ref[2 + win]), 0.0, NEG)


def exact_dot(a, b):
    high = a.astype(bf16)
    rest = a - high.astype(f32)
    mid = rest.astype(bf16)
    low = (rest - mid.astype(f32)).astype(bf16)
    b = b.astype(bf16)
    return dot(high, b) + dot(mid, b) + dot(low, b)


def spots(core, shape, full, part):
    l = lax.broadcasted_iota(jnp.int32, shape, full)
    m = lax.broadcasted_iota(jnp.int32, shape, part)
    q = (m * 2731) >> 16
    return l == m + FR * (q + core)


def spots_t(core):
    return spots(core, (DC, D), 1, 0)


def params(**kw):
    return pltpu.CompilerParams(vmem_limit_bytes=VMEM_LIMIT, **kw)


def cost(flops, bytes_accessed, transcendentals=0):
    return pl.CostEstimate(
        flops=int(flops), bytes_accessed=int(bytes_accessed), transcendentals=int(transcendentals)
    )


def dot(a, b):
    return jnp.dot(a, b, preferred_element_type=f32)


def dot_t(a, b):
    return lax.dot_general(a, b, (((1,), (1,)), ((), ())), preferred_element_type=f32)


def t_dot(a, b):
    return lax.dot_general(a, b, (((0,), (0,)), ((), ())), preferred_element_type=f32)


def stats(z):
    mean_val = jnp.mean(z, axis=-1, keepdims=True)
    centred = z - mean_val
    variance = jnp.mean(centred * centred, axis=-1, keepdims=True)
    inv_std = lax.rsqrt(variance + EPS_NORM)
    return centred * inv_std, inv_std


def norm_back(grad, normed, inv_std, gain):
    e = grad * gain
    return inv_std * (
        e
        - jnp.mean(e, axis=-1, keepdims=True)
        - normed * jnp.mean(e * normed, axis=-1, keepdims=True)
    )


def swap_halves(u):
    lanes = u.shape[1]
    lane = lax.broadcasted_iota(jnp.int32, u.shape, 1)
    up = pltpu.roll(u, lanes - HD // 2, 1)
    down = pltpu.roll(u, HD // 2, 1)
    return jnp.where((lane & (HD - 1)) < HD // 2, up, down)


TURN = 1.5707963267948966


def sin_cos(a):
    k = jnp.floor(a * (1.0 / TURN) + 0.5)
    r = ((a - k * 1.5703125) - k * 4.837512969970703125e-4) - k * 7.54978995489188216e-8
    z = r * r
    s = ((-1.9515295891e-4 * z + 8.3321608736e-3) * z - 1.6666654611e-1) * z * r + r
    c = ((2.443315711809948e-5 * z - 1.388731625493765e-3) * z + 4.166664568298827e-2) * z * z - 0.5 * z + 1.0
    quarter = k.astype(jnp.int32)
    odd = (quarter & 1) == 1
    sine = jnp.where(odd, c, s)
    cosine = jnp.where(odd, s, c)
    sine = jnp.where((quarter & 2) == 0, sine, -sine)
    cosine = jnp.where(((quarter + 1) & 2) == 0, cosine, -cosine)
    return sine, cosine


def share_kernel(place_ref, w_ref, v_ref, out_ref):
    core = place_ref[0]
    w = w_ref[...].astype(bf16)
    cols = []
    for p in range(PAIRS):
        for i in range(3):
            at = i * D + p * 128
            cols.append(jnp.where(core == 0, w[:, at : at + 128], w[:, at + DC : at + DC + 128]))
    v = jnp.concatenate([v_ref[...], jnp.zeros((128 - v_ref.shape[0], KR), f32)], axis=0)
    v = jnp.concatenate([v, jnp.zeros((128, 128 - KR), f32)], axis=1)
    cols.append(v.T[:KR, :].astype(bf16))
    share = jnp.concatenate(cols, axis=1)
    for n in range(PLANE):
        out_ref[n] = share


def share_call(place, w, vectors):
    whole = lambda a: pl.BlockSpec(a.shape, lambda i, c: (0, 0))
    return pl.pallas_call(
        share_kernel,
        grid_spec=pltpu.PrefetchScalarGridSpec(
            num_scalar_prefetch=1,
            grid=(1,),
            in_specs=[whole(w), whole(vectors)],
            out_specs=pl.BlockSpec((PLANE, KR, 3 * DC + 128), lambda i, c: (0, 0, 0)),
        ),
        out_shape=jax.ShapeDtypeStruct((PLANE, KR, 3 * DC + 128), bf16),
        compiler_params=params(),
        cost_estimate=cost(KR * D * 3, 1e6),
    )(place, w, vectors)


def gy_kernel(place_ref, c_ref, co_ref, gy_ref):
    i = pl.program_id(0)
    keep = usable_rows(place_ref, i ^ place_ref[0], S)
    gy_ref[...] = (jnp.where(i == 0, c_ref[...], co_ref[...]).astype(f32) * keep).astype(bf16)


def gy_call(place, c, co):
    whole = pl.BlockSpec((S, D), lambda i, c: (0, 0))
    return pl.pallas_call(
        gy_kernel,
        grid_spec=pltpu.PrefetchScalarGridSpec(
            num_scalar_prefetch=1,
            grid=(CORES,),
            in_specs=[whole, whole],
            out_specs=pl.BlockSpec((S, D), lambda i, c: (i, 0)),
        ),
        out_shape=jax.ShapeDtypeStruct((T, D), bf16),
        compiler_params=params(),
        cost_estimate=cost(4 * T * D, T * D * 4),
    )(place, c, co)


def qkv_kernel(
    place_ref, x_ref, xo_ref, ints_ref, w0, w1, w2, w3, v0, v1, v2, v3,
    vec_ref, ht_ref, cos_ref, sin_ref, q_out, k_out, v_out, b1_ref, pos_ref,
    w_s, full_s, rows_s, freq_s,
):
    core = place_ref[0]

    @pl.when(pl.program_id(0) == 0)
    def _():
        lay_out(place_ref, (w0, w1, w2, w3), w_s)
        lay_out(place_ref, (v0, v1, v2, v3), full_s)
        rows_s[...] = full_s[...].astype(f32).T[:16, :]
        vec_ref[...] = rows_s[...]
        late = rows_s[8:16, :].astype(bf16)
        units = dot(late, spots(core, (D, DC), 0, 1).astype(bf16))
        for r in range(FC // DC):
            b1_ref[:, r * DC : (r + 1) * DC] = units[2 + r : 3 + r, :]
        src = lax.broadcasted_iota(jnp.int32, (D, DC), 0)
        dst = lax.broadcasted_iota(jnp.int32, (D, DC), 1)
        want = core * (DC // 2) + (dst // HD) * (HD // 2) + (dst & (HD // 2 - 1))
        freq_s[0:8, :] = dot(late, (src == want).astype(bf16))
        freq_s[8:16, :] = dot(late, (src == want + D // 2).astype(bf16))

    i = pl.program_id(0)
    x = jnp.where(i < pl.num_programs(0) // CORES, x_ref[...], xo_ref[...])
    h = stats(x.astype(f32))[0] * rows_s[0:1, :] + rows_s[1:2, :]
    pos = ints_ref[...].astype(f32).T
    pos_ref[...] = pos
    ht_ref[...] = h.T.astype(bf16)
    acc = dot(h.astype(bf16), w_s[...])
    angle = pos[:, 1:2] * freq_s[1:2, :] + pos[:, 0:1] * freq_s[9:10, :]
    lane = lax.broadcasted_iota(jnp.int32, (1, DC), 1)
    sign = jnp.where((lane & (HD - 1)) < HD // 2, -1.0, 1.0)
    small = jnp.max(jnp.abs(angle)) < 8000.0

    @pl.when(small)
    def _():
        sine, cosine = sin_cos(angle)
        cos_ref[...] = cosine
        sin_ref[...] = sine * sign

    @pl.when(jnp.logical_not(small))
    def _():
        cos_ref[...] = jnp.cos(angle)
        sin_ref[...] = jnp.sin(angle) * sign

    cosine, sine = cos_ref[...], sin_ref[...]
    at = pl.ds(pl.multiple_of(core * DC, DC), DC)
    part = lambda i: jnp.concatenate([acc[:, (3 * p + i) * 128 : (3 * p + i + 1) * 128] for p in range(PAIRS)], axis=1)
    q = part(0) + rows_s[4:5, at]
    k = part(1) + rows_s[5:6, at]
    q_out[...] = ((q * cosine + swap_halves(q) * sine) * HD ** (-0.5)).astype(bf16)
    k_out[...] = (k * cosine + swap_halves(k) * sine).astype(bf16)
    v_out[...] = (part(2) + rows_s[6:7, at]).astype(bf16)


def qkv_call(place, x, xo, ints, pieces):
    rows = S
    tile = lambda n: pl.BlockSpec((rows, n), lambda i, c: (i, 0))
    keep = lambda *n: pl.BlockSpec(n, lambda i, c: (0,) * len(n))
    return pl.pallas_call(
        qkv_kernel,
        grid_spec=pltpu.PrefetchScalarGridSpec(
            num_scalar_prefetch=1,
            grid=(CORES,),
            in_specs=[keep(S, D), keep(S, D), pl.BlockSpec((None, 8, S), lambda i, c: (i, 0, 0))]
            + [keep(QUARTER, 3 * DC)] * 4
            + [pl.BlockSpec((QUARTER, 128), lambda i, c: (0, 3 * DC // 128))] * 4,
            out_specs=[keep(16, D), pl.BlockSpec((None, D, rows), lambda i, c: (i, 0, 0))]
            + [tile(DC)] * 5
            + [keep(1, FC), tile(8)],
            scratch_shapes=[
                pltpu.VMEM((D, 3 * DC), bf16),
                pltpu.VMEM((D, 128), bf16),
                pltpu.VMEM((16, D), f32),
                pltpu.VMEM((16, DC), f32),
            ],
        ),
        out_shape=[
            jax.ShapeDtypeStruct((16, D), f32),
            jax.ShapeDtypeStruct((CORES, D, S), bf16),
            jax.ShapeDtypeStruct((T, DC), f32),
            jax.ShapeDtypeStruct((T, DC), f32),
            *[jax.ShapeDtypeStruct((T, DC), bf16)] * 3,
            jax.ShapeDtypeStruct((1, FC), f32),
            jax.ShapeDtypeStruct((T, 8), f32),
        ],
        compiler_params=params(),
        cost_estimate=cost(2 * T * D * 3 * DC + 60 * T * DC, T * D * 6 + D * 3 * DC * 2 + T * DC * 14),
    )(place, x, xo, ints, *pieces, *pieces)


def softmax_head(q, k, v, mine, bias):
    s = dot_t(jnp.where(mine, q, jnp.zeros_like(q)), k) + bias
    e = jnp.exp(s - jnp.max(s, axis=-1, keepdims=True))
    p = e * (1.0 / jnp.sum(e, axis=-1, keepdims=True))
    return p


def attn_fwd_kernel(
    place_ref, q0, k0, v0, q1, k1, v1, o_ref, p0_ref, p1_ref
):
    lane = lax.broadcasted_iota(jnp.int32, (1, 2 * HD), 1)
    low = lane < HD
    q, k, v = q1[0], k1[0], v1[0]
    mixes = []
    bias = key_bias(place_ref)
    for head, mine in ((0, low), (1, ~low)):
        p = softmax_head(q, k, v, mine, bias).astype(bf16)
        p1_ref[head] = p
        mixes.append(dot(p, v))
    mix = jnp.where(low, mixes[0], mixes[1])
    o_ref[1] = jnp.where(usable_rows(place_ref, 1, S) > 0, mix, v.astype(f32)).astype(bf16)
    o_ref[0] = v0[0]
    for win, base in enumerate(WINDOWS):
        q, k, v = (r[0, base : base + WIN, :] for r in (q0, k0, v0))
        own = own_rows(win)
        bias = key_bias(place_ref, win)
        mixes = []
        for head, mine in ((0, low), (1, ~low)):
            p = softmax_head(q, k, v, mine, bias)
            p = (p * own).astype(bf16)
            p0_ref[head, win] = p
            mixes.append(dot(p, v))
        mix = jnp.where(low, mixes[0], mixes[1])
        use = (own * usable_rows(place_ref, 0, WIN, base)) > 0
        before = o_ref[0, base : base + WIN, :].astype(f32)
        o_ref[0, base : base + WIN, :] = jnp.where(use, mix, before).astype(bf16)


def attn_fwd_call(place, q, k, v):
    block = lambda g: pl.BlockSpec((1, S, 2 * HD), lambda p, c: (g ^ c[0], 0, p))
    q, k, v = (a.reshape(CORES, S, DC) for a in (q, k, v))
    return pl.pallas_call(
        attn_fwd_kernel,
        grid_spec=pltpu.PrefetchScalarGridSpec(
            num_scalar_prefetch=1,
            grid=(PAIRS,),
            in_specs=[block(0)] * 3 + [block(1)] * 3,
            out_specs=[
                pl.BlockSpec((CORES, S, 2 * HD), lambda p, c: (0, 0, p)),
                pl.BlockSpec((2, 2, WIN, WIN), lambda p, c: (p, 0, 0, 0)),
                pl.BlockSpec((2, S, S), lambda p, c: (p, 0, 0)),
            ],
        ),
        out_shape=[
            jax.ShapeDtypeStruct((CORES, S, DC), bf16),
            jax.ShapeDtypeStruct((HC, 2, WIN, WIN), bf16),
            jax.ShapeDtypeStruct((HC, S, S), bf16),
        ],
        compiler_params=params(),
        cost_estimate=cost(4 * HC * (S * S + 2 * WIN * WIN) * 128, 12e6, HC * S * S),
    )(place, q, k, v, q, k, v)


def proj_kernel(place_ref, mine_ref, other_ref, x_ref, xo_ref, w0, w1, w2, w3, v_ref, after_ref, n2_ref, r2_ref, h2_ref, w_s):
    @pl.when(pl.program_id(0) == 0)
    def _():
        lay_out(place_ref, (w0, w1, w2, w3), w_s)

    core = place_ref[0]
    at = lambda c: pl.ds(pl.multiple_of(c * DC, DC), DC)
    branch = dot(mine_ref[0], w_s[at(core), :]) + dot(other_ref[0], w_s[at(1 - core), :])
    x = jnp.where(pl.program_id(0) < pl.num_programs(0) // CORES, x_ref[...], xo_ref[...])
    after = x.astype(f32) + (branch + v_ref[7:8, :])
    normed, inv_std = stats(after)
    n2_ref[...] = normed
    r2_ref[...] = jnp.broadcast_to(inv_std, r2_ref.shape)

    @pl.when(pl.program_id(0) < pl.num_programs(0) // CORES)
    def _():
        after_ref[...] = after

    h2_ref[...] = (normed * v_ref[2:3, :] + v_ref[3:4, :]).astype(bf16)


def proj_call(place, mine, other, x, xo, pieces, vec):
    rows = 288
    half = S // rows
    tile = lambda n: pl.BlockSpec((rows, n), lambda i, c: (i, 0))
    whole = lambda a: pl.BlockSpec(a.shape, lambda i, c: (0,) * a.ndim)
    return pl.pallas_call(
        proj_kernel,
        grid_spec=pltpu.PrefetchScalarGridSpec(
            num_scalar_prefetch=1,
            grid=(T // rows,),
            in_specs=[
                pl.BlockSpec((1, rows, DC), lambda i, c: ((i // half) ^ c[0], i % half, 0)),
                pl.BlockSpec((1, rows, DC), lambda i, c: ((i // half) ^ c[0], i % half, 0)),
                pl.BlockSpec((rows, D), lambda i, c: (jnp.minimum(i, half - 1), 0)),
                pl.BlockSpec((rows, D), lambda i, c: (jnp.maximum(i - half, 0), 0)),
            ]
            + [pl.BlockSpec((QUARTER, D), lambda i, c: (0, FC // D))] * 4
            + [whole(vec)],
            out_specs=[pl.BlockSpec((rows, D), lambda i, c: (jnp.minimum(i, half - 1), 0)), tile(D), tile(8), tile(D)],
            scratch_shapes=[pltpu.VMEM((D, D), bf16)],
        ),
        out_shape=[
            jax.ShapeDtypeStruct((S, D), f32),
            jax.ShapeDtypeStruct((T, D), f32),
            jax.ShapeDtypeStruct((T, 8), f32),
            jax.ShapeDtypeStruct((T, D), bf16),
        ],
        compiler_params=params(),
        cost_estimate=cost(2 * T * D * D, T * D * 10 + D * D * 2),
    )(place, mine, other, x, xo, *pieces, vec)


PACK = 4 * DC + 128
K0 = (2.0 / 3.141592653589793) ** 0.5
FT = 768


def gelu_slope(u):
    sq = u * u
    th = jnp.tanh(u * (K0 + (K0 * 0.044715) * sq))
    half = 0.5 + 0.5 * th
    return u * half, half + (u * (half - half * half)) * (2 * K0 + (6 * K0 * 0.044715) * sq)


def mlp_kernel(
    place_ref, h2_ref, gy_ref, w10, w11, w12, w13, w2_ref, b1_ref, mlp_ref, mlpo_ref, gh2b_ref, act_ref, gup_ref, gb1_ref, w1_s
):
    i = pl.program_id(0)

    @pl.when(i == 0)
    def _():
        lay_out(place_ref, (w10, w11, w12, w13), w1_s)
        gb1_ref[...] = jnp.zeros_like(gb1_ref)

    for f in range(FC // FT):
        c = slice(f * FT, (f + 1) * FT)
        act, slope = gelu_slope(dot(h2_ref[...], w1_s[:, c]) + b1_ref[:, c])
        act_ref[:, c] = act.astype(bf16)
        gup = (dot_t(gy_ref[...], w2_ref[c, :]) * slope).astype(bf16)
        gup_ref[:, c] = gup
        gb1_ref[:, c] += jnp.sum(gup.astype(f32), axis=0, keepdims=True)
    gh2b_ref[...] = dot_t(gup_ref[...], w1_s[...]).astype(bf16)
    mlp = dot(act_ref[...], w2_ref[...])
    half = pl.num_programs(0) // CORES

    @pl.when(i < half)
    def _():
        mlp_ref[...] = mlp

    @pl.when(i >= half)
    def _():
        mlpo_ref[...] = mlp


def mlp_call(place, h2, gy, pieces, w2, b1):
    rows = 288
    half = S // rows
    tile = lambda n: pl.BlockSpec((rows, n), lambda i, c: (i, 0))
    whole = lambda a: pl.BlockSpec(a.shape, lambda i, c: (0,) * a.ndim)
    return pl.pallas_call(
        mlp_kernel,
        grid_spec=pltpu.PrefetchScalarGridSpec(
            num_scalar_prefetch=1,
            grid=(T // rows,),
            in_specs=[tile(D), tile(D)]
            + [pl.BlockSpec((QUARTER, FC), lambda i, c: (0, 0))] * 4
            + [whole(w2), whole(b1)],
            out_specs=[
                pl.BlockSpec((rows, D), lambda i, c: (jnp.minimum(i, half - 1), 0)),
                pl.BlockSpec((rows, D), lambda i, c: (jnp.maximum(i - half, 0), 0)),
                tile(D),
                tile(FC),
                tile(FC),
                pl.BlockSpec((1, FC), lambda i, c: (0, 0)),
            ],
            scratch_shapes=[pltpu.VMEM((D, FC), bf16)],
        ),
        out_shape=[
            jax.ShapeDtypeStruct((S, D), f32),
            jax.ShapeDtypeStruct((S, D), f32),
            jax.ShapeDtypeStruct((T, D), bf16),
            jax.ShapeDtypeStruct((T, FC), bf16),
            jax.ShapeDtypeStruct((T, FC), bf16),
            jax.ShapeDtypeStruct((1, FC), f32),
        ],
        compiler_params=params(),
        cost_estimate=cost(8 * T * D * FC, 30e6, T * FC),
    )(place, h2, gy, *pieces, w2, b1)


def by_line(place_ref, value, block, out_ref):
    core = place_ref[0]
    for n in range(PLANE):
        to = jnp.where(core == 0, n, (n % SIDE) * SIDE + n // SIDE)
        out_ref[pl.ds(pl.multiple_of(to * block, block), block), :] = value[n * block : (n + 1) * block, :].astype(bf16)


def fc2_grad_kernel(place_ref, act_ref, gy_ref, out_ref):
    value = t_dot(act_ref[...], gy_ref[...])
    block = SIDE * FR
    for n in range(FT // block):
        m = pl.program_id(0) * (FT // block) + n
        to = jnp.where(place_ref[0] == 0, m, (m & (SIDE - 1)) * SIDE + m // SIDE)
        out_ref[pl.ds(pl.multiple_of(to * block, block), block), :] = value[n * block : (n + 1) * block, :].astype(bf16)


def fc2_grad_call(place, act, gy):
    return pl.pallas_call(
        fc2_grad_kernel,
        grid_spec=pltpu.PrefetchScalarGridSpec(
            num_scalar_prefetch=1,
            grid=(FC // FT,),
            in_specs=[pl.BlockSpec((T, FT), lambda i, c: (0, i)), pl.BlockSpec((T, D), lambda i, c: (0, 0))],
            out_specs=pl.BlockSpec((FC, D), lambda i, c: (0, 0)),
        ),
        out_shape=jax.ShapeDtypeStruct((FC, D), bf16),
        compiler_params=params(),
        cost_estimate=cost(2 * T * D * FC, T * (D + FC) * 2 + D * FC * 2),
    )(place, act, gy)


def mid_kernel(
    place_ref, h2_ref, gup_ref, n2_ref, r2_ref, gy_ref, gh2_ref, other_ref, v_ref, gw_ref, ga_ref, gab_ref, sums_ref
):
    i = pl.program_id(0)
    by_line(place_ref, t_dot(h2_ref[...], gup_ref[...]), BLOCK, gw_ref)
    normed, inv_std = n2_ref[...], r2_ref[:, 0:1]
    gh2 = gh2_ref[...].astype(f32) + other_ref[...].astype(f32)
    gy = gy_ref[...].astype(f32)
    ga = gy + norm_back(gh2, normed, inv_std, v_ref[2:3, :])
    gab = ga.astype(bf16)
    gab_ref[...] = gab
    mine = (i < pl.num_programs(0) // CORES).astype(f32)
    sums = [
        mine * jnp.sum(a, axis=0, keepdims=True) for a in (gh2 * normed, gh2, gab.astype(f32), gy)
    ] + [jnp.zeros((4, D), f32)]
    sums = jnp.concatenate(sums, axis=0)

    @pl.when(i == 0)
    def _():
        sums_ref[...] = sums

    @pl.when(i > 0)
    def _():
        sums_ref[...] += sums

    @pl.when(i < pl.num_programs(0) // CORES)
    def _():
        ga_ref[...] = ga


def mid_call(place, h2, gup, n2, r2, gy, gh2, other, vec):
    rows = 288
    half = S // rows
    cols = FC * rows // T
    tile = lambda n: pl.BlockSpec((rows, n), lambda i, c: (i, 0))
    flipped = pl.BlockSpec((rows, D), lambda i, c: ((i + half) % (2 * half), 0))
    whole = lambda a: pl.BlockSpec(a.shape, lambda i, c: (0,) * a.ndim)
    return pl.pallas_call(
        mid_kernel,
        grid_spec=pltpu.PrefetchScalarGridSpec(
            num_scalar_prefetch=1,
            grid=(T // rows,),
            in_specs=[whole(h2), pl.BlockSpec((T, cols), lambda i, c: (0, i))]
            + [tile(D), tile(8), tile(D), tile(D), flipped, whole(vec)],
            out_specs=[
                pl.BlockSpec((D, cols), lambda i, c: (0, i)),
                pl.BlockSpec((rows, D), lambda i, c: (jnp.minimum(i, half - 1), 0)),
                tile(D),
                pl.BlockSpec((8, D), lambda i, c: (0, 0)),
            ],
        ),
        out_shape=[
            jax.ShapeDtypeStruct((D, FC), bf16),
            jax.ShapeDtypeStruct((S, D), f32),
            jax.ShapeDtypeStruct((T, D), bf16),
            jax.ShapeDtypeStruct((8, D), f32),
        ],
        compiler_params=params(),
        cost_estimate=cost(2 * T * D * FC, T * D * 18 + T * FC * 2 + D * FC * 2),
    )(place, h2, gup, n2, r2, gy, gh2, other, vec)


def back_head(q_t, k, v, do, do_t, delta, p, mine, head):
    gp = dot_t(jnp.where(mine, do, jnp.zeros_like(do)), v)
    gs = (p.astype(f32) * (gp - delta)).astype(bf16)
    at = slice(head * HD, (head + 1) * HD)
    return dot(gs, k), dot(q_t[at, :], gs), dot(do_t[at, :], p)


def deltas(do, o, low):
    prod = do.astype(f32) * o.astype(f32)
    d0 = jnp.sum(jnp.where(low, prod, 0.0), axis=-1, keepdims=True)
    d1 = jnp.sum(jnp.where(low, 0.0, prod), axis=-1, keepdims=True)
    return d0, d1


def attn_bwd_kernel(
    place_ref,
    q0, k0, v0, o0, p0, cos0, sin0, pos0,
    q1, k1, v1, o1, p1, cos1, sin1, pos1,
    h1t_ref, ga_ref, cols_ref, mine_ref, other_ref, y0, y1, y2, y3, w0, w1, w2, w3,
    x_ref, xo_ref, mid_ref, gb1_ref,
    gw0, gw1, gw2, gw3, gh_ref, gho_ref,
    gq_s, gk_s, gv_s, gw_s, y_s, do_s, gqkv_s, att_s, rows_s, full_s, w_s,
):
    lane = lax.broadcasted_iota(jnp.int32, (1, 2 * HD), 1)
    low = lane < HD
    pair = pl.program_id(0)
    core = place_ref[0]

    @pl.when(pair == 0)
    def _():
        lay_out(place_ref, (y0, y1, y2, y3), y_s)

    wy = y_s[pl.ds(pl.multiple_of(core * DC + pair * 2 * HD, 2 * HD), 2 * HD), :]
    for frame in range(CORES):
        do_s[frame] = dot_t(ga_ref[frame], wy).astype(bf16)

    def finish(frame, q, k, cos_ref, sin_ref, pos_ref):
        cosine, sine = cos_ref[0], sin_ref[0]
        gq = gq_s[...] * HD ** (-0.5)
        gk = gk_s[...]
        sq, sk = swap_halves(gq), swap_halves(gk)
        turn = (q.astype(f32) * HD**0.5) * sq + k.astype(f32) * sk
        gq = (gq * cosine - sq * sine).astype(bf16)
        gk = (gk * cosine - sk * sine).astype(bf16)
        gv = gv_s[...].astype(bf16)
        for i, g in enumerate((gq, gk, gv)):
            gqkv_s[frame ^ core, :, pl.ds(pl.multiple_of(pair * 6 * HD + i * 2 * HD, 2 * HD), 2 * HD)] = g
        pos = pos_ref[0]
        col = jnp.sum(turn * pos[:, 1:2], axis=0, keepdims=True)
        row = jnp.sum(turn * pos[:, 0:1], axis=0, keepdims=True)
        bias = [jnp.sum(g.astype(f32), axis=0, keepdims=True) for g in (gq, gk, gv)]
        return jnp.concatenate([col, row] + bias, axis=0)

    q, k, v, do = q1[0], k1[0], v1[0], do_s[1 ^ core]
    d = deltas(do, o1[0], low)
    q_t, do_t = q.astype(f32).T.astype(bf16), do.astype(f32).T.astype(bf16)
    out = [
        back_head(q_t, k, v, do, do_t, d[head], p1[head], mine, head)
        for head, mine in ((0, low), (1, ~low))
    ]
    gq_s[...] = jnp.where(low, out[0][0], out[1][0])
    gk_s[...] = jnp.concatenate([out[0][1], out[1][1]], axis=0).T
    gv_s[...] = jnp.concatenate([out[0][2], out[1][2]], axis=0).T
    sums1 = finish(1, q, k, cos1, sin1, pos1)
    gq_s[...] = jnp.zeros_like(gq_s)
    gk_s[...] = jnp.zeros_like(gk_s)
    gv_s[...] = jnp.zeros_like(gv_s)
    for win, base in enumerate(WINDOWS):
        at = pl.ds(base, WIN)
        q, k, v, o = (r[0, at, :] for r in (q0, k0, v0, o0))
        do = do_s[core, at, :]
        d = deltas(do, o, low)
        q_t, do_t = q.astype(f32).T.astype(bf16), do.astype(f32).T.astype(bf16)
        out = [
            back_head(q_t, k, v, do, do_t, d[head], p0[head, win], mine, head)
            for head, mine in ((0, low), (1, ~low))
        ]
        gq_s[at, :] += jnp.where(low, out[0][0], out[1][0])
        gk_s[at, :] += jnp.concatenate([out[0][1], out[1][1]], axis=0).T
        gv_s[at, :] += jnp.concatenate([out[0][2], out[1][2]], axis=0).T
    sums0 = finish(0, q0[0], k0[0], cos0, sin0, pos0)
    att_s[pair, 0:5, :] = sums0 + sums1

    gw = jnp.zeros((D, 6 * HD), f32)
    gw_mine = jnp.zeros((2 * HD, DC), f32)
    gw_other = jnp.zeros((2 * HD, DC), f32)
    for frame in range(CORES):
        cols = cols_ref[frame].astype(f32).T.astype(bf16)
        gw_mine += dot(cols, mine_ref[frame ^ core])
        gw_other += dot(cols, other_ref[frame ^ core])
        gw += dot(h1t_ref[frame], gqkv_s[frame, :, pl.ds(pl.multiple_of(pair * 6 * HD, 6 * HD), 6 * HD)])
    gw_s[:, : 6 * HD] = gw.astype(bf16)
    at = lambda c: pl.ds(pl.multiple_of(c * DC, DC), DC)
    gw_s[at(core), 6 * HD :] = gw_mine.T.astype(bf16)
    gw_s[at(1 - core), 6 * HD :] = gw_other.T.astype(bf16)
    to_chips(place_ref, gw_s, (gw0, gw1, gw2, gw3), pl.ds(pl.multiple_of(pair * 8 * HD, 8 * HD), 8 * HD))

    @pl.when(pair == PAIRS - 1)
    def _():
        lay_out(place_ref, (w0, w1, w2, w3), w_s)
        rows_s[...] = jnp.zeros_like(rows_s)
        for frame, x, out in ((0, x_ref, gh_ref), (1, xo_ref, gho_ref)):
            for half in range(2):
                at = slice(half * (S // 2), (half + 1) * (S // 2))
                gh = dot_t(gqkv_s[frame, at, :], w_s[...])
                out[at, :] = gh
                normed, _ = stats(x[at, :].astype(f32))
                rows_s[0:1, :] += jnp.sum(gh * normed, axis=0, keepdims=True)
                rows_s[1:2, :] += jnp.sum(gh, axis=0, keepdims=True)
        rows_s[2:4, :] = mid_ref[0:2, :]
        rows_s[7:9, :] = mid_ref[2:4, :]
        att = jnp.concatenate([att_s[p] for p in range(PAIRS)], axis=1)
        rows_s[4:7, pl.ds(pl.multiple_of(core * DC, DC), DC)] = att[2:5, :]
        src = lax.broadcasted_iota(jnp.int32, (DC, D), 0)
        dst = lax.broadcasted_iota(jnp.int32, (DC, D), 1)
        want = core * (DC // 2) + (src // HD) * (HD // 2) + (src & (HD // 2 - 1))
        side = lax.broadcasted_iota(jnp.int32, (1, DC), 1)
        turn = jnp.where((side & (HD - 1)) < HD // 2, att, -att)
        rows_s[9:10, :] = exact_dot(turn, dst == want)[0:1, :] + exact_dot(turn, dst == want + D // 2)[1:2, :]
        gb1 = jnp.concatenate([gb1_ref[:, r * DC : (r + 1) * DC] for r in range(FC // DC)] * 2, axis=0)
        rows_s[10:14, :] = exact_dot(gb1, spots_t(core))[:4, :]
        full_s[...] = rows_s[...].T.astype(bf16)
        to_chips(place_ref, full_s, (gw0, gw1, gw2, gw3), slice(4 * DC, PACK))


def to_chips(place_ref, full_ref, outs, cols):
    for d, out in enumerate(outs):
        a = (place_ref[1] + d) & (SIDE - 1)
        for g in range(SIDE):
            at = pl.multiple_of(natural(place_ref[0], a, g) * BLOCK, BLOCK)
            out[g * BLOCK : (g + 1) * BLOCK, cols] = full_ref[pl.ds(at, BLOCK), :]


def attn_bwd_call(
    place, q, k, v, ga, mine, other, p0, p1, cosine, sine, pos, h1t, pieces, proj_pieces, x, xo, mid, gb1
):
    q, k, v, cosine, sine, pos, ga = (a.reshape(CORES, S, -1) for a in (q, k, v, cosine, sine, pos, ga))
    block = lambda g: pl.BlockSpec((1, S, 2 * HD), lambda p, c: (g ^ c[0], 0, p))
    own = lambda g: pl.BlockSpec((1, S, 2 * HD), lambda p, c: (g, 0, p))
    at = lambda g: pl.BlockSpec((1, S, 8), lambda p, c: (g ^ c[0], 0, 0))
    whole = lambda a: pl.BlockSpec(a.shape, lambda p, c: (0,) * a.ndim)
    keep = lambda *n: pl.BlockSpec(n, lambda p, c: (0,) * len(n))
    return pl.pallas_call(
        attn_bwd_kernel,
        grid_spec=pltpu.PrefetchScalarGridSpec(
            num_scalar_prefetch=1,
            grid=(PAIRS,),
            in_specs=[block(0)] * 3
            + [own(0), pl.BlockSpec((2, 2, WIN, WIN), lambda p, c: (p, 0, 0, 0))]
            + [block(0)] * 2
            + [at(0)]
            + [block(1)] * 3
            + [own(1), pl.BlockSpec((2, S, S), lambda p, c: (p, 0, 0))]
            + [block(1)] * 2
            + [at(1)]
            + [whole(h1t), whole(ga)]
            + [pl.BlockSpec((CORES, S, 2 * HD), lambda p, c: (0, 0, PAIRS * c[0] + p))]
            + [whole(mine), whole(other)]
            + [pl.BlockSpec((QUARTER, D), lambda p, c: (0, FC // D))] * 4
            + [keep(QUARTER, 3 * DC)] * 4
            + [whole(a) for a in (x, xo, mid, gb1)],
            out_specs=[keep(QUARTER, PACK)] * 4 + [keep(S, D)] * 2,
            scratch_shapes=[pltpu.VMEM((S, 2 * HD), f32)] * 3
            + [pltpu.VMEM((D, 8 * HD), bf16), pltpu.VMEM((D, D), bf16), pltpu.VMEM((CORES, S, 2 * HD), bf16)]
            + [pltpu.VMEM((CORES, S, 3 * DC), bf16), pltpu.VMEM((PAIRS, 8, 2 * HD), f32)]
            + [pltpu.VMEM((128, D), f32), pltpu.VMEM((D, 128), bf16), pltpu.VMEM((D, 3 * DC), bf16)],
        ),
        out_shape=[
            *[jax.ShapeDtypeStruct((QUARTER, PACK), bf16)] * 4,
            *[jax.ShapeDtypeStruct((S, D), f32)] * 2,
        ],
        compiler_params=params(),
        cost_estimate=cost(10 * HC * S * S * 128 + 4 * T * D * 4 * DC, 36e6),
    )(
        place,
        q, k, v, mine, p0, cosine, sine, pos,
        q, k, v, mine, p1, cosine, sine, pos,
        h1t, ga, ga, mine, other, *proj_pieces, *pieces, x, xo, mid, gb1,
    )


def last_kernel(x_ref, ga_ref, gh_ref, other_ref, after_ref, mlp_ref, mlpo_ref, v_ref, gt_ref, out_ref):
    normed, inv_std = stats(x_ref[...].astype(f32))
    gt_ref[...] = ga_ref[...] + norm_back(gh_ref[...] + other_ref[...], normed, inv_std, v_ref[0:1, :])
    out_ref[...] = (after_ref[...] + (mlp_ref[...] + mlpo_ref[...] + v_ref[8:9, :])).astype(bf16)


def last_call(x, ga, gh, other, after, mlp, mlp_other, vec):
    rows = 288
    tile = lambda n: pl.BlockSpec((rows, n), lambda i: (i, 0))
    return pl.pallas_call(
        last_kernel,
        grid=(S // rows,),
        in_specs=[tile(D)] * 7 + [pl.BlockSpec(vec.shape, lambda i: (0, 0))],
        out_specs=[tile(D), tile(D)],
        out_shape=[jax.ShapeDtypeStruct((S, D), f32), jax.ShapeDtypeStruct((S, D), bf16)],
        compiler_params=params(),
        cost_estimate=cost(30 * S * D, S * D * 28),
    )(x, ga, gh, other, after, mlp, mlp_other, vec)


WIDE = PACK + FC


def pack_kernel(q0, q1, q2, q3, f_ref, out_ref):
    total = q0[...].astype(f32) + q1[...].astype(f32) + q2[...].astype(f32) + q3[...].astype(f32)
    fc1 = f_ref[...].astype(f32)
    for n in range(PLANE):
        at = slice(n * KR, (n + 1) * KR)
        out_ref[n, :, :PACK] = total[at, :].astype(bf16)
        out_ref[n, :, PACK:] = fc1[at, :].astype(bf16)


def pack_call(parts, fc1):
    return pl.pallas_call(
        pack_kernel,
        out_shape=jax.ShapeDtypeStruct((PLANE, KR, WIDE), bf16),
        compiler_params=params(),
        cost_estimate=cost(QUARTER * PACK * 4, QUARTER * PACK * 10),
    )(*parts, fc1)


def sum_kernel(in_ref, out_ref):
    total = in_ref[0].astype(f32)
    for n in range(1, PLANE):
        total += in_ref[n].astype(f32)
    out_ref[...] = total


def sum_call(packed):
    return pl.pallas_call(
        sum_kernel,
        out_shape=jax.ShapeDtypeStruct(packed.shape[1:], f32),
        compiler_params=params(),
        cost_estimate=cost(packed.size, packed.size * 2),
    )(packed)


def fc2_kernel(place_ref, mine_ref, other_ref, out_ref, sq_ref):
    first = place_ref[0] == 0
    a, b = mine_ref[...], other_ref[...]
    out_ref[:FR, :] = jnp.where(first, a, b)
    out_ref[FR:, :] = jnp.where(first, b, a)
    total = jnp.sum(a * a + b * b, axis=(0, 1), keepdims=True)
    sq_ref[...] = jnp.broadcast_to(total, sq_ref.shape)


def fc2_call(place, mine, other):
    whole = lambda a: pl.BlockSpec(a.shape, lambda i, c: (0,) * len(a.shape))
    shapes = [jax.ShapeDtypeStruct(s, f32) for s in ((2 * FR, D), (8, 128))]
    return pl.pallas_call(
        fc2_kernel,
        grid_spec=pltpu.PrefetchScalarGridSpec(
            num_scalar_prefetch=1,
            grid=(1,),
            in_specs=[whole(mine), whole(other)],
            out_specs=[whole(a) for a in shapes],
        ),
        out_shape=shapes,
        compiler_params=params(),
        cost_estimate=cost(6 * FR * D, FR * D * 16),
    )(place, mine, other)


def norm_kernel(g_ref, o_ref, sq_ref, out_ref):
    g, o = g_ref[...], o_ref[...]
    part = jnp.sum(g * g + o * o, axis=(0, 1), keepdims=True)
    cross = g[:, 4 * DC : PACK] * o[:, 4 * DC : PACK]
    part += 2.0 * jnp.sum(cross, axis=(0, 1), keepdims=True)
    out_ref[...] = jnp.broadcast_to((part + sq_ref[0:1, 0:1])[None], out_ref.shape)


def norm_call(g, o, squares):
    return pl.pallas_call(
        norm_kernel,
        out_shape=jax.ShapeDtypeStruct((CHIPS, 8, 128), f32),
        compiler_params=params(),
        cost_estimate=cost(4 * KR * PACK, 1e6),
    )(g, o, squares)


RATES = (D ** (-0.5), max(1, 2 * D // S) ** (-0.5), D ** (-0.5), FF ** (-0.5), RATE_VECTOR)


def adam_kernel(place_ref, norm_ref, mine_ref, other_ref, g2_ref, *refs):
    masters, firsts, seconds = refs[0:5], refs[5:10], refs[10:15]
    outs = refs[15:30]
    norm_out, bias_out = refs[30:32]
    core = place_ref[0]
    mine, other = mine_ref[...], other_ref[...]
    g0 = jnp.where(core == 0, mine, other)
    g1 = jnp.where(core == 0, other, mine)
    total = jnp.sum(jnp.sum(norm_ref[...], axis=0)[0:1, 0:1], axis=(0, 1), keepdims=True)
    grad_norm = jnp.sqrt(total)
    norm_out[...] = jnp.broadcast_to(grad_norm, norm_out.shape)
    clip = jnp.minimum(1.0, CLIP_LIMIT / (grad_norm + 1e-06))

    def update(i, at, grad):
        clipped = grad * clip
        master = masters[i][at]
        first = BETA_ONE * firsts[i][at] + (1.0 - BETA_ONE) * clipped
        second = BETA_TWO * seconds[i][at] + (1.0 - BETA_TWO) * clipped * clipped
        first_hat = first / (1.0 - BETA_ONE**STEP)
        second_hat = second / (1.0 - BETA_TWO**STEP)
        decay = 0.0 if i == 4 else DECAY_RATE
        outs[3 * i][at] = master - RATES[i] * (first_hat / (jnp.sqrt(second_hat) + ADAM_EPS) + decay * master)
        outs[3 * i + 1][at] = first
        outs[3 * i + 2][at] = second

    rows = slice(None)
    for c, g in ((0, g0), (1, g1)):
        for p in range(PAIRS):
            for i in range(3):
                col = i * D + c * DC + p * 128
                update(0, (rows, slice(col, col + 128)), g[:, (4 * p + i) * 128 : (4 * p + i + 1) * 128])
            col = c * DC + p * 128
            update(1, (rows, slice(col, col + 128)), g[:, (4 * p + 3) * 128 : (4 * p + 4) * 128])
    for r in range(FC // DC):
        at = slice(PACK + r * DC, PACK + (r + 1) * DC)
        part = exact_dot(g0[:, at], spots_t(0)) + exact_dot(g1[:, at], spots_t(1))
        update(2, (rows, slice(r * D, (r + 1) * D)), part)
    update(3, (rows, rows), g2_ref[...])
    vec = (g0 + g1)[:, 4 * DC : 4 * DC + 128]
    vec = jnp.concatenate([vec, jnp.zeros((16 - KR, 128), f32)], axis=0).T[:16, :KR]
    update(4, (rows, rows), vec[: masters[4].shape[0], :])
    bias_out[...] = vec[7:8, :] * clip


def adam_call(place, norm, mine, other, g2, masters, firsts, seconds):
    whole = lambda a: pl.BlockSpec(a.shape, lambda i, c: (0,) * len(a.shape))
    args = [norm, mine, other, g2, *masters, *firsts, *seconds]
    shapes = [jax.ShapeDtypeStruct(m.shape, f32) for m in masters for _ in range(3)]
    shapes += [jax.ShapeDtypeStruct((1, 128), f32), jax.ShapeDtypeStruct((1, KR), f32)]
    return pl.pallas_call(
        adam_kernel,
        grid_spec=pltpu.PrefetchScalarGridSpec(
            num_scalar_prefetch=1,
            grid=(1,),
            in_specs=[whole(a) for a in args],
            out_specs=[whole(a) for a in shapes],
        ),
        out_shape=shapes,
        compiler_params=params(),
        cost_estimate=cost(20 * KR * FF * 3, 3e6),
    )(place, *args)


def local(
    tokens,
    cotangent,
    counts,
    patch_row,
    patch_col,
    w_qkv,
    w_proj,
    w_fc1,
    w_fc2,
    vectors,
    m_qkv,
    v_qkv,
    m_proj,
    v_proj,
    m_fc1,
    v_fc1,
    m_fc2,
    v_fc2,
    m_vectors,
    v_vectors,
):
    core = lax.axis_index("grp")
    chip = lax.axis_index("dp")
    first_core = core == 0
    along = jnp.where(first_core, chip // PLANE, (chip // SIDE) % SIDE)
    vr = vectors.shape[0]

    def swap(a):
        return lax.ppermute(a, "grp", [(0, 1), (1, 0)])

    def along_line(quarter):
        return [quarter] + [shift(quarter, d) for d in range(1, SIDE)]

    def line_sum(whole):
        return lax.psum_scatter(whole, BOTH, scatter_dimension=0, axis_index_groups=lines(), tiled=True)

    fc2_b = w_fc2.astype(bf16)
    share_fc2 = jnp.where(first_core, fc2_b[:FR], fc2_b[FR:])
    me = jnp.stack([core, along]).astype(jnp.int32)
    shares = share_call(me, w_qkv, vectors)
    shares, share_fc2 = lax.optimization_barrier((shares, share_fc2))
    full_fc2 = lax.all_gather(share_fc2, "dp", axis=0, tiled=True)
    fc1_b = w_fc1.astype(bf16).reshape(KR, CHIPS, CORES, FR)
    share_fc1 = jnp.where(first_core, fc1_b[:, :, 0], fc1_b[:, :, 1]).reshape(KR, FC)
    share = jnp.concatenate([share_fc1, w_proj.astype(bf16)], axis=1)
    share = jnp.broadcast_to(share[None], (PLANE,) + share.shape)

    x_own = tokens.reshape(S, D)
    cot_own = cotangent.reshape(S, D)
    x_other, cot_other = swap(x_own), swap(cot_own)
    ints = jnp.concatenate(
        [
            patch_row.reshape(1, S),
            patch_col.reshape(1, S),
            jnp.pad(counts.reshape(1, 2), ((0, 0), (0, S - 2))),
            jnp.zeros((5, S), jnp.int32),
        ]
    )
    ints = jnp.stack([ints, swap(ints)])
    counts0 = jnp.where(first_core, ints[0, 2, :2], ints[1, 2, :2])
    counts1 = jnp.where(first_core, ints[1, 2, :1], ints[0, 2, :1])
    place = jnp.concatenate([jnp.stack([core, along]).astype(jnp.int32), counts0, counts1])

    quarter = plane_swap(shares).reshape(QUARTER, 3 * DC + 128)
    quarter, share, ints, x_other, cot_other = lax.optimization_barrier(
        (quarter, share, ints, x_other, cot_other)
    )
    qkv_pieces = along_line(quarter)
    share, qkv_pieces[1] = lax.optimization_barrier((share, qkv_pieces[1]))
    quarter = plane_swap(share).reshape(QUARTER, FC + D)

    vec, h1t, cosine, sine, q, k, v, b1, pos = qkv_call(place, x_own, x_other, ints, qkv_pieces)
    q, quarter = lax.optimization_barrier((q, quarter))
    pieces = along_line(quarter)
    mine, p0, p1 = attn_fwd_call(place, q, k, v)
    mine, pieces[1], pieces[3] = lax.optimization_barrier((mine, pieces[1], pieces[3]))
    other = swap(mine)
    cot_other, mine = lax.optimization_barrier((cot_other, mine))
    gy = gy_call(place, cot_own, cot_other)
    other, gy = lax.optimization_barrier((other, gy))
    after, n2, r2, h2 = proj_call(place, mine, other, x_own, x_other, pieces, vec)
    mlp, mlp_part, gh2, act, gup, gb1 = mlp_call(place, h2, gy, pieces, full_fc2, b1)
    other_gh2 = swap(gh2)
    mlp_other = swap(mlp_part)

    gw2 = fc2_grad_call(place, act, gy)
    gw2, other_gh2 = lax.optimization_barrier((gw2, other_gh2))
    sum_fc2 = line_sum(gw2)
    gw1, ga, gab, sums_mid = mid_call(place, h2, gup, n2, r2, gy, gh2, other_gh2, vec)
    sum_fc1 = line_sum(gw1)
    *gw, gh1, gh1_part = attn_bwd_call(
        place, q, k, v, gab, mine, other, p0, p1, cosine, sine, pos, h1t, qkv_pieces, pieces,
        x_own, x_other, sums_mid, gb1,
    )
    gh1_other = swap(gh1_part)

    got_fc2 = plane_swap(sum_fc2.reshape(PLANE, FR, D))
    parts = [gw[0]] + [shift(gw[d], d) for d in range(1, SIDE)]
    got_fc2, sum_fc1 = lax.optimization_barrier((got_fc2, sum_fc1))
    g_fc2 = sum_call(got_fc2)
    g2, squares = fc2_call(place, g_fc2, swap(g_fc2))
    got = plane_swap(pack_call(parts, sum_fc1))
    got, g2, squares = lax.optimization_barrier((got, g2, squares))
    grads = sum_call(got)

    grads_other = swap(grads)
    squares = norm_call(grads, grads_other, squares)
    squares, gh1 = lax.optimization_barrier((squares, gh1))
    norms = lax.all_to_all(squares, "dp", 0, 0)
    gt, mixed = last_call(x_own, ga, gh1, gh1_other, after, mlp, mlp_other, vec)
    norms, gt, mixed = lax.optimization_barrier((norms, gt, mixed))
    *updates, grad_norm, bias_proj_grad = adam_call(
        place,
        norms,
        grads,
        grads_other,
        g2,
        (w_qkv, w_proj, w_fc1, w_fc2, vectors),
        (m_qkv, m_proj, m_fc1, m_fc2, m_vectors),
        (v_qkv, v_proj, v_fc1, v_fc2, v_vectors),
    )
    return (
        mixed.reshape(1, 1, S, D),
        gt.reshape(1, 1, S, D),
        grad_norm[0, 0],
        *updates,
        bias_proj_grad.reshape(KR),
    )


def solution(mesh):
    frame = P("grp", "dp", None, None)
    ints = P("grp", "dp", None)
    rows = P("dp", None)
    cols = P(None, "dp")
    return jax.shard_map(
        local,
        mesh=mesh,
        in_specs=(frame, frame, ints, ints, ints, rows, rows, rows, rows, cols) + (rows,) * 8 + (cols,) * 2,
        out_specs=(frame, frame, P()) + (rows,) * 12 + (cols,) * 3 + (P("dp"),),
        check_vma=False,
    )
```

```python
import jax
import jax.numpy as jnp
from jax import lax
from jax.experimental import pallas as pl
from jax.experimental.pallas import tpu as pltpu
from jax.sharding import PartitionSpec as P

D = 768
H = 12
HD = 64
FF = 3072
STEP = 10
A = 196
S = 576

CORES = 2
HC = H // CORES
DC = D // CORES
FC = FF // CORES
PAIRS = HC // 2
T = CORES * S

WIN = 208
WINDOWS = (0, 192)

EPS_NORM = 1e-06
BETA_ONE = 0.9
BETA_TWO = 0.95
ADAM_EPS = 1e-08
DECAY_RATE = 0.05
RATE_VECTOR = 0.8
CLIP_LIMIT = 1.0
NEG = -1e30

bf16 = jnp.bfloat16
f32 = jnp.float32
VMEM_LIMIT = 56 * 1024 * 1024


SIDE = 4
CHIPS = SIDE**3
PLANE = SIDE * SIDE
KR = D // CHIPS
FR = FC // CHIPS
BLOCK = SIDE * KR
QUARTER = PLANE * KR
BOTH = ("grp", "dp")


def device(core, x, y, z):
    return ((core * SIDE + x) * SIDE + y) * SIDE + z


def lines():
    r = range(SIDE)
    return [[device(0, a, g, z) for a in r] for g in r for z in r] + [
        [device(1, g, a, z) for a in r] for g in r for z in r
    ]


def planes():
    r = range(SIDE)
    return [[device(0, a, g, z) for g in r for z in r] for a in r] + [
        [device(1, g, a, z) for g in r for z in r] for a in r
    ]


def shift(value, d):
    pairs = [(group[i], group[(i + d) % SIDE]) for group in lines() for i in range(SIDE)]
    return lax.ppermute(value, BOTH, pairs)


def plane_swap(value):
    return lax.all_to_all(value, BOTH, 0, 0, axis_index_groups=planes())


def natural(core, a, g):
    return jnp.where(core == 0, SIDE * a + g, SIDE * g + a)


def lay_out(place_ref, pieces, full_ref):
    core, me = place_ref[0], place_ref[1]
    for d, piece in enumerate(pieces):
        a = (me + SIDE - d) & (SIDE - 1)
        for g in range(SIDE):
            at = pl.multiple_of(natural(core, a, g) * BLOCK, BLOCK)
            full_ref[pl.ds(at, BLOCK), :] = piece[g * BLOCK : (g + 1) * BLOCK, :]


def usable_rows(place_ref, group, rows, base=0):
    slot = lax.broadcasted_iota(jnp.int32, (rows, 1), 0) + base
    first = ((slot < A) & (slot < place_ref[2])) | ((slot >= A) & (slot < 2 * A) & (slot - A < place_ref[3]))
    first = first.astype(f32)
    second = (slot < place_ref[4]).astype(f32)
    if isinstance(group, int):
        return second if group else first
    return jnp.where(group == 0, first, second)


def own_rows(win):
    row = lax.broadcasted_iota(jnp.int32, (WIN, 1), 0) + (WINDOWS[win] - win * A)
    return ((row >= 0) & (row < A)).astype(f32)


def key_bias(place_ref, win=None):
    if win is None:
        key = lax.broadcasted_iota(jnp.int32, (1, S), 1)
        return jnp.where(key < place_ref[4], 0.0, NEG)
    key = lax.broadcasted_iota(jnp.int32, (1, WIN), 1) + (WINDOWS[win] - win * A)
    return jnp.where((key >= 0) & (key < place_ref[2 + win]), 0.0, NEG)


def exact_dot(a, b):
    high = a.astype(bf16)
    rest = a - high.astype(f32)
    mid = rest.astype(bf16)
    low = (rest - mid.astype(f32)).astype(bf16)
    b = b.astype(bf16)
    return dot(high, b) + dot(mid, b) + dot(low, b)


def spots(core, shape, full, part):
    l = lax.broadcasted_iota(jnp.int32, shape, full)
    m = lax.broadcasted_iota(jnp.int32, shape, part)
    q = (m * 2731) >> 16
    return l == m + FR * (q + core)


def spots_t(core):
    return spots(core, (DC, D), 1, 0)


def params(**kw):
    return pltpu.CompilerParams(vmem_limit_bytes=VMEM_LIMIT, **kw)


def cost(flops, bytes_accessed, transcendentals=0):
    return pl.CostEstimate(
        flops=int(flops), bytes_accessed=int(bytes_accessed), transcendentals=int(transcendentals)
    )


def dot(a, b):
    return jnp.dot(a, b, preferred_element_type=f32)


def dot_t(a, b):
    return lax.dot_general(a, b, (((1,), (1,)), ((), ())), preferred_element_type=f32)


def t_dot(a, b):
    return lax.dot_general(a, b, (((0,), (0,)), ((), ())), preferred_element_type=f32)


def stats(z):
    mean_val = jnp.mean(z, axis=-1, keepdims=True)
    centred = z - mean_val
    variance = jnp.mean(centred * centred, axis=-1, keepdims=True)
    inv_std = lax.rsqrt(variance + EPS_NORM)
    return centred * inv_std, inv_std


def norm_back(grad, normed, inv_std, gain):
    e = grad * gain
    return inv_std * (
        e
        - jnp.mean(e, axis=-1, keepdims=True)
        - normed * jnp.mean(e * normed, axis=-1, keepdims=True)
    )


def swap_halves(u):
    lanes = u.shape[1]
    lane = lax.broadcasted_iota(jnp.int32, u.shape, 1)
    up = pltpu.roll(u, lanes - HD // 2, 1)
    down = pltpu.roll(u, HD // 2, 1)
    return jnp.where((lane & (HD - 1)) < HD // 2, up, down)


TURN = 1.5707963267948966


def sin_cos(a):
    k = jnp.floor(a * (1.0 / TURN) + 0.5)
    r = ((a - k * 1.5703125) - k * 4.837512969970703125e-4) - k * 7.54978995489188216e-8
    z = r * r
    s = ((-1.9515295891e-4 * z + 8.3321608736e-3) * z - 1.6666654611e-1) * z * r + r
    c = ((2.443315711809948e-5 * z - 1.388731625493765e-3) * z + 4.166664568298827e-2) * z * z - 0.5 * z + 1.0
    quarter = k.astype(jnp.int32)
    odd = (quarter & 1) == 1
    sine = jnp.where(odd, c, s)
    cosine = jnp.where(odd, s, c)
    sine = jnp.where((quarter & 2) == 0, sine, -sine)
    cosine = jnp.where(((quarter + 1) & 2) == 0, cosine, -cosine)
    return sine, cosine


def share_kernel(place_ref, w_ref, v_ref, f_ref, out_ref, fc2_ref):
    core = place_ref[0]
    w = w_ref[...].astype(bf16)
    cols = []
    for p in range(PAIRS):
        for i in range(3):
            at = i * D + p * 128
            cols.append(jnp.where(core == 0, w[:, at : at + 128], w[:, at + DC : at + DC + 128]))
    v = jnp.concatenate([v_ref[...], jnp.zeros((128 - v_ref.shape[0], KR), f32)], axis=0)
    v = jnp.concatenate([v, jnp.zeros((128, 128 - KR), f32)], axis=1)
    cols.append(v.T[:KR, :].astype(bf16))
    share = jnp.concatenate(cols, axis=1)
    for n in range(PLANE):
        out_ref[n] = share
    fc2_ref[...] = jnp.where(core == 0, f_ref[:FR, :], f_ref[FR:, :]).astype(bf16)


def share_call(place, w, vectors, w_fc2):
    whole = lambda a: pl.BlockSpec(a.shape, lambda i, c: (0, 0))
    return pl.pallas_call(
        share_kernel,
        grid_spec=pltpu.PrefetchScalarGridSpec(
            num_scalar_prefetch=1,
            grid=(1,),
            in_specs=[whole(w), whole(vectors), whole(w_fc2)],
            out_specs=[
                pl.BlockSpec((PLANE, KR, 3 * DC + 128), lambda i, c: (0, 0, 0)),
                pl.BlockSpec((FR, D), lambda i, c: (0, 0)),
            ],
        ),
        out_shape=[
            jax.ShapeDtypeStruct((PLANE, KR, 3 * DC + 128), bf16),
            jax.ShapeDtypeStruct((FR, D), bf16),
        ],
        compiler_params=params(),
        cost_estimate=cost(KR * D * 3, 1e6),
    )(place, w, vectors, w_fc2)


def gy_kernel(place_ref, c_ref, co_ref, gy_ref):
    i = pl.program_id(0)
    keep = usable_rows(place_ref, i ^ place_ref[0], S)
    gy_ref[...] = (jnp.where(i == 0, c_ref[...], co_ref[...]).astype(f32) * keep).astype(bf16)


def gy_call(place, c, co):
    whole = pl.BlockSpec((S, D), lambda i, c: (0, 0))
    return pl.pallas_call(
        gy_kernel,
        grid_spec=pltpu.PrefetchScalarGridSpec(
            num_scalar_prefetch=1,
            grid=(CORES,),
            in_specs=[whole, whole],
            out_specs=pl.BlockSpec((S, D), lambda i, c: (i, 0)),
        ),
        out_shape=jax.ShapeDtypeStruct((T, D), bf16),
        compiler_params=params(),
        cost_estimate=cost(4 * T * D, T * D * 4),
    )(place, c, co)


def qkv_kernel(
    place_ref, x_ref, xo_ref, ints_ref, w0, w1, w2, w3, v0, v1, v2, v3,
    vec_ref, ht_ref, cos_ref, sin_ref, q_out, k_out, v_out, b1_ref, pos_ref,
    w_s, full_s, rows_s, freq_s,
):
    core = place_ref[0]

    @pl.when(pl.program_id(0) == 0)
    def _():
        lay_out(place_ref, (w0, w1, w2, w3), w_s)
        lay_out(place_ref, (v0, v1, v2, v3), full_s)
        rows_s[...] = full_s[...].astype(f32).T[:16, :]
        vec_ref[...] = rows_s[...]
        late = rows_s[8:16, :].astype(bf16)
        units = dot(late, spots(core, (D, DC), 0, 1).astype(bf16))
        for r in range(FC // DC):
            b1_ref[:, r * DC : (r + 1) * DC] = units[2 + r : 3 + r, :]
        src = lax.broadcasted_iota(jnp.int32, (D, DC), 0)
        dst = lax.broadcasted_iota(jnp.int32, (D, DC), 1)
        want = core * (DC // 2) + (dst // HD) * (HD // 2) + (dst & (HD // 2 - 1))
        freq_s[0:8, :] = dot(late, (src == want).astype(bf16))
        freq_s[8:16, :] = dot(late, (src == want + D // 2).astype(bf16))

    i = pl.program_id(0)
    x = jnp.where(i < pl.num_programs(0) // CORES, x_ref[...], xo_ref[...])
    h = stats(x.astype(f32))[0] * rows_s[0:1, :] + rows_s[1:2, :]
    pos = ints_ref[...].astype(f32).T
    pos_ref[...] = pos
    ht_ref[...] = h.T.astype(bf16)
    acc = dot(h.astype(bf16), w_s[...])
    angle = pos[:, 1:2] * freq_s[1:2, :] + pos[:, 0:1] * freq_s[9:10, :]
    lane = lax.broadcasted_iota(jnp.int32, (1, DC), 1)
    sign = jnp.where((lane & (HD - 1)) < HD // 2, -1.0, 1.0)
    small = jnp.max(jnp.abs(angle)) < 8000.0

    @pl.when(small)
    def _():
        sine, cosine = sin_cos(angle)
        cos_ref[...] = cosine
        sin_ref[...] = sine * sign

    @pl.when(jnp.logical_not(small))
    def _():
        cos_ref[...] = jnp.cos(angle)
        sin_ref[...] = jnp.sin(angle) * sign

    cosine, sine = cos_ref[...], sin_ref[...]
    at = pl.ds(pl.multiple_of(core * DC, DC), DC)
    part = lambda i: jnp.concatenate([acc[:, (3 * p + i) * 128 : (3 * p + i + 1) * 128] for p in range(PAIRS)], axis=1)
    q = part(0) + rows_s[4:5, at]
    k = part(1) + rows_s[5:6, at]
    q_out[...] = ((q * cosine + swap_halves(q) * sine) * HD ** (-0.5)).astype(bf16)
    k_out[...] = (k * cosine + swap_halves(k) * sine).astype(bf16)
    v_out[...] = (part(2) + rows_s[6:7, at]).astype(bf16)


def qkv_call(place, x, xo, ints, pieces):
    rows = S
    tile = lambda n: pl.BlockSpec((rows, n), lambda i, c: (i, 0))
    keep = lambda *n: pl.BlockSpec(n, lambda i, c: (0,) * len(n))
    return pl.pallas_call(
        qkv_kernel,
        grid_spec=pltpu.PrefetchScalarGridSpec(
            num_scalar_prefetch=1,
            grid=(CORES,),
            in_specs=[keep(S, D), keep(S, D), pl.BlockSpec((None, 8, S), lambda i, c: (i, 0, 0))]
            + [keep(QUARTER, 3 * DC)] * 4
            + [pl.BlockSpec((QUARTER, 128), lambda i, c: (0, 3 * DC // 128))] * 4,
            out_specs=[keep(16, D), pl.BlockSpec((None, D, rows), lambda i, c: (i, 0, 0))]
            + [tile(DC)] * 5
            + [keep(1, FC), tile(8)],
            scratch_shapes=[
                pltpu.VMEM((D, 3 * DC), bf16),
                pltpu.VMEM((D, 128), bf16),
                pltpu.VMEM((16, D), f32),
                pltpu.VMEM((16, DC), f32),
            ],
        ),
        out_shape=[
            jax.ShapeDtypeStruct((16, D), f32),
            jax.ShapeDtypeStruct((CORES, D, S), bf16),
            jax.ShapeDtypeStruct((T, DC), f32),
            jax.ShapeDtypeStruct((T, DC), f32),
            *[jax.ShapeDtypeStruct((T, DC), bf16)] * 3,
            jax.ShapeDtypeStruct((1, FC), f32),
            jax.ShapeDtypeStruct((T, 8), f32),
        ],
        compiler_params=params(),
        cost_estimate=cost(2 * T * D * 3 * DC + 60 * T * DC, T * D * 6 + D * 3 * DC * 2 + T * DC * 14),
    )(place, x, xo, ints, *pieces, *pieces)


def softmax_head(q, k, v, mine, bias):
    s = dot_t(jnp.where(mine, q, jnp.zeros_like(q)), k) + bias
    e = jnp.exp(s - jnp.max(s, axis=-1, keepdims=True))
    p = e * (1.0 / jnp.sum(e, axis=-1, keepdims=True))
    return p


def attn_fwd_kernel(
    place_ref, q0, k0, v0, q1, k1, v1, o_ref, p0_ref, p1_ref
):
    lane = lax.broadcasted_iota(jnp.int32, (1, 2 * HD), 1)
    low = lane < HD
    q, k, v = q1[0], k1[0], v1[0]
    mixes = []
    bias = key_bias(place_ref)
    for head, mine in ((0, low), (1, ~low)):
        p = softmax_head(q, k, v, mine, bias).astype(bf16)
        p1_ref[head] = p
        mixes.append(dot(p, v))
    mix = jnp.where(low, mixes[0], mixes[1])
    o_ref[1] = jnp.where(usable_rows(place_ref, 1, S) > 0, mix, v.astype(f32)).astype(bf16)
    o_ref[0] = v0[0]
    for win, base in enumerate(WINDOWS):
        q, k, v = (r[0, base : base + WIN, :] for r in (q0, k0, v0))
        own = own_rows(win)
        bias = key_bias(place_ref, win)
        mixes = []
        for head, mine in ((0, low), (1, ~low)):
            p = softmax_head(q, k, v, mine, bias)
            p = (p * own).astype(bf16)
            p0_ref[head, win] = p
            mixes.append(dot(p, v))
        mix = jnp.where(low, mixes[0], mixes[1])
        use = (own * usable_rows(place_ref, 0, WIN, base)) > 0
        before = o_ref[0, base : base + WIN, :].astype(f32)
        o_ref[0, base : base + WIN, :] = jnp.where(use, mix, before).astype(bf16)


def attn_fwd_call(place, q, k, v):
    block = lambda g: pl.BlockSpec((1, S, 2 * HD), lambda p, c: (g ^ c[0], 0, p))
    q, k, v = (a.reshape(CORES, S, DC) for a in (q, k, v))
    return pl.pallas_call(
        attn_fwd_kernel,
        grid_spec=pltpu.PrefetchScalarGridSpec(
            num_scalar_prefetch=1,
            grid=(PAIRS,),
            in_specs=[block(0)] * 3 + [block(1)] * 3,
            out_specs=[
                pl.BlockSpec((CORES, S, 2 * HD), lambda p, c: (0, 0, p)),
                pl.BlockSpec((2, 2, WIN, WIN), lambda p, c: (p, 0, 0, 0)),
                pl.BlockSpec((2, S, S), lambda p, c: (p, 0, 0)),
            ],
        ),
        out_shape=[
            jax.ShapeDtypeStruct((CORES, S, DC), bf16),
            jax.ShapeDtypeStruct((HC, 2, WIN, WIN), bf16),
            jax.ShapeDtypeStruct((HC, S, S), bf16),
        ],
        compiler_params=params(),
        cost_estimate=cost(4 * HC * (S * S + 2 * WIN * WIN) * 128, 12e6, HC * S * S),
    )(place, q, k, v, q, k, v)


def proj_kernel(place_ref, mine_ref, other_ref, x_ref, xo_ref, w0, w1, w2, w3, v_ref, after_ref, n2_ref, r2_ref, h2_ref, w_s):
    @pl.when(pl.program_id(0) == 0)
    def _():
        lay_out(place_ref, (w0, w1, w2, w3), w_s)

    core = place_ref[0]
    at = lambda c: pl.ds(pl.multiple_of(c * DC, DC), DC)
    branch = dot(mine_ref[0], w_s[at(core), :]) + dot(other_ref[0], w_s[at(1 - core), :])
    x = jnp.where(pl.program_id(0) < pl.num_programs(0) // CORES, x_ref[...], xo_ref[...])
    after = x.astype(f32) + (branch + v_ref[7:8, :])
    normed, inv_std = stats(after)
    n2_ref[...] = normed
    r2_ref[...] = jnp.broadcast_to(inv_std, r2_ref.shape)

    @pl.when(pl.program_id(0) < pl.num_programs(0) // CORES)
    def _():
        after_ref[...] = after

    h2_ref[...] = (normed * v_ref[2:3, :] + v_ref[3:4, :]).astype(bf16)


def proj_call(place, mine, other, x, xo, pieces, vec):
    rows = 288
    half = S // rows
    tile = lambda n: pl.BlockSpec((rows, n), lambda i, c: (i, 0))
    whole = lambda a: pl.BlockSpec(a.shape, lambda i, c: (0,) * a.ndim)
    return pl.pallas_call(
        proj_kernel,
        grid_spec=pltpu.PrefetchScalarGridSpec(
            num_scalar_prefetch=1,
            grid=(T // rows,),
            in_specs=[
                pl.BlockSpec((1, rows, DC), lambda i, c: ((i // half) ^ c[0], i % half, 0)),
                pl.BlockSpec((1, rows, DC), lambda i, c: ((i // half) ^ c[0], i % half, 0)),
                pl.BlockSpec((rows, D), lambda i, c: (jnp.minimum(i, half - 1), 0)),
                pl.BlockSpec((rows, D), lambda i, c: (jnp.maximum(i - half, 0), 0)),
            ]
            + [pl.BlockSpec((QUARTER, D), lambda i, c: (0, FC // D))] * 4
            + [whole(vec)],
            out_specs=[pl.BlockSpec((rows, D), lambda i, c: (jnp.minimum(i, half - 1), 0)), tile(D), tile(8), tile(D)],
            scratch_shapes=[pltpu.VMEM((D, D), bf16)],
        ),
        out_shape=[
            jax.ShapeDtypeStruct((S, D), f32),
            jax.ShapeDtypeStruct((T, D), f32),
            jax.ShapeDtypeStruct((T, 8), f32),
            jax.ShapeDtypeStruct((T, D), bf16),
        ],
        compiler_params=params(),
        cost_estimate=cost(2 * T * D * D, T * D * 10 + D * D * 2),
    )(place, mine, other, x, xo, *pieces, vec)


PACK = 4 * DC + 128
K0 = (2.0 / 3.141592653589793) ** 0.5
FT = 768


def gelu_slope(u):
    sq = u * u
    th = jnp.tanh(u * (K0 + (K0 * 0.044715) * sq))
    half = 0.5 + 0.5 * th
    return u * half, half + (u * (half - half * half)) * (2 * K0 + (6 * K0 * 0.044715) * sq)


def mlp_kernel(
    place_ref, h2_ref, gy_ref, w10, w11, w12, w13, w2_ref, b1_ref, mlp_ref, mlpo_ref, gh2b_ref, act_ref, gup_ref, gb1_ref, w1_s
):
    i = pl.program_id(0)

    @pl.when(i == 0)
    def _():
        lay_out(place_ref, (w10, w11, w12, w13), w1_s)
        gb1_ref[...] = jnp.zeros_like(gb1_ref)

    for f in range(FC // FT):
        c = slice(f * FT, (f + 1) * FT)
        act, slope = gelu_slope(dot(h2_ref[...], w1_s[:, c]) + b1_ref[:, c])
        act_ref[:, c] = act.astype(bf16)
        gup = (dot_t(gy_ref[...], w2_ref[c, :]) * slope).astype(bf16)
        gup_ref[:, c] = gup
        gb1_ref[:, c] += jnp.sum(gup.astype(f32), axis=0, keepdims=True)
    gh2b_ref[...] = dot_t(gup_ref[...], w1_s[...]).astype(bf16)
    mlp = dot(act_ref[...], w2_ref[...])
    half = pl.num_programs(0) // CORES

    @pl.when(i < half)
    def _():
        mlp_ref[...] = mlp

    @pl.when(i >= half)
    def _():
        mlpo_ref[...] = mlp


def mlp_call(place, h2, gy, pieces, w2, b1):
    rows = 288
    half = S // rows
    tile = lambda n: pl.BlockSpec((rows, n), lambda i, c: (i, 0))
    whole = lambda a: pl.BlockSpec(a.shape, lambda i, c: (0,) * a.ndim)
    return pl.pallas_call(
        mlp_kernel,
        grid_spec=pltpu.PrefetchScalarGridSpec(
            num_scalar_prefetch=1,
            grid=(T // rows,),
            in_specs=[tile(D), tile(D)]
            + [pl.BlockSpec((QUARTER, FC), lambda i, c: (0, 0))] * 4
            + [whole(w2), whole(b1)],
            out_specs=[
                pl.BlockSpec((rows, D), lambda i, c: (jnp.minimum(i, half - 1), 0)),
                pl.BlockSpec((rows, D), lambda i, c: (jnp.maximum(i - half, 0), 0)),
                tile(D),
                tile(FC),
                tile(FC),
                pl.BlockSpec((1, FC), lambda i, c: (0, 0)),
            ],
            scratch_shapes=[pltpu.VMEM((D, FC), bf16)],
        ),
        out_shape=[
            jax.ShapeDtypeStruct((S, D), f32),
            jax.ShapeDtypeStruct((S, D), f32),
            jax.ShapeDtypeStruct((T, D), bf16),
            jax.ShapeDtypeStruct((T, FC), bf16),
            jax.ShapeDtypeStruct((T, FC), bf16),
            jax.ShapeDtypeStruct((1, FC), f32),
        ],
        compiler_params=params(),
        cost_estimate=cost(8 * T * D * FC, 30e6, T * FC),
    )(place, h2, gy, *pieces, w2, b1)


def by_line(place_ref, value, block, out_ref):
    core = place_ref[0]
    for n in range(PLANE):
        to = jnp.where(core == 0, n, (n % SIDE) * SIDE + n // SIDE)
        out_ref[pl.ds(pl.multiple_of(to * block, block), block), :] = value[n * block : (n + 1) * block, :].astype(bf16)


def fc2_grad_kernel(place_ref, act_ref, gy_ref, out_ref):
    value = t_dot(act_ref[...], gy_ref[...])
    block = SIDE * FR
    for n in range(FT // block):
        m = pl.program_id(0) * (FT // block) + n
        to = jnp.where(place_ref[0] == 0, m, (m & (SIDE - 1)) * SIDE + m // SIDE)
        out_ref[pl.ds(pl.multiple_of(to * block, block), block), :] = value[n * block : (n + 1) * block, :].astype(bf16)


def fc2_grad_call(place, act, gy):
    return pl.pallas_call(
        fc2_grad_kernel,
        grid_spec=pltpu.PrefetchScalarGridSpec(
            num_scalar_prefetch=1,
            grid=(FC // FT,),
            in_specs=[pl.BlockSpec((T, FT), lambda i, c: (0, i)), pl.BlockSpec((T, D), lambda i, c: (0, 0))],
            out_specs=pl.BlockSpec((FC, D), lambda i, c: (0, 0)),
        ),
        out_shape=jax.ShapeDtypeStruct((FC, D), bf16),
        compiler_params=params(),
        cost_estimate=cost(2 * T * D * FC, T * (D + FC) * 2 + D * FC * 2),
    )(place, act, gy)


def mid_kernel(
    place_ref, h2_ref, gup_ref, n2_ref, r2_ref, gy_ref, gh2_ref, other_ref, v_ref, gw_ref, ga_ref, gab_ref, sums_ref
):
    i = pl.program_id(0)
    by_line(place_ref, t_dot(h2_ref[...], gup_ref[...]), BLOCK, gw_ref)
    normed, inv_std = n2_ref[...], r2_ref[:, 0:1]
    gh2 = gh2_ref[...].astype(f32) + other_ref[...].astype(f32)
    gy = gy_ref[...].astype(f32)
    ga = gy + norm_back(gh2, normed, inv_std, v_ref[2:3, :])
    gab = ga.astype(bf16)
    gab_ref[...] = gab
    mine = (i < pl.num_programs(0) // CORES).astype(f32)
    sums = [
        mine * jnp.sum(a, axis=0, keepdims=True) for a in (gh2 * normed, gh2, gab.astype(f32), gy)
    ] + [jnp.zeros((4, D), f32)]
    sums = jnp.concatenate(sums, axis=0)

    @pl.when(i == 0)
    def _():
        sums_ref[...] = sums

    @pl.when(i > 0)
    def _():
        sums_ref[...] += sums

    @pl.when(i < pl.num_programs(0) // CORES)
    def _():
        ga_ref[...] = ga


def mid_call(place, h2, gup, n2, r2, gy, gh2, other, vec):
    rows = 288
    half = S // rows
    cols = FC * rows // T
    tile = lambda n: pl.BlockSpec((rows, n), lambda i, c: (i, 0))
    flipped = pl.BlockSpec((rows, D), lambda i, c: ((i + half) % (2 * half), 0))
    whole = lambda a: pl.BlockSpec(a.shape, lambda i, c: (0,) * a.ndim)
    return pl.pallas_call(
        mid_kernel,
        grid_spec=pltpu.PrefetchScalarGridSpec(
            num_scalar_prefetch=1,
            grid=(T // rows,),
            in_specs=[whole(h2), pl.BlockSpec((T, cols), lambda i, c: (0, i))]
            + [tile(D), tile(8), tile(D), tile(D), flipped, whole(vec)],
            out_specs=[
                pl.BlockSpec((D, cols), lambda i, c: (0, i)),
                pl.BlockSpec((rows, D), lambda i, c: (jnp.minimum(i, half - 1), 0)),
                tile(D),
                pl.BlockSpec((8, D), lambda i, c: (0, 0)),
            ],
        ),
        out_shape=[
            jax.ShapeDtypeStruct((D, FC), bf16),
            jax.ShapeDtypeStruct((S, D), f32),
            jax.ShapeDtypeStruct((T, D), bf16),
            jax.ShapeDtypeStruct((8, D), f32),
        ],
        compiler_params=params(),
        cost_estimate=cost(2 * T * D * FC, T * D * 18 + T * FC * 2 + D * FC * 2),
    )(place, h2, gup, n2, r2, gy, gh2, other, vec)


def back_head(q_t, k, v, do, do_t, delta, p, mine, head):
    gp = dot_t(jnp.where(mine, do, jnp.zeros_like(do)), v)
    gs = (p.astype(f32) * (gp - delta)).astype(bf16)
    at = slice(head * HD, (head + 1) * HD)
    return dot(gs, k), dot(q_t[at, :], gs), dot(do_t[at, :], p)


def deltas(do, o, low):
    prod = do.astype(f32) * o.astype(f32)
    d0 = jnp.sum(jnp.where(low, prod, 0.0), axis=-1, keepdims=True)
    d1 = jnp.sum(jnp.where(low, 0.0, prod), axis=-1, keepdims=True)
    return d0, d1


def attn_bwd_kernel(
    place_ref,
    q0, k0, v0, o0, p0, cos0, sin0, pos0,
    q1, k1, v1, o1, p1, cos1, sin1, pos1,
    h1t_ref, ga_ref, cols_ref, mine_ref, other_ref, y0, y1, y2, y3, w0, w1, w2, w3,
    x_ref, xo_ref, mid_ref, gb1_ref,
    gw0, gw1, gw2, gw3, gh_ref, gho_ref,
    gq_s, gk_s, gv_s, gw_s, y_s, do_s, gqkv_s, att_s, rows_s, full_s, w_s,
):
    lane = lax.broadcasted_iota(jnp.int32, (1, 2 * HD), 1)
    low = lane < HD
    pair = pl.program_id(0)
    core = place_ref[0]

    @pl.when(pair == 0)
    def _():
        lay_out(place_ref, (y0, y1, y2, y3), y_s)

    wy = y_s[pl.ds(pl.multiple_of(core * DC + pair * 2 * HD, 2 * HD), 2 * HD), :]
    for frame in range(CORES):
        do_s[frame] = dot_t(ga_ref[frame], wy).astype(bf16)

    def finish(frame, q, k, cos_ref, sin_ref, pos_ref):
        cosine, sine = cos_ref[0], sin_ref[0]
        gq = gq_s[...] * HD ** (-0.5)
        gk = gk_s[...]
        sq, sk = swap_halves(gq), swap_halves(gk)
        turn = (q.astype(f32) * HD**0.5) * sq + k.astype(f32) * sk
        gq = (gq * cosine - sq * sine).astype(bf16)
        gk = (gk * cosine - sk * sine).astype(bf16)
        gv = gv_s[...].astype(bf16)
        for i, g in enumerate((gq, gk, gv)):
            gqkv_s[frame ^ core, :, pl.ds(pl.multiple_of(pair * 6 * HD + i * 2 * HD, 2 * HD), 2 * HD)] = g
        pos = pos_ref[0]
        col = jnp.sum(turn * pos[:, 1:2], axis=0, keepdims=True)
        row = jnp.sum(turn * pos[:, 0:1], axis=0, keepdims=True)
        bias = [jnp.sum(g.astype(f32), axis=0, keepdims=True) for g in (gq, gk, gv)]
        return jnp.concatenate([col, row] + bias, axis=0)

    q, k, v, do = q1[0], k1[0], v1[0], do_s[1 ^ core]
    d = deltas(do, o1[0], low)
    q_t, do_t = q.astype(f32).T.astype(bf16), do.astype(f32).T.astype(bf16)
    out = [
        back_head(q_t, k, v, do, do_t, d[head], p1[head], mine, head)
        for head, mine in ((0, low), (1, ~low))
    ]
    gq_s[...] = jnp.where(low, out[0][0], out[1][0])
    gk_s[...] = jnp.concatenate([out[0][1], out[1][1]], axis=0).T
    gv_s[...] = jnp.concatenate([out[0][2], out[1][2]], axis=0).T
    sums1 = finish(1, q, k, cos1, sin1, pos1)
    gq_s[...] = jnp.zeros_like(gq_s)
    gk_s[...] = jnp.zeros_like(gk_s)
    gv_s[...] = jnp.zeros_like(gv_s)
    for win, base in enumerate(WINDOWS):
        at = pl.ds(base, WIN)
        q, k, v, o = (r[0, at, :] for r in (q0, k0, v0, o0))
        do = do_s[core, at, :]
        d = deltas(do, o, low)
        q_t, do_t = q.astype(f32).T.astype(bf16), do.astype(f32).T.astype(bf16)
        out = [
            back_head(q_t, k, v, do, do_t, d[head], p0[head, win], mine, head)
            for head, mine in ((0, low), (1, ~low))
        ]
        gq_s[at, :] += jnp.where(low, out[0][0], out[1][0])
        gk_s[at, :] += jnp.concatenate([out[0][1], out[1][1]], axis=0).T
        gv_s[at, :] += jnp.concatenate([out[0][2], out[1][2]], axis=0).T
    sums0 = finish(0, q0[0], k0[0], cos0, sin0, pos0)
    att_s[pair, 0:5, :] = sums0 + sums1

    gw = jnp.zeros((D, 6 * HD), f32)
    gw_mine = jnp.zeros((2 * HD, DC), f32)
    gw_other = jnp.zeros((2 * HD, DC), f32)
    for frame in range(CORES):
        cols = cols_ref[frame].astype(f32).T.astype(bf16)
        gw_mine += dot(cols, mine_ref[frame ^ core])
        gw_other += dot(cols, other_ref[frame ^ core])
        gw += dot(h1t_ref[frame], gqkv_s[frame, :, pl.ds(pl.multiple_of(pair * 6 * HD, 6 * HD), 6 * HD)])
    gw_s[:, : 6 * HD] = gw.astype(bf16)
    at = lambda c: pl.ds(pl.multiple_of(c * DC, DC), DC)
    gw_s[at(core), 6 * HD :] = gw_mine.T.astype(bf16)
    gw_s[at(1 - core), 6 * HD :] = gw_other.T.astype(bf16)
    to_chips(place_ref, gw_s, (gw0, gw1, gw2, gw3), pl.ds(pl.multiple_of(pair * 8 * HD, 8 * HD), 8 * HD))

    @pl.when(pair == PAIRS - 1)
    def _():
        lay_out(place_ref, (w0, w1, w2, w3), w_s)
        rows_s[...] = jnp.zeros_like(rows_s)
        for frame, x, out in ((0, x_ref, gh_ref), (1, xo_ref, gho_ref)):
            for half in range(2):
                at = slice(half * (S // 2), (half + 1) * (S // 2))
                gh = dot_t(gqkv_s[frame, at, :], w_s[...])
                out[at, :] = gh
                normed, _ = stats(x[at, :].astype(f32))
                rows_s[0:1, :] += jnp.sum(gh * normed, axis=0, keepdims=True)
                rows_s[1:2, :] += jnp.sum(gh, axis=0, keepdims=True)
        rows_s[2:4, :] = mid_ref[0:2, :]
        rows_s[7:9, :] = mid_ref[2:4, :]
        att = jnp.concatenate([att_s[p] for p in range(PAIRS)], axis=1)
        rows_s[4:7, pl.ds(pl.multiple_of(core * DC, DC), DC)] = att[2:5, :]
        src = lax.broadcasted_iota(jnp.int32, (DC, D), 0)
        dst = lax.broadcasted_iota(jnp.int32, (DC, D), 1)
        want = core * (DC // 2) + (src // HD) * (HD // 2) + (src & (HD // 2 - 1))
        side = lax.broadcasted_iota(jnp.int32, (1, DC), 1)
        turn = jnp.where((side & (HD - 1)) < HD // 2, att, -att)
        rows_s[9:10, :] = exact_dot(turn, dst == want)[0:1, :] + exact_dot(turn, dst == want + D // 2)[1:2, :]
        gb1 = jnp.concatenate([gb1_ref[:, r * DC : (r + 1) * DC] for r in range(FC // DC)] * 2, axis=0)
        rows_s[10:14, :] = exact_dot(gb1, spots_t(core))[:4, :]
        full_s[...] = rows_s[...].T.astype(bf16)
        to_chips(place_ref, full_s, (gw0, gw1, gw2, gw3), slice(4 * DC, PACK))


def to_chips(place_ref, full_ref, outs, cols):
    for d, out in enumerate(outs):
        a = (place_ref[1] + d) & (SIDE - 1)
        for g in range(SIDE):
            at = pl.multiple_of(natural(place_ref[0], a, g) * BLOCK, BLOCK)
            out[g * BLOCK : (g + 1) * BLOCK, cols] = full_ref[pl.ds(at, BLOCK), :]


def attn_bwd_call(
    place, q, k, v, ga, mine, other, p0, p1, cosine, sine, pos, h1t, pieces, proj_pieces, x, xo, mid, gb1
):
    q, k, v, cosine, sine, pos, ga = (a.reshape(CORES, S, -1) for a in (q, k, v, cosine, sine, pos, ga))
    block = lambda g: pl.BlockSpec((1, S, 2 * HD), lambda p, c: (g ^ c[0], 0, p))
    own = lambda g: pl.BlockSpec((1, S, 2 * HD), lambda p, c: (g, 0, p))
    at = lambda g: pl.BlockSpec((1, S, 8), lambda p, c: (g ^ c[0], 0, 0))
    whole = lambda a: pl.BlockSpec(a.shape, lambda p, c: (0,) * a.ndim)
    keep = lambda *n: pl.BlockSpec(n, lambda p, c: (0,) * len(n))
    return pl.pallas_call(
        attn_bwd_kernel,
        grid_spec=pltpu.PrefetchScalarGridSpec(
            num_scalar_prefetch=1,
            grid=(PAIRS,),
            in_specs=[block(0)] * 3
            + [own(0), pl.BlockSpec((2, 2, WIN, WIN), lambda p, c: (p, 0, 0, 0))]
            + [block(0)] * 2
            + [at(0)]
            + [block(1)] * 3
            + [own(1), pl.BlockSpec((2, S, S), lambda p, c: (p, 0, 0))]
            + [block(1)] * 2
            + [at(1)]
            + [whole(h1t), whole(ga)]
            + [pl.BlockSpec((CORES, S, 2 * HD), lambda p, c: (0, 0, PAIRS * c[0] + p))]
            + [whole(mine), whole(other)]
            + [pl.BlockSpec((QUARTER, D), lambda p, c: (0, FC // D))] * 4
            + [keep(QUARTER, 3 * DC)] * 4
            + [whole(a) for a in (x, xo, mid, gb1)],
            out_specs=[keep(QUARTER, PACK)] * 4 + [keep(S, D)] * 2,
            scratch_shapes=[pltpu.VMEM((S, 2 * HD), f32)] * 3
            + [pltpu.VMEM((D, 8 * HD), bf16), pltpu.VMEM((D, D), bf16), pltpu.VMEM((CORES, S, 2 * HD), bf16)]
            + [pltpu.VMEM((CORES, S, 3 * DC), bf16), pltpu.VMEM((PAIRS, 8, 2 * HD), f32)]
            + [pltpu.VMEM((128, D), f32), pltpu.VMEM((D, 128), bf16), pltpu.VMEM((D, 3 * DC), bf16)],
        ),
        out_shape=[
            *[jax.ShapeDtypeStruct((QUARTER, PACK), bf16)] * 4,
            *[jax.ShapeDtypeStruct((S, D), f32)] * 2,
        ],
        compiler_params=params(),
        cost_estimate=cost(10 * HC * S * S * 128 + 4 * T * D * 4 * DC, 36e6),
    )(
        place,
        q, k, v, mine, p0, cosine, sine, pos,
        q, k, v, mine, p1, cosine, sine, pos,
        h1t, ga, ga, mine, other, *proj_pieces, *pieces, x, xo, mid, gb1,
    )


def last_kernel(x_ref, ga_ref, gh_ref, other_ref, after_ref, mlp_ref, mlpo_ref, v_ref, gt_ref, out_ref):
    normed, inv_std = stats(x_ref[...].astype(f32))
    gt_ref[...] = ga_ref[...] + norm_back(gh_ref[...] + other_ref[...], normed, inv_std, v_ref[0:1, :])
    out_ref[...] = (after_ref[...] + (mlp_ref[...] + mlpo_ref[...] + v_ref[8:9, :])).astype(bf16)


def last_call(x, ga, gh, other, after, mlp, mlp_other, vec):
    rows = 288
    tile = lambda n: pl.BlockSpec((rows, n), lambda i: (i, 0))
    return pl.pallas_call(
        last_kernel,
        grid=(S // rows,),
        in_specs=[tile(D)] * 7 + [pl.BlockSpec(vec.shape, lambda i: (0, 0))],
        out_specs=[tile(D), tile(D)],
        out_shape=[jax.ShapeDtypeStruct((S, D), f32), jax.ShapeDtypeStruct((S, D), bf16)],
        compiler_params=params(),
        cost_estimate=cost(30 * S * D, S * D * 28),
    )(x, ga, gh, other, after, mlp, mlp_other, vec)


WIDE = PACK + 2 * FC


def pack_kernel(q0, q1, q2, q3, f1_ref, f2_ref, out_ref):
    total = q0[...].astype(f32) + q1[...].astype(f32) + q2[...].astype(f32) + q3[...].astype(f32)
    f1 = f1_ref[...].astype(f32)
    f2 = f2_ref[...].astype(f32)
    for n in range(PLANE):
        at = slice(n * KR, (n + 1) * KR)
        out_ref[n, :, :PACK] = total[at, :].astype(bf16)
        out_ref[n, :, PACK : PACK + FC] = f1[at, :].astype(bf16)
        for h in range(2):
            to = PACK + FC + h * D
            out_ref[n, :, to : to + D] = f2[(2 * n + h) * KR : (2 * n + h + 1) * KR, :].astype(bf16)


def pack_call(parts, fc1, fc2):
    return pl.pallas_call(
        pack_kernel,
        out_shape=jax.ShapeDtypeStruct((PLANE, KR, WIDE), bf16),
        compiler_params=params(),
        cost_estimate=cost(QUARTER * PACK * 4, QUARTER * PACK * 14),
    )(*parts, fc1, fc2)


def sum_kernel(in_ref, out_ref):
    total = in_ref[0].astype(f32)
    for n in range(1, PLANE):
        total += in_ref[n].astype(f32)
    out_ref[...] = total


def sum_call(packed):
    return pl.pallas_call(
        sum_kernel,
        out_shape=jax.ShapeDtypeStruct(packed.shape[1:], f32),
        compiler_params=params(),
        cost_estimate=cost(packed.size, packed.size * 2),
    )(packed)


def norm_kernel(g_ref, o_ref, out_ref):
    g, o = g_ref[...], o_ref[...]
    part = jnp.sum(g * g + o * o, axis=(0, 1), keepdims=True)
    cross = g[:, 4 * DC : PACK] * o[:, 4 * DC : PACK]
    part += 2.0 * jnp.sum(cross, axis=(0, 1), keepdims=True)
    out_ref[...] = jnp.broadcast_to(part[None], out_ref.shape)


def norm_call(g, o):
    return pl.pallas_call(
        norm_kernel,
        out_shape=jax.ShapeDtypeStruct((CHIPS, 8, 128), f32),
        compiler_params=params(),
        cost_estimate=cost(4 * KR * WIDE, 1e6),
    )(g, o)


RATES = (D ** (-0.5), max(1, 2 * D // S) ** (-0.5), D ** (-0.5), FF ** (-0.5), RATE_VECTOR)


def adam_kernel(place_ref, norm_ref, mine_ref, other_ref, *refs):
    masters, firsts, seconds = refs[0:5], refs[5:10], refs[10:15]
    outs = refs[15:30]
    norm_out, bias_out = refs[30:32]
    core = place_ref[0]
    mine, other = mine_ref[...], other_ref[...]
    g0 = jnp.where(core == 0, mine, other)
    g1 = jnp.where(core == 0, other, mine)
    total = jnp.sum(jnp.sum(norm_ref[...], axis=0)[0:1, 0:1], axis=(0, 1), keepdims=True)
    grad_norm = jnp.sqrt(total)
    norm_out[...] = jnp.broadcast_to(grad_norm, norm_out.shape)
    clip = jnp.minimum(1.0, CLIP_LIMIT / (grad_norm + 1e-06))

    def update(i, at, grad):
        clipped = grad * clip
        master = masters[i][at]
        first = BETA_ONE * firsts[i][at] + (1.0 - BETA_ONE) * clipped
        second = BETA_TWO * seconds[i][at] + (1.0 - BETA_TWO) * clipped * clipped
        first_hat = first / (1.0 - BETA_ONE**STEP)
        second_hat = second / (1.0 - BETA_TWO**STEP)
        decay = 0.0 if i == 4 else DECAY_RATE
        outs[3 * i][at] = master - RATES[i] * (first_hat / (jnp.sqrt(second_hat) + ADAM_EPS) + decay * master)
        outs[3 * i + 1][at] = first
        outs[3 * i + 2][at] = second

    rows = slice(None)
    for c, g in ((0, g0), (1, g1)):
        for p in range(PAIRS):
            for i in range(3):
                col = i * D + c * DC + p * 128
                update(0, (rows, slice(col, col + 128)), g[:, (4 * p + i) * 128 : (4 * p + i + 1) * 128])
            col = c * DC + p * 128
            update(1, (rows, slice(col, col + 128)), g[:, (4 * p + 3) * 128 : (4 * p + 4) * 128])
    for r in range(FC // DC):
        at = slice(PACK + r * DC, PACK + (r + 1) * DC)
        part = exact_dot(g0[:, at], spots_t(0)) + exact_dot(g1[:, at], spots_t(1))
        update(2, (rows, slice(r * D, (r + 1) * D)), part)
    for c, g in ((0, g0), (1, g1)):
        for h in range(2):
            row = c * FR + h * KR
            to = PACK + FC + h * D
            update(3, (slice(row, row + KR), rows), g[:, to : to + D])
    vec = (g0 + g1)[:, 4 * DC : 4 * DC + 128]
    vec = jnp.concatenate([vec, jnp.zeros((16 - KR, 128), f32)], axis=0).T[:16, :KR]
    update(4, (rows, rows), vec[: masters[4].shape[0], :])
    bias_out[...] = vec[7:8, :] * clip


def adam_call(place, norm, mine, other, masters, firsts, seconds):
    whole = lambda a: pl.BlockSpec(a.shape, lambda i, c: (0,) * len(a.shape))
    args = [norm, mine, other, *masters, *firsts, *seconds]
    shapes = [jax.ShapeDtypeStruct(m.shape, f32) for m in masters for _ in range(3)]
    shapes += [jax.ShapeDtypeStruct((1, 128), f32), jax.ShapeDtypeStruct((1, KR), f32)]
    return pl.pallas_call(
        adam_kernel,
        grid_spec=pltpu.PrefetchScalarGridSpec(
            num_scalar_prefetch=1,
            grid=(1,),
            in_specs=[whole(a) for a in args],
            out_specs=[whole(a) for a in shapes],
        ),
        out_shape=shapes,
        compiler_params=params(),
        cost_estimate=cost(20 * KR * FF * 3, 3e6),
    )(place, *args)


def local(
    tokens,
    cotangent,
    counts,
    patch_row,
    patch_col,
    w_qkv,
    w_proj,
    w_fc1,
    w_fc2,
    vectors,
    m_qkv,
    v_qkv,
    m_proj,
    v_proj,
    m_fc1,
    v_fc1,
    m_fc2,
    v_fc2,
    m_vectors,
    v_vectors,
):
    core = lax.axis_index("grp")
    chip = lax.axis_index("dp")
    first_core = core == 0
    along = jnp.where(first_core, chip // PLANE, (chip // SIDE) % SIDE)
    vr = vectors.shape[0]

    def swap(a):
        return lax.ppermute(a, "grp", [(0, 1), (1, 0)])

    def along_line(quarter):
        return [quarter] + [shift(quarter, d) for d in range(1, SIDE)]

    def line_sum(whole):
        return lax.psum_scatter(whole, BOTH, scatter_dimension=0, axis_index_groups=lines(), tiled=True)

    me = jnp.stack([core, along]).astype(jnp.int32)
    shares, share_fc2 = share_call(me, w_qkv, vectors, w_fc2)
    full_fc2 = lax.all_gather(share_fc2, "dp", axis=0, tiled=True)
    fc1_b = w_fc1.astype(bf16).reshape(KR, CHIPS, CORES, FR)
    share_fc1 = jnp.where(first_core, fc1_b[:, :, 0], fc1_b[:, :, 1]).reshape(KR, FC)
    share = jnp.concatenate([share_fc1, w_proj.astype(bf16)], axis=1)
    share = jnp.broadcast_to(share[None], (PLANE,) + share.shape)

    x_own = tokens.reshape(S, D)
    cot_own = cotangent.reshape(S, D)
    x_other, cot_other = swap(x_own), swap(cot_own)
    ints = jnp.concatenate(
        [
            patch_row.reshape(1, S),
            patch_col.reshape(1, S),
            jnp.pad(counts.reshape(1, 2), ((0, 0), (0, S - 2))),
            jnp.zeros((5, S), jnp.int32),
        ]
    )
    ints = jnp.stack([ints, swap(ints)])
    counts0 = jnp.where(first_core, ints[0, 2, :2], ints[1, 2, :2])
    counts1 = jnp.where(first_core, ints[1, 2, :1], ints[0, 2, :1])
    place = jnp.concatenate([jnp.stack([core, along]).astype(jnp.int32), counts0, counts1])

    quarter = plane_swap(shares).reshape(QUARTER, 3 * DC + 128)
    quarter, share, x_other, cot_other = lax.optimization_barrier((quarter, share, x_other, cot_other))
    qkv_pieces = along_line(quarter)
    share, qkv_pieces = lax.optimization_barrier((share, qkv_pieces))
    quarter = plane_swap(share).reshape(QUARTER, FC + D)

    vec, h1t, cosine, sine, q, k, v, b1, pos = qkv_call(place, x_own, x_other, ints, qkv_pieces)
    q, quarter = lax.optimization_barrier((q, quarter))
    pieces = along_line(quarter)
    mine, p0, p1 = attn_fwd_call(place, q, k, v)
    mine, pieces[1], pieces[3] = lax.optimization_barrier((mine, pieces[1], pieces[3]))
    other = swap(mine)
    cot_other, mine = lax.optimization_barrier((cot_other, mine))
    gy = gy_call(place, cot_own, cot_other)
    other, gy = lax.optimization_barrier((other, gy))
    after, n2, r2, h2 = proj_call(place, mine, other, x_own, x_other, pieces, vec)
    mlp, mlp_part, gh2, act, gup, gb1 = mlp_call(place, h2, gy, pieces, full_fc2, b1)
    other_gh2 = swap(gh2)
    mlp_other = swap(mlp_part)

    gw2 = fc2_grad_call(place, act, gy)
    gw2, other_gh2 = lax.optimization_barrier((gw2, other_gh2))
    sum_fc2 = line_sum(gw2)
    gw1, ga, gab, sums_mid = mid_call(place, h2, gup, n2, r2, gy, gh2, other_gh2, vec)
    sum_fc1 = line_sum(gw1)
    *gw, gh1, gh1_part = attn_bwd_call(
        place, q, k, v, gab, mine, other, p0, p1, cosine, sine, pos, h1t, qkv_pieces, pieces,
        x_own, x_other, sums_mid, gb1,
    )
    gh1_other = swap(gh1_part)

    parts = [gw[0]] + [shift(gw[d], d) for d in range(1, SIDE)]
    got = plane_swap(pack_call(parts, sum_fc1, sum_fc2))
    gt, mixed = last_call(x_own, ga, gh1, gh1_other, after, mlp, mlp_other, vec)
    got, gt, mixed = lax.optimization_barrier((got, gt, mixed))
    grads = sum_call(got)

    grads_other = swap(grads)
    norms = lax.all_to_all(norm_call(grads, grads_other), "dp", 0, 0)
    *updates, grad_norm, bias_proj_grad = adam_call(
        place,
        norms,
        grads,
        grads_other,
        (w_qkv, w_proj, w_fc1, w_fc2, vectors),
        (m_qkv, m_proj, m_fc1, m_fc2, m_vectors),
        (v_qkv, v_proj, v_fc1, v_fc2, v_vectors),
    )
    return (
        mixed.reshape(1, 1, S, D),
        gt.reshape(1, 1, S, D),
        grad_norm[0, 0],
        *updates,
        bias_proj_grad.reshape(KR),
    )


def solution(mesh):
    frame = P("grp", "dp", None, None)
    ints = P("grp", "dp", None)
    rows = P("dp", None)
    cols = P(None, "dp")
    return jax.shard_map(
        local,
        mesh=mesh,
        in_specs=(frame, frame, ints, ints, ints, rows, rows, rows, rows, cols) + (rows,) * 8 + (cols,) * 2,
        out_specs=(frame, frame, P()) + (rows,) * 12 + (cols,) * 3 + (P("dp"),),
        check_vma=False,
    )
```

```python
import jax
import jax.numpy as jnp
from jax import lax
from jax.experimental import pallas as pl
from jax.experimental.pallas import tpu as pltpu
from jax.sharding import PartitionSpec as P

D = 768
H = 12
HD = 64
FF = 3072
STEP = 10
A = 196
S = 576

CORES = 2
HC = H // CORES
DC = D // CORES
FC = FF // CORES
PAIRS = HC // 2
T = CORES * S

WIN = 208
WINDOWS = (0, 192)

EPS_NORM = 1e-06
BETA_ONE = 0.9
BETA_TWO = 0.95
ADAM_EPS = 1e-08
DECAY_RATE = 0.05
RATE_VECTOR = 0.8
CLIP_LIMIT = 1.0
NEG = -1e30

bf16 = jnp.bfloat16
f32 = jnp.float32
VMEM_LIMIT = 56 * 1024 * 1024


SIDE = 4
CHIPS = SIDE**3
PLANE = SIDE * SIDE
KR = D // CHIPS
FR = FC // CHIPS
BLOCK = SIDE * KR
QUARTER = PLANE * KR
BOTH = ("grp", "dp")


def device(core, x, y, z):
    return ((core * SIDE + x) * SIDE + y) * SIDE + z


def lines():
    r = range(SIDE)
    return [[device(0, a, g, z) for a in r] for g in r for z in r] + [
        [device(1, g, a, z) for a in r] for g in r for z in r
    ]


def planes():
    r = range(SIDE)
    return [[device(0, a, g, z) for g in r for z in r] for a in r] + [
        [device(1, g, a, z) for g in r for z in r] for a in r
    ]


def shift(value, d):
    pairs = [(group[i], group[(i + d) % SIDE]) for group in lines() for i in range(SIDE)]
    return lax.ppermute(value, BOTH, pairs)


def plane_swap(value):
    return lax.all_to_all(value, BOTH, 0, 0, axis_index_groups=planes())


def natural(core, a, g):
    return jnp.where(core == 0, SIDE * a + g, SIDE * g + a)


def lay_out(place_ref, pieces, full_ref):
    core, me = place_ref[0], place_ref[1]
    for d, piece in enumerate(pieces):
        a = (me + SIDE - d) & (SIDE - 1)
        for g in range(SIDE):
            at = pl.multiple_of(natural(core, a, g) * BLOCK, BLOCK)
            full_ref[pl.ds(at, BLOCK), :] = piece[g * BLOCK : (g + 1) * BLOCK, :]


def usable_rows(place_ref, group, rows, base=0):
    slot = lax.broadcasted_iota(jnp.int32, (rows, 1), 0) + base
    first = ((slot < A) & (slot < place_ref[2])) | ((slot >= A) & (slot < 2 * A) & (slot - A < place_ref[3]))
    first = first.astype(f32)
    second = (slot < place_ref[4]).astype(f32)
    if isinstance(group, int):
        return second if group else first
    return jnp.where(group == 0, first, second)


def own_rows(win):
    row = lax.broadcasted_iota(jnp.int32, (WIN, 1), 0) + (WINDOWS[win] - win * A)
    return ((row >= 0) & (row < A)).astype(f32)


def key_bias(place_ref, win=None):
    if win is None:
        key = lax.broadcasted_iota(jnp.int32, (1, S), 1)
        return jnp.where(key < place_ref[4], 0.0, NEG)
    key = lax.broadcasted_iota(jnp.int32, (1, WIN), 1) + (WINDOWS[win] - win * A)
    return jnp.where((key >= 0) & (key < place_ref[2 + win]), 0.0, NEG)


def exact_dot(a, b):
    high = a.astype(bf16)
    rest = a - high.astype(f32)
    mid = rest.astype(bf16)
    low = (rest - mid.astype(f32)).astype(bf16)
    b = b.astype(bf16)
    return dot(high, b) + dot(mid, b) + dot(low, b)


def spots(core, shape, full, part):
    l = lax.broadcasted_iota(jnp.int32, shape, full)
    m = lax.broadcasted_iota(jnp.int32, shape, part)
    q = (m * 2731) >> 16
    return l == m + FR * (q + core)


def spots_t(core):
    return spots(core, (DC, D), 1, 0)


def params(**kw):
    return pltpu.CompilerParams(vmem_limit_bytes=VMEM_LIMIT, **kw)


def cost(flops, bytes_accessed, transcendentals=0):
    return pl.CostEstimate(
        flops=int(flops), bytes_accessed=int(bytes_accessed), transcendentals=int(transcendentals)
    )


def dot(a, b):
    return jnp.dot(a, b, preferred_element_type=f32)


def dot_t(a, b):
    return lax.dot_general(a, b, (((1,), (1,)), ((), ())), preferred_element_type=f32)


def t_dot(a, b):
    return lax.dot_general(a, b, (((0,), (0,)), ((), ())), preferred_element_type=f32)


def stats(z):
    mean_val = jnp.mean(z, axis=-1, keepdims=True)
    centred = z - mean_val
    variance = jnp.mean(centred * centred, axis=-1, keepdims=True)
    inv_std = lax.rsqrt(variance + EPS_NORM)
    return centred * inv_std, inv_std


def norm_back(grad, normed, inv_std, gain):
    e = grad * gain
    return inv_std * (
        e
        - jnp.mean(e, axis=-1, keepdims=True)
        - normed * jnp.mean(e * normed, axis=-1, keepdims=True)
    )


def swap_halves(u):
    lanes = u.shape[1]
    lane = lax.broadcasted_iota(jnp.int32, u.shape, 1)
    up = pltpu.roll(u, lanes - HD // 2, 1)
    down = pltpu.roll(u, HD // 2, 1)
    return jnp.where((lane & (HD - 1)) < HD // 2, up, down)


TURN = 1.5707963267948966


def sin_cos(a):
    k = jnp.floor(a * (1.0 / TURN) + 0.5)
    r = ((a - k * 1.5703125) - k * 4.837512969970703125e-4) - k * 7.54978995489188216e-8
    z = r * r
    s = ((-1.9515295891e-4 * z + 8.3321608736e-3) * z - 1.6666654611e-1) * z * r + r
    c = ((2.443315711809948e-5 * z - 1.388731625493765e-3) * z + 4.166664568298827e-2) * z * z - 0.5 * z + 1.0
    quarter = k.astype(jnp.int32)
    odd = (quarter & 1) == 1
    sine = jnp.where(odd, c, s)
    cosine = jnp.where(odd, s, c)
    sine = jnp.where((quarter & 2) == 0, sine, -sine)
    cosine = jnp.where(((quarter + 1) & 2) == 0, cosine, -cosine)
    return sine, cosine


def share_kernel(place_ref, w_ref, v_ref, f_ref, out_ref, fc2_ref):
    core = place_ref[0]
    w = w_ref[...].astype(bf16)
    cols = []
    for p in range(PAIRS):
        for i in range(3):
            at = i * D + p * 128
            cols.append(jnp.where(core == 0, w[:, at : at + 128], w[:, at + DC : at + DC + 128]))
    v = jnp.concatenate([v_ref[...], jnp.zeros((128 - v_ref.shape[0], KR), f32)], axis=0)
    v = jnp.concatenate([v, jnp.zeros((128, 128 - KR), f32)], axis=1)
    cols.append(v.T[:KR, :].astype(bf16))
    share = jnp.concatenate(cols, axis=1)
    for n in range(PLANE):
        out_ref[n] = share
    fc2_ref[...] = jnp.where(core == 0, f_ref[:FR, :], f_ref[FR:, :]).astype(bf16)


def share_call(place, w, vectors, w_fc2):
    whole = lambda a: pl.BlockSpec(a.shape, lambda i, c: (0, 0))
    return pl.pallas_call(
        share_kernel,
        grid_spec=pltpu.PrefetchScalarGridSpec(
            num_scalar_prefetch=1,
            grid=(1,),
            in_specs=[whole(w), whole(vectors), whole(w_fc2)],
            out_specs=[
                pl.BlockSpec((PLANE, KR, 3 * DC + 128), lambda i, c: (0, 0, 0)),
                pl.BlockSpec((FR, D), lambda i, c: (0, 0)),
            ],
        ),
        out_shape=[
            jax.ShapeDtypeStruct((PLANE, KR, 3 * DC + 128), bf16),
            jax.ShapeDtypeStruct((FR, D), bf16),
        ],
        compiler_params=params(),
        cost_estimate=cost(KR * D * 3, 1e6),
    )(place, w, vectors, w_fc2)


def gy_kernel(place_ref, c_ref, co_ref, gy_ref):
    i = pl.program_id(0)
    keep = usable_rows(place_ref, i ^ place_ref[0], S)
    gy_ref[...] = (jnp.where(i == 0, c_ref[...], co_ref[...]).astype(f32) * keep).astype(bf16)


def gy_call(place, c, co):
    whole = pl.BlockSpec((S, D), lambda i, c: (0, 0))
    return pl.pallas_call(
        gy_kernel,
        grid_spec=pltpu.PrefetchScalarGridSpec(
            num_scalar_prefetch=1,
            grid=(CORES,),
            in_specs=[whole, whole],
            out_specs=pl.BlockSpec((S, D), lambda i, c: (i, 0)),
        ),
        out_shape=jax.ShapeDtypeStruct((T, D), bf16),
        compiler_params=params(),
        cost_estimate=cost(4 * T * D, T * D * 4),
    )(place, c, co)


def qkv_kernel(
    place_ref, x_ref, xo_ref, ints_ref, w0, w1, w2, w3, v0, v1, v2, v3,
    vec_ref, ht_ref, cos_ref, sin_ref, q_out, k_out, v_out, b1_ref, pos_ref,
    w_s, full_s, rows_s, freq_s,
):
    core = place_ref[0]

    @pl.when(pl.program_id(0) == 0)
    def _():
        lay_out(place_ref, (w0, w1, w2, w3), w_s)
        lay_out(place_ref, (v0, v1, v2, v3), full_s)
        rows_s[...] = full_s[...].astype(f32).T[:16, :]
        vec_ref[...] = rows_s[...]
        late = rows_s[8:16, :].astype(bf16)
        units = dot(late, spots(core, (D, DC), 0, 1).astype(bf16))
        for r in range(FC // DC):
            b1_ref[:, r * DC : (r + 1) * DC] = units[2 + r : 3 + r, :]
        src = lax.broadcasted_iota(jnp.int32, (D, DC), 0)
        dst = lax.broadcasted_iota(jnp.int32, (D, DC), 1)
        want = core * (DC // 2) + (dst // HD) * (HD // 2) + (dst & (HD // 2 - 1))
        freq_s[0:8, :] = dot(late, (src == want).astype(bf16))
        freq_s[8:16, :] = dot(late, (src == want + D // 2).astype(bf16))

    i = pl.program_id(0)
    x = jnp.where(i < pl.num_programs(0) // CORES, x_ref[...], xo_ref[...])
    h = stats(x.astype(f32))[0] * rows_s[0:1, :] + rows_s[1:2, :]
    pos = ints_ref[...].astype(f32).T
    pos_ref[...] = pos
    ht_ref[...] = h.T.astype(bf16)
    acc = dot(h.astype(bf16), w_s[...])
    angle = pos[:, 1:2] * freq_s[1:2, :] + pos[:, 0:1] * freq_s[9:10, :]
    lane = lax.broadcasted_iota(jnp.int32, (1, DC), 1)
    sign = jnp.where((lane & (HD - 1)) < HD // 2, -1.0, 1.0)
    small = jnp.max(jnp.abs(angle)) < 8000.0

    @pl.when(small)
    def _():
        sine, cosine = sin_cos(angle)
        cos_ref[...] = cosine
        sin_ref[...] = sine * sign

    @pl.when(jnp.logical_not(small))
    def _():
        cos_ref[...] = jnp.cos(angle)
        sin_ref[...] = jnp.sin(angle) * sign

    cosine, sine = cos_ref[...], sin_ref[...]
    at = pl.ds(pl.multiple_of(core * DC, DC), DC)
    part = lambda i: jnp.concatenate([acc[:, (3 * p + i) * 128 : (3 * p + i + 1) * 128] for p in range(PAIRS)], axis=1)
    q = part(0) + rows_s[4:5, at]
    k = part(1) + rows_s[5:6, at]
    q_out[...] = ((q * cosine + swap_halves(q) * sine) * HD ** (-0.5)).astype(bf16)
    k_out[...] = (k * cosine + swap_halves(k) * sine).astype(bf16)
    v_out[...] = (part(2) + rows_s[6:7, at]).astype(bf16)


def qkv_call(place, x, xo, ints, pieces):
    rows = S
    tile = lambda n: pl.BlockSpec((rows, n), lambda i, c: (i, 0))
    keep = lambda *n: pl.BlockSpec(n, lambda i, c: (0,) * len(n))
    return pl.pallas_call(
        qkv_kernel,
        grid_spec=pltpu.PrefetchScalarGridSpec(
            num_scalar_prefetch=1,
            grid=(CORES,),
            in_specs=[keep(S, D), keep(S, D), pl.BlockSpec((None, 8, S), lambda i, c: (i, 0, 0))]
            + [keep(QUARTER, 3 * DC)] * 4
            + [pl.BlockSpec((QUARTER, 128), lambda i, c: (0, 3 * DC // 128))] * 4,
            out_specs=[keep(16, D), pl.BlockSpec((None, D, rows), lambda i, c: (i, 0, 0))]
            + [tile(DC)] * 5
            + [keep(1, FC), tile(8)],
            scratch_shapes=[
                pltpu.VMEM((D, 3 * DC), bf16),
                pltpu.VMEM((D, 128), bf16),
                pltpu.VMEM((16, D), f32),
                pltpu.VMEM((16, DC), f32),
            ],
        ),
        out_shape=[
            jax.ShapeDtypeStruct((16, D), f32),
            jax.ShapeDtypeStruct((CORES, D, S), bf16),
            jax.ShapeDtypeStruct((T, DC), f32),
            jax.ShapeDtypeStruct((T, DC), f32),
            *[jax.ShapeDtypeStruct((T, DC), bf16)] * 3,
            jax.ShapeDtypeStruct((1, FC), f32),
            jax.ShapeDtypeStruct((T, 8), f32),
        ],
        compiler_params=params(),
        cost_estimate=cost(2 * T * D * 3 * DC + 60 * T * DC, T * D * 6 + D * 3 * DC * 2 + T * DC * 14),
    )(place, x, xo, ints, *pieces, *pieces)


def softmax_head(q, k, v, mine, bias):
    s = dot_t(jnp.where(mine, q, jnp.zeros_like(q)), k) + bias
    e = jnp.exp(s - jnp.max(s, axis=-1, keepdims=True))
    p = e * (1.0 / jnp.sum(e, axis=-1, keepdims=True))
    return p


def attn_fwd_kernel(
    place_ref, q0, k0, v0, q1, k1, v1, o_ref, p0_ref, p1_ref
):
    lane = lax.broadcasted_iota(jnp.int32, (1, 2 * HD), 1)
    low = lane < HD
    q, k, v = q1[0], k1[0], v1[0]
    mixes = []
    bias = key_bias(place_ref)
    for head, mine in ((0, low), (1, ~low)):
        p = softmax_head(q, k, v, mine, bias).astype(bf16)
        p1_ref[head] = p
        mixes.append(dot(p, v))
    mix = jnp.where(low, mixes[0], mixes[1])
    o_ref[1] = jnp.where(usable_rows(place_ref, 1, S) > 0, mix, v.astype(f32)).astype(bf16)
    o_ref[0] = v0[0]
    for win, base in enumerate(WINDOWS):
        q, k, v = (r[0, base : base + WIN, :] for r in (q0, k0, v0))
        own = own_rows(win)
        bias = key_bias(place_ref, win)
        mixes = []
        for head, mine in ((0, low), (1, ~low)):
            p = softmax_head(q, k, v, mine, bias)
            p = (p * own).astype(bf16)
            p0_ref[head, win] = p
            mixes.append(dot(p, v))
        mix = jnp.where(low, mixes[0], mixes[1])
        use = (own * usable_rows(place_ref, 0, WIN, base)) > 0
        before = o_ref[0, base : base + WIN, :].astype(f32)
        o_ref[0, base : base + WIN, :] = jnp.where(use, mix, before).astype(bf16)


def attn_fwd_call(place, q, k, v):
    block = lambda g: pl.BlockSpec((1, S, 2 * HD), lambda p, c: (g ^ c[0], 0, p))
    q, k, v = (a.reshape(CORES, S, DC) for a in (q, k, v))
    return pl.pallas_call(
        attn_fwd_kernel,
        grid_spec=pltpu.PrefetchScalarGridSpec(
            num_scalar_prefetch=1,
            grid=(PAIRS,),
            in_specs=[block(0)] * 3 + [block(1)] * 3,
            out_specs=[
                pl.BlockSpec((CORES, S, 2 * HD), lambda p, c: (0, 0, p)),
                pl.BlockSpec((2, 2, WIN, WIN), lambda p, c: (p, 0, 0, 0)),
                pl.BlockSpec((2, S, S), lambda p, c: (p, 0, 0)),
            ],
        ),
        out_shape=[
            jax.ShapeDtypeStruct((CORES, S, DC), bf16),
            jax.ShapeDtypeStruct((HC, 2, WIN, WIN), bf16),
            jax.ShapeDtypeStruct((HC, S, S), bf16),
        ],
        compiler_params=params(),
        cost_estimate=cost(4 * HC * (S * S + 2 * WIN * WIN) * 128, 12e6, HC * S * S),
    )(place, q, k, v, q, k, v)


def proj_kernel(place_ref, mine_ref, other_ref, x_ref, xo_ref, w0, w1, w2, w3, v_ref, after_ref, n2_ref, r2_ref, h2_ref, w_s):
    @pl.when(pl.program_id(0) == 0)
    def _():
        lay_out(place_ref, (w0, w1, w2, w3), w_s)

    core = place_ref[0]
    at = lambda c: pl.ds(pl.multiple_of(c * DC, DC), DC)
    branch = dot(mine_ref[0], w_s[at(core), :]) + dot(other_ref[0], w_s[at(1 - core), :])
    x = jnp.where(pl.program_id(0) < pl.num_programs(0) // CORES, x_ref[...], xo_ref[...])
    after = x.astype(f32) + (branch + v_ref[7:8, :])
    normed, inv_std = stats(after)
    n2_ref[...] = normed
    r2_ref[...] = jnp.broadcast_to(inv_std, r2_ref.shape)

    @pl.when(pl.program_id(0) < pl.num_programs(0) // CORES)
    def _():
        after_ref[...] = after

    h2_ref[...] = (normed * v_ref[2:3, :] + v_ref[3:4, :]).astype(bf16)


def proj_call(place, mine, other, x, xo, pieces, vec):
    rows = 288
    half = S // rows
    tile = lambda n: pl.BlockSpec((rows, n), lambda i, c: (i, 0))
    whole = lambda a: pl.BlockSpec(a.shape, lambda i, c: (0,) * a.ndim)
    return pl.pallas_call(
        proj_kernel,
        grid_spec=pltpu.PrefetchScalarGridSpec(
            num_scalar_prefetch=1,
            grid=(T // rows,),
            in_specs=[
                pl.BlockSpec((1, rows, DC), lambda i, c: ((i // half) ^ c[0], i % half, 0)),
                pl.BlockSpec((1, rows, DC), lambda i, c: ((i // half) ^ c[0], i % half, 0)),
                pl.BlockSpec((rows, D), lambda i, c: (jnp.minimum(i, half - 1), 0)),
                pl.BlockSpec((rows, D), lambda i, c: (jnp.maximum(i - half, 0), 0)),
            ]
            + [pl.BlockSpec((QUARTER, D), lambda i, c: (0, FC // D))] * 4
            + [whole(vec)],
            out_specs=[pl.BlockSpec((rows, D), lambda i, c: (jnp.minimum(i, half - 1), 0)), tile(D), tile(8), tile(D)],
            scratch_shapes=[pltpu.VMEM((D, D), bf16)],
        ),
        out_shape=[
            jax.ShapeDtypeStruct((S, D), f32),
            jax.ShapeDtypeStruct((T, D), f32),
            jax.ShapeDtypeStruct((T, 8), f32),
            jax.ShapeDtypeStruct((T, D), bf16),
        ],
        compiler_params=params(),
        cost_estimate=cost(2 * T * D * D, T * D * 10 + D * D * 2),
    )(place, mine, other, x, xo, *pieces, vec)


PACK = 4 * DC + 128
K0 = (2.0 / 3.141592653589793) ** 0.5
FT = 768


def gelu_slope(u):
    sq = u * u
    th = jnp.tanh(u * (K0 + (K0 * 0.044715) * sq))
    half = 0.5 + 0.5 * th
    return u * half, half + (u * (half - half * half)) * (2 * K0 + (6 * K0 * 0.044715) * sq)


def mlp_kernel(
    place_ref, h2_ref, gy_ref, w10, w11, w12, w13, w2_ref, b1_ref, mlp_ref, mlpo_ref, gh2b_ref, act_ref, gup_ref, gb1_ref, w1_s
):
    i = pl.program_id(0)

    @pl.when(i == 0)
    def _():
        lay_out(place_ref, (w10, w11, w12, w13), w1_s)
        gb1_ref[...] = jnp.zeros_like(gb1_ref)

    for f in range(FC // FT):
        c = slice(f * FT, (f + 1) * FT)
        act, slope = gelu_slope(dot(h2_ref[...], w1_s[:, c]) + b1_ref[:, c])
        act_ref[:, c] = act.astype(bf16)
        gup = (dot_t(gy_ref[...], w2_ref[c, :]) * slope).astype(bf16)
        gup_ref[:, c] = gup
        gb1_ref[:, c] += jnp.sum(gup.astype(f32), axis=0, keepdims=True)
    gh2b_ref[...] = dot_t(gup_ref[...], w1_s[...]).astype(bf16)
    mlp = dot(act_ref[...], w2_ref[...])
    half = pl.num_programs(0) // CORES

    @pl.when(i < half)
    def _():
        mlp_ref[...] = mlp

    @pl.when(i >= half)
    def _():
        mlpo_ref[...] = mlp


def mlp_call(place, h2, gy, pieces, w2, b1):
    rows = 288
    half = S // rows
    tile = lambda n: pl.BlockSpec((rows, n), lambda i, c: (i, 0))
    whole = lambda a: pl.BlockSpec(a.shape, lambda i, c: (0,) * a.ndim)
    return pl.pallas_call(
        mlp_kernel,
        grid_spec=pltpu.PrefetchScalarGridSpec(
            num_scalar_prefetch=1,
            grid=(T // rows,),
            in_specs=[tile(D), tile(D)]
            + [pl.BlockSpec((QUARTER, FC), lambda i, c: (0, 0))] * 4
            + [whole(w2), whole(b1)],
            out_specs=[
                pl.BlockSpec((rows, D), lambda i, c: (jnp.minimum(i, half - 1), 0)),
                pl.BlockSpec((rows, D), lambda i, c: (jnp.maximum(i - half, 0), 0)),
                tile(D),
                tile(FC),
                tile(FC),
                pl.BlockSpec((1, FC), lambda i, c: (0, 0)),
            ],
            scratch_shapes=[pltpu.VMEM((D, FC), bf16)],
        ),
        out_shape=[
            jax.ShapeDtypeStruct((S, D), f32),
            jax.ShapeDtypeStruct((S, D), f32),
            jax.ShapeDtypeStruct((T, D), bf16),
            jax.ShapeDtypeStruct((T, FC), bf16),
            jax.ShapeDtypeStruct((T, FC), bf16),
            jax.ShapeDtypeStruct((1, FC), f32),
        ],
        compiler_params=params(),
        cost_estimate=cost(8 * T * D * FC, 30e6, T * FC),
    )(place, h2, gy, *pieces, w2, b1)


def by_line(place_ref, value, block, out_ref):
    core = place_ref[0]
    for n in range(PLANE):
        to = jnp.where(core == 0, n, (n % SIDE) * SIDE + n // SIDE)
        out_ref[pl.ds(pl.multiple_of(to * block, block), block), :] = value[n * block : (n + 1) * block, :].astype(bf16)


def fc2_grad_kernel(place_ref, act_ref, gy_ref, out_ref):
    value = t_dot(act_ref[...], gy_ref[...])
    block = SIDE * FR
    for n in range(FT // block):
        m = pl.program_id(0) * (FT // block) + n
        to = jnp.where(place_ref[0] == 0, m, (m & (SIDE - 1)) * SIDE + m // SIDE)
        out_ref[pl.ds(pl.multiple_of(to * block, block), block), :] = value[n * block : (n + 1) * block, :].astype(bf16)


def fc2_grad_call(place, act, gy):
    return pl.pallas_call(
        fc2_grad_kernel,
        grid_spec=pltpu.PrefetchScalarGridSpec(
            num_scalar_prefetch=1,
            grid=(FC // FT,),
            in_specs=[pl.BlockSpec((T, FT), lambda i, c: (0, i)), pl.BlockSpec((T, D), lambda i, c: (0, 0))],
            out_specs=pl.BlockSpec((FC, D), lambda i, c: (0, 0)),
        ),
        out_shape=jax.ShapeDtypeStruct((FC, D), bf16),
        compiler_params=params(),
        cost_estimate=cost(2 * T * D * FC, T * (D + FC) * 2 + D * FC * 2),
    )(place, act, gy)


def mid_kernel(
    place_ref, h2_ref, gup_ref, n2_ref, r2_ref, gy_ref, gh2_ref, other_ref, v_ref, gw_ref, ga_ref, gab_ref, sums_ref
):
    i = pl.program_id(0)
    by_line(place_ref, t_dot(h2_ref[...], gup_ref[...]), BLOCK, gw_ref)
    normed, inv_std = n2_ref[...], r2_ref[:, 0:1]
    gh2 = gh2_ref[...].astype(f32) + other_ref[...].astype(f32)
    gy = gy_ref[...].astype(f32)
    ga = gy + norm_back(gh2, normed, inv_std, v_ref[2:3, :])
    gab = ga.astype(bf16)
    gab_ref[...] = gab
    mine = (i < pl.num_programs(0) // CORES).astype(f32)
    sums = [
        mine * jnp.sum(a, axis=0, keepdims=True) for a in (gh2 * normed, gh2, gab.astype(f32), gy)
    ] + [jnp.zeros((4, D), f32)]
    sums = jnp.concatenate(sums, axis=0)

    @pl.when(i == 0)
    def _():
        sums_ref[...] = sums

    @pl.when(i > 0)
    def _():
        sums_ref[...] += sums

    @pl.when(i < pl.num_programs(0) // CORES)
    def _():
        ga_ref[...] = ga


def mid_call(place, h2, gup, n2, r2, gy, gh2, other, vec):
    rows = 288
    half = S // rows
    cols = FC * rows // T
    tile = lambda n: pl.BlockSpec((rows, n), lambda i, c: (i, 0))
    flipped = pl.BlockSpec((rows, D), lambda i, c: ((i + half) % (2 * half), 0))
    whole = lambda a: pl.BlockSpec(a.shape, lambda i, c: (0,) * a.ndim)
    return pl.pallas_call(
        mid_kernel,
        grid_spec=pltpu.PrefetchScalarGridSpec(
            num_scalar_prefetch=1,
            grid=(T // rows,),
            in_specs=[whole(h2), pl.BlockSpec((T, cols), lambda i, c: (0, i))]
            + [tile(D), tile(8), tile(D), tile(D), flipped, whole(vec)],
            out_specs=[
                pl.BlockSpec((D, cols), lambda i, c: (0, i)),
                pl.BlockSpec((rows, D), lambda i, c: (jnp.minimum(i, half - 1), 0)),
                tile(D),
                pl.BlockSpec((8, D), lambda i, c: (0, 0)),
            ],
        ),
        out_shape=[
            jax.ShapeDtypeStruct((D, FC), bf16),
            jax.ShapeDtypeStruct((S, D), f32),
            jax.ShapeDtypeStruct((T, D), bf16),
            jax.ShapeDtypeStruct((8, D), f32),
        ],
        compiler_params=params(),
        cost_estimate=cost(2 * T * D * FC, T * D * 18 + T * FC * 2 + D * FC * 2),
    )(place, h2, gup, n2, r2, gy, gh2, other, vec)


def back_head(q_t, k, v, do, do_t, delta, p, mine, head):
    gp = dot_t(jnp.where(mine, do, jnp.zeros_like(do)), v)
    gs = (p.astype(f32) * (gp - delta)).astype(bf16)
    at = slice(head * HD, (head + 1) * HD)
    return dot(gs, k), dot(q_t[at, :], gs), dot(do_t[at, :], p)


def deltas(do, o, low):
    prod = do.astype(f32) * o.astype(f32)
    d0 = jnp.sum(jnp.where(low, prod, 0.0), axis=-1, keepdims=True)
    d1 = jnp.sum(jnp.where(low, 0.0, prod), axis=-1, keepdims=True)
    return d0, d1


def attn_bwd_kernel(
    place_ref,
    q0, k0, v0, o0, p0, cos0, sin0, pos0,
    q1, k1, v1, o1, p1, cos1, sin1, pos1,
    h1t_ref, ga_ref, cols_ref, mine_ref, other_ref, y0, y1, y2, y3, w0, w1, w2, w3,
    x_ref, xo_ref, mid_ref, gb1_ref,
    gw0, gw1, gw2, gw3, gh_ref, gho_ref,
    gq_s, gk_s, gv_s, gw_s, y_s, do_s, gqkv_s, att_s, rows_s, full_s, w_s,
):
    lane = lax.broadcasted_iota(jnp.int32, (1, 2 * HD), 1)
    low = lane < HD
    pair = pl.program_id(0)
    core = place_ref[0]

    @pl.when(pair == 0)
    def _():
        lay_out(place_ref, (y0, y1, y2, y3), y_s)

    wy = y_s[pl.ds(pl.multiple_of(core * DC + pair * 2 * HD, 2 * HD), 2 * HD), :]
    for frame in range(CORES):
        do_s[frame] = dot_t(ga_ref[frame], wy).astype(bf16)

    def finish(frame, q, k, cos_ref, sin_ref, pos_ref):
        cosine, sine = cos_ref[0], sin_ref[0]
        gq = gq_s[...] * HD ** (-0.5)
        gk = gk_s[...]
        sq, sk = swap_halves(gq), swap_halves(gk)
        turn = (q.astype(f32) * HD**0.5) * sq + k.astype(f32) * sk
        gq = (gq * cosine - sq * sine).astype(bf16)
        gk = (gk * cosine - sk * sine).astype(bf16)
        gv = gv_s[...].astype(bf16)
        for i, g in enumerate((gq, gk, gv)):
            gqkv_s[frame ^ core, :, pl.ds(pl.multiple_of(pair * 6 * HD + i * 2 * HD, 2 * HD), 2 * HD)] = g
        pos = pos_ref[0]
        col = jnp.sum(turn * pos[:, 1:2], axis=0, keepdims=True)
        row = jnp.sum(turn * pos[:, 0:1], axis=0, keepdims=True)
        bias = [jnp.sum(g.astype(f32), axis=0, keepdims=True) for g in (gq, gk, gv)]
        return jnp.concatenate([col, row] + bias, axis=0)

    q, k, v, do = q1[0], k1[0], v1[0], do_s[1 ^ core]
    d = deltas(do, o1[0], low)
    q_t, do_t = q.astype(f32).T.astype(bf16), do.astype(f32).T.astype(bf16)
    out = [
        back_head(q_t, k, v, do, do_t, d[head], p1[head], mine, head)
        for head, mine in ((0, low), (1, ~low))
    ]
    gq_s[...] = jnp.where(low, out[0][0], out[1][0])
    gk_s[...] = jnp.concatenate([out[0][1], out[1][1]], axis=0).T
    gv_s[...] = jnp.concatenate([out[0][2], out[1][2]], axis=0).T
    sums1 = finish(1, q, k, cos1, sin1, pos1)
    gq_s[...] = jnp.zeros_like(gq_s)
    gk_s[...] = jnp.zeros_like(gk_s)
    gv_s[...] = jnp.zeros_like(gv_s)
    for win, base in enumerate(WINDOWS):
        at = pl.ds(base, WIN)
        q, k, v, o = (r[0, at, :] for r in (q0, k0, v0, o0))
        do = do_s[core, at, :]
        d = deltas(do, o, low)
        q_t, do_t = q.astype(f32).T.astype(bf16), do.astype(f32).T.astype(bf16)
        out = [
            back_head(q_t, k, v, do, do_t, d[head], p0[head, win], mine, head)
            for head, mine in ((0, low), (1, ~low))
        ]
        gq_s[at, :] += jnp.where(low, out[0][0], out[1][0])
        gk_s[at, :] += jnp.concatenate([out[0][1], out[1][1]], axis=0).T
        gv_s[at, :] += jnp.concatenate([out[0][2], out[1][2]], axis=0).T
    sums0 = finish(0, q0[0], k0[0], cos0, sin0, pos0)
    att_s[pair, 0:5, :] = sums0 + sums1

    gw = jnp.zeros((D, 6 * HD), f32)
    gw_mine = jnp.zeros((2 * HD, DC), f32)
    gw_other = jnp.zeros((2 * HD, DC), f32)
    for frame in range(CORES):
        cols = cols_ref[frame].astype(f32).T.astype(bf16)
        gw_mine += dot(cols, mine_ref[frame ^ core])
        gw_other += dot(cols, other_ref[frame ^ core])
        gw += dot(h1t_ref[frame], gqkv_s[frame, :, pl.ds(pl.multiple_of(pair * 6 * HD, 6 * HD), 6 * HD)])
    gw_s[:, : 6 * HD] = gw.astype(bf16)
    at = lambda c: pl.ds(pl.multiple_of(c * DC, DC), DC)
    gw_s[at(core), 6 * HD :] = gw_mine.T.astype(bf16)
    gw_s[at(1 - core), 6 * HD :] = gw_other.T.astype(bf16)
    to_chips(place_ref, gw_s, (gw0, gw1, gw2, gw3), pl.ds(pl.multiple_of(pair * 8 * HD, 8 * HD), 8 * HD))

    @pl.when(pair == PAIRS - 1)
    def _():
        lay_out(place_ref, (w0, w1, w2, w3), w_s)
        rows_s[...] = jnp.zeros_like(rows_s)
        for frame, x, out in ((0, x_ref, gh_ref), (1, xo_ref, gho_ref)):
            for half in range(2):
                at = slice(half * (S // 2), (half + 1) * (S // 2))
                gh = dot_t(gqkv_s[frame, at, :], w_s[...])
                out[at, :] = gh
                normed, _ = stats(x[at, :].astype(f32))
                rows_s[0:1, :] += jnp.sum(gh * normed, axis=0, keepdims=True)
                rows_s[1:2, :] += jnp.sum(gh, axis=0, keepdims=True)
        rows_s[2:4, :] = mid_ref[0:2, :]
        rows_s[7:9, :] = mid_ref[2:4, :]
        att = jnp.concatenate([att_s[p] for p in range(PAIRS)], axis=1)
        rows_s[4:7, pl.ds(pl.multiple_of(core * DC, DC), DC)] = att[2:5, :]
        src = lax.broadcasted_iota(jnp.int32, (DC, D), 0)
        dst = lax.broadcasted_iota(jnp.int32, (DC, D), 1)
        want = core * (DC // 2) + (src // HD) * (HD // 2) + (src & (HD // 2 - 1))
        side = lax.broadcasted_iota(jnp.int32, (1, DC), 1)
        turn = jnp.where((side & (HD - 1)) < HD // 2, att, -att)
        rows_s[9:10, :] = exact_dot(turn, dst == want)[0:1, :] + exact_dot(turn, dst == want + D // 2)[1:2, :]
        gb1 = jnp.concatenate([gb1_ref[:, r * DC : (r + 1) * DC] for r in range(FC // DC)] * 2, axis=0)
        rows_s[10:14, :] = exact_dot(gb1, spots_t(core))[:4, :]
        full_s[...] = rows_s[...].T.astype(bf16)
        to_chips(place_ref, full_s, (gw0, gw1, gw2, gw3), slice(4 * DC, PACK))


def to_chips(place_ref, full_ref, outs, cols):
    for d, out in enumerate(outs):
        a = (place_ref[1] + d) & (SIDE - 1)
        for g in range(SIDE):
            at = pl.multiple_of(natural(place_ref[0], a, g) * BLOCK, BLOCK)
            out[g * BLOCK : (g + 1) * BLOCK, cols] = full_ref[pl.ds(at, BLOCK), :]


def attn_bwd_call(
    place, q, k, v, ga, mine, other, p0, p1, cosine, sine, pos, h1t, pieces, proj_pieces, x, xo, mid, gb1
):
    q, k, v, cosine, sine, pos, ga = (a.reshape(CORES, S, -1) for a in (q, k, v, cosine, sine, pos, ga))
    block = lambda g: pl.BlockSpec((1, S, 2 * HD), lambda p, c: (g ^ c[0], 0, p))
    own = lambda g: pl.BlockSpec((1, S, 2 * HD), lambda p, c: (g, 0, p))
    at = lambda g: pl.BlockSpec((1, S, 8), lambda p, c: (g ^ c[0], 0, 0))
    whole = lambda a: pl.BlockSpec(a.shape, lambda p, c: (0,) * a.ndim)
    keep = lambda *n: pl.BlockSpec(n, lambda p, c: (0,) * len(n))
    return pl.pallas_call(
        attn_bwd_kernel,
        grid_spec=pltpu.PrefetchScalarGridSpec(
            num_scalar_prefetch=1,
            grid=(PAIRS,),
            in_specs=[block(0)] * 3
            + [own(0), pl.BlockSpec((2, 2, WIN, WIN), lambda p, c: (p, 0, 0, 0))]
            + [block(0)] * 2
            + [at(0)]
            + [block(1)] * 3
            + [own(1), pl.BlockSpec((2, S, S), lambda p, c: (p, 0, 0))]
            + [block(1)] * 2
            + [at(1)]
            + [whole(h1t), whole(ga)]
            + [pl.BlockSpec((CORES, S, 2 * HD), lambda p, c: (0, 0, PAIRS * c[0] + p))]
            + [whole(mine), whole(other)]
            + [pl.BlockSpec((QUARTER, D), lambda p, c: (0, FC // D))] * 4
            + [keep(QUARTER, 3 * DC)] * 4
            + [whole(a) for a in (x, xo, mid, gb1)],
            out_specs=[keep(QUARTER, PACK)] * 4 + [keep(S, D)] * 2,
            scratch_shapes=[pltpu.VMEM((S, 2 * HD), f32)] * 3
            + [pltpu.VMEM((D, 8 * HD), bf16), pltpu.VMEM((D, D), bf16), pltpu.VMEM((CORES, S, 2 * HD), bf16)]
            + [pltpu.VMEM((CORES, S, 3 * DC), bf16), pltpu.VMEM((PAIRS, 8, 2 * HD), f32)]
            + [pltpu.VMEM((128, D), f32), pltpu.VMEM((D, 128), bf16), pltpu.VMEM((D, 3 * DC), bf16)],
        ),
        out_shape=[
            *[jax.ShapeDtypeStruct((QUARTER, PACK), bf16)] * 4,
            *[jax.ShapeDtypeStruct((S, D), f32)] * 2,
        ],
        compiler_params=params(),
        cost_estimate=cost(10 * HC * S * S * 128 + 4 * T * D * 4 * DC, 36e6),
    )(
        place,
        q, k, v, mine, p0, cosine, sine, pos,
        q, k, v, mine, p1, cosine, sine, pos,
        h1t, ga, ga, mine, other, *proj_pieces, *pieces, x, xo, mid, gb1,
    )


def last_kernel(x_ref, ga_ref, gh_ref, other_ref, after_ref, mlp_ref, mlpo_ref, v_ref, gt_ref, out_ref):
    normed, inv_std = stats(x_ref[...].astype(f32))
    gt_ref[...] = ga_ref[...] + norm_back(gh_ref[...] + other_ref[...], normed, inv_std, v_ref[0:1, :])
    out_ref[...] = (after_ref[...] + (mlp_ref[...] + mlpo_ref[...] + v_ref[8:9, :])).astype(bf16)


def last_call(x, ga, gh, other, after, mlp, mlp_other, vec):
    rows = 288
    tile = lambda n: pl.BlockSpec((rows, n), lambda i: (i, 0))
    return pl.pallas_call(
        last_kernel,
        grid=(S // rows,),
        in_specs=[tile(D)] * 7 + [pl.BlockSpec(vec.shape, lambda i: (0, 0))],
        out_specs=[tile(D), tile(D)],
        out_shape=[jax.ShapeDtypeStruct((S, D), f32), jax.ShapeDtypeStruct((S, D), bf16)],
        compiler_params=params(),
        cost_estimate=cost(30 * S * D, S * D * 28),
    )(x, ga, gh, other, after, mlp, mlp_other, vec)


WIDE = PACK + FC


def pack_kernel(q0, q1, q2, q3, f_ref, out_ref):
    total = q0[...].astype(f32) + q1[...].astype(f32) + q2[...].astype(f32) + q3[...].astype(f32)
    fc1 = f_ref[...].astype(f32)
    for n in range(PLANE):
        at = slice(n * KR, (n + 1) * KR)
        out_ref[n, :, :PACK] = total[at, :].astype(bf16)
        out_ref[n, :, PACK:] = fc1[at, :].astype(bf16)


def pack_call(parts, fc1):
    return pl.pallas_call(
        pack_kernel,
        out_shape=jax.ShapeDtypeStruct((PLANE, KR, WIDE), bf16),
        compiler_params=params(),
        cost_estimate=cost(QUARTER * PACK * 4, QUARTER * PACK * 10),
    )(*parts, fc1)


def sum_kernel(in_ref, out_ref):
    total = in_ref[0].astype(f32)
    for n in range(1, PLANE):
        total += in_ref[n].astype(f32)
    out_ref[...] = total


def sum_call(packed):
    return pl.pallas_call(
        sum_kernel,
        out_shape=jax.ShapeDtypeStruct(packed.shape[1:], f32),
        compiler_params=params(),
        cost_estimate=cost(packed.size, packed.size * 2),
    )(packed)


def fc2_kernel(place_ref, mine_ref, other_ref, out_ref, sq_ref):
    first = place_ref[0] == 0
    a, b = mine_ref[...], other_ref[...]
    out_ref[:FR, :] = jnp.where(first, a, b)
    out_ref[FR:, :] = jnp.where(first, b, a)
    total = jnp.sum(a * a + b * b, axis=(0, 1), keepdims=True)
    sq_ref[...] = jnp.broadcast_to(total, sq_ref.shape)


def fc2_call(place, mine, other):
    whole = lambda a: pl.BlockSpec(a.shape, lambda i, c: (0,) * len(a.shape))
    shapes = [jax.ShapeDtypeStruct(s, f32) for s in ((2 * FR, D), (8, 128))]
    return pl.pallas_call(
        fc2_kernel,
        grid_spec=pltpu.PrefetchScalarGridSpec(
            num_scalar_prefetch=1,
            grid=(1,),
            in_specs=[whole(mine), whole(other)],
            out_specs=[whole(a) for a in shapes],
        ),
        out_shape=shapes,
        compiler_params=params(),
        cost_estimate=cost(6 * FR * D, FR * D * 16),
    )(place, mine, other)


def norm_kernel(g_ref, o_ref, sq_ref, out_ref):
    g, o = g_ref[...], o_ref[...]
    part = jnp.sum(g * g + o * o, axis=(0, 1), keepdims=True)
    cross = g[:, 4 * DC : PACK] * o[:, 4 * DC : PACK]
    part += 2.0 * jnp.sum(cross, axis=(0, 1), keepdims=True)
    out_ref[...] = jnp.broadcast_to((part + sq_ref[0:1, 0:1])[None], out_ref.shape)


def norm_call(g, o, squares):
    return pl.pallas_call(
        norm_kernel,
        out_shape=jax.ShapeDtypeStruct((CHIPS, 8, 128), f32),
        compiler_params=params(),
        cost_estimate=cost(4 * KR * PACK, 1e6),
    )(g, o, squares)


RATES = (D ** (-0.5), max(1, 2 * D // S) ** (-0.5), D ** (-0.5), FF ** (-0.5), RATE_VECTOR)


def adam_kernel(place_ref, norm_ref, mine_ref, other_ref, g2_ref, *refs):
    masters, firsts, seconds = refs[0:5], refs[5:10], refs[10:15]
    outs = refs[15:30]
    norm_out, bias_out = refs[30:32]
    core = place_ref[0]
    mine, other = mine_ref[...], other_ref[...]
    g0 = jnp.where(core == 0, mine, other)
    g1 = jnp.where(core == 0, other, mine)
    total = jnp.sum(jnp.sum(norm_ref[...], axis=0)[0:1, 0:1], axis=(0, 1), keepdims=True)
    grad_norm = jnp.sqrt(total)
    norm_out[...] = jnp.broadcast_to(grad_norm, norm_out.shape)
    clip = jnp.minimum(1.0, CLIP_LIMIT / (grad_norm + 1e-06))

    def update(i, at, grad):
        clipped = grad * clip
        master = masters[i][at]
        first = BETA_ONE * firsts[i][at] + (1.0 - BETA_ONE) * clipped
        second = BETA_TWO * seconds[i][at] + (1.0 - BETA_TWO) * clipped * clipped
        first_hat = first / (1.0 - BETA_ONE**STEP)
        second_hat = second / (1.0 - BETA_TWO**STEP)
        decay = 0.0 if i == 4 else DECAY_RATE
        outs[3 * i][at] = master - RATES[i] * (first_hat / (jnp.sqrt(second_hat) + ADAM_EPS) + decay * master)
        outs[3 * i + 1][at] = first
        outs[3 * i + 2][at] = second

    rows = slice(None)
    for c, g in ((0, g0), (1, g1)):
        for p in range(PAIRS):
            for i in range(3):
                col = i * D + c * DC + p * 128
                update(0, (rows, slice(col, col + 128)), g[:, (4 * p + i) * 128 : (4 * p + i + 1) * 128])
            col = c * DC + p * 128
            update(1, (rows, slice(col, col + 128)), g[:, (4 * p + 3) * 128 : (4 * p + 4) * 128])
    for r in range(FC // DC):
        at = slice(PACK + r * DC, PACK + (r + 1) * DC)
        part = exact_dot(g0[:, at], spots_t(0)) + exact_dot(g1[:, at], spots_t(1))
        update(2, (rows, slice(r * D, (r + 1) * D)), part)
    update(3, (rows, rows), g2_ref[...])
    vec = (g0 + g1)[:, 4 * DC : 4 * DC + 128]
    vec = jnp.concatenate([vec, jnp.zeros((16 - KR, 128), f32)], axis=0).T[:16, :KR]
    update(4, (rows, rows), vec[: masters[4].shape[0], :])
    bias_out[...] = vec[7:8, :] * clip


def adam_call(place, norm, mine, other, g2, masters, firsts, seconds):
    whole = lambda a: pl.BlockSpec(a.shape, lambda i, c: (0,) * len(a.shape))
    args = [norm, mine, other, g2, *masters, *firsts, *seconds]
    shapes = [jax.ShapeDtypeStruct(m.shape, f32) for m in masters for _ in range(3)]
    shapes += [jax.ShapeDtypeStruct((1, 128), f32), jax.ShapeDtypeStruct((1, KR), f32)]
    return pl.pallas_call(
        adam_kernel,
        grid_spec=pltpu.PrefetchScalarGridSpec(
            num_scalar_prefetch=1,
            grid=(1,),
            in_specs=[whole(a) for a in args],
            out_specs=[whole(a) for a in shapes],
        ),
        out_shape=shapes,
        compiler_params=params(),
        cost_estimate=cost(20 * KR * FF * 3, 3e6),
    )(place, *args)


def local(
    tokens,
    cotangent,
    counts,
    patch_row,
    patch_col,
    w_qkv,
    w_proj,
    w_fc1,
    w_fc2,
    vectors,
    m_qkv,
    v_qkv,
    m_proj,
    v_proj,
    m_fc1,
    v_fc1,
    m_fc2,
    v_fc2,
    m_vectors,
    v_vectors,
):
    core = lax.axis_index("grp")
    chip = lax.axis_index("dp")
    first_core = core == 0
    along = jnp.where(first_core, chip // PLANE, (chip // SIDE) % SIDE)
    vr = vectors.shape[0]

    def swap(a):
        return lax.ppermute(a, "grp", [(0, 1), (1, 0)])

    def along_line(quarter):
        return [quarter] + [shift(quarter, d) for d in range(1, SIDE)]

    def line_sum(whole):
        return lax.psum_scatter(whole, BOTH, scatter_dimension=0, axis_index_groups=lines(), tiled=True)

    me = jnp.stack([core, along]).astype(jnp.int32)
    shares, share_fc2 = share_call(me, w_qkv, vectors, w_fc2)
    full_fc2 = lax.all_gather(share_fc2, "dp", axis=0, tiled=True)
    quarter = plane_swap(shares).reshape(QUARTER, 3 * DC + 128)
    qkv_pieces = along_line(quarter)
    fc1_b = w_fc1.astype(bf16).reshape(KR, CHIPS, CORES, FR)
    share_fc1 = jnp.where(first_core, fc1_b[:, :, 0], fc1_b[:, :, 1]).reshape(KR, FC)
    share = jnp.concatenate([share_fc1, w_proj.astype(bf16)], axis=1)
    share = jnp.broadcast_to(share[None], (PLANE,) + share.shape)
    share, qkv_pieces[1] = lax.optimization_barrier((share, qkv_pieces[1]))
    quarter = plane_swap(share).reshape(QUARTER, FC + D)

    x_own = tokens.reshape(S, D)
    cot_own = cotangent.reshape(S, D)
    x_other, cot_other = swap(x_own), swap(cot_own)
    ints = jnp.concatenate(
        [
            patch_row.reshape(1, S),
            patch_col.reshape(1, S),
            jnp.pad(counts.reshape(1, 2), ((0, 0), (0, S - 2))),
            jnp.zeros((5, S), jnp.int32),
        ]
    )
    ints = jnp.stack([ints, swap(ints)])
    counts0 = jnp.where(first_core, ints[0, 2, :2], ints[1, 2, :2])
    counts1 = jnp.where(first_core, ints[1, 2, :1], ints[0, 2, :1])
    place = jnp.concatenate([jnp.stack([core, along]).astype(jnp.int32), counts0, counts1])

    vec, h1t, cosine, sine, q, k, v, b1, pos = qkv_call(place, x_own, x_other, ints, qkv_pieces)
    q, quarter = lax.optimization_barrier((q, quarter))
    pieces = along_line(quarter)
    mine, p0, p1 = attn_fwd_call(place, q, k, v)
    mine, pieces[1], pieces[3], cot_other = lax.optimization_barrier((mine, pieces[1], pieces[3], cot_other))
    other = swap(mine)
    gy = gy_call(place, cot_own, cot_other)
    other, gy = lax.optimization_barrier((other, gy))
    after, n2, r2, h2 = proj_call(place, mine, other, x_own, x_other, pieces, vec)
    mlp, mlp_part, gh2, act, gup, gb1 = mlp_call(place, h2, gy, pieces, full_fc2, b1)
    other_gh2 = swap(gh2)
    mlp_other = swap(mlp_part)

    gw2 = fc2_grad_call(place, act, gy)
    gw2, other_gh2 = lax.optimization_barrier((gw2, other_gh2))
    sum_fc2 = line_sum(gw2)
    gw1, ga, gab, sums_mid = mid_call(place, h2, gup, n2, r2, gy, gh2, other_gh2, vec)
    sum_fc1 = line_sum(gw1)
    *gw, gh1, gh1_part = attn_bwd_call(
        place, q, k, v, gab, mine, other, p0, p1, cosine, sine, pos, h1t, qkv_pieces, pieces,
        x_own, x_other, sums_mid, gb1,
    )
    gh1_other = swap(gh1_part)

    got_fc2 = plane_swap(sum_fc2.reshape(PLANE, FR, D))
    parts = [gw[0]] + [shift(gw[d], d) for d in range(1, SIDE)]
    got_fc2, sum_fc1 = lax.optimization_barrier((got_fc2, sum_fc1))
    g_fc2 = sum_call(got_fc2)
    g2, squares = fc2_call(place, g_fc2, swap(g_fc2))
    packed, gh1 = lax.optimization_barrier((pack_call(parts, sum_fc1), gh1))
    got = plane_swap(packed)
    gt, mixed = last_call(x_own, ga, gh1, gh1_other, after, mlp, mlp_other, vec)
    got, g2, squares, gt, mixed = lax.optimization_barrier((got, g2, squares, gt, mixed))
    grads = sum_call(got)

    grads_other = swap(grads)
    norms = lax.all_to_all(norm_call(grads, grads_other, squares), "dp", 0, 0)
    *updates, grad_norm, bias_proj_grad = adam_call(
        place,
        norms,
        grads,
        grads_other,
        g2,
        (w_qkv, w_proj, w_fc1, w_fc2, vectors),
        (m_qkv, m_proj, m_fc1, m_fc2, m_vectors),
        (v_qkv, v_proj, v_fc1, v_fc2, v_vectors),
    )
    return (
        mixed.reshape(1, 1, S, D),
        gt.reshape(1, 1, S, D),
        grad_norm[0, 0],
        *updates,
        bias_proj_grad.reshape(KR),
    )


def solution(mesh):
    frame = P("grp", "dp", None, None)
    ints = P("grp", "dp", None)
    rows = P("dp", None)
    cols = P(None, "dp")
    return jax.shard_map(
        local,
        mesh=mesh,
        in_specs=(frame, frame, ints, ints, ints, rows, rows, rows, rows, cols) + (rows,) * 8 + (cols,) * 2,
        out_specs=(frame, frame, P()) + (rows,) * 12 + (cols,) * 3 + (P("dp"),),
        check_vma=False,
    )
```

```python
import jax
import jax.numpy as jnp
from jax import lax
from jax.experimental import pallas as pl
from jax.experimental.pallas import tpu as pltpu
from jax.sharding import PartitionSpec as P

D = 768
H = 12
HD = 64
FF = 3072
STEP = 10
A = 196
S = 576

CORES = 2
HC = H // CORES
DC = D // CORES
FC = FF // CORES
PAIRS = HC // 2
T = CORES * S

WIN = 208
WINDOWS = (0, 192)

EPS_NORM = 1e-06
BETA_ONE = 0.9
BETA_TWO = 0.95
ADAM_EPS = 1e-08
DECAY_RATE = 0.05
RATE_VECTOR = 0.8
CLIP_LIMIT = 1.0
NEG = -1e30

bf16 = jnp.bfloat16
f32 = jnp.float32
VMEM_LIMIT = 28 * 1024 * 1024


SIDE = 4
CHIPS = SIDE**3
PLANE = SIDE * SIDE
KR = D // CHIPS
FR = FC // CHIPS
BLOCK = SIDE * KR
QUARTER = PLANE * KR
BOTH = ("grp", "dp")


def device(core, x, y, z):
    return ((core * SIDE + x) * SIDE + y) * SIDE + z


def lines():
    r = range(SIDE)
    return [[device(0, a, g, z) for a in r] for g in r for z in r] + [
        [device(1, g, a, z) for a in r] for g in r for z in r
    ]


def planes():
    r = range(SIDE)
    return [[device(0, a, g, z) for g in r for z in r] for a in r] + [
        [device(1, g, a, z) for g in r for z in r] for a in r
    ]


def shift(value, d):
    pairs = [(group[i], group[(i + d) % SIDE]) for group in lines() for i in range(SIDE)]
    return lax.ppermute(value, BOTH, pairs)


def plane_swap(value):
    return lax.all_to_all(value, BOTH, 0, 0, axis_index_groups=planes())


def natural(core, a, g):
    return jnp.where(core == 0, SIDE * a + g, SIDE * g + a)


def lay_out(place_ref, pieces, full_ref):
    core, me = place_ref[0], place_ref[1]
    for d, piece in enumerate(pieces):
        a = (me + SIDE - d) & (SIDE - 1)
        for g in range(SIDE):
            at = pl.multiple_of(natural(core, a, g) * BLOCK, BLOCK)
            full_ref[pl.ds(at, BLOCK), :] = piece[g * BLOCK : (g + 1) * BLOCK, :]


def usable_rows(place_ref, group, rows, base=0):
    slot = lax.broadcasted_iota(jnp.int32, (rows, 1), 0) + base
    first = ((slot < A) & (slot < place_ref[2])) | ((slot >= A) & (slot < 2 * A) & (slot - A < place_ref[3]))
    first = first.astype(f32)
    second = (slot < place_ref[4]).astype(f32)
    if isinstance(group, int):
        return second if group else first
    return jnp.where(group == 0, first, second)


def own_rows(win):
    row = lax.broadcasted_iota(jnp.int32, (WIN, 1), 0) + (WINDOWS[win] - win * A)
    return ((row >= 0) & (row < A)).astype(f32)


def key_bias(place_ref, win=None):
    if win is None:
        key = lax.broadcasted_iota(jnp.int32, (1, S), 1)
        return jnp.where(key < place_ref[4], 0.0, NEG)
    key = lax.broadcasted_iota(jnp.int32, (1, WIN), 1) + (WINDOWS[win] - win * A)
    return jnp.where((key >= 0) & (key < place_ref[2 + win]), 0.0, NEG)


def exact_dot(a, b):
    high = a.astype(bf16)
    rest = a - high.astype(f32)
    mid = rest.astype(bf16)
    low = (rest - mid.astype(f32)).astype(bf16)
    b = b.astype(bf16)
    return dot(high, b) + dot(mid, b) + dot(low, b)


def spots(core, shape, full, part):
    l = lax.broadcasted_iota(jnp.int32, shape, full)
    m = lax.broadcasted_iota(jnp.int32, shape, part)
    q = (m * 2731) >> 16
    return l == m + FR * (q + core)


def spots_t(core):
    return spots(core, (DC, D), 1, 0)


def params(**kw):
    return pltpu.CompilerParams(vmem_limit_bytes=VMEM_LIMIT, **kw)


def cost(flops, bytes_accessed, transcendentals=0):
    return pl.CostEstimate(
        flops=int(flops), bytes_accessed=int(bytes_accessed), transcendentals=int(transcendentals)
    )


def dot(a, b):
    return jnp.dot(a, b, preferred_element_type=f32)


def dot_t(a, b):
    return lax.dot_general(a, b, (((1,), (1,)), ((), ())), preferred_element_type=f32)


def t_dot(a, b):
    return lax.dot_general(a, b, (((0,), (0,)), ((), ())), preferred_element_type=f32)


def stats(z):
    mean_val = jnp.mean(z, axis=-1, keepdims=True)
    centred = z - mean_val
    variance = jnp.mean(centred * centred, axis=-1, keepdims=True)
    inv_std = lax.rsqrt(variance + EPS_NORM)
    return centred * inv_std, inv_std


def norm_back(grad, normed, inv_std, gain):
    e = grad * gain
    return inv_std * (
        e
        - jnp.mean(e, axis=-1, keepdims=True)
        - normed * jnp.mean(e * normed, axis=-1, keepdims=True)
    )


def swap_halves(u):
    lanes = u.shape[1]
    lane = lax.broadcasted_iota(jnp.int32, u.shape, 1)
    up = pltpu.roll(u, lanes - HD // 2, 1)
    down = pltpu.roll(u, HD // 2, 1)
    return jnp.where((lane & (HD - 1)) < HD // 2, up, down)


TURN = 1.5707963267948966


def sin_cos(a):
    k = jnp.floor(a * (1.0 / TURN) + 0.5)
    r = ((a - k * 1.5703125) - k * 4.837512969970703125e-4) - k * 7.54978995489188216e-8
    z = r * r
    s = ((-1.9515295891e-4 * z + 8.3321608736e-3) * z - 1.6666654611e-1) * z * r + r
    c = ((2.443315711809948e-5 * z - 1.388731625493765e-3) * z + 4.166664568298827e-2) * z * z - 0.5 * z + 1.0
    quarter = k.astype(jnp.int32)
    odd = (quarter & 1) == 1
    sine = jnp.where(odd, c, s)
    cosine = jnp.where(odd, s, c)
    sine = jnp.where((quarter & 2) == 0, sine, -sine)
    cosine = jnp.where(((quarter + 1) & 2) == 0, cosine, -cosine)
    return sine, cosine


def share_kernel(place_ref, w_ref, v_ref, f_ref, out_ref, fc2_ref):
    core = place_ref[0]
    w = w_ref[...].astype(bf16)
    cols = []
    for p in range(PAIRS):
        for i in range(3):
            at = i * D + p * 128
            cols.append(jnp.where(core == 0, w[:, at : at + 128], w[:, at + DC : at + DC + 128]))
    v = jnp.concatenate([v_ref[...], jnp.zeros((128 - v_ref.shape[0], KR), f32)], axis=0)
    v = jnp.concatenate([v, jnp.zeros((128, 128 - KR), f32)], axis=1)
    cols.append(v.T[:KR, :].astype(bf16))
    share = jnp.concatenate(cols, axis=1)
    for n in range(PLANE):
        out_ref[n] = share
    fc2_ref[...] = jnp.where(core == 0, f_ref[:FR, :], f_ref[FR:, :]).astype(bf16)


def share_call(place, w, vectors, w_fc2):
    whole = lambda a: pl.BlockSpec(a.shape, lambda i, c: (0, 0))
    return pl.pallas_call(
        share_kernel,
        grid_spec=pltpu.PrefetchScalarGridSpec(
            num_scalar_prefetch=1,
            grid=(1,),
            in_specs=[whole(w), whole(vectors), whole(w_fc2)],
            out_specs=[
                pl.BlockSpec((PLANE, KR, 3 * DC + 128), lambda i, c: (0, 0, 0)),
                pl.BlockSpec((FR, D), lambda i, c: (0, 0)),
            ],
        ),
        out_shape=[
            jax.ShapeDtypeStruct((PLANE, KR, 3 * DC + 128), bf16),
            jax.ShapeDtypeStruct((FR, D), bf16),
        ],
        compiler_params=params(),
        cost_estimate=cost(KR * D * 3, 1e6),
    )(place, w, vectors, w_fc2)


def gy_kernel(place_ref, c_ref, co_ref, gy_ref):
    i = pl.program_id(0)
    keep = usable_rows(place_ref, i ^ place_ref[0], S)
    gy_ref[...] = (jnp.where(i == 0, c_ref[...], co_ref[...]).astype(f32) * keep).astype(bf16)


def gy_call(place, c, co):
    whole = pl.BlockSpec((S, D), lambda i, c: (0, 0))
    return pl.pallas_call(
        gy_kernel,
        grid_spec=pltpu.PrefetchScalarGridSpec(
            num_scalar_prefetch=1,
            grid=(CORES,),
            in_specs=[whole, whole],
            out_specs=pl.BlockSpec((S, D), lambda i, c: (i, 0)),
        ),
        out_shape=jax.ShapeDtypeStruct((T, D), bf16),
        compiler_params=params(),
        cost_estimate=cost(4 * T * D, T * D * 4),
    )(place, c, co)


def qkv_kernel(
    place_ref, x_ref, xo_ref, ints_ref, w0, w1, w2, w3, v0, v1, v2, v3,
    vec_ref, ht_ref, cos_ref, sin_ref, q_out, k_out, v_out, b1_ref, pos_ref,
    w_s, full_s, rows_s, freq_s,
):
    core = place_ref[0]

    @pl.when(pl.program_id(0) == 0)
    def _():
        lay_out(place_ref, (w0, w1, w2, w3), w_s)
        lay_out(place_ref, (v0, v1, v2, v3), full_s)
        rows_s[...] = full_s[...].astype(f32).T[:16, :]
        vec_ref[...] = rows_s[...]
        late = rows_s[8:16, :].astype(bf16)
        units = dot(late, spots(core, (D, DC), 0, 1).astype(bf16))
        for r in range(FC // DC):
            b1_ref[:, r * DC : (r + 1) * DC] = units[2 + r : 3 + r, :]
        src = lax.broadcasted_iota(jnp.int32, (D, DC), 0)
        dst = lax.broadcasted_iota(jnp.int32, (D, DC), 1)
        want = core * (DC // 2) + (dst // HD) * (HD // 2) + (dst & (HD // 2 - 1))
        freq_s[0:8, :] = dot(late, (src == want).astype(bf16))
        freq_s[8:16, :] = dot(late, (src == want + D // 2).astype(bf16))

    i = pl.program_id(0)
    x = jnp.where(i < pl.num_programs(0) // CORES, x_ref[...], xo_ref[...])
    h = stats(x.astype(f32))[0] * rows_s[0:1, :] + rows_s[1:2, :]
    pos = ints_ref[...].astype(f32).T
    pos_ref[...] = pos
    ht_ref[...] = h.T.astype(bf16)
    acc = dot(h.astype(bf16), w_s[...])
    angle = pos[:, 1:2] * freq_s[1:2, :] + pos[:, 0:1] * freq_s[9:10, :]
    lane = lax.broadcasted_iota(jnp.int32, (1, DC), 1)
    sign = jnp.where((lane & (HD - 1)) < HD // 2, -1.0, 1.0)
    small = jnp.max(jnp.abs(angle)) < 8000.0

    @pl.when(small)
    def _():
        sine, cosine = sin_cos(angle)
        cos_ref[...] = cosine
        sin_ref[...] = sine * sign

    @pl.when(jnp.logical_not(small))
    def _():
        cos_ref[...] = jnp.cos(angle)
        sin_ref[...] = jnp.sin(angle) * sign

    cosine, sine = cos_ref[...], sin_ref[...]
    at = pl.ds(pl.multiple_of(core * DC, DC), DC)
    part = lambda i: jnp.concatenate([acc[:, (3 * p + i) * 128 : (3 * p + i + 1) * 128] for p in range(PAIRS)], axis=1)
    q = part(0) + rows_s[4:5, at]
    k = part(1) + rows_s[5:6, at]
    q_out[...] = ((q * cosine + swap_halves(q) * sine) * HD ** (-0.5)).astype(bf16)
    k_out[...] = (k * cosine + swap_halves(k) * sine).astype(bf16)
    v_out[...] = (part(2) + rows_s[6:7, at]).astype(bf16)


def qkv_call(place, x, xo, ints, pieces):
    rows = S
    tile = lambda n: pl.BlockSpec((rows, n), lambda i, c: (i, 0))
    keep = lambda *n: pl.BlockSpec(n, lambda i, c: (0,) * len(n))
    return pl.pallas_call(
        qkv_kernel,
        grid_spec=pltpu.PrefetchScalarGridSpec(
            num_scalar_prefetch=1,
            grid=(CORES,),
            in_specs=[keep(S, D), keep(S, D), pl.BlockSpec((None, 8, S), lambda i, c: (i, 0, 0))]
            + [keep(QUARTER, 3 * DC)] * 4
            + [pl.BlockSpec((QUARTER, 128), lambda i, c: (0, 3 * DC // 128))] * 4,
            out_specs=[keep(16, D), pl.BlockSpec((None, D, rows), lambda i, c: (i, 0, 0))]
            + [tile(DC)] * 5
            + [keep(1, FC), tile(8)],
            scratch_shapes=[
                pltpu.VMEM((D, 3 * DC), bf16),
                pltpu.VMEM((D, 128), bf16),
                pltpu.VMEM((16, D), f32),
                pltpu.VMEM((16, DC), f32),
            ],
        ),
        out_shape=[
            jax.ShapeDtypeStruct((16, D), f32),
            jax.ShapeDtypeStruct((CORES, D, S), bf16),
            jax.ShapeDtypeStruct((T, DC), f32),
            jax.ShapeDtypeStruct((T, DC), f32),
            *[jax.ShapeDtypeStruct((T, DC), bf16)] * 3,
            jax.ShapeDtypeStruct((1, FC), f32),
            jax.ShapeDtypeStruct((T, 8), f32),
        ],
        compiler_params=params(),
        cost_estimate=cost(2 * T * D * 3 * DC + 60 * T * DC, T * D * 6 + D * 3 * DC * 2 + T * DC * 14),
    )(place, x, xo, ints, *pieces, *pieces)


def softmax_head(q, k, v, mine, bias):
    s = dot_t(jnp.where(mine, q, jnp.zeros_like(q)), k) + bias
    e = jnp.exp(s - jnp.max(s, axis=-1, keepdims=True))
    p = e * (1.0 / jnp.sum(e, axis=-1, keepdims=True))
    return p


def attn_fwd_kernel(
    place_ref, q0, k0, v0, q1, k1, v1, o_ref, p0_ref, p1_ref
):
    lane = lax.broadcasted_iota(jnp.int32, (1, 2 * HD), 1)
    low = lane < HD
    q, k, v = q1[0], k1[0], v1[0]
    mixes = []
    bias = key_bias(place_ref)
    for head, mine in ((0, low), (1, ~low)):
        p = softmax_head(q, k, v, mine, bias).astype(bf16)
        p1_ref[head] = p
        mixes.append(dot(p, v))
    mix = jnp.where(low, mixes[0], mixes[1])
    o_ref[1] = jnp.where(usable_rows(place_ref, 1, S) > 0, mix, v.astype(f32)).astype(bf16)
    o_ref[0] = v0[0]
    for win, base in enumerate(WINDOWS):
        q, k, v = (r[0, base : base + WIN, :] for r in (q0, k0, v0))
        own = own_rows(win)
        bias = key_bias(place_ref, win)
        mixes = []
        for head, mine in ((0, low), (1, ~low)):
            p = softmax_head(q, k, v, mine, bias)
            p = (p * own).astype(bf16)
            p0_ref[head, win] = p
            mixes.append(dot(p, v))
        mix = jnp.where(low, mixes[0], mixes[1])
        use = (own * usable_rows(place_ref, 0, WIN, base)) > 0
        before = o_ref[0, base : base + WIN, :].astype(f32)
        o_ref[0, base : base + WIN, :] = jnp.where(use, mix, before).astype(bf16)


def attn_fwd_call(place, q, k, v):
    block = lambda g: pl.BlockSpec((1, S, 2 * HD), lambda p, c: (g ^ c[0], 0, p))
    q, k, v = (a.reshape(CORES, S, DC) for a in (q, k, v))
    return pl.pallas_call(
        attn_fwd_kernel,
        grid_spec=pltpu.PrefetchScalarGridSpec(
            num_scalar_prefetch=1,
            grid=(PAIRS,),
            in_specs=[block(0)] * 3 + [block(1)] * 3,
            out_specs=[
                pl.BlockSpec((CORES, S, 2 * HD), lambda p, c: (0, 0, p)),
                pl.BlockSpec((2, 2, WIN, WIN), lambda p, c: (p, 0, 0, 0)),
                pl.BlockSpec((2, S, S), lambda p, c: (p, 0, 0)),
            ],
        ),
        out_shape=[
            jax.ShapeDtypeStruct((CORES, S, DC), bf16),
            jax.ShapeDtypeStruct((HC, 2, WIN, WIN), bf16),
            jax.ShapeDtypeStruct((HC, S, S), bf16),
        ],
        compiler_params=params(),
        cost_estimate=cost(4 * HC * (S * S + 2 * WIN * WIN) * 128, 12e6, HC * S * S),
    )(place, q, k, v, q, k, v)


def proj_kernel(place_ref, mine_ref, other_ref, x_ref, xo_ref, w0, w1, w2, w3, v_ref, after_ref, n2_ref, r2_ref, h2_ref, w_s):
    @pl.when(pl.program_id(0) == 0)
    def _():
        lay_out(place_ref, (w0, w1, w2, w3), w_s)

    core = place_ref[0]
    at = lambda c: pl.ds(pl.multiple_of(c * DC, DC), DC)
    branch = dot(mine_ref[0], w_s[at(core), :]) + dot(other_ref[0], w_s[at(1 - core), :])
    x = jnp.where(pl.program_id(0) < pl.num_programs(0) // CORES, x_ref[...], xo_ref[...])
    after = x.astype(f32) + (branch + v_ref[7:8, :])
    normed, inv_std = stats(after)
    n2_ref[...] = normed
    r2_ref[...] = jnp.broadcast_to(inv_std, r2_ref.shape)

    @pl.when(pl.program_id(0) < pl.num_programs(0) // CORES)
    def _():
        after_ref[...] = after

    h2_ref[...] = (normed * v_ref[2:3, :] + v_ref[3:4, :]).astype(bf16)


def proj_call(place, mine, other, x, xo, pieces, vec):
    rows = 288
    half = S // rows
    tile = lambda n: pl.BlockSpec((rows, n), lambda i, c: (i, 0))
    whole = lambda a: pl.BlockSpec(a.shape, lambda i, c: (0,) * a.ndim)
    return pl.pallas_call(
        proj_kernel,
        grid_spec=pltpu.PrefetchScalarGridSpec(
            num_scalar_prefetch=1,
            grid=(T // rows,),
            in_specs=[
                pl.BlockSpec((1, rows, DC), lambda i, c: ((i // half) ^ c[0], i % half, 0)),
                pl.BlockSpec((1, rows, DC), lambda i, c: ((i // half) ^ c[0], i % half, 0)),
                pl.BlockSpec((rows, D), lambda i, c: (jnp.minimum(i, half - 1), 0)),
                pl.BlockSpec((rows, D), lambda i, c: (jnp.maximum(i - half, 0), 0)),
            ]
            + [pl.BlockSpec((QUARTER, D), lambda i, c: (0, FC // D))] * 4
            + [whole(vec)],
            out_specs=[pl.BlockSpec((rows, D), lambda i, c: (jnp.minimum(i, half - 1), 0)), tile(D), tile(8), tile(D)],
            scratch_shapes=[pltpu.VMEM((D, D), bf16)],
        ),
        out_shape=[
            jax.ShapeDtypeStruct((S, D), f32),
            jax.ShapeDtypeStruct((T, D), f32),
            jax.ShapeDtypeStruct((T, 8), f32),
            jax.ShapeDtypeStruct((T, D), bf16),
        ],
        compiler_params=params(),
        cost_estimate=cost(2 * T * D * D, T * D * 10 + D * D * 2),
    )(place, mine, other, x, xo, *pieces, vec)


PACK = 4 * DC + 128
K0 = (2.0 / 3.141592653589793) ** 0.5
FT = 768


def gelu_slope(u):
    sq = u * u
    th = jnp.tanh(u * (K0 + (K0 * 0.044715) * sq))
    half = 0.5 + 0.5 * th
    return u * half, half + (u * (half - half * half)) * (2 * K0 + (6 * K0 * 0.044715) * sq)


def mlp_kernel(
    place_ref, h2_ref, gy_ref, w10, w11, w12, w13, w2_ref, b1_ref, mlp_ref, mlpo_ref, gh2b_ref, act_ref, gup_ref, gb1_ref, w1_s
):
    i = pl.program_id(0)

    @pl.when(i == 0)
    def _():
        lay_out(place_ref, (w10, w11, w12, w13), w1_s)
        gb1_ref[...] = jnp.zeros_like(gb1_ref)

    for f in range(FC // FT):
        c = slice(f * FT, (f + 1) * FT)
        act, slope = gelu_slope(dot(h2_ref[...], w1_s[:, c]) + b1_ref[:, c])
        act_ref[:, c] = act.astype(bf16)
        gup = (dot_t(gy_ref[...], w2_ref[c, :]) * slope).astype(bf16)
        gup_ref[:, c] = gup
        gb1_ref[:, c] += jnp.sum(gup.astype(f32), axis=0, keepdims=True)
    gh2b_ref[...] = dot_t(gup_ref[...], w1_s[...]).astype(bf16)
    mlp = dot(act_ref[...], w2_ref[...])
    half = pl.num_programs(0) // CORES

    @pl.when(i < half)
    def _():
        mlp_ref[...] = mlp

    @pl.when(i >= half)
    def _():
        mlpo_ref[...] = mlp


def mlp_call(place, h2, gy, pieces, w2, b1):
    rows = 288
    half = S // rows
    tile = lambda n: pl.BlockSpec((rows, n), lambda i, c: (i, 0))
    whole = lambda a: pl.BlockSpec(a.shape, lambda i, c: (0,) * a.ndim)
    return pl.pallas_call(
        mlp_kernel,
        grid_spec=pltpu.PrefetchScalarGridSpec(
            num_scalar_prefetch=1,
            grid=(T // rows,),
            in_specs=[tile(D), tile(D)]
            + [pl.BlockSpec((QUARTER, FC), lambda i, c: (0, 0))] * 4
            + [whole(w2), whole(b1)],
            out_specs=[
                pl.BlockSpec((rows, D), lambda i, c: (jnp.minimum(i, half - 1), 0)),
                pl.BlockSpec((rows, D), lambda i, c: (jnp.maximum(i - half, 0), 0)),
                tile(D),
                tile(FC),
                tile(FC),
                pl.BlockSpec((1, FC), lambda i, c: (0, 0)),
            ],
            scratch_shapes=[pltpu.VMEM((D, FC), bf16)],
        ),
        out_shape=[
            jax.ShapeDtypeStruct((S, D), f32),
            jax.ShapeDtypeStruct((S, D), f32),
            jax.ShapeDtypeStruct((T, D), bf16),
            jax.ShapeDtypeStruct((T, FC), bf16),
            jax.ShapeDtypeStruct((T, FC), bf16),
            jax.ShapeDtypeStruct((1, FC), f32),
        ],
        compiler_params=params(),
        cost_estimate=cost(8 * T * D * FC, 30e6, T * FC),
    )(place, h2, gy, *pieces, w2, b1)


def by_line(place_ref, value, block, out_ref):
    core = place_ref[0]
    for n in range(PLANE):
        to = jnp.where(core == 0, n, (n % SIDE) * SIDE + n // SIDE)
        out_ref[pl.ds(pl.multiple_of(to * block, block), block), :] = value[n * block : (n + 1) * block, :].astype(bf16)


def fc2_grad_kernel(place_ref, act_ref, gy_ref, out_ref):
    value = t_dot(act_ref[...], gy_ref[...])
    block = SIDE * FR
    for n in range(FT // block):
        m = pl.program_id(0) * (FT // block) + n
        to = jnp.where(place_ref[0] == 0, m, (m & (SIDE - 1)) * SIDE + m // SIDE)
        out_ref[pl.ds(pl.multiple_of(to * block, block), block), :] = value[n * block : (n + 1) * block, :].astype(bf16)


def fc2_grad_call(place, act, gy):
    return pl.pallas_call(
        fc2_grad_kernel,
        grid_spec=pltpu.PrefetchScalarGridSpec(
            num_scalar_prefetch=1,
            grid=(FC // FT,),
            in_specs=[pl.BlockSpec((T, FT), lambda i, c: (0, i)), pl.BlockSpec((T, D), lambda i, c: (0, 0))],
            out_specs=pl.BlockSpec((FC, D), lambda i, c: (0, 0)),
        ),
        out_shape=jax.ShapeDtypeStruct((FC, D), bf16),
        compiler_params=params(),
        cost_estimate=cost(2 * T * D * FC, T * (D + FC) * 2 + D * FC * 2),
    )(place, act, gy)


def mid_kernel(
    place_ref, h2_ref, gup_ref, n2_ref, r2_ref, gy_ref, gh2_ref, other_ref, v_ref, gw_ref, ga_ref, gab_ref, sums_ref
):
    i = pl.program_id(0)
    by_line(place_ref, t_dot(h2_ref[...], gup_ref[...]), BLOCK, gw_ref)
    normed, inv_std = n2_ref[...], r2_ref[:, 0:1]
    gh2 = gh2_ref[...].astype(f32) + other_ref[...].astype(f32)
    gy = gy_ref[...].astype(f32)
    ga = gy + norm_back(gh2, normed, inv_std, v_ref[2:3, :])
    gab = ga.astype(bf16)
    gab_ref[...] = gab
    mine = (i < pl.num_programs(0) // CORES).astype(f32)
    sums = [
        mine * jnp.sum(a, axis=0, keepdims=True) for a in (gh2 * normed, gh2, gab.astype(f32), gy)
    ] + [jnp.zeros((4, D), f32)]
    sums = jnp.concatenate(sums, axis=0)

    @pl.when(i == 0)
    def _():
        sums_ref[...] = sums

    @pl.when(i > 0)
    def _():
        sums_ref[...] += sums

    @pl.when(i < pl.num_programs(0) // CORES)
    def _():
        ga_ref[...] = ga


def mid_call(place, h2, gup, n2, r2, gy, gh2, other, vec):
    rows = 288
    half = S // rows
    cols = FC * rows // T
    tile = lambda n: pl.BlockSpec((rows, n), lambda i, c: (i, 0))
    flipped = pl.BlockSpec((rows, D), lambda i, c: ((i + half) % (2 * half), 0))
    whole = lambda a: pl.BlockSpec(a.shape, lambda i, c: (0,) * a.ndim)
    return pl.pallas_call(
        mid_kernel,
        grid_spec=pltpu.PrefetchScalarGridSpec(
            num_scalar_prefetch=1,
            grid=(T // rows,),
            in_specs=[whole(h2), pl.BlockSpec((T, cols), lambda i, c: (0, i))]
            + [tile(D), tile(8), tile(D), tile(D), flipped, whole(vec)],
            out_specs=[
                pl.BlockSpec((D, cols), lambda i, c: (0, i)),
                pl.BlockSpec((rows, D), lambda i, c: (jnp.minimum(i, half - 1), 0)),
                tile(D),
                pl.BlockSpec((8, D), lambda i, c: (0, 0)),
            ],
        ),
        out_shape=[
            jax.ShapeDtypeStruct((D, FC), bf16),
            jax.ShapeDtypeStruct((S, D), f32),
            jax.ShapeDtypeStruct((T, D), bf16),
            jax.ShapeDtypeStruct((8, D), f32),
        ],
        compiler_params=params(),
        cost_estimate=cost(2 * T * D * FC, T * D * 18 + T * FC * 2 + D * FC * 2),
    )(place, h2, gup, n2, r2, gy, gh2, other, vec)


def back_head(q_t, k, v, do, do_t, delta, p, mine, head):
    gp = dot_t(jnp.where(mine, do, jnp.zeros_like(do)), v)
    gs = (p.astype(f32) * (gp - delta)).astype(bf16)
    at = slice(head * HD, (head + 1) * HD)
    return dot(gs, k), dot(q_t[at, :], gs), dot(do_t[at, :], p)


def deltas(do, o, low):
    prod = do.astype(f32) * o.astype(f32)
    d0 = jnp.sum(jnp.where(low, prod, 0.0), axis=-1, keepdims=True)
    d1 = jnp.sum(jnp.where(low, 0.0, prod), axis=-1, keepdims=True)
    return d0, d1


def attn_bwd_kernel(
    place_ref,
    q0, k0, v0, o0, p0, cos0, sin0, pos0,
    q1, k1, v1, o1, p1, cos1, sin1, pos1,
    h1t_ref, ga_ref, cols_ref, mine_ref, other_ref, y0, y1, y2, y3, w0, w1, w2, w3,
    x_ref, xo_ref, mid_ref, gb1_ref,
    gw0, gw1, gw2, gw3, gh_ref, gho_ref,
    gq_s, gk_s, gv_s, gw_s, y_s, do_s, gqkv_s, att_s, rows_s, full_s, w_s,
):
    lane = lax.broadcasted_iota(jnp.int32, (1, 2 * HD), 1)
    low = lane < HD
    pair = pl.program_id(0)
    core = place_ref[0]

    @pl.when(pair == 0)
    def _():
        lay_out(place_ref, (y0, y1, y2, y3), y_s)

    wy = y_s[pl.ds(pl.multiple_of(core * DC + pair * 2 * HD, 2 * HD), 2 * HD), :]
    for frame in range(CORES):
        do_s[frame] = dot_t(ga_ref[frame], wy).astype(bf16)

    def finish(frame, q, k, cos_ref, sin_ref, pos_ref):
        cosine, sine = cos_ref[0], sin_ref[0]
        gq = gq_s[...] * HD ** (-0.5)
        gk = gk_s[...]
        sq, sk = swap_halves(gq), swap_halves(gk)
        turn = (q.astype(f32) * HD**0.5) * sq + k.astype(f32) * sk
        gq = (gq * cosine - sq * sine).astype(bf16)
        gk = (gk * cosine - sk * sine).astype(bf16)
        gv = gv_s[...].astype(bf16)
        for i, g in enumerate((gq, gk, gv)):
            gqkv_s[frame ^ core, :, pl.ds(pl.multiple_of(pair * 6 * HD + i * 2 * HD, 2 * HD), 2 * HD)] = g
        pos = pos_ref[0]
        col = jnp.sum(turn * pos[:, 1:2], axis=0, keepdims=True)
        row = jnp.sum(turn * pos[:, 0:1], axis=0, keepdims=True)
        bias = [jnp.sum(g.astype(f32), axis=0, keepdims=True) for g in (gq, gk, gv)]
        return jnp.concatenate([col, row] + bias, axis=0)

    q, k, v, do = q1[0], k1[0], v1[0], do_s[1 ^ core]
    d = deltas(do, o1[0], low)
    q_t, do_t = q.astype(f32).T.astype(bf16), do.astype(f32).T.astype(bf16)
    out = [
        back_head(q_t, k, v, do, do_t, d[head], p1[head], mine, head)
        for head, mine in ((0, low), (1, ~low))
    ]
    gq_s[...] = jnp.where(low, out[0][0], out[1][0])
    gk_s[...] = jnp.concatenate([out[0][1], out[1][1]], axis=0).T
    gv_s[...] = jnp.concatenate([out[0][2], out[1][2]], axis=0).T
    sums1 = finish(1, q, k, cos1, sin1, pos1)
    gq_s[...] = jnp.zeros_like(gq_s)
    gk_s[...] = jnp.zeros_like(gk_s)
    gv_s[...] = jnp.zeros_like(gv_s)
    for win, base in enumerate(WINDOWS):
        at = pl.ds(base, WIN)
        q, k, v, o = (r[0, at, :] for r in (q0, k0, v0, o0))
        do = do_s[core, at, :]
        d = deltas(do, o, low)
        q_t, do_t = q.astype(f32).T.astype(bf16), do.astype(f32).T.astype(bf16)
        out = [
            back_head(q_t, k, v, do, do_t, d[head], p0[head, win], mine, head)
            for head, mine in ((0, low), (1, ~low))
        ]
        gq_s[at, :] += jnp.where(low, out[0][0], out[1][0])
        gk_s[at, :] += jnp.concatenate([out[0][1], out[1][1]], axis=0).T
        gv_s[at, :] += jnp.concatenate([out[0][2], out[1][2]], axis=0).T
    sums0 = finish(0, q0[0], k0[0], cos0, sin0, pos0)
    att_s[pair, 0:5, :] = sums0 + sums1

    gw = jnp.zeros((D, 6 * HD), f32)
    gw_mine = jnp.zeros((2 * HD, DC), f32)
    gw_other = jnp.zeros((2 * HD, DC), f32)
    for frame in range(CORES):
        cols = cols_ref[frame].astype(f32).T.astype(bf16)
        gw_mine += dot(cols, mine_ref[frame ^ core])
        gw_other += dot(cols, other_ref[frame ^ core])
        gw += dot(h1t_ref[frame], gqkv_s[frame, :, pl.ds(pl.multiple_of(pair * 6 * HD, 6 * HD), 6 * HD)])
    gw_s[:, : 6 * HD] = gw.astype(bf16)
    at = lambda c: pl.ds(pl.multiple_of(c * DC, DC), DC)
    gw_s[at(core), 6 * HD :] = gw_mine.T.astype(bf16)
    gw_s[at(1 - core), 6 * HD :] = gw_other.T.astype(bf16)
    to_chips(place_ref, gw_s, (gw0, gw1, gw2, gw3), pl.ds(pl.multiple_of(pair * 8 * HD, 8 * HD), 8 * HD))

    @pl.when(pair == PAIRS - 1)
    def _():
        lay_out(place_ref, (w0, w1, w2, w3), w_s)
        rows_s[...] = jnp.zeros_like(rows_s)
        for frame, x, out in ((0, x_ref, gh_ref), (1, xo_ref, gho_ref)):
            for half in range(2):
                at = slice(half * (S // 2), (half + 1) * (S // 2))
                gh = dot_t(gqkv_s[frame, at, :], w_s[...])
                out[at, :] = gh
                normed, _ = stats(x[at, :].astype(f32))
                rows_s[0:1, :] += jnp.sum(gh * normed, axis=0, keepdims=True)
                rows_s[1:2, :] += jnp.sum(gh, axis=0, keepdims=True)
        rows_s[2:4, :] = mid_ref[0:2, :]
        rows_s[7:9, :] = mid_ref[2:4, :]
        att = jnp.concatenate([att_s[p] for p in range(PAIRS)], axis=1)
        rows_s[4:7, pl.ds(pl.multiple_of(core * DC, DC), DC)] = att[2:5, :]
        src = lax.broadcasted_iota(jnp.int32, (DC, D), 0)
        dst = lax.broadcasted_iota(jnp.int32, (DC, D), 1)
        want = core * (DC // 2) + (src // HD) * (HD // 2) + (src & (HD // 2 - 1))
        side = lax.broadcasted_iota(jnp.int32, (1, DC), 1)
        turn = jnp.where((side & (HD - 1)) < HD // 2, att, -att)
        rows_s[9:10, :] = exact_dot(turn, dst == want)[0:1, :] + exact_dot(turn, dst == want + D // 2)[1:2, :]
        gb1 = jnp.concatenate([gb1_ref[:, r * DC : (r + 1) * DC] for r in range(FC // DC)] * 2, axis=0)
        rows_s[10:14, :] = exact_dot(gb1, spots_t(core))[:4, :]
        full_s[...] = rows_s[...].T.astype(bf16)
        to_chips(place_ref, full_s, (gw0, gw1, gw2, gw3), slice(4 * DC, PACK))


def to_chips(place_ref, full_ref, outs, cols):
    for d, out in enumerate(outs):
        a = (place_ref[1] + d) & (SIDE - 1)
        for g in range(SIDE):
            at = pl.multiple_of(natural(place_ref[0], a, g) * BLOCK, BLOCK)
            out[g * BLOCK : (g + 1) * BLOCK, cols] = full_ref[pl.ds(at, BLOCK), :]


def attn_bwd_call(
    place, q, k, v, ga, mine, other, p0, p1, cosine, sine, pos, h1t, pieces, proj_pieces, x, xo, mid, gb1
):
    q, k, v, cosine, sine, pos, ga = (a.reshape(CORES, S, -1) for a in (q, k, v, cosine, sine, pos, ga))
    block = lambda g: pl.BlockSpec((1, S, 2 * HD), lambda p, c: (g ^ c[0], 0, p))
    own = lambda g: pl.BlockSpec((1, S, 2 * HD), lambda p, c: (g, 0, p))
    at = lambda g: pl.BlockSpec((1, S, 8), lambda p, c: (g ^ c[0], 0, 0))
    whole = lambda a: pl.BlockSpec(a.shape, lambda p, c: (0,) * a.ndim)
    keep = lambda *n: pl.BlockSpec(n, lambda p, c: (0,) * len(n))
    return pl.pallas_call(
        attn_bwd_kernel,
        grid_spec=pltpu.PrefetchScalarGridSpec(
            num_scalar_prefetch=1,
            grid=(PAIRS,),
            in_specs=[block(0)] * 3
            + [own(0), pl.BlockSpec((2, 2, WIN, WIN), lambda p, c: (p, 0, 0, 0))]
            + [block(0)] * 2
            + [at(0)]
            + [block(1)] * 3
            + [own(1), pl.BlockSpec((2, S, S), lambda p, c: (p, 0, 0))]
            + [block(1)] * 2
            + [at(1)]
            + [whole(h1t), whole(ga)]
            + [pl.BlockSpec((CORES, S, 2 * HD), lambda p, c: (0, 0, PAIRS * c[0] + p))]
            + [whole(mine), whole(other)]
            + [pl.BlockSpec((QUARTER, D), lambda p, c: (0, FC // D))] * 4
            + [keep(QUARTER, 3 * DC)] * 4
            + [whole(a) for a in (x, xo, mid, gb1)],
            out_specs=[keep(QUARTER, PACK)] * 4 + [keep(S, D)] * 2,
            scratch_shapes=[pltpu.VMEM((S, 2 * HD), f32)] * 3
            + [pltpu.VMEM((D, 8 * HD), bf16), pltpu.VMEM((D, D), bf16), pltpu.VMEM((CORES, S, 2 * HD), bf16)]
            + [pltpu.VMEM((CORES, S, 3 * DC), bf16), pltpu.VMEM((PAIRS, 8, 2 * HD), f32)]
            + [pltpu.VMEM((128, D), f32), pltpu.VMEM((D, 128), bf16), pltpu.VMEM((D, 3 * DC), bf16)],
        ),
        out_shape=[
            *[jax.ShapeDtypeStruct((QUARTER, PACK), bf16)] * 4,
            *[jax.ShapeDtypeStruct((S, D), f32)] * 2,
        ],
        compiler_params=params(),
        cost_estimate=cost(10 * HC * S * S * 128 + 4 * T * D * 4 * DC, 36e6),
    )(
        place,
        q, k, v, mine, p0, cosine, sine, pos,
        q, k, v, mine, p1, cosine, sine, pos,
        h1t, ga, ga, mine, other, *proj_pieces, *pieces, x, xo, mid, gb1,
    )


def last_kernel(x_ref, ga_ref, gh_ref, other_ref, after_ref, mlp_ref, mlpo_ref, v_ref, gt_ref, out_ref):
    normed, inv_std = stats(x_ref[...].astype(f32))
    gt_ref[...] = ga_ref[...] + norm_back(gh_ref[...] + other_ref[...], normed, inv_std, v_ref[0:1, :])
    out_ref[...] = (after_ref[...] + (mlp_ref[...] + mlpo_ref[...] + v_ref[8:9, :])).astype(bf16)


def last_call(x, ga, gh, other, after, mlp, mlp_other, vec):
    rows = 288
    tile = lambda n: pl.BlockSpec((rows, n), lambda i: (i, 0))
    return pl.pallas_call(
        last_kernel,
        grid=(S // rows,),
        in_specs=[tile(D)] * 7 + [pl.BlockSpec(vec.shape, lambda i: (0, 0))],
        out_specs=[tile(D), tile(D)],
        out_shape=[jax.ShapeDtypeStruct((S, D), f32), jax.ShapeDtypeStruct((S, D), bf16)],
        compiler_params=params(),
        cost_estimate=cost(30 * S * D, S * D * 28),
    )(x, ga, gh, other, after, mlp, mlp_other, vec)


WIDE = PACK + FC


def pack_kernel(q0, q1, q2, q3, f_ref, out_ref):
    total = q0[...].astype(f32) + q1[...].astype(f32) + q2[...].astype(f32) + q3[...].astype(f32)
    fc1 = f_ref[...].astype(f32)
    for n in range(PLANE):
        at = slice(n * KR, (n + 1) * KR)
        out_ref[n, :, :PACK] = total[at, :].astype(bf16)
        out_ref[n, :, PACK:] = fc1[at, :].astype(bf16)


def pack_call(parts, fc1):
    return pl.pallas_call(
        pack_kernel,
        out_shape=jax.ShapeDtypeStruct((PLANE, KR, WIDE), bf16),
        compiler_params=params(),
        cost_estimate=cost(QUARTER * PACK * 4, QUARTER * PACK * 10),
    )(*parts, fc1)


def sum_kernel(in_ref, out_ref):
    total = in_ref[0].astype(f32)
    for n in range(1, PLANE):
        total += in_ref[n].astype(f32)
    out_ref[...] = total


def sum_call(packed):
    return pl.pallas_call(
        sum_kernel,
        out_shape=jax.ShapeDtypeStruct(packed.shape[1:], f32),
        compiler_params=params(),
        cost_estimate=cost(packed.size, packed.size * 2),
    )(packed)


def fc2_kernel(place_ref, mine_ref, other_ref, out_ref, sq_ref):
    first = place_ref[0] == 0
    a, b = mine_ref[...], other_ref[...]
    out_ref[:FR, :] = jnp.where(first, a, b)
    out_ref[FR:, :] = jnp.where(first, b, a)
    total = jnp.sum(a * a + b * b, axis=(0, 1), keepdims=True)
    sq_ref[...] = jnp.broadcast_to(total, sq_ref.shape)


def fc2_call(place, mine, other):
    whole = lambda a: pl.BlockSpec(a.shape, lambda i, c: (0,) * len(a.shape))
    shapes = [jax.ShapeDtypeStruct(s, f32) for s in ((2 * FR, D), (8, 128))]
    return pl.pallas_call(
        fc2_kernel,
        grid_spec=pltpu.PrefetchScalarGridSpec(
            num_scalar_prefetch=1,
            grid=(1,),
            in_specs=[whole(mine), whole(other)],
            out_specs=[whole(a) for a in shapes],
        ),
        out_shape=shapes,
        compiler_params=params(),
        cost_estimate=cost(6 * FR * D, FR * D * 16),
    )(place, mine, other)


def norm_kernel(g_ref, o_ref, sq_ref, out_ref):
    g, o = g_ref[...], o_ref[...]
    part = jnp.sum(g * g + o * o, axis=(0, 1), keepdims=True)
    cross = g[:, 4 * DC : PACK] * o[:, 4 * DC : PACK]
    part += 2.0 * jnp.sum(cross, axis=(0, 1), keepdims=True)
    out_ref[...] = jnp.broadcast_to((part + sq_ref[0:1, 0:1])[None], out_ref.shape)


def norm_call(g, o, squares):
    return pl.pallas_call(
        norm_kernel,
        out_shape=jax.ShapeDtypeStruct((CHIPS, 8, 128), f32),
        compiler_params=params(),
        cost_estimate=cost(4 * KR * PACK, 1e6),
    )(g, o, squares)


RATES = (D ** (-0.5), max(1, 2 * D // S) ** (-0.5), D ** (-0.5), FF ** (-0.5), RATE_VECTOR)


def adam_kernel(place_ref, norm_ref, mine_ref, other_ref, g2_ref, *refs):
    masters, firsts, seconds = refs[0:5], refs[5:10], refs[10:15]
    outs = refs[15:30]
    norm_out, bias_out = refs[30:32]
    core = place_ref[0]
    mine, other = mine_ref[...], other_ref[...]
    g0 = jnp.where(core == 0, mine, other)
    g1 = jnp.where(core == 0, other, mine)
    total = jnp.sum(jnp.sum(norm_ref[...], axis=0)[0:1, 0:1], axis=(0, 1), keepdims=True)
    grad_norm = jnp.sqrt(total)
    norm_out[...] = jnp.broadcast_to(grad_norm, norm_out.shape)
    clip = jnp.minimum(1.0, CLIP_LIMIT / (grad_norm + 1e-06))

    def update(i, at, grad):
        clipped = grad * clip
        master = masters[i][at]
        first = BETA_ONE * firsts[i][at] + (1.0 - BETA_ONE) * clipped
        second = BETA_TWO * seconds[i][at] + (1.0 - BETA_TWO) * clipped * clipped
        first_hat = first / (1.0 - BETA_ONE**STEP)
        second_hat = second / (1.0 - BETA_TWO**STEP)
        decay = 0.0 if i == 4 else DECAY_RATE
        outs[3 * i][at] = master - RATES[i] * (first_hat / (jnp.sqrt(second_hat) + ADAM_EPS) + decay * master)
        outs[3 * i + 1][at] = first
        outs[3 * i + 2][at] = second

    rows = slice(None)
    for c, g in ((0, g0), (1, g1)):
        for p in range(PAIRS):
            for i in range(3):
                col = i * D + c * DC + p * 128
                update(0, (rows, slice(col, col + 128)), g[:, (4 * p + i) * 128 : (4 * p + i + 1) * 128])
            col = c * DC + p * 128
            update(1, (rows, slice(col, col + 128)), g[:, (4 * p + 3) * 128 : (4 * p + 4) * 128])
    for r in range(FC // DC):
        at = slice(PACK + r * DC, PACK + (r + 1) * DC)
        part = exact_dot(g0[:, at], spots_t(0)) + exact_dot(g1[:, at], spots_t(1))
        update(2, (rows, slice(r * D, (r + 1) * D)), part)
    update(3, (rows, rows), g2_ref[...])
    vec = (g0 + g1)[:, 4 * DC : 4 * DC + 128]
    vec = jnp.concatenate([vec, jnp.zeros((16 - KR, 128), f32)], axis=0).T[:16, :KR]
    update(4, (rows, rows), vec[: masters[4].shape[0], :])
    bias_out[...] = vec[7:8, :] * clip


def adam_call(place, norm, mine, other, g2, masters, firsts, seconds):
    whole = lambda a: pl.BlockSpec(a.shape, lambda i, c: (0,) * len(a.shape))
    args = [norm, mine, other, g2, *masters, *firsts, *seconds]
    shapes = [jax.ShapeDtypeStruct(m.shape, f32) for m in masters for _ in range(3)]
    shapes += [jax.ShapeDtypeStruct((1, 128), f32), jax.ShapeDtypeStruct((1, KR), f32)]
    return pl.pallas_call(
        adam_kernel,
        grid_spec=pltpu.PrefetchScalarGridSpec(
            num_scalar_prefetch=1,
            grid=(1,),
            in_specs=[whole(a) for a in args],
            out_specs=[whole(a) for a in shapes],
        ),
        out_shape=shapes,
        compiler_params=params(),
        cost_estimate=cost(20 * KR * FF * 3, 3e6),
    )(place, *args)


def local(
    tokens,
    cotangent,
    counts,
    patch_row,
    patch_col,
    w_qkv,
    w_proj,
    w_fc1,
    w_fc2,
    vectors,
    m_qkv,
    v_qkv,
    m_proj,
    v_proj,
    m_fc1,
    v_fc1,
    m_fc2,
    v_fc2,
    m_vectors,
    v_vectors,
):
    core = lax.axis_index("grp")
    chip = lax.axis_index("dp")
    first_core = core == 0
    along = jnp.where(first_core, chip // PLANE, (chip // SIDE) % SIDE)
    vr = vectors.shape[0]

    def swap(a):
        return lax.ppermute(a, "grp", [(0, 1), (1, 0)])

    def along_line(quarter):
        return [quarter] + [shift(quarter, d) for d in range(1, SIDE)]

    def line_sum(whole):
        return lax.psum_scatter(whole, BOTH, scatter_dimension=0, axis_index_groups=lines(), tiled=True)

    me = jnp.stack([core, along]).astype(jnp.int32)
    shares, share_fc2 = share_call(me, w_qkv, vectors, w_fc2)
    full_fc2 = lax.all_gather(share_fc2, "dp", axis=0, tiled=True)
    quarter = plane_swap(shares).reshape(QUARTER, 3 * DC + 128)
    qkv_pieces = along_line(quarter)
    fc1_b = w_fc1.astype(bf16).reshape(KR, CHIPS, CORES, FR)
    share_fc1 = jnp.where(first_core, fc1_b[:, :, 0], fc1_b[:, :, 1]).reshape(KR, FC)
    share = jnp.concatenate([share_fc1, w_proj.astype(bf16)], axis=1)
    share = jnp.broadcast_to(share[None], (PLANE,) + share.shape)
    share, qkv_pieces[1] = lax.optimization_barrier((share, qkv_pieces[1]))
    quarter = plane_swap(share).reshape(QUARTER, FC + D)

    x_own = tokens.reshape(S, D)
    cot_own = cotangent.reshape(S, D)
    x_other, cot_other = swap(x_own), swap(cot_own)
    ints = jnp.concatenate(
        [
            patch_row.reshape(1, S),
            patch_col.reshape(1, S),
            jnp.pad(counts.reshape(1, 2), ((0, 0), (0, S - 2))),
            jnp.zeros((5, S), jnp.int32),
        ]
    )
    ints = jnp.stack([ints, swap(ints)])
    counts0 = jnp.where(first_core, ints[0, 2, :2], ints[1, 2, :2])
    counts1 = jnp.where(first_core, ints[1, 2, :1], ints[0, 2, :1])
    place = jnp.concatenate([jnp.stack([core, along]).astype(jnp.int32), counts0, counts1])

    vec, h1t, cosine, sine, q, k, v, b1, pos = qkv_call(place, x_own, x_other, ints, qkv_pieces)
    q, quarter = lax.optimization_barrier((q, quarter))
    pieces = along_line(quarter)
    mine, p0, p1 = attn_fwd_call(place, q, k, v)
    mine, pieces, cot_other = lax.optimization_barrier((mine, pieces, cot_other))
    other = swap(mine)
    gy = gy_call(place, cot_own, cot_other)
    other, gy = lax.optimization_barrier((other, gy))
    after, n2, r2, h2 = proj_call(place, mine, other, x_own, x_other, pieces, vec)
    mlp, mlp_part, gh2, act, gup, gb1 = mlp_call(place, h2, gy, pieces, full_fc2, b1)
    other_gh2 = swap(gh2)
    mlp_other = swap(mlp_part)

    gw2 = fc2_grad_call(place, act, gy)
    gw2, other_gh2 = lax.optimization_barrier((gw2, other_gh2))
    sum_fc2 = line_sum(gw2)
    gw1, ga, gab, sums_mid = mid_call(place, h2, gup, n2, r2, gy, gh2, other_gh2, vec)
    sum_fc1 = line_sum(gw1)
    *gw, gh1, gh1_part = attn_bwd_call(
        place, q, k, v, gab, mine, other, p0, p1, cosine, sine, pos, h1t, qkv_pieces, pieces,
        x_own, x_other, sums_mid, gb1,
    )
    gh1_other = swap(gh1_part)

    got_fc2 = plane_swap(sum_fc2.reshape(PLANE, FR, D))
    parts = [gw[0]] + [shift(gw[d], d) for d in range(1, SIDE)]
    got_fc2, sum_fc1 = lax.optimization_barrier((got_fc2, sum_fc1))
    g_fc2 = sum_call(got_fc2)
    g2, squares = fc2_call(place, g_fc2, swap(g_fc2))
    packed, gh1 = lax.optimization_barrier((pack_call(parts, sum_fc1), gh1))
    got = plane_swap(packed)
    gt, mixed = last_call(x_own, ga, gh1, gh1_other, after, mlp, mlp_other, vec)
    got, g2, squares, gt, mixed = lax.optimization_barrier((got, g2, squares, gt, mixed))
    grads = sum_call(got)

    grads_other = swap(grads)
    norms = lax.all_to_all(norm_call(grads, grads_other, squares), "dp", 0, 0)
    *updates, grad_norm, bias_proj_grad = adam_call(
        place,
        norms,
        grads,
        grads_other,
        g2,
        (w_qkv, w_proj, w_fc1, w_fc2, vectors),
        (m_qkv, m_proj, m_fc1, m_fc2, m_vectors),
        (v_qkv, v_proj, v_fc1, v_fc2, v_vectors),
    )
    return (
        mixed.reshape(1, 1, S, D),
        gt.reshape(1, 1, S, D),
        grad_norm[0, 0],
        *updates,
        bias_proj_grad.reshape(KR),
    )


def solution(mesh):
    frame = P("grp", "dp", None, None)
    ints = P("grp", "dp", None)
    rows = P("dp", None)
    cols = P(None, "dp")
    return jax.shard_map(
        local,
        mesh=mesh,
        in_specs=(frame, frame, ints, ints, ints, rows, rows, rows, rows, cols) + (rows,) * 8 + (cols,) * 2,
        out_specs=(frame, frame, P()) + (rows,) * 12 + (cols,) * 3 + (P("dp"),),
        check_vma=False,
    )
```

```python
import jax
import jax.numpy as jnp
from jax import lax
from jax.experimental import pallas as pl
from jax.experimental.pallas import tpu as pltpu
from jax.sharding import PartitionSpec as P

D = 768
H = 12
HD = 64
FF = 3072
STEP = 10
A = 196
S = 576

CORES = 2
HC = H // CORES
DC = D // CORES
FC = FF // CORES
PAIRS = HC // 2
T = CORES * S

WIN = 208
WINDOWS = (0, 192)

EPS_NORM = 1e-06
BETA_ONE = 0.9
BETA_TWO = 0.95
ADAM_EPS = 1e-08
DECAY_RATE = 0.05
RATE_VECTOR = 0.8
CLIP_LIMIT = 1.0
NEG = -1e30

bf16 = jnp.bfloat16
f32 = jnp.float32
VMEM_LIMIT = 56 * 1024 * 1024


SIDE = 4
CHIPS = SIDE**3
PLANE = SIDE * SIDE
KR = D // CHIPS
FR = FC // CHIPS
BLOCK = SIDE * KR
QUARTER = PLANE * KR
BOTH = ("grp", "dp")


def device(core, x, y, z):
    return ((core * SIDE + x) * SIDE + y) * SIDE + z


def lines():
    r = range(SIDE)
    return [[device(0, a, g, z) for a in r] for g in r for z in r] + [
        [device(1, g, a, z) for a in r] for g in r for z in r
    ]


def planes():
    r = range(SIDE)
    return [[device(0, a, g, z) for g in r for z in r] for a in r] + [
        [device(1, g, a, z) for g in r for z in r] for a in r
    ]


def shift(value, d):
    pairs = [(group[i], group[(i + d) % SIDE]) for group in lines() for i in range(SIDE)]
    return lax.ppermute(value, BOTH, pairs)


def plane_swap(value):
    return lax.all_to_all(value, BOTH, 0, 0, axis_index_groups=planes())


def natural(core, a, g):
    return jnp.where(core == 0, SIDE * a + g, SIDE * g + a)


def lay_out(place_ref, pieces, full_ref):
    core, me = place_ref[0], place_ref[1]
    for d, piece in enumerate(pieces):
        a = (me + SIDE - d) & (SIDE - 1)
        for g in range(SIDE):
            at = pl.multiple_of(natural(core, a, g) * BLOCK, BLOCK)
            full_ref[pl.ds(at, BLOCK), :] = piece[g * BLOCK : (g + 1) * BLOCK, :]


def usable_rows(place_ref, group, rows, base=0):
    slot = lax.broadcasted_iota(jnp.int32, (rows, 1), 0) + base
    first = ((slot < A) & (slot < place_ref[2])) | ((slot >= A) & (slot < 2 * A) & (slot - A < place_ref[3]))
    first = first.astype(f32)
    second = (slot < place_ref[4]).astype(f32)
    if isinstance(group, int):
        return second if group else first
    return jnp.where(group == 0, first, second)


def own_rows(win):
    row = lax.broadcasted_iota(jnp.int32, (WIN, 1), 0) + (WINDOWS[win] - win * A)
    return ((row >= 0) & (row < A)).astype(f32)


def key_bias(place_ref, win=None):
    if win is None:
        key = lax.broadcasted_iota(jnp.int32, (1, S), 1)
        return jnp.where(key < place_ref[4], 0.0, NEG)
    key = lax.broadcasted_iota(jnp.int32, (1, WIN), 1) + (WINDOWS[win] - win * A)
    return jnp.where((key >= 0) & (key < place_ref[2 + win]), 0.0, NEG)


def exact_dot(a, b):
    high = a.astype(bf16)
    rest = a - high.astype(f32)
    mid = rest.astype(bf16)
    low = (rest - mid.astype(f32)).astype(bf16)
    b = b.astype(bf16)
    return dot(high, b) + dot(mid, b) + dot(low, b)


def spots(core, shape, full, part):
    l = lax.broadcasted_iota(jnp.int32, shape, full)
    m = lax.broadcasted_iota(jnp.int32, shape, part)
    q = (m * 2731) >> 16
    return l == m + FR * (q + core)


def spots_t(core):
    return spots(core, (DC, D), 1, 0)


SMALL_LIMIT = 16 * 1024 * 1024


def params(limit=VMEM_LIMIT):
    return pltpu.CompilerParams(vmem_limit_bytes=limit)


def cost(flops, bytes_accessed, transcendentals=0):
    return pl.CostEstimate(
        flops=int(flops), bytes_accessed=int(bytes_accessed), transcendentals=int(transcendentals)
    )


def dot(a, b):
    return jnp.dot(a, b, preferred_element_type=f32)


def dot_t(a, b):
    return lax.dot_general(a, b, (((1,), (1,)), ((), ())), preferred_element_type=f32)


def t_dot(a, b):
    return lax.dot_general(a, b, (((0,), (0,)), ((), ())), preferred_element_type=f32)


def stats(z):
    mean_val = jnp.mean(z, axis=-1, keepdims=True)
    centred = z - mean_val
    variance = jnp.mean(centred * centred, axis=-1, keepdims=True)
    inv_std = lax.rsqrt(variance + EPS_NORM)
    return centred * inv_std, inv_std


def norm_back(grad, normed, inv_std, gain):
    e = grad * gain
    return inv_std * (
        e
        - jnp.mean(e, axis=-1, keepdims=True)
        - normed * jnp.mean(e * normed, axis=-1, keepdims=True)
    )


def swap_halves(u):
    lanes = u.shape[1]
    lane = lax.broadcasted_iota(jnp.int32, u.shape, 1)
    up = pltpu.roll(u, lanes - HD // 2, 1)
    down = pltpu.roll(u, HD // 2, 1)
    return jnp.where((lane & (HD - 1)) < HD // 2, up, down)


TURN = 1.5707963267948966


def sin_cos(a):
    k = jnp.floor(a * (1.0 / TURN) + 0.5)
    r = ((a - k * 1.5703125) - k * 4.837512969970703125e-4) - k * 7.54978995489188216e-8
    z = r * r
    s = ((-1.9515295891e-4 * z + 8.3321608736e-3) * z - 1.6666654611e-1) * z * r + r
    c = ((2.443315711809948e-5 * z - 1.388731625493765e-3) * z + 4.166664568298827e-2) * z * z - 0.5 * z + 1.0
    quarter = k.astype(jnp.int32)
    odd = (quarter & 1) == 1
    sine = jnp.where(odd, c, s)
    cosine = jnp.where(odd, s, c)
    sine = jnp.where((quarter & 2) == 0, sine, -sine)
    cosine = jnp.where(((quarter + 1) & 2) == 0, cosine, -cosine)
    return sine, cosine


def share_kernel(place_ref, w_ref, v_ref, f_ref, out_ref, fc2_ref):
    core = place_ref[0]
    w = w_ref[...].astype(bf16)
    cols = []
    for p in range(PAIRS):
        for i in range(3):
            at = i * D + p * 128
            cols.append(jnp.where(core == 0, w[:, at : at + 128], w[:, at + DC : at + DC + 128]))
    v = jnp.concatenate([v_ref[...], jnp.zeros((128 - v_ref.shape[0], KR), f32)], axis=0)
    v = jnp.concatenate([v, jnp.zeros((128, 128 - KR), f32)], axis=1)
    cols.append(v.T[:KR, :].astype(bf16))
    share = jnp.concatenate(cols, axis=1)
    for n in range(PLANE):
        out_ref[n] = share
    fc2_ref[...] = jnp.where(core == 0, f_ref[:FR, :], f_ref[FR:, :]).astype(bf16)


def share_call(place, w, vectors, w_fc2):
    whole = lambda a: pl.BlockSpec(a.shape, lambda i, c: (0, 0))
    return pl.pallas_call(
        share_kernel,
        grid_spec=pltpu.PrefetchScalarGridSpec(
            num_scalar_prefetch=1,
            grid=(1,),
            in_specs=[whole(w), whole(vectors), whole(w_fc2)],
            out_specs=[
                pl.BlockSpec((PLANE, KR, 3 * DC + 128), lambda i, c: (0, 0, 0)),
                pl.BlockSpec((FR, D), lambda i, c: (0, 0)),
            ],
        ),
        out_shape=[
            jax.ShapeDtypeStruct((PLANE, KR, 3 * DC + 128), bf16),
            jax.ShapeDtypeStruct((FR, D), bf16),
        ],
        compiler_params=params(),
        cost_estimate=cost(KR * D * 3, 1e6),
    )(place, w, vectors, w_fc2)


def gy_kernel(place_ref, c_ref, co_ref, gy_ref):
    i = pl.program_id(0)
    keep = usable_rows(place_ref, i ^ place_ref[0], S)
    gy_ref[...] = (jnp.where(i == 0, c_ref[...], co_ref[...]).astype(f32) * keep).astype(bf16)


def gy_call(place, c, co):
    whole = pl.BlockSpec((S, D), lambda i, c: (0, 0))
    return pl.pallas_call(
        gy_kernel,
        grid_spec=pltpu.PrefetchScalarGridSpec(
            num_scalar_prefetch=1,
            grid=(CORES,),
            in_specs=[whole, whole],
            out_specs=pl.BlockSpec((S, D), lambda i, c: (i, 0)),
        ),
        out_shape=jax.ShapeDtypeStruct((T, D), bf16),
        compiler_params=params(),
        cost_estimate=cost(4 * T * D, T * D * 4),
    )(place, c, co)


def qkv_kernel(
    place_ref, x_ref, xo_ref, ints_ref, w0, w1, w2, w3, v0, v1, v2, v3,
    vec_ref, ht_ref, cos_ref, sin_ref, q_out, k_out, v_out, b1_ref, pos_ref,
    w_s, full_s, rows_s, freq_s,
):
    core = place_ref[0]

    @pl.when(pl.program_id(0) == 0)
    def _():
        lay_out(place_ref, (w0, w1, w2, w3), w_s)
        lay_out(place_ref, (v0, v1, v2, v3), full_s)
        rows_s[...] = full_s[...].astype(f32).T[:16, :]
        vec_ref[...] = rows_s[...]
        late = rows_s[8:16, :].astype(bf16)
        units = dot(late, spots(core, (D, DC), 0, 1).astype(bf16))
        for r in range(FC // DC):
            b1_ref[:, r * DC : (r + 1) * DC] = units[2 + r : 3 + r, :]
        src = lax.broadcasted_iota(jnp.int32, (D, DC), 0)
        dst = lax.broadcasted_iota(jnp.int32, (D, DC), 1)
        want = core * (DC // 2) + (dst // HD) * (HD // 2) + (dst & (HD // 2 - 1))
        freq_s[0:8, :] = dot(late, (src == want).astype(bf16))
        freq_s[8:16, :] = dot(late, (src == want + D // 2).astype(bf16))

    i = pl.program_id(0)
    x = jnp.where(i < pl.num_programs(0) // CORES, x_ref[...], xo_ref[...])
    h = stats(x.astype(f32))[0] * rows_s[0:1, :] + rows_s[1:2, :]
    pos = ints_ref[...].astype(f32).T
    pos_ref[...] = pos
    ht_ref[...] = h.T.astype(bf16)
    acc = dot(h.astype(bf16), w_s[...])
    angle = pos[:, 1:2] * freq_s[1:2, :] + pos[:, 0:1] * freq_s[9:10, :]
    lane = lax.broadcasted_iota(jnp.int32, (1, DC), 1)
    sign = jnp.where((lane & (HD - 1)) < HD // 2, -1.0, 1.0)
    small = jnp.max(jnp.abs(angle)) < 8000.0

    @pl.when(small)
    def _():
        sine, cosine = sin_cos(angle)
        cos_ref[...] = cosine
        sin_ref[...] = sine * sign

    @pl.when(jnp.logical_not(small))
    def _():
        cos_ref[...] = jnp.cos(angle)
        sin_ref[...] = jnp.sin(angle) * sign

    cosine, sine = cos_ref[...], sin_ref[...]
    at = pl.ds(pl.multiple_of(core * DC, DC), DC)
    part = lambda i: jnp.concatenate([acc[:, (3 * p + i) * 128 : (3 * p + i + 1) * 128] for p in range(PAIRS)], axis=1)
    q = part(0) + rows_s[4:5, at]
    k = part(1) + rows_s[5:6, at]
    q_out[...] = ((q * cosine + swap_halves(q) * sine) * HD ** (-0.5)).astype(bf16)
    k_out[...] = (k * cosine + swap_halves(k) * sine).astype(bf16)
    v_out[...] = (part(2) + rows_s[6:7, at]).astype(bf16)


def qkv_call(place, x, xo, ints, pieces):
    rows = S
    tile = lambda n: pl.BlockSpec((rows, n), lambda i, c: (i, 0))
    keep = lambda *n: pl.BlockSpec(n, lambda i, c: (0,) * len(n))
    return pl.pallas_call(
        qkv_kernel,
        grid_spec=pltpu.PrefetchScalarGridSpec(
            num_scalar_prefetch=1,
            grid=(CORES,),
            in_specs=[keep(S, D), keep(S, D), pl.BlockSpec((None, 8, S), lambda i, c: (i, 0, 0))]
            + [keep(QUARTER, 3 * DC)] * 4
            + [pl.BlockSpec((QUARTER, 128), lambda i, c: (0, 3 * DC // 128))] * 4,
            out_specs=[keep(16, D), pl.BlockSpec((None, D, rows), lambda i, c: (i, 0, 0))]
            + [tile(DC)] * 5
            + [keep(1, FC), tile(8)],
            scratch_shapes=[
                pltpu.VMEM((D, 3 * DC), bf16),
                pltpu.VMEM((D, 128), bf16),
                pltpu.VMEM((16, D), f32),
                pltpu.VMEM((16, DC), f32),
            ],
        ),
        out_shape=[
            jax.ShapeDtypeStruct((16, D), f32),
            jax.ShapeDtypeStruct((CORES, D, S), bf16),
            jax.ShapeDtypeStruct((T, DC), f32),
            jax.ShapeDtypeStruct((T, DC), f32),
            *[jax.ShapeDtypeStruct((T, DC), bf16)] * 3,
            jax.ShapeDtypeStruct((1, FC), f32),
            jax.ShapeDtypeStruct((T, 8), f32),
        ],
        compiler_params=params(),
        cost_estimate=cost(2 * T * D * 3 * DC + 60 * T * DC, T * D * 6 + D * 3 * DC * 2 + T * DC * 14),
    )(place, x, xo, ints, *pieces, *pieces)


def softmax_head(q, k, v, mine, bias):
    s = dot_t(jnp.where(mine, q, jnp.zeros_like(q)), k) + bias
    e = jnp.exp(s - jnp.max(s, axis=-1, keepdims=True))
    p = e * (1.0 / jnp.sum(e, axis=-1, keepdims=True))
    return p


def attn_fwd_kernel(
    place_ref, q0, k0, v0, q1, k1, v1, o_ref, p0_ref, p1_ref
):
    lane = lax.broadcasted_iota(jnp.int32, (1, 2 * HD), 1)
    low = lane < HD
    q, k, v = q1[0], k1[0], v1[0]
    mixes = []
    bias = key_bias(place_ref)
    for head, mine in ((0, low), (1, ~low)):
        p = softmax_head(q, k, v, mine, bias).astype(bf16)
        p1_ref[head] = p
        mixes.append(dot(p, v))
    mix = jnp.where(low, mixes[0], mixes[1])
    o_ref[1] = jnp.where(usable_rows(place_ref, 1, S) > 0, mix, v.astype(f32)).astype(bf16)
    o_ref[0] = v0[0]
    for win, base in enumerate(WINDOWS):
        q, k, v = (r[0, base : base + WIN, :] for r in (q0, k0, v0))
        own = own_rows(win)
        bias = key_bias(place_ref, win)
        mixes = []
        for head, mine in ((0, low), (1, ~low)):
            p = softmax_head(q, k, v, mine, bias)
            p = (p * own).astype(bf16)
            p0_ref[head, win] = p
            mixes.append(dot(p, v))
        mix = jnp.where(low, mixes[0], mixes[1])
        use = (own * usable_rows(place_ref, 0, WIN, base)) > 0
        before = o_ref[0, base : base + WIN, :].astype(f32)
        o_ref[0, base : base + WIN, :] = jnp.where(use, mix, before).astype(bf16)


def attn_fwd_call(place, q, k, v):
    block = lambda g: pl.BlockSpec((1, S, 2 * HD), lambda p, c: (g ^ c[0], 0, p))
    q, k, v = (a.reshape(CORES, S, DC) for a in (q, k, v))
    return pl.pallas_call(
        attn_fwd_kernel,
        grid_spec=pltpu.PrefetchScalarGridSpec(
            num_scalar_prefetch=1,
            grid=(PAIRS,),
            in_specs=[block(0)] * 3 + [block(1)] * 3,
            out_specs=[
                pl.BlockSpec((CORES, S, 2 * HD), lambda p, c: (0, 0, p)),
                pl.BlockSpec((2, 2, WIN, WIN), lambda p, c: (p, 0, 0, 0)),
                pl.BlockSpec((2, S, S), lambda p, c: (p, 0, 0)),
            ],
        ),
        out_shape=[
            jax.ShapeDtypeStruct((CORES, S, DC), bf16),
            jax.ShapeDtypeStruct((HC, 2, WIN, WIN), bf16),
            jax.ShapeDtypeStruct((HC, S, S), bf16),
        ],
        compiler_params=params(),
        cost_estimate=cost(4 * HC * (S * S + 2 * WIN * WIN) * 128, 12e6, HC * S * S),
    )(place, q, k, v, q, k, v)


def proj_kernel(place_ref, mine_ref, other_ref, x_ref, xo_ref, w0, w1, w2, w3, v_ref, after_ref, n2_ref, r2_ref, h2_ref, w_s):
    @pl.when(pl.program_id(0) == 0)
    def _():
        lay_out(place_ref, (w0, w1, w2, w3), w_s)

    core = place_ref[0]
    at = lambda c: pl.ds(pl.multiple_of(c * DC, DC), DC)
    branch = dot(mine_ref[0], w_s[at(core), :]) + dot(other_ref[0], w_s[at(1 - core), :])
    x = jnp.where(pl.program_id(0) < pl.num_programs(0) // CORES, x_ref[...], xo_ref[...])
    after = x.astype(f32) + (branch + v_ref[7:8, :])
    normed, inv_std = stats(after)
    n2_ref[...] = normed
    r2_ref[...] = jnp.broadcast_to(inv_std, r2_ref.shape)

    @pl.when(pl.program_id(0) < pl.num_programs(0) // CORES)
    def _():
        after_ref[...] = after

    h2_ref[...] = (normed * v_ref[2:3, :] + v_ref[3:4, :]).astype(bf16)


def proj_call(place, mine, other, x, xo, pieces, vec):
    rows = 288
    half = S // rows
    tile = lambda n: pl.BlockSpec((rows, n), lambda i, c: (i, 0))
    whole = lambda a: pl.BlockSpec(a.shape, lambda i, c: (0,) * a.ndim)
    return pl.pallas_call(
        proj_kernel,
        grid_spec=pltpu.PrefetchScalarGridSpec(
            num_scalar_prefetch=1,
            grid=(T // rows,),
            in_specs=[
                pl.BlockSpec((1, rows, DC), lambda i, c: ((i // half) ^ c[0], i % half, 0)),
                pl.BlockSpec((1, rows, DC), lambda i, c: ((i // half) ^ c[0], i % half, 0)),
                pl.BlockSpec((rows, D), lambda i, c: (jnp.minimum(i, half - 1), 0)),
                pl.BlockSpec((rows, D), lambda i, c: (jnp.maximum(i - half, 0), 0)),
            ]
            + [pl.BlockSpec((QUARTER, D), lambda i, c: (0, FC // D))] * 4
            + [whole(vec)],
            out_specs=[pl.BlockSpec((rows, D), lambda i, c: (jnp.minimum(i, half - 1), 0)), tile(D), tile(8), tile(D)],
            scratch_shapes=[pltpu.VMEM((D, D), bf16)],
        ),
        out_shape=[
            jax.ShapeDtypeStruct((S, D), f32),
            jax.ShapeDtypeStruct((T, D), f32),
            jax.ShapeDtypeStruct((T, 8), f32),
            jax.ShapeDtypeStruct((T, D), bf16),
        ],
        compiler_params=params(),
        cost_estimate=cost(2 * T * D * D, T * D * 10 + D * D * 2),
    )(place, mine, other, x, xo, *pieces, vec)


PACK = 4 * DC + 128
K0 = (2.0 / 3.141592653589793) ** 0.5
FT = 768


def gelu_slope(u):
    sq = u * u
    th = jnp.tanh(u * (K0 + (K0 * 0.044715) * sq))
    half = 0.5 + 0.5 * th
    return u * half, half + (u * (half - half * half)) * (2 * K0 + (6 * K0 * 0.044715) * sq)


def mlp_kernel(
    place_ref, h2_ref, gy_ref, w10, w11, w12, w13, w2_ref, b1_ref, mlp_ref, mlpo_ref, gh2b_ref, act_ref, gup_ref, gb1_ref, w1_s
):
    i = pl.program_id(0)

    @pl.when(i == 0)
    def _():
        lay_out(place_ref, (w10, w11, w12, w13), w1_s)
        gb1_ref[...] = jnp.zeros_like(gb1_ref)

    for f in range(FC // FT):
        c = slice(f * FT, (f + 1) * FT)
        act, slope = gelu_slope(dot(h2_ref[...], w1_s[:, c]) + b1_ref[:, c])
        act_ref[:, c] = act.astype(bf16)
        gup = (dot_t(gy_ref[...], w2_ref[c, :]) * slope).astype(bf16)
        gup_ref[:, c] = gup
        gb1_ref[:, c] += jnp.sum(gup.astype(f32), axis=0, keepdims=True)
    gh2b_ref[...] = dot_t(gup_ref[...], w1_s[...]).astype(bf16)
    mlp = dot(act_ref[...], w2_ref[...])
    half = pl.num_programs(0) // CORES

    @pl.when(i < half)
    def _():
        mlp_ref[...] = mlp

    @pl.when(i >= half)
    def _():
        mlpo_ref[...] = mlp


def mlp_call(place, h2, gy, pieces, w2, b1):
    rows = 288
    half = S // rows
    tile = lambda n: pl.BlockSpec((rows, n), lambda i, c: (i, 0))
    whole = lambda a: pl.BlockSpec(a.shape, lambda i, c: (0,) * a.ndim)
    return pl.pallas_call(
        mlp_kernel,
        grid_spec=pltpu.PrefetchScalarGridSpec(
            num_scalar_prefetch=1,
            grid=(T // rows,),
            in_specs=[tile(D), tile(D)]
            + [pl.BlockSpec((QUARTER, FC), lambda i, c: (0, 0))] * 4
            + [whole(w2), whole(b1)],
            out_specs=[
                pl.BlockSpec((rows, D), lambda i, c: (jnp.minimum(i, half - 1), 0)),
                pl.BlockSpec((rows, D), lambda i, c: (jnp.maximum(i - half, 0), 0)),
                tile(D),
                tile(FC),
                tile(FC),
                pl.BlockSpec((1, FC), lambda i, c: (0, 0)),
            ],
            scratch_shapes=[pltpu.VMEM((D, FC), bf16)],
        ),
        out_shape=[
            jax.ShapeDtypeStruct((S, D), f32),
            jax.ShapeDtypeStruct((S, D), f32),
            jax.ShapeDtypeStruct((T, D), bf16),
            jax.ShapeDtypeStruct((T, FC), bf16),
            jax.ShapeDtypeStruct((T, FC), bf16),
            jax.ShapeDtypeStruct((1, FC), f32),
        ],
        compiler_params=params(),
        cost_estimate=cost(8 * T * D * FC, 30e6, T * FC),
    )(place, h2, gy, *pieces, w2, b1)


def by_line(place_ref, value, block, out_ref):
    core = place_ref[0]
    for n in range(PLANE):
        to = jnp.where(core == 0, n, (n % SIDE) * SIDE + n // SIDE)
        out_ref[pl.ds(pl.multiple_of(to * block, block), block), :] = value[n * block : (n + 1) * block, :].astype(bf16)


def fc2_grad_kernel(place_ref, act_ref, gy_ref, out_ref):
    value = t_dot(act_ref[...], gy_ref[...])
    block = SIDE * FR
    for n in range(FT // block):
        m = pl.program_id(0) * (FT // block) + n
        to = jnp.where(place_ref[0] == 0, m, (m & (SIDE - 1)) * SIDE + m // SIDE)
        out_ref[pl.ds(pl.multiple_of(to * block, block), block), :] = value[n * block : (n + 1) * block, :].astype(bf16)


def fc2_grad_call(place, act, gy):
    return pl.pallas_call(
        fc2_grad_kernel,
        grid_spec=pltpu.PrefetchScalarGridSpec(
            num_scalar_prefetch=1,
            grid=(FC // FT,),
            in_specs=[pl.BlockSpec((T, FT), lambda i, c: (0, i)), pl.BlockSpec((T, D), lambda i, c: (0, 0))],
            out_specs=pl.BlockSpec((FC, D), lambda i, c: (0, 0)),
        ),
        out_shape=jax.ShapeDtypeStruct((FC, D), bf16),
        compiler_params=params(),
        cost_estimate=cost(2 * T * D * FC, T * (D + FC) * 2 + D * FC * 2),
    )(place, act, gy)


def mid_kernel(
    place_ref, h2_ref, gup_ref, n2_ref, r2_ref, gy_ref, gh2_ref, other_ref, v_ref, gw_ref, ga_ref, gab_ref, sums_ref
):
    i = pl.program_id(0)
    by_line(place_ref, t_dot(h2_ref[...], gup_ref[...]), BLOCK, gw_ref)
    normed, inv_std = n2_ref[...], r2_ref[:, 0:1]
    gh2 = gh2_ref[...].astype(f32) + other_ref[...].astype(f32)
    gy = gy_ref[...].astype(f32)
    ga = gy + norm_back(gh2, normed, inv_std, v_ref[2:3, :])
    gab = ga.astype(bf16)
    gab_ref[...] = gab
    mine = (i < pl.num_programs(0) // CORES).astype(f32)
    sums = [
        mine * jnp.sum(a, axis=0, keepdims=True) for a in (gh2 * normed, gh2, gab.astype(f32), gy)
    ] + [jnp.zeros((4, D), f32)]
    sums = jnp.concatenate(sums, axis=0)

    @pl.when(i == 0)
    def _():
        sums_ref[...] = sums

    @pl.when(i > 0)
    def _():
        sums_ref[...] += sums

    @pl.when(i < pl.num_programs(0) // CORES)
    def _():
        ga_ref[...] = ga


def mid_call(place, h2, gup, n2, r2, gy, gh2, other, vec):
    rows = 288
    half = S // rows
    cols = FC * rows // T
    tile = lambda n: pl.BlockSpec((rows, n), lambda i, c: (i, 0))
    flipped = pl.BlockSpec((rows, D), lambda i, c: ((i + half) % (2 * half), 0))
    whole = lambda a: pl.BlockSpec(a.shape, lambda i, c: (0,) * a.ndim)
    return pl.pallas_call(
        mid_kernel,
        grid_spec=pltpu.PrefetchScalarGridSpec(
            num_scalar_prefetch=1,
            grid=(T // rows,),
            in_specs=[whole(h2), pl.BlockSpec((T, cols), lambda i, c: (0, i))]
            + [tile(D), tile(8), tile(D), tile(D), flipped, whole(vec)],
            out_specs=[
                pl.BlockSpec((D, cols), lambda i, c: (0, i)),
                pl.BlockSpec((rows, D), lambda i, c: (jnp.minimum(i, half - 1), 0)),
                tile(D),
                pl.BlockSpec((8, D), lambda i, c: (0, 0)),
            ],
        ),
        out_shape=[
            jax.ShapeDtypeStruct((D, FC), bf16),
            jax.ShapeDtypeStruct((S, D), f32),
            jax.ShapeDtypeStruct((T, D), bf16),
            jax.ShapeDtypeStruct((8, D), f32),
        ],
        compiler_params=params(),
        cost_estimate=cost(2 * T * D * FC, T * D * 18 + T * FC * 2 + D * FC * 2),
    )(place, h2, gup, n2, r2, gy, gh2, other, vec)


def back_head(q_t, k, v, do, do_t, delta, p, mine, head):
    gp = dot_t(jnp.where(mine, do, jnp.zeros_like(do)), v)
    gs = (p.astype(f32) * (gp - delta)).astype(bf16)
    at = slice(head * HD, (head + 1) * HD)
    return dot(gs, k), dot(q_t[at, :], gs), dot(do_t[at, :], p)


def deltas(do, o, low):
    prod = do.astype(f32) * o.astype(f32)
    d0 = jnp.sum(jnp.where(low, prod, 0.0), axis=-1, keepdims=True)
    d1 = jnp.sum(jnp.where(low, 0.0, prod), axis=-1, keepdims=True)
    return d0, d1


def attn_bwd_kernel(
    place_ref,
    q0, k0, v0, o0, p0, cos0, sin0, pos0,
    q1, k1, v1, o1, p1, cos1, sin1, pos1,
    h1t_ref, ga_ref, cols_ref, mine_ref, other_ref, y0, y1, y2, y3, w0, w1, w2, w3,
    x_ref, xo_ref, mid_ref, gb1_ref,
    gw0, gw1, gw2, gw3, gh_ref, gho_ref,
    gq_s, gk_s, gv_s, gw_s, y_s, do_s, gqkv_s, att_s, rows_s, full_s, w_s,
):
    lane = lax.broadcasted_iota(jnp.int32, (1, 2 * HD), 1)
    low = lane < HD
    pair = pl.program_id(0)
    core = place_ref[0]

    @pl.when(pair == 0)
    def _():
        lay_out(place_ref, (y0, y1, y2, y3), y_s)

    wy = y_s[pl.ds(pl.multiple_of(core * DC + pair * 2 * HD, 2 * HD), 2 * HD), :]
    for frame in range(CORES):
        do_s[frame] = dot_t(ga_ref[frame], wy).astype(bf16)

    def finish(frame, q, k, cos_ref, sin_ref, pos_ref):
        cosine, sine = cos_ref[0], sin_ref[0]
        gq = gq_s[...] * HD ** (-0.5)
        gk = gk_s[...]
        sq, sk = swap_halves(gq), swap_halves(gk)
        turn = (q.astype(f32) * HD**0.5) * sq + k.astype(f32) * sk
        gq = (gq * cosine - sq * sine).astype(bf16)
        gk = (gk * cosine - sk * sine).astype(bf16)
        gv = gv_s[...].astype(bf16)
        for i, g in enumerate((gq, gk, gv)):
            gqkv_s[frame ^ core, :, pl.ds(pl.multiple_of(pair * 6 * HD + i * 2 * HD, 2 * HD), 2 * HD)] = g
        pos = pos_ref[0]
        col = jnp.sum(turn * pos[:, 1:2], axis=0, keepdims=True)
        row = jnp.sum(turn * pos[:, 0:1], axis=0, keepdims=True)
        bias = [jnp.sum(g.astype(f32), axis=0, keepdims=True) for g in (gq, gk, gv)]
        return jnp.concatenate([col, row] + bias, axis=0)

    q, k, v, do = q1[0], k1[0], v1[0], do_s[1 ^ core]
    d = deltas(do, o1[0], low)
    q_t, do_t = q.astype(f32).T.astype(bf16), do.astype(f32).T.astype(bf16)
    out = [
        back_head(q_t, k, v, do, do_t, d[head], p1[head], mine, head)
        for head, mine in ((0, low), (1, ~low))
    ]
    gq_s[...] = jnp.where(low, out[0][0], out[1][0])
    gk_s[...] = jnp.concatenate([out[0][1], out[1][1]], axis=0).T
    gv_s[...] = jnp.concatenate([out[0][2], out[1][2]], axis=0).T
    sums1 = finish(1, q, k, cos1, sin1, pos1)
    gq_s[...] = jnp.zeros_like(gq_s)
    gk_s[...] = jnp.zeros_like(gk_s)
    gv_s[...] = jnp.zeros_like(gv_s)
    for win, base in enumerate(WINDOWS):
        at = pl.ds(base, WIN)
        q, k, v, o = (r[0, at, :] for r in (q0, k0, v0, o0))
        do = do_s[core, at, :]
        d = deltas(do, o, low)
        q_t, do_t = q.astype(f32).T.astype(bf16), do.astype(f32).T.astype(bf16)
        out = [
            back_head(q_t, k, v, do, do_t, d[head], p0[head, win], mine, head)
            for head, mine in ((0, low), (1, ~low))
        ]
        gq_s[at, :] += jnp.where(low, out[0][0], out[1][0])
        gk_s[at, :] += jnp.concatenate([out[0][1], out[1][1]], axis=0).T
        gv_s[at, :] += jnp.concatenate([out[0][2], out[1][2]], axis=0).T
    sums0 = finish(0, q0[0], k0[0], cos0, sin0, pos0)
    att_s[pair, 0:5, :] = sums0 + sums1

    gw = jnp.zeros((D, 6 * HD), f32)
    gw_mine = jnp.zeros((2 * HD, DC), f32)
    gw_other = jnp.zeros((2 * HD, DC), f32)
    for frame in range(CORES):
        cols = cols_ref[frame].astype(f32).T.astype(bf16)
        gw_mine += dot(cols, mine_ref[frame ^ core])
        gw_other += dot(cols, other_ref[frame ^ core])
        gw += dot(h1t_ref[frame], gqkv_s[frame, :, pl.ds(pl.multiple_of(pair * 6 * HD, 6 * HD), 6 * HD)])
    gw_s[:, : 6 * HD] = gw.astype(bf16)
    at = lambda c: pl.ds(pl.multiple_of(c * DC, DC), DC)
    gw_s[at(core), 6 * HD :] = gw_mine.T.astype(bf16)
    gw_s[at(1 - core), 6 * HD :] = gw_other.T.astype(bf16)
    to_chips(place_ref, gw_s, (gw0, gw1, gw2, gw3), pl.ds(pl.multiple_of(pair * 8 * HD, 8 * HD), 8 * HD))

    @pl.when(pair == PAIRS - 1)
    def _():
        lay_out(place_ref, (w0, w1, w2, w3), w_s)
        rows_s[...] = jnp.zeros_like(rows_s)
        for frame, x, out in ((0, x_ref, gh_ref), (1, xo_ref, gho_ref)):
            for half in range(2):
                at = slice(half * (S // 2), (half + 1) * (S // 2))
                gh = dot_t(gqkv_s[frame, at, :], w_s[...])
                out[at, :] = gh
                normed, _ = stats(x[at, :].astype(f32))
                rows_s[0:1, :] += jnp.sum(gh * normed, axis=0, keepdims=True)
                rows_s[1:2, :] += jnp.sum(gh, axis=0, keepdims=True)
        rows_s[2:4, :] = mid_ref[0:2, :]
        rows_s[7:9, :] = mid_ref[2:4, :]
        att = jnp.concatenate([att_s[p] for p in range(PAIRS)], axis=1)
        rows_s[4:7, pl.ds(pl.multiple_of(core * DC, DC), DC)] = att[2:5, :]
        src = lax.broadcasted_iota(jnp.int32, (DC, D), 0)
        dst = lax.broadcasted_iota(jnp.int32, (DC, D), 1)
        want = core * (DC // 2) + (src // HD) * (HD // 2) + (src & (HD // 2 - 1))
        side = lax.broadcasted_iota(jnp.int32, (1, DC), 1)
        turn = jnp.where((side & (HD - 1)) < HD // 2, att, -att)
        rows_s[9:10, :] = exact_dot(turn, dst == want)[0:1, :] + exact_dot(turn, dst == want + D // 2)[1:2, :]
        gb1 = jnp.concatenate([gb1_ref[:, r * DC : (r + 1) * DC] for r in range(FC // DC)] * 2, axis=0)
        rows_s[10:14, :] = exact_dot(gb1, spots_t(core))[:4, :]
        full_s[...] = rows_s[...].T.astype(bf16)
        to_chips(place_ref, full_s, (gw0, gw1, gw2, gw3), slice(4 * DC, PACK))


def to_chips(place_ref, full_ref, outs, cols):
    for d, out in enumerate(outs):
        a = (place_ref[1] + d) & (SIDE - 1)
        for g in range(SIDE):
            at = pl.multiple_of(natural(place_ref[0], a, g) * BLOCK, BLOCK)
            out[g * BLOCK : (g + 1) * BLOCK, cols] = full_ref[pl.ds(at, BLOCK), :]


def attn_bwd_call(
    place, q, k, v, ga, mine, other, p0, p1, cosine, sine, pos, h1t, pieces, proj_pieces, x, xo, mid, gb1
):
    q, k, v, cosine, sine, pos, ga = (a.reshape(CORES, S, -1) for a in (q, k, v, cosine, sine, pos, ga))
    block = lambda g: pl.BlockSpec((1, S, 2 * HD), lambda p, c: (g ^ c[0], 0, p))
    own = lambda g: pl.BlockSpec((1, S, 2 * HD), lambda p, c: (g, 0, p))
    at = lambda g: pl.BlockSpec((1, S, 8), lambda p, c: (g ^ c[0], 0, 0))
    whole = lambda a: pl.BlockSpec(a.shape, lambda p, c: (0,) * a.ndim)
    keep = lambda *n: pl.BlockSpec(n, lambda p, c: (0,) * len(n))
    return pl.pallas_call(
        attn_bwd_kernel,
        grid_spec=pltpu.PrefetchScalarGridSpec(
            num_scalar_prefetch=1,
            grid=(PAIRS,),
            in_specs=[block(0)] * 3
            + [own(0), pl.BlockSpec((2, 2, WIN, WIN), lambda p, c: (p, 0, 0, 0))]
            + [block(0)] * 2
            + [at(0)]
            + [block(1)] * 3
            + [own(1), pl.BlockSpec((2, S, S), lambda p, c: (p, 0, 0))]
            + [block(1)] * 2
            + [at(1)]
            + [whole(h1t), whole(ga)]
            + [pl.BlockSpec((CORES, S, 2 * HD), lambda p, c: (0, 0, PAIRS * c[0] + p))]
            + [whole(mine), whole(other)]
            + [pl.BlockSpec((QUARTER, D), lambda p, c: (0, FC // D))] * 4
            + [keep(QUARTER, 3 * DC)] * 4
            + [whole(a) for a in (x, xo, mid, gb1)],
            out_specs=[keep(QUARTER, PACK)] * 4 + [keep(S, D)] * 2,
            scratch_shapes=[pltpu.VMEM((S, 2 * HD), f32)] * 3
            + [pltpu.VMEM((D, 8 * HD), bf16), pltpu.VMEM((D, D), bf16), pltpu.VMEM((CORES, S, 2 * HD), bf16)]
            + [pltpu.VMEM((CORES, S, 3 * DC), bf16), pltpu.VMEM((PAIRS, 8, 2 * HD), f32)]
            + [pltpu.VMEM((128, D), f32), pltpu.VMEM((D, 128), bf16), pltpu.VMEM((D, 3 * DC), bf16)],
        ),
        out_shape=[
            *[jax.ShapeDtypeStruct((QUARTER, PACK), bf16)] * 4,
            *[jax.ShapeDtypeStruct((S, D), f32)] * 2,
        ],
        compiler_params=params(),
        cost_estimate=cost(10 * HC * S * S * 128 + 4 * T * D * 4 * DC, 36e6),
    )(
        place,
        q, k, v, mine, p0, cosine, sine, pos,
        q, k, v, mine, p1, cosine, sine, pos,
        h1t, ga, ga, mine, other, *proj_pieces, *pieces, x, xo, mid, gb1,
    )


def last_kernel(x_ref, ga_ref, gh_ref, other_ref, v_ref, gt_ref):
    normed, inv_std = stats(x_ref[...].astype(f32))
    gt_ref[...] = ga_ref[...] + norm_back(gh_ref[...] + other_ref[...], normed, inv_std, v_ref[0:1, :])


def mixed_kernel(after_ref, mlp_ref, mlpo_ref, v_ref, out_ref):
    out_ref[...] = (after_ref[...] + (mlp_ref[...] + mlpo_ref[...] + v_ref[8:9, :])).astype(bf16)


def by_rows(kernel, out_type, flops, *args):
    rows = 288
    tile = pl.BlockSpec((rows, D), lambda i: (i, 0))
    return pl.pallas_call(
        kernel,
        grid=(S // rows,),
        in_specs=[tile] * (len(args) - 1) + [pl.BlockSpec(args[-1].shape, lambda i: (0, 0))],
        out_specs=tile,
        out_shape=jax.ShapeDtypeStruct((S, D), out_type),
        compiler_params=params(),
        cost_estimate=cost(flops * S * D, S * D * 16),
    )(*args)


WIDE = PACK + FC


def pack_kernel(q0, q1, q2, q3, f_ref, out_ref):
    total = q0[...].astype(f32) + q1[...].astype(f32) + q2[...].astype(f32) + q3[...].astype(f32)
    fc1 = f_ref[...].astype(f32)
    for n in range(PLANE):
        at = slice(n * KR, (n + 1) * KR)
        out_ref[n, :, :PACK] = total[at, :].astype(bf16)
        out_ref[n, :, PACK:] = fc1[at, :].astype(bf16)


def pack_call(parts, fc1):
    return pl.pallas_call(
        pack_kernel,
        out_shape=jax.ShapeDtypeStruct((PLANE, KR, WIDE), bf16),
        compiler_params=params(),
        cost_estimate=cost(QUARTER * PACK * 4, QUARTER * PACK * 10),
    )(*parts, fc1)


def sum_kernel(in_ref, out_ref):
    total = in_ref[0].astype(f32)
    for n in range(1, PLANE):
        total += in_ref[n].astype(f32)
    out_ref[...] = total


def sum_call(packed):
    return pl.pallas_call(
        sum_kernel,
        out_shape=jax.ShapeDtypeStruct(packed.shape[1:], f32),
        compiler_params=params(SMALL_LIMIT),
        cost_estimate=cost(packed.size, packed.size * 2),
    )(packed)


def fc2_kernel(place_ref, mine_ref, other_ref, out_ref, sq_ref):
    first = place_ref[0] == 0
    a, b = mine_ref[...], other_ref[...]
    out_ref[:FR, :] = jnp.where(first, a, b)
    out_ref[FR:, :] = jnp.where(first, b, a)
    total = jnp.sum(a * a + b * b, axis=(0, 1), keepdims=True)
    sq_ref[...] = jnp.broadcast_to(total, sq_ref.shape)


def fc2_call(place, mine, other):
    whole = lambda a: pl.BlockSpec(a.shape, lambda i, c: (0,) * len(a.shape))
    shapes = [jax.ShapeDtypeStruct(s, f32) for s in ((2 * FR, D), (8, 128))]
    return pl.pallas_call(
        fc2_kernel,
        grid_spec=pltpu.PrefetchScalarGridSpec(
            num_scalar_prefetch=1,
            grid=(1,),
            in_specs=[whole(mine), whole(other)],
            out_specs=[whole(a) for a in shapes],
        ),
        out_shape=shapes,
        compiler_params=params(SMALL_LIMIT),
        cost_estimate=cost(6 * FR * D, FR * D * 16),
    )(place, mine, other)


def norm_kernel(g_ref, o_ref, sq_ref, out_ref):
    g, o = g_ref[...], o_ref[...]
    part = jnp.sum(g * g + o * o, axis=(0, 1), keepdims=True)
    cross = g[:, 4 * DC : PACK] * o[:, 4 * DC : PACK]
    part += 2.0 * jnp.sum(cross, axis=(0, 1), keepdims=True)
    out_ref[...] = jnp.broadcast_to((part + sq_ref[0:1, 0:1])[None], out_ref.shape)


def norm_call(g, o, squares):
    return pl.pallas_call(
        norm_kernel,
        out_shape=jax.ShapeDtypeStruct((CHIPS, 8, 128), f32),
        compiler_params=params(SMALL_LIMIT),
        cost_estimate=cost(4 * KR * PACK, 1e6),
    )(g, o, squares)


RATES = (D ** (-0.5), max(1, 2 * D // S) ** (-0.5), D ** (-0.5), FF ** (-0.5), RATE_VECTOR)


def adam_kernel(place_ref, norm_ref, mine_ref, other_ref, g2_ref, *refs):
    masters, firsts, seconds = refs[0:5], refs[5:10], refs[10:15]
    outs = refs[15:30]
    norm_out, bias_out = refs[30:32]
    core = place_ref[0]
    mine, other = mine_ref[...], other_ref[...]
    g0 = jnp.where(core == 0, mine, other)
    g1 = jnp.where(core == 0, other, mine)
    total = jnp.sum(jnp.sum(norm_ref[...], axis=0)[0:1, 0:1], axis=(0, 1), keepdims=True)
    grad_norm = jnp.sqrt(total)
    norm_out[...] = jnp.broadcast_to(grad_norm, norm_out.shape)
    clip = jnp.minimum(1.0, CLIP_LIMIT / (grad_norm + 1e-06))

    def update(i, at, grad):
        clipped = grad * clip
        master = masters[i][at]
        first = BETA_ONE * firsts[i][at] + (1.0 - BETA_ONE) * clipped
        second = BETA_TWO * seconds[i][at] + (1.0 - BETA_TWO) * clipped * clipped
        first_hat = first / (1.0 - BETA_ONE**STEP)
        second_hat = second / (1.0 - BETA_TWO**STEP)
        decay = 0.0 if i == 4 else DECAY_RATE
        outs[3 * i][at] = master - RATES[i] * (first_hat / (jnp.sqrt(second_hat) + ADAM_EPS) + decay * master)
        outs[3 * i + 1][at] = first
        outs[3 * i + 2][at] = second

    rows = slice(None)
    for c, g in ((0, g0), (1, g1)):
        for p in range(PAIRS):
            for i in range(3):
                col = i * D + c * DC + p * 128
                update(0, (rows, slice(col, col + 128)), g[:, (4 * p + i) * 128 : (4 * p + i + 1) * 128])
            col = c * DC + p * 128
            update(1, (rows, slice(col, col + 128)), g[:, (4 * p + 3) * 128 : (4 * p + 4) * 128])
    for r in range(FC // DC):
        at = slice(PACK + r * DC, PACK + (r + 1) * DC)
        part = exact_dot(g0[:, at], spots_t(0)) + exact_dot(g1[:, at], spots_t(1))
        update(2, (rows, slice(r * D, (r + 1) * D)), part)
    update(3, (rows, rows), g2_ref[...])
    vec = (g0 + g1)[:, 4 * DC : 4 * DC + 128]
    vec = jnp.concatenate([vec, jnp.zeros((16 - KR, 128), f32)], axis=0).T[:16, :KR]
    update(4, (rows, rows), vec[: masters[4].shape[0], :])
    bias_out[...] = vec[7:8, :] * clip


def adam_call(place, norm, mine, other, g2, masters, firsts, seconds):
    whole = lambda a: pl.BlockSpec(a.shape, lambda i, c: (0,) * len(a.shape))
    args = [norm, mine, other, g2, *masters, *firsts, *seconds]
    shapes = [jax.ShapeDtypeStruct(m.shape, f32) for m in masters for _ in range(3)]
    shapes += [jax.ShapeDtypeStruct((1, 128), f32), jax.ShapeDtypeStruct((1, KR), f32)]
    return pl.pallas_call(
        adam_kernel,
        grid_spec=pltpu.PrefetchScalarGridSpec(
            num_scalar_prefetch=1,
            grid=(1,),
            in_specs=[whole(a) for a in args],
            out_specs=[whole(a) for a in shapes],
        ),
        out_shape=shapes,
        compiler_params=params(SMALL_LIMIT),
        cost_estimate=cost(20 * KR * FF * 3, 3e6),
    )(place, *args)


def local(
    tokens,
    cotangent,
    counts,
    patch_row,
    patch_col,
    w_qkv,
    w_proj,
    w_fc1,
    w_fc2,
    vectors,
    m_qkv,
    v_qkv,
    m_proj,
    v_proj,
    m_fc1,
    v_fc1,
    m_fc2,
    v_fc2,
    m_vectors,
    v_vectors,
):
    core = lax.axis_index("grp")
    chip = lax.axis_index("dp")
    first_core = core == 0
    along = jnp.where(first_core, chip // PLANE, (chip // SIDE) % SIDE)
    vr = vectors.shape[0]

    def swap(a):
        return lax.ppermute(a, "grp", [(0, 1), (1, 0)])

    def along_line(quarter):
        return [quarter] + [shift(quarter, d) for d in range(1, SIDE)]

    def line_sum(whole):
        return lax.psum_scatter(whole, BOTH, scatter_dimension=0, axis_index_groups=lines(), tiled=True)

    me = jnp.stack([core, along]).astype(jnp.int32)
    shares, share_fc2 = share_call(me, w_qkv, vectors, w_fc2)
    full_fc2 = lax.all_gather(share_fc2, "dp", axis=0, tiled=True)
    quarter = plane_swap(shares).reshape(QUARTER, 3 * DC + 128)
    qkv_pieces = along_line(quarter)
    fc1_b = w_fc1.astype(bf16).reshape(KR, CHIPS, CORES, FR)
    share_fc1 = jnp.where(first_core, fc1_b[:, :, 0], fc1_b[:, :, 1]).reshape(KR, FC)
    share = jnp.concatenate([share_fc1, w_proj.astype(bf16)], axis=1)
    share = jnp.broadcast_to(share[None], (PLANE,) + share.shape)
    share, qkv_pieces[1] = lax.optimization_barrier((share, qkv_pieces[1]))
    quarter = plane_swap(share).reshape(QUARTER, FC + D)

    x_own = tokens.reshape(S, D)
    cot_own = cotangent.reshape(S, D)
    x_other, cot_other = swap(x_own), swap(cot_own)
    ints = jnp.concatenate(
        [
            patch_row.reshape(1, S),
            patch_col.reshape(1, S),
            jnp.pad(counts.reshape(1, 2), ((0, 0), (0, S - 2))),
            jnp.zeros((5, S), jnp.int32),
        ]
    )
    ints = jnp.stack([ints, swap(ints)])
    counts0 = jnp.where(first_core, ints[0, 2, :2], ints[1, 2, :2])
    counts1 = jnp.where(first_core, ints[1, 2, :1], ints[0, 2, :1])
    place = jnp.concatenate([jnp.stack([core, along]).astype(jnp.int32), counts0, counts1])

    vec, h1t, cosine, sine, q, k, v, b1, pos = qkv_call(place, x_own, x_other, ints, qkv_pieces)
    q, quarter = lax.optimization_barrier((q, quarter))
    pieces = along_line(quarter)
    mine, p0, p1 = attn_fwd_call(place, q, k, v)
    mine, pieces[1], pieces[3], cot_other = lax.optimization_barrier((mine, pieces[1], pieces[3], cot_other))
    other = swap(mine)
    gy = gy_call(place, cot_own, cot_other)
    other, gy = lax.optimization_barrier((other, gy))
    after, n2, r2, h2 = proj_call(place, mine, other, x_own, x_other, pieces, vec)
    mlp, mlp_part, gh2, act, gup, gb1 = mlp_call(place, h2, gy, pieces, full_fc2, b1)
    other_gh2 = swap(gh2)
    mlp_other = swap(mlp_part)

    gw2 = fc2_grad_call(place, act, gy)
    gw2, other_gh2 = lax.optimization_barrier((gw2, other_gh2))
    sum_fc2 = line_sum(gw2)
    gw1, ga, gab, sums_mid = mid_call(place, h2, gup, n2, r2, gy, gh2, other_gh2, vec)
    sum_fc1 = line_sum(gw1)
    *gw, gh1, gh1_part = attn_bwd_call(
        place, q, k, v, gab, mine, other, p0, p1, cosine, sine, pos, h1t, qkv_pieces, pieces,
        x_own, x_other, sums_mid, gb1,
    )
    gh1_other = swap(gh1_part)

    got_fc2 = plane_swap(sum_fc2.reshape(PLANE, FR, D))
    parts = [gw[0]] + [shift(gw[d], d) for d in range(1, SIDE)]
    got_fc2, sum_fc1 = lax.optimization_barrier((got_fc2, sum_fc1))
    g_fc2 = sum_call(got_fc2)
    g2, squares = fc2_call(place, g_fc2, swap(g_fc2))
    packed, gh1 = lax.optimization_barrier((pack_call(parts, sum_fc1), gh1))
    got = plane_swap(packed)
    gt = by_rows(last_kernel, f32, 25, x_own, ga, gh1, gh1_other, vec)
    got, g2, squares, gt = lax.optimization_barrier((got, g2, squares, gt))
    grads = sum_call(got)

    grads_other = swap(grads)
    squares, mlp = lax.optimization_barrier((norm_call(grads, grads_other, squares), mlp))
    norms = lax.all_to_all(squares, "dp", 0, 0)
    mixed = by_rows(mixed_kernel, bf16, 4, after, mlp, mlp_other, vec)
    norms, mixed = lax.optimization_barrier((norms, mixed))
    *updates, grad_norm, bias_proj_grad = adam_call(
        place,
        norms,
        grads,
        grads_other,
        g2,
        (w_qkv, w_proj, w_fc1, w_fc2, vectors),
        (m_qkv, m_proj, m_fc1, m_fc2, m_vectors),
        (v_qkv, v_proj, v_fc1, v_fc2, v_vectors),
    )
    return (
        mixed.reshape(1, 1, S, D),
        gt.reshape(1, 1, S, D),
        grad_norm[0, 0],
        *updates,
        bias_proj_grad.reshape(KR),
    )


def solution(mesh):
    frame = P("grp", "dp", None, None)
    ints = P("grp", "dp", None)
    rows = P("dp", None)
    cols = P(None, "dp")
    return jax.shard_map(
        local,
        mesh=mesh,
        in_specs=(frame, frame, ints, ints, ints, rows, rows, rows, rows, cols) + (rows,) * 8 + (cols,) * 2,
        out_specs=(frame, frame, P()) + (rows,) * 12 + (cols,) * 3 + (P("dp"),),
        check_vma=False,
    )
```

```python
import jax
import jax.numpy as jnp
from jax import lax
from jax.experimental import pallas as pl
from jax.experimental.pallas import tpu as pltpu
from jax.sharding import PartitionSpec as P

D = 768
H = 12
HD = 64
FF = 3072
STEP = 10
A = 196
S = 576

CORES = 2
HC = H // CORES
DC = D // CORES
FC = FF // CORES
PAIRS = HC // 2
T = CORES * S

WIN = 208
WINDOWS = (0, 192)

EPS_NORM = 1e-06
BETA_ONE = 0.9
BETA_TWO = 0.95
ADAM_EPS = 1e-08
DECAY_RATE = 0.05
RATE_VECTOR = 0.8
CLIP_LIMIT = 1.0
NEG = -1e30

bf16 = jnp.bfloat16
f32 = jnp.float32
VMEM_LIMIT = 56 * 1024 * 1024


SIDE = 4
CHIPS = SIDE**3
PLANE = SIDE * SIDE
KR = D // CHIPS
FR = FC // CHIPS
BLOCK = SIDE * KR
QUARTER = PLANE * KR
BOTH = ("grp", "dp")


def device(core, x, y, z):
    return ((core * SIDE + x) * SIDE + y) * SIDE + z


def lines():
    r = range(SIDE)
    return [[device(0, a, g, z) for a in r] for g in r for z in r] + [
        [device(1, g, a, z) for a in r] for g in r for z in r
    ]


def planes():
    r = range(SIDE)
    return [[device(0, a, g, z) for g in r for z in r] for a in r] + [
        [device(1, g, a, z) for g in r for z in r] for a in r
    ]


def shift(value, d):
    pairs = [(group[i], group[(i + d) % SIDE]) for group in lines() for i in range(SIDE)]
    return lax.ppermute(value, BOTH, pairs)


def plane_swap(value):
    return lax.all_to_all(value, BOTH, 0, 0, axis_index_groups=planes())


def natural(core, a, g):
    return jnp.where(core == 0, SIDE * a + g, SIDE * g + a)


def lay_out(place_ref, pieces, full_ref, cols=slice(None)):
    core, me = place_ref[0], place_ref[1]
    for d, piece in enumerate(pieces):
        a = (me + SIDE - d) & (SIDE - 1)
        for g in range(SIDE):
            at = pl.multiple_of(natural(core, a, g) * BLOCK, BLOCK)
            full_ref[pl.ds(at, BLOCK), :] = piece[g * BLOCK : (g + 1) * BLOCK, cols]


QKV = slice(0, 3 * DC)
PROJ = slice(3 * DC + 128, 3 * DC + 128 + D)
SHARE = 3 * DC + 128 + D


def usable_rows(place_ref, group, rows, base=0):
    slot = lax.broadcasted_iota(jnp.int32, (rows, 1), 0) + base
    first = ((slot < A) & (slot < place_ref[2])) | ((slot >= A) & (slot < 2 * A) & (slot - A < place_ref[3]))
    first = first.astype(f32)
    second = (slot < place_ref[4]).astype(f32)
    if isinstance(group, int):
        return second if group else first
    return jnp.where(group == 0, first, second)


def own_rows(win):
    row = lax.broadcasted_iota(jnp.int32, (WIN, 1), 0) + (WINDOWS[win] - win * A)
    return ((row >= 0) & (row < A)).astype(f32)


def key_bias(place_ref, win=None):
    if win is None:
        key = lax.broadcasted_iota(jnp.int32, (1, S), 1)
        return jnp.where(key < place_ref[4], 0.0, NEG)
    key = lax.broadcasted_iota(jnp.int32, (1, WIN), 1) + (WINDOWS[win] - win * A)
    return jnp.where((key >= 0) & (key < place_ref[2 + win]), 0.0, NEG)


def exact_dot(a, b):
    high = a.astype(bf16)
    rest = a - high.astype(f32)
    mid = rest.astype(bf16)
    low = (rest - mid.astype(f32)).astype(bf16)
    b = b.astype(bf16)
    return dot(high, b) + dot(mid, b) + dot(low, b)


def spots(core, shape, full, part):
    l = lax.broadcasted_iota(jnp.int32, shape, full)
    m = lax.broadcasted_iota(jnp.int32, shape, part)
    q = (m * 2731) >> 16
    return l == m + FR * (q + core)


def spots_t(core):
    return spots(core, (DC, D), 1, 0)


SMALL_LIMIT = 16 * 1024 * 1024


def params(limit=VMEM_LIMIT):
    return pltpu.CompilerParams(vmem_limit_bytes=limit)


def cost(flops, bytes_accessed, transcendentals=0):
    return pl.CostEstimate(
        flops=int(flops), bytes_accessed=int(bytes_accessed), transcendentals=int(transcendentals)
    )


def dot(a, b):
    return jnp.dot(a, b, preferred_element_type=f32)


def dot_t(a, b):
    return lax.dot_general(a, b, (((1,), (1,)), ((), ())), preferred_element_type=f32)


def t_dot(a, b):
    return lax.dot_general(a, b, (((0,), (0,)), ((), ())), preferred_element_type=f32)


def stats(z):
    mean_val = jnp.mean(z, axis=-1, keepdims=True)
    centred = z - mean_val
    variance = jnp.mean(centred * centred, axis=-1, keepdims=True)
    inv_std = lax.rsqrt(variance + EPS_NORM)
    return centred * inv_std, inv_std


def norm_back(grad, normed, inv_std, gain):
    e = grad * gain
    return inv_std * (
        e
        - jnp.mean(e, axis=-1, keepdims=True)
        - normed * jnp.mean(e * normed, axis=-1, keepdims=True)
    )


def swap_halves(u):
    lanes = u.shape[1]
    lane = lax.broadcasted_iota(jnp.int32, u.shape, 1)
    up = pltpu.roll(u, lanes - HD // 2, 1)
    down = pltpu.roll(u, HD // 2, 1)
    return jnp.where((lane & (HD - 1)) < HD // 2, up, down)


TURN = 1.5707963267948966


def sin_cos(a):
    k = jnp.floor(a * (1.0 / TURN) + 0.5)
    r = ((a - k * 1.5703125) - k * 4.837512969970703125e-4) - k * 7.54978995489188216e-8
    z = r * r
    s = ((-1.9515295891e-4 * z + 8.3321608736e-3) * z - 1.6666654611e-1) * z * r + r
    c = ((2.443315711809948e-5 * z - 1.388731625493765e-3) * z + 4.166664568298827e-2) * z * z - 0.5 * z + 1.0
    quarter = k.astype(jnp.int32)
    odd = (quarter & 1) == 1
    sine = jnp.where(odd, c, s)
    cosine = jnp.where(odd, s, c)
    sine = jnp.where((quarter & 2) == 0, sine, -sine)
    cosine = jnp.where(((quarter + 1) & 2) == 0, cosine, -cosine)
    return sine, cosine


def share_kernel(place_ref, w_ref, v_ref, p_ref, f_ref, out_ref, fc2_ref):
    core = place_ref[0]
    w = w_ref[...].astype(bf16)
    cols = []
    for p in range(PAIRS):
        for i in range(3):
            at = i * D + p * 128
            cols.append(jnp.where(core == 0, w[:, at : at + 128], w[:, at + DC : at + DC + 128]))
    v = jnp.concatenate([v_ref[...], jnp.zeros((128 - v_ref.shape[0], KR), f32)], axis=0)
    v = jnp.concatenate([v, jnp.zeros((128, 128 - KR), f32)], axis=1)
    cols.append(v.T[:KR, :].astype(bf16))
    cols.append(p_ref[...].astype(bf16))
    share = jnp.concatenate(cols, axis=1)
    for n in range(PLANE):
        out_ref[n] = share
    fc2_ref[...] = jnp.where(core == 0, f_ref[:FR, :], f_ref[FR:, :]).astype(bf16)


def share_call(place, w, vectors, w_proj, w_fc2):
    whole = lambda a: pl.BlockSpec(a.shape, lambda i, c: (0, 0))
    return pl.pallas_call(
        share_kernel,
        grid_spec=pltpu.PrefetchScalarGridSpec(
            num_scalar_prefetch=1,
            grid=(1,),
            in_specs=[whole(a) for a in (w, vectors, w_proj, w_fc2)],
            out_specs=[
                pl.BlockSpec((PLANE, KR, SHARE), lambda i, c: (0, 0, 0)),
                pl.BlockSpec((FR, D), lambda i, c: (0, 0)),
            ],
        ),
        out_shape=[
            jax.ShapeDtypeStruct((PLANE, KR, SHARE), bf16),
            jax.ShapeDtypeStruct((FR, D), bf16),
        ],
        compiler_params=params(),
        cost_estimate=cost(KR * D * 3, 1e6),
    )(place, w, vectors, w_proj, w_fc2)


def gy_kernel(place_ref, c_ref, co_ref, gy_ref):
    i = pl.program_id(0)
    keep = usable_rows(place_ref, i ^ place_ref[0], S)
    gy_ref[...] = (jnp.where(i == 0, c_ref[...], co_ref[...]).astype(f32) * keep).astype(bf16)


def gy_call(place, c, co):
    whole = pl.BlockSpec((S, D), lambda i, c: (0, 0))
    return pl.pallas_call(
        gy_kernel,
        grid_spec=pltpu.PrefetchScalarGridSpec(
            num_scalar_prefetch=1,
            grid=(CORES,),
            in_specs=[whole, whole],
            out_specs=pl.BlockSpec((S, D), lambda i, c: (i, 0)),
        ),
        out_shape=jax.ShapeDtypeStruct((T, D), bf16),
        compiler_params=params(),
        cost_estimate=cost(4 * T * D, T * D * 4),
    )(place, c, co)


def qkv_kernel(
    place_ref, x_ref, xo_ref, ints_ref, w0, w1, w2, w3, v0, v1, v2, v3,
    vec_ref, ht_ref, cos_ref, sin_ref, q_out, k_out, v_out, b1_ref, pos_ref,
    w_s, full_s, rows_s, freq_s,
):
    core = place_ref[0]

    @pl.when(pl.program_id(0) == 0)
    def _():
        lay_out(place_ref, (w0, w1, w2, w3), w_s)
        lay_out(place_ref, (v0, v1, v2, v3), full_s)
        rows_s[...] = full_s[...].astype(f32).T[:16, :]
        vec_ref[...] = rows_s[...]
        late = rows_s[8:16, :].astype(bf16)
        units = dot(late, spots(core, (D, DC), 0, 1).astype(bf16))
        for r in range(FC // DC):
            b1_ref[:, r * DC : (r + 1) * DC] = units[2 + r : 3 + r, :]
        src = lax.broadcasted_iota(jnp.int32, (D, DC), 0)
        dst = lax.broadcasted_iota(jnp.int32, (D, DC), 1)
        want = core * (DC // 2) + (dst // HD) * (HD // 2) + (dst & (HD // 2 - 1))
        freq_s[0:8, :] = dot(late, (src == want).astype(bf16))
        freq_s[8:16, :] = dot(late, (src == want + D // 2).astype(bf16))

    i = pl.program_id(0)
    x = jnp.where(i < pl.num_programs(0) // CORES, x_ref[...], xo_ref[...])
    h = stats(x.astype(f32))[0] * rows_s[0:1, :] + rows_s[1:2, :]
    pos = ints_ref[...].astype(f32).T
    pos_ref[...] = pos
    ht_ref[...] = h.T.astype(bf16)
    acc = dot(h.astype(bf16), w_s[...])
    angle = pos[:, 1:2] * freq_s[1:2, :] + pos[:, 0:1] * freq_s[9:10, :]
    lane = lax.broadcasted_iota(jnp.int32, (1, DC), 1)
    sign = jnp.where((lane & (HD - 1)) < HD // 2, -1.0, 1.0)
    small = jnp.max(jnp.abs(angle)) < 8000.0

    @pl.when(small)
    def _():
        sine, cosine = sin_cos(angle)
        cos_ref[...] = cosine
        sin_ref[...] = sine * sign

    @pl.when(jnp.logical_not(small))
    def _():
        cos_ref[...] = jnp.cos(angle)
        sin_ref[...] = jnp.sin(angle) * sign

    cosine, sine = cos_ref[...], sin_ref[...]
    at = pl.ds(pl.multiple_of(core * DC, DC), DC)
    part = lambda i: jnp.concatenate([acc[:, (3 * p + i) * 128 : (3 * p + i + 1) * 128] for p in range(PAIRS)], axis=1)
    q = part(0) + rows_s[4:5, at]
    k = part(1) + rows_s[5:6, at]
    q_out[...] = ((q * cosine + swap_halves(q) * sine) * HD ** (-0.5)).astype(bf16)
    k_out[...] = (k * cosine + swap_halves(k) * sine).astype(bf16)
    v_out[...] = (part(2) + rows_s[6:7, at]).astype(bf16)


def qkv_call(place, x, xo, ints, pieces):
    rows = S
    tile = lambda n: pl.BlockSpec((rows, n), lambda i, c: (i, 0))
    keep = lambda *n: pl.BlockSpec(n, lambda i, c: (0,) * len(n))
    return pl.pallas_call(
        qkv_kernel,
        grid_spec=pltpu.PrefetchScalarGridSpec(
            num_scalar_prefetch=1,
            grid=(CORES,),
            in_specs=[keep(S, D), keep(S, D), pl.BlockSpec((None, 8, S), lambda i, c: (i, 0, 0))]
            + [keep(QUARTER, 3 * DC)] * 4
            + [pl.BlockSpec((QUARTER, 128), lambda i, c: (0, 3 * DC // 128))] * 4,
            out_specs=[keep(16, D), pl.BlockSpec((None, D, rows), lambda i, c: (i, 0, 0))]
            + [tile(DC)] * 5
            + [keep(1, FC), tile(8)],
            scratch_shapes=[
                pltpu.VMEM((D, 3 * DC), bf16),
                pltpu.VMEM((D, 128), bf16),
                pltpu.VMEM((16, D), f32),
                pltpu.VMEM((16, DC), f32),
            ],
        ),
        out_shape=[
            jax.ShapeDtypeStruct((16, D), f32),
            jax.ShapeDtypeStruct((CORES, D, S), bf16),
            jax.ShapeDtypeStruct((T, DC), f32),
            jax.ShapeDtypeStruct((T, DC), f32),
            *[jax.ShapeDtypeStruct((T, DC), bf16)] * 3,
            jax.ShapeDtypeStruct((1, FC), f32),
            jax.ShapeDtypeStruct((T, 8), f32),
        ],
        compiler_params=params(),
        cost_estimate=cost(2 * T * D * 3 * DC + 60 * T * DC, T * D * 6 + D * 3 * DC * 2 + T * DC * 14),
    )(place, x, xo, ints, *pieces, *pieces)


def softmax_head(q, k, v, mine, bias):
    s = dot_t(jnp.where(mine, q, jnp.zeros_like(q)), k) + bias
    e = jnp.exp(s - jnp.max(s, axis=-1, keepdims=True))
    p = e * (1.0 / jnp.sum(e, axis=-1, keepdims=True))
    return p


def attn_fwd_kernel(
    place_ref, q0, k0, v0, q1, k1, v1, o_ref, p0_ref, p1_ref
):
    lane = lax.broadcasted_iota(jnp.int32, (1, 2 * HD), 1)
    low = lane < HD
    q, k, v = q1[0], k1[0], v1[0]
    mixes = []
    bias = key_bias(place_ref)
    for head, mine in ((0, low), (1, ~low)):
        p = softmax_head(q, k, v, mine, bias).astype(bf16)
        p1_ref[head] = p
        mixes.append(dot(p, v))
    mix = jnp.where(low, mixes[0], mixes[1])
    o_ref[1] = jnp.where(usable_rows(place_ref, 1, S) > 0, mix, v.astype(f32)).astype(bf16)
    o_ref[0] = v0[0]
    for win, base in enumerate(WINDOWS):
        q, k, v = (r[0, base : base + WIN, :] for r in (q0, k0, v0))
        own = own_rows(win)
        bias = key_bias(place_ref, win)
        mixes = []
        for head, mine in ((0, low), (1, ~low)):
            p = softmax_head(q, k, v, mine, bias)
            p = (p * own).astype(bf16)
            p0_ref[head, win] = p
            mixes.append(dot(p, v))
        mix = jnp.where(low, mixes[0], mixes[1])
        use = (own * usable_rows(place_ref, 0, WIN, base)) > 0
        before = o_ref[0, base : base + WIN, :].astype(f32)
        o_ref[0, base : base + WIN, :] = jnp.where(use, mix, before).astype(bf16)


def attn_fwd_call(place, q, k, v):
    block = lambda g: pl.BlockSpec((1, S, 2 * HD), lambda p, c: (g ^ c[0], 0, p))
    q, k, v = (a.reshape(CORES, S, DC) for a in (q, k, v))
    return pl.pallas_call(
        attn_fwd_kernel,
        grid_spec=pltpu.PrefetchScalarGridSpec(
            num_scalar_prefetch=1,
            grid=(PAIRS,),
            in_specs=[block(0)] * 3 + [block(1)] * 3,
            out_specs=[
                pl.BlockSpec((CORES, S, 2 * HD), lambda p, c: (0, 0, p)),
                pl.BlockSpec((2, 2, WIN, WIN), lambda p, c: (p, 0, 0, 0)),
                pl.BlockSpec((2, S, S), lambda p, c: (p, 0, 0)),
            ],
        ),
        out_shape=[
            jax.ShapeDtypeStruct((CORES, S, DC), bf16),
            jax.ShapeDtypeStruct((HC, 2, WIN, WIN), bf16),
            jax.ShapeDtypeStruct((HC, S, S), bf16),
        ],
        compiler_params=params(),
        cost_estimate=cost(4 * HC * (S * S + 2 * WIN * WIN) * 128, 12e6, HC * S * S),
    )(place, q, k, v, q, k, v)


def proj_kernel(place_ref, mine_ref, other_ref, x_ref, xo_ref, w0, w1, w2, w3, v_ref, after_ref, n2_ref, r2_ref, h2_ref, w_s):
    @pl.when(pl.program_id(0) == 0)
    def _():
        lay_out(place_ref, (w0, w1, w2, w3), w_s, PROJ)

    core = place_ref[0]
    at = lambda c: pl.ds(pl.multiple_of(c * DC, DC), DC)
    branch = dot(mine_ref[0], w_s[at(core), :]) + dot(other_ref[0], w_s[at(1 - core), :])
    x = jnp.where(pl.program_id(0) < pl.num_programs(0) // CORES, x_ref[...], xo_ref[...])
    after = x.astype(f32) + (branch + v_ref[7:8, :])
    normed, inv_std = stats(after)
    n2_ref[...] = normed
    r2_ref[...] = jnp.broadcast_to(inv_std, r2_ref.shape)

    @pl.when(pl.program_id(0) < pl.num_programs(0) // CORES)
    def _():
        after_ref[...] = after

    h2_ref[...] = (normed * v_ref[2:3, :] + v_ref[3:4, :]).astype(bf16)


def proj_call(place, mine, other, x, xo, pieces, vec):
    rows = 288
    half = S // rows
    tile = lambda n: pl.BlockSpec((rows, n), lambda i, c: (i, 0))
    whole = lambda a: pl.BlockSpec(a.shape, lambda i, c: (0,) * a.ndim)
    return pl.pallas_call(
        proj_kernel,
        grid_spec=pltpu.PrefetchScalarGridSpec(
            num_scalar_prefetch=1,
            grid=(T // rows,),
            in_specs=[
                pl.BlockSpec((1, rows, DC), lambda i, c: ((i // half) ^ c[0], i % half, 0)),
                pl.BlockSpec((1, rows, DC), lambda i, c: ((i // half) ^ c[0], i % half, 0)),
                pl.BlockSpec((rows, D), lambda i, c: (jnp.minimum(i, half - 1), 0)),
                pl.BlockSpec((rows, D), lambda i, c: (jnp.maximum(i - half, 0), 0)),
            ]
            + [whole(a) for a in pieces]
            + [whole(vec)],
            out_specs=[pl.BlockSpec((rows, D), lambda i, c: (jnp.minimum(i, half - 1), 0)), tile(D), tile(8), tile(D)],
            scratch_shapes=[pltpu.VMEM((D, D), bf16)],
        ),
        out_shape=[
            jax.ShapeDtypeStruct((S, D), f32),
            jax.ShapeDtypeStruct((T, D), f32),
            jax.ShapeDtypeStruct((T, 8), f32),
            jax.ShapeDtypeStruct((T, D), bf16),
        ],
        compiler_params=params(),
        cost_estimate=cost(2 * T * D * D, T * D * 10 + D * D * 2),
    )(place, mine, other, x, xo, *pieces, vec)


PACK = 4 * DC + 128
K0 = (2.0 / 3.141592653589793) ** 0.5
FT = 768


def gelu_slope(u):
    sq = u * u
    th = jnp.tanh(u * (K0 + (K0 * 0.044715) * sq))
    half = 0.5 + 0.5 * th
    return u * half, half + (u * (half - half * half)) * (2 * K0 + (6 * K0 * 0.044715) * sq)


def mlp_kernel(
    place_ref, h2_ref, gy_ref, w10, w11, w12, w13, w2_ref, b1_ref, mlp_ref, mlpo_ref, gh2b_ref, act_ref, gup_ref, gb1_ref, w1_s
):
    i = pl.program_id(0)

    @pl.when(i == 0)
    def _():
        lay_out(place_ref, (w10, w11, w12, w13), w1_s)
        gb1_ref[...] = jnp.zeros_like(gb1_ref)

    for f in range(FC // FT):
        c = slice(f * FT, (f + 1) * FT)
        act, slope = gelu_slope(dot(h2_ref[...], w1_s[:, c]) + b1_ref[:, c])
        act_ref[:, c] = act.astype(bf16)
        gup = (dot_t(gy_ref[...], w2_ref[c, :]) * slope).astype(bf16)
        gup_ref[:, c] = gup
        gb1_ref[:, c] += jnp.sum(gup.astype(f32), axis=0, keepdims=True)
    gh2b_ref[...] = dot_t(gup_ref[...], w1_s[...]).astype(bf16)
    mlp = dot(act_ref[...], w2_ref[...])
    half = pl.num_programs(0) // CORES

    @pl.when(i < half)
    def _():
        mlp_ref[...] = mlp

    @pl.when(i >= half)
    def _():
        mlpo_ref[...] = mlp


def mlp_call(place, h2, gy, pieces, w2, b1):
    rows = 288
    half = S // rows
    tile = lambda n: pl.BlockSpec((rows, n), lambda i, c: (i, 0))
    whole = lambda a: pl.BlockSpec(a.shape, lambda i, c: (0,) * a.ndim)
    return pl.pallas_call(
        mlp_kernel,
        grid_spec=pltpu.PrefetchScalarGridSpec(
            num_scalar_prefetch=1,
            grid=(T // rows,),
            in_specs=[tile(D), tile(D)]
            + [pl.BlockSpec((QUARTER, FC), lambda i, c: (0, 0))] * 4
            + [whole(w2), whole(b1)],
            out_specs=[
                pl.BlockSpec((rows, D), lambda i, c: (jnp.minimum(i, half - 1), 0)),
                pl.BlockSpec((rows, D), lambda i, c: (jnp.maximum(i - half, 0), 0)),
                tile(D),
                tile(FC),
                tile(FC),
                pl.BlockSpec((1, FC), lambda i, c: (0, 0)),
            ],
            scratch_shapes=[pltpu.VMEM((D, FC), bf16)],
        ),
        out_shape=[
            jax.ShapeDtypeStruct((S, D), f32),
            jax.ShapeDtypeStruct((S, D), f32),
            jax.ShapeDtypeStruct((T, D), bf16),
            jax.ShapeDtypeStruct((T, FC), bf16),
            jax.ShapeDtypeStruct((T, FC), bf16),
            jax.ShapeDtypeStruct((1, FC), f32),
        ],
        compiler_params=params(),
        cost_estimate=cost(8 * T * D * FC, 30e6, T * FC),
    )(place, h2, gy, *pieces, w2, b1)


def by_line(place_ref, value, block, out_ref):
    core = place_ref[0]
    for n in range(PLANE):
        to = jnp.where(core == 0, n, (n % SIDE) * SIDE + n // SIDE)
        out_ref[pl.ds(pl.multiple_of(to * block, block), block), :] = value[n * block : (n + 1) * block, :].astype(bf16)


def fc2_grad_kernel(place_ref, act_ref, gy_ref, out_ref):
    value = t_dot(act_ref[...], gy_ref[...])
    block = SIDE * FR
    for n in range(FT // block):
        m = pl.program_id(0) * (FT // block) + n
        to = jnp.where(place_ref[0] == 0, m, (m & (SIDE - 1)) * SIDE + m // SIDE)
        out_ref[pl.ds(pl.multiple_of(to * block, block), block), :] = value[n * block : (n + 1) * block, :].astype(bf16)


def fc2_grad_call(place, act, gy):
    return pl.pallas_call(
        fc2_grad_kernel,
        grid_spec=pltpu.PrefetchScalarGridSpec(
            num_scalar_prefetch=1,
            grid=(FC // FT,),
            in_specs=[pl.BlockSpec((T, FT), lambda i, c: (0, i)), pl.BlockSpec((T, D), lambda i, c: (0, 0))],
            out_specs=pl.BlockSpec((FC, D), lambda i, c: (0, 0)),
        ),
        out_shape=jax.ShapeDtypeStruct((FC, D), bf16),
        compiler_params=params(),
        cost_estimate=cost(2 * T * D * FC, T * (D + FC) * 2 + D * FC * 2),
    )(place, act, gy)


def mid_kernel(
    place_ref, h2_ref, gup_ref, n2_ref, r2_ref, gy_ref, gh2_ref, other_ref, v_ref, gw_ref, ga_ref, gab_ref, sums_ref
):
    i = pl.program_id(0)
    by_line(place_ref, t_dot(h2_ref[...], gup_ref[...]), BLOCK, gw_ref)
    normed, inv_std = n2_ref[...], r2_ref[:, 0:1]
    gh2 = gh2_ref[...].astype(f32) + other_ref[...].astype(f32)
    gy = gy_ref[...].astype(f32)
    ga = gy + norm_back(gh2, normed, inv_std, v_ref[2:3, :])
    gab = ga.astype(bf16)
    gab_ref[...] = gab
    mine = (i < pl.num_programs(0) // CORES).astype(f32)
    sums = [
        mine * jnp.sum(a, axis=0, keepdims=True) for a in (gh2 * normed, gh2, gab.astype(f32), gy)
    ] + [jnp.zeros((4, D), f32)]
    sums = jnp.concatenate(sums, axis=0)

    @pl.when(i == 0)
    def _():
        sums_ref[...] = sums

    @pl.when(i > 0)
    def _():
        sums_ref[...] += sums

    @pl.when(i < pl.num_programs(0) // CORES)
    def _():
        ga_ref[...] = ga


def mid_call(place, h2, gup, n2, r2, gy, gh2, other, vec):
    rows = 288
    half = S // rows
    cols = FC * rows // T
    tile = lambda n: pl.BlockSpec((rows, n), lambda i, c: (i, 0))
    flipped = pl.BlockSpec((rows, D), lambda i, c: ((i + half) % (2 * half), 0))
    whole = lambda a: pl.BlockSpec(a.shape, lambda i, c: (0,) * a.ndim)
    return pl.pallas_call(
        mid_kernel,
        grid_spec=pltpu.PrefetchScalarGridSpec(
            num_scalar_prefetch=1,
            grid=(T // rows,),
            in_specs=[whole(h2), pl.BlockSpec((T, cols), lambda i, c: (0, i))]
            + [tile(D), tile(8), tile(D), tile(D), flipped, whole(vec)],
            out_specs=[
                pl.BlockSpec((D, cols), lambda i, c: (0, i)),
                pl.BlockSpec((rows, D), lambda i, c: (jnp.minimum(i, half - 1), 0)),
                tile(D),
                pl.BlockSpec((8, D), lambda i, c: (0, 0)),
            ],
        ),
        out_shape=[
            jax.ShapeDtypeStruct((D, FC), bf16),
            jax.ShapeDtypeStruct((S, D), f32),
            jax.ShapeDtypeStruct((T, D), bf16),
            jax.ShapeDtypeStruct((8, D), f32),
        ],
        compiler_params=params(),
        cost_estimate=cost(2 * T * D * FC, T * D * 18 + T * FC * 2 + D * FC * 2),
    )(place, h2, gup, n2, r2, gy, gh2, other, vec)


def back_head(q_t, k, v, do, do_t, delta, p, mine, head):
    gp = dot_t(jnp.where(mine, do, jnp.zeros_like(do)), v)
    gs = (p.astype(f32) * (gp - delta)).astype(bf16)
    at = slice(head * HD, (head + 1) * HD)
    return dot(gs, k), dot(q_t[at, :], gs), dot(do_t[at, :], p)


def deltas(do, o, low):
    prod = do.astype(f32) * o.astype(f32)
    d0 = jnp.sum(jnp.where(low, prod, 0.0), axis=-1, keepdims=True)
    d1 = jnp.sum(jnp.where(low, 0.0, prod), axis=-1, keepdims=True)
    return d0, d1


def attn_bwd_kernel(
    place_ref,
    q0, k0, v0, o0, p0, cos0, sin0, pos0,
    q1, k1, v1, o1, p1, cos1, sin1, pos1,
    h1t_ref, ga_ref, cols_ref, mine_ref, other_ref, w0, w1, w2, w3,
    x_ref, xo_ref, mid_ref, gb1_ref,
    gw0, gw1, gw2, gw3, gh_ref, gho_ref,
    gq_s, gk_s, gv_s, gw_s, y_s, do_s, gqkv_s, att_s, rows_s, full_s, w_s,
):
    lane = lax.broadcasted_iota(jnp.int32, (1, 2 * HD), 1)
    low = lane < HD
    pair = pl.program_id(0)
    core = place_ref[0]

    @pl.when(pair == 0)
    def _():
        lay_out(place_ref, (w0, w1, w2, w3), y_s, PROJ)

    wy = y_s[pl.ds(pl.multiple_of(core * DC + pair * 2 * HD, 2 * HD), 2 * HD), :]
    for frame in range(CORES):
        do_s[frame] = dot_t(ga_ref[frame], wy).astype(bf16)

    def finish(frame, q, k, cos_ref, sin_ref, pos_ref):
        cosine, sine = cos_ref[0], sin_ref[0]
        gq = gq_s[...] * HD ** (-0.5)
        gk = gk_s[...]
        sq, sk = swap_halves(gq), swap_halves(gk)
        turn = (q.astype(f32) * HD**0.5) * sq + k.astype(f32) * sk
        gq = (gq * cosine - sq * sine).astype(bf16)
        gk = (gk * cosine - sk * sine).astype(bf16)
        gv = gv_s[...].astype(bf16)
        for i, g in enumerate((gq, gk, gv)):
            gqkv_s[frame ^ core, :, pl.ds(pl.multiple_of(pair * 6 * HD + i * 2 * HD, 2 * HD), 2 * HD)] = g
        pos = pos_ref[0]
        col = jnp.sum(turn * pos[:, 1:2], axis=0, keepdims=True)
        row = jnp.sum(turn * pos[:, 0:1], axis=0, keepdims=True)
        bias = [jnp.sum(g.astype(f32), axis=0, keepdims=True) for g in (gq, gk, gv)]
        return jnp.concatenate([col, row] + bias, axis=0)

    q, k, v, do = q1[0], k1[0], v1[0], do_s[1 ^ core]
    d = deltas(do, o1[0], low)
    q_t, do_t = q.astype(f32).T.astype(bf16), do.astype(f32).T.astype(bf16)
    out = [
        back_head(q_t, k, v, do, do_t, d[head], p1[head], mine, head)
        for head, mine in ((0, low), (1, ~low))
    ]
    gq_s[...] = jnp.where(low, out[0][0], out[1][0])
    gk_s[...] = jnp.concatenate([out[0][1], out[1][1]], axis=0).T
    gv_s[...] = jnp.concatenate([out[0][2], out[1][2]], axis=0).T
    sums1 = finish(1, q, k, cos1, sin1, pos1)
    gq_s[...] = jnp.zeros_like(gq_s)
    gk_s[...] = jnp.zeros_like(gk_s)
    gv_s[...] = jnp.zeros_like(gv_s)
    for win, base in enumerate(WINDOWS):
        at = pl.ds(base, WIN)
        q, k, v, o = (r[0, at, :] for r in (q0, k0, v0, o0))
        do = do_s[core, at, :]
        d = deltas(do, o, low)
        q_t, do_t = q.astype(f32).T.astype(bf16), do.astype(f32).T.astype(bf16)
        out = [
            back_head(q_t, k, v, do, do_t, d[head], p0[head, win], mine, head)
            for head, mine in ((0, low), (1, ~low))
        ]
        gq_s[at, :] += jnp.where(low, out[0][0], out[1][0])
        gk_s[at, :] += jnp.concatenate([out[0][1], out[1][1]], axis=0).T
        gv_s[at, :] += jnp.concatenate([out[0][2], out[1][2]], axis=0).T
    sums0 = finish(0, q0[0], k0[0], cos0, sin0, pos0)
    att_s[pair, 0:5, :] = sums0 + sums1

    gw = jnp.zeros((D, 6 * HD), f32)
    gw_mine = jnp.zeros((2 * HD, DC), f32)
    gw_other = jnp.zeros((2 * HD, DC), f32)
    for frame in range(CORES):
        cols = cols_ref[frame].astype(f32).T.astype(bf16)
        gw_mine += dot(cols, mine_ref[frame ^ core])
        gw_other += dot(cols, other_ref[frame ^ core])
        gw += dot(h1t_ref[frame], gqkv_s[frame, :, pl.ds(pl.multiple_of(pair * 6 * HD, 6 * HD), 6 * HD)])
    gw_s[:, : 6 * HD] = gw.astype(bf16)
    at = lambda c: pl.ds(pl.multiple_of(c * DC, DC), DC)
    gw_s[at(core), 6 * HD :] = gw_mine.T.astype(bf16)
    gw_s[at(1 - core), 6 * HD :] = gw_other.T.astype(bf16)
    to_chips(place_ref, gw_s, (gw0, gw1, gw2, gw3), pl.ds(pl.multiple_of(pair * 8 * HD, 8 * HD), 8 * HD))

    @pl.when(pair == PAIRS - 1)
    def _():
        lay_out(place_ref, (w0, w1, w2, w3), w_s, QKV)
        rows_s[...] = jnp.zeros_like(rows_s)
        for frame, x, out in ((0, x_ref, gh_ref), (1, xo_ref, gho_ref)):
            for half in range(2):
                at = slice(half * (S // 2), (half + 1) * (S // 2))
                gh = dot_t(gqkv_s[frame, at, :], w_s[...])
                out[at, :] = gh
                normed, _ = stats(x[at, :].astype(f32))
                rows_s[0:1, :] += jnp.sum(gh * normed, axis=0, keepdims=True)
                rows_s[1:2, :] += jnp.sum(gh, axis=0, keepdims=True)
        rows_s[2:4, :] = mid_ref[0:2, :]
        rows_s[7:9, :] = mid_ref[2:4, :]
        att = jnp.concatenate([att_s[p] for p in range(PAIRS)], axis=1)
        rows_s[4:7, pl.ds(pl.multiple_of(core * DC, DC), DC)] = att[2:5, :]
        src = lax.broadcasted_iota(jnp.int32, (DC, D), 0)
        dst = lax.broadcasted_iota(jnp.int32, (DC, D), 1)
        want = core * (DC // 2) + (src // HD) * (HD // 2) + (src & (HD // 2 - 1))
        side = lax.broadcasted_iota(jnp.int32, (1, DC), 1)
        turn = jnp.where((side & (HD - 1)) < HD // 2, att, -att)
        rows_s[9:10, :] = exact_dot(turn, dst == want)[0:1, :] + exact_dot(turn, dst == want + D // 2)[1:2, :]
        gb1 = jnp.concatenate([gb1_ref[:, r * DC : (r + 1) * DC] for r in range(FC // DC)] * 2, axis=0)
        rows_s[10:14, :] = exact_dot(gb1, spots_t(core))[:4, :]
        full_s[...] = rows_s[...].T.astype(bf16)
        to_chips(place_ref, full_s, (gw0, gw1, gw2, gw3), slice(4 * DC, PACK))


def to_chips(place_ref, full_ref, outs, cols):
    for d, out in enumerate(outs):
        a = (place_ref[1] + d) & (SIDE - 1)
        for g in range(SIDE):
            at = pl.multiple_of(natural(place_ref[0], a, g) * BLOCK, BLOCK)
            out[g * BLOCK : (g + 1) * BLOCK, cols] = full_ref[pl.ds(at, BLOCK), :]


def attn_bwd_call(
    place, q, k, v, ga, mine, other, p0, p1, cosine, sine, pos, h1t, pieces, x, xo, mid, gb1
):
    q, k, v, cosine, sine, pos, ga = (a.reshape(CORES, S, -1) for a in (q, k, v, cosine, sine, pos, ga))
    block = lambda g: pl.BlockSpec((1, S, 2 * HD), lambda p, c: (g ^ c[0], 0, p))
    own = lambda g: pl.BlockSpec((1, S, 2 * HD), lambda p, c: (g, 0, p))
    at = lambda g: pl.BlockSpec((1, S, 8), lambda p, c: (g ^ c[0], 0, 0))
    whole = lambda a: pl.BlockSpec(a.shape, lambda p, c: (0,) * a.ndim)
    keep = lambda *n: pl.BlockSpec(n, lambda p, c: (0,) * len(n))
    return pl.pallas_call(
        attn_bwd_kernel,
        grid_spec=pltpu.PrefetchScalarGridSpec(
            num_scalar_prefetch=1,
            grid=(PAIRS,),
            in_specs=[block(0)] * 3
            + [own(0), pl.BlockSpec((2, 2, WIN, WIN), lambda p, c: (p, 0, 0, 0))]
            + [block(0)] * 2
            + [at(0)]
            + [block(1)] * 3
            + [own(1), pl.BlockSpec((2, S, S), lambda p, c: (p, 0, 0))]
            + [block(1)] * 2
            + [at(1)]
            + [whole(h1t), whole(ga)]
            + [pl.BlockSpec((CORES, S, 2 * HD), lambda p, c: (0, 0, PAIRS * c[0] + p))]
            + [whole(mine), whole(other)]
            + [whole(a) for a in pieces]
            + [whole(a) for a in (x, xo, mid, gb1)],
            out_specs=[keep(QUARTER, PACK)] * 4 + [keep(S, D)] * 2,
            scratch_shapes=[pltpu.VMEM((S, 2 * HD), f32)] * 3
            + [pltpu.VMEM((D, 8 * HD), bf16), pltpu.VMEM((D, D), bf16), pltpu.VMEM((CORES, S, 2 * HD), bf16)]
            + [pltpu.VMEM((CORES, S, 3 * DC), bf16), pltpu.VMEM((PAIRS, 8, 2 * HD), f32)]
            + [pltpu.VMEM((128, D), f32), pltpu.VMEM((D, 128), bf16), pltpu.VMEM((D, 3 * DC), bf16)],
        ),
        out_shape=[
            *[jax.ShapeDtypeStruct((QUARTER, PACK), bf16)] * 4,
            *[jax.ShapeDtypeStruct((S, D), f32)] * 2,
        ],
        compiler_params=params(),
        cost_estimate=cost(10 * HC * S * S * 128 + 4 * T * D * 4 * DC, 36e6),
    )(
        place,
        q, k, v, mine, p0, cosine, sine, pos,
        q, k, v, mine, p1, cosine, sine, pos,
        h1t, ga, ga, mine, other, *pieces, x, xo, mid, gb1,
    )


def last_kernel(x_ref, ga_ref, gh_ref, other_ref, v_ref, gt_ref):
    normed, inv_std = stats(x_ref[...].astype(f32))
    gt_ref[...] = ga_ref[...] + norm_back(gh_ref[...] + other_ref[...], normed, inv_std, v_ref[0:1, :])


def mixed_kernel(after_ref, mlp_ref, mlpo_ref, v_ref, out_ref):
    out_ref[...] = (after_ref[...] + (mlp_ref[...] + mlpo_ref[...] + v_ref[8:9, :])).astype(bf16)


def by_rows(kernel, out_type, flops, *args):
    rows = 288
    tile = pl.BlockSpec((rows, D), lambda i: (i, 0))
    return pl.pallas_call(
        kernel,
        grid=(S // rows,),
        in_specs=[tile] * (len(args) - 1) + [pl.BlockSpec(args[-1].shape, lambda i: (0, 0))],
        out_specs=tile,
        out_shape=jax.ShapeDtypeStruct((S, D), out_type),
        compiler_params=params(),
        cost_estimate=cost(flops * S * D, S * D * 16),
    )(*args)


WIDE = PACK + FC


def pack_kernel(q0, q1, q2, q3, f_ref, out_ref):
    total = q0[...].astype(f32) + q1[...].astype(f32) + q2[...].astype(f32) + q3[...].astype(f32)
    fc1 = f_ref[...].astype(f32)
    for n in range(PLANE):
        at = slice(n * KR, (n + 1) * KR)
        out_ref[n, :, :PACK] = total[at, :].astype(bf16)
        out_ref[n, :, PACK:] = fc1[at, :].astype(bf16)


def pack_call(parts, fc1):
    return pl.pallas_call(
        pack_kernel,
        out_shape=jax.ShapeDtypeStruct((PLANE, KR, WIDE), bf16),
        compiler_params=params(),
        cost_estimate=cost(QUARTER * PACK * 4, QUARTER * PACK * 10),
    )(*parts, fc1)


def sum_kernel(in_ref, out_ref):
    total = in_ref[0].astype(f32)
    for n in range(1, PLANE):
        total += in_ref[n].astype(f32)
    out_ref[...] = total


def sum_call(packed):
    return pl.pallas_call(
        sum_kernel,
        out_shape=jax.ShapeDtypeStruct(packed.shape[1:], f32),
        compiler_params=params(SMALL_LIMIT),
        cost_estimate=cost(packed.size, packed.size * 2),
    )(packed)


def fc2_kernel(place_ref, mine_ref, other_ref, out_ref, sq_ref):
    first = place_ref[0] == 0
    a, b = mine_ref[...], other_ref[...]
    out_ref[:FR, :] = jnp.where(first, a, b)
    out_ref[FR:, :] = jnp.where(first, b, a)
    total = jnp.sum(a * a + b * b, axis=(0, 1), keepdims=True)
    sq_ref[...] = jnp.broadcast_to(total, sq_ref.shape)


def fc2_call(place, mine, other):
    whole = lambda a: pl.BlockSpec(a.shape, lambda i, c: (0,) * len(a.shape))
    shapes = [jax.ShapeDtypeStruct(s, f32) for s in ((2 * FR, D), (8, 128))]
    return pl.pallas_call(
        fc2_kernel,
        grid_spec=pltpu.PrefetchScalarGridSpec(
            num_scalar_prefetch=1,
            grid=(1,),
            in_specs=[whole(mine), whole(other)],
            out_specs=[whole(a) for a in shapes],
        ),
        out_shape=shapes,
        compiler_params=params(SMALL_LIMIT),
        cost_estimate=cost(6 * FR * D, FR * D * 16),
    )(place, mine, other)


def norm_kernel(g_ref, o_ref, sq_ref, out_ref):
    g, o = g_ref[...], o_ref[...]
    part = jnp.sum(g * g + o * o, axis=(0, 1), keepdims=True)
    cross = g[:, 4 * DC : PACK] * o[:, 4 * DC : PACK]
    part += 2.0 * jnp.sum(cross, axis=(0, 1), keepdims=True)
    out_ref[...] = jnp.broadcast_to((part + sq_ref[0:1, 0:1])[None], out_ref.shape)


def norm_call(g, o, squares):
    return pl.pallas_call(
        norm_kernel,
        out_shape=jax.ShapeDtypeStruct((CHIPS, 8, 128), f32),
        compiler_params=params(SMALL_LIMIT),
        cost_estimate=cost(4 * KR * PACK, 1e6),
    )(g, o, squares)


RATES = (D ** (-0.5), max(1, 2 * D // S) ** (-0.5), D ** (-0.5), FF ** (-0.5), RATE_VECTOR)


def adam_kernel(place_ref, norm_ref, mine_ref, other_ref, g2_ref, *refs):
    masters, firsts, seconds = refs[0:5], refs[5:10], refs[10:15]
    outs = refs[15:30]
    norm_out, bias_out = refs[30:32]
    core = place_ref[0]
    mine, other = mine_ref[...], other_ref[...]
    g0 = jnp.where(core == 0, mine, other)
    g1 = jnp.where(core == 0, other, mine)
    total = jnp.sum(jnp.sum(norm_ref[...], axis=0)[0:1, 0:1], axis=(0, 1), keepdims=True)
    grad_norm = jnp.sqrt(total)
    norm_out[...] = jnp.broadcast_to(grad_norm, norm_out.shape)
    clip = jnp.minimum(1.0, CLIP_LIMIT / (grad_norm + 1e-06))

    def update(i, at, grad):
        clipped = grad * clip
        master = masters[i][at]
        first = BETA_ONE * firsts[i][at] + (1.0 - BETA_ONE) * clipped
        second = BETA_TWO * seconds[i][at] + (1.0 - BETA_TWO) * clipped * clipped
        first_hat = first / (1.0 - BETA_ONE**STEP)
        second_hat = second / (1.0 - BETA_TWO**STEP)
        decay = 0.0 if i == 4 else DECAY_RATE
        outs[3 * i][at] = master - RATES[i] * (first_hat / (jnp.sqrt(second_hat) + ADAM_EPS) + decay * master)
        outs[3 * i + 1][at] = first
        outs[3 * i + 2][at] = second

    rows = slice(None)
    for c, g in ((0, g0), (1, g1)):
        for p in range(PAIRS):
            for i in range(3):
                col = i * D + c * DC + p * 128
                update(0, (rows, slice(col, col + 128)), g[:, (4 * p + i) * 128 : (4 * p + i + 1) * 128])
            col = c * DC + p * 128
            update(1, (rows, slice(col, col + 128)), g[:, (4 * p + 3) * 128 : (4 * p + 4) * 128])
    for r in range(FC // DC):
        at = slice(PACK + r * DC, PACK + (r + 1) * DC)
        part = exact_dot(g0[:, at], spots_t(0)) + exact_dot(g1[:, at], spots_t(1))
        update(2, (rows, slice(r * D, (r + 1) * D)), part)
    update(3, (rows, rows), g2_ref[...])
    vec = (g0 + g1)[:, 4 * DC : 4 * DC + 128]
    vec = jnp.concatenate([vec, jnp.zeros((16 - KR, 128), f32)], axis=0).T[:16, :KR]
    update(4, (rows, rows), vec[: masters[4].shape[0], :])
    bias_out[...] = vec[7:8, :] * clip


def adam_call(place, norm, mine, other, g2, masters, firsts, seconds):
    whole = lambda a: pl.BlockSpec(a.shape, lambda i, c: (0,) * len(a.shape))
    args = [norm, mine, other, g2, *masters, *firsts, *seconds]
    shapes = [jax.ShapeDtypeStruct(m.shape, f32) for m in masters for _ in range(3)]
    shapes += [jax.ShapeDtypeStruct((1, 128), f32), jax.ShapeDtypeStruct((1, KR), f32)]
    return pl.pallas_call(
        adam_kernel,
        grid_spec=pltpu.PrefetchScalarGridSpec(
            num_scalar_prefetch=1,
            grid=(1,),
            in_specs=[whole(a) for a in args],
            out_specs=[whole(a) for a in shapes],
        ),
        out_shape=shapes,
        compiler_params=params(SMALL_LIMIT),
        cost_estimate=cost(20 * KR * FF * 3, 3e6),
    )(place, *args)


def local(
    tokens,
    cotangent,
    counts,
    patch_row,
    patch_col,
    w_qkv,
    w_proj,
    w_fc1,
    w_fc2,
    vectors,
    m_qkv,
    v_qkv,
    m_proj,
    v_proj,
    m_fc1,
    v_fc1,
    m_fc2,
    v_fc2,
    m_vectors,
    v_vectors,
):
    core = lax.axis_index("grp")
    chip = lax.axis_index("dp")
    first_core = core == 0
    along = jnp.where(first_core, chip // PLANE, (chip // SIDE) % SIDE)
    vr = vectors.shape[0]

    def swap(a):
        return lax.ppermute(a, "grp", [(0, 1), (1, 0)])

    def along_line(quarter):
        return [quarter] + [shift(quarter, d) for d in range(1, SIDE)]

    def line_sum(whole):
        return lax.psum_scatter(whole, BOTH, scatter_dimension=0, axis_index_groups=lines(), tiled=True)

    me = jnp.stack([core, along]).astype(jnp.int32)
    shares, share_fc2 = share_call(me, w_qkv, vectors, w_proj, w_fc2)
    full_fc2 = lax.all_gather(share_fc2, "dp", axis=0, tiled=True)
    quarter = plane_swap(shares).reshape(QUARTER, SHARE)
    qkv_pieces = along_line(quarter)
    fc1_b = w_fc1.astype(bf16).reshape(KR, CHIPS, CORES, FR)
    share_fc1 = jnp.where(first_core, fc1_b[:, :, 0], fc1_b[:, :, 1]).reshape(KR, FC)
    share = jnp.broadcast_to(share_fc1[None], (PLANE, KR, FC))
    share, qkv_pieces[1] = lax.optimization_barrier((share, qkv_pieces[1]))
    quarter = plane_swap(share).reshape(QUARTER, FC)

    x_own = tokens.reshape(S, D)
    cot_own = cotangent.reshape(S, D)
    x_other, cot_other = swap(x_own), swap(cot_own)
    ints = jnp.concatenate(
        [
            patch_row.reshape(1, S),
            patch_col.reshape(1, S),
            jnp.pad(counts.reshape(1, 2), ((0, 0), (0, S - 2))),
            jnp.zeros((5, S), jnp.int32),
        ]
    )
    ints = jnp.stack([ints, swap(ints)])
    counts0 = jnp.where(first_core, ints[0, 2, :2], ints[1, 2, :2])
    counts1 = jnp.where(first_core, ints[1, 2, :1], ints[0, 2, :1])
    place = jnp.concatenate([jnp.stack([core, along]).astype(jnp.int32), counts0, counts1])

    vec, h1t, cosine, sine, q, k, v, b1, pos = qkv_call(place, x_own, x_other, ints, qkv_pieces)
    q, quarter = lax.optimization_barrier((q, quarter))
    pieces = along_line(quarter)
    mine, p0, p1 = attn_fwd_call(place, q, k, v)
    mine, pieces[1], pieces[3], cot_other = lax.optimization_barrier((mine, pieces[1], pieces[3], cot_other))
    other = swap(mine)
    gy = gy_call(place, cot_own, cot_other)
    other, gy = lax.optimization_barrier((other, gy))
    after, n2, r2, h2 = proj_call(place, mine, other, x_own, x_other, qkv_pieces, vec)
    mlp, mlp_part, gh2, act, gup, gb1 = mlp_call(place, h2, gy, pieces, full_fc2, b1)
    other_gh2 = swap(gh2)
    mlp_other = swap(mlp_part)

    gw2 = fc2_grad_call(place, act, gy)
    gw2, other_gh2 = lax.optimization_barrier((gw2, other_gh2))
    sum_fc2 = line_sum(gw2)
    gw1, ga, gab, sums_mid = mid_call(place, h2, gup, n2, r2, gy, gh2, other_gh2, vec)
    sum_fc1 = line_sum(gw1)
    *gw, gh1, gh1_part = attn_bwd_call(
        place, q, k, v, gab, mine, other, p0, p1, cosine, sine, pos, h1t, qkv_pieces,
        x_own, x_other, sums_mid, gb1,
    )

    got_fc2 = plane_swap(sum_fc2.reshape(PLANE, FR, D))
    parts = [gw[0]] + [shift(gw[d], d) for d in range(1, SIDE)]
    got_fc2, sum_fc1 = lax.optimization_barrier((got_fc2, sum_fc1))
    g_fc2 = sum_call(got_fc2)
    g2, squares = fc2_call(place, g_fc2, swap(g_fc2))
    packed, gh1, gh1_part = lax.optimization_barrier((pack_call(parts, sum_fc1), gh1, gh1_part))
    gh1_other = swap(gh1_part)
    got = plane_swap(packed)
    gt = by_rows(last_kernel, f32, 25, x_own, ga, gh1, gh1_other, vec)
    got, g2, squares, gt = lax.optimization_barrier((got, g2, squares, gt))
    grads = sum_call(got)

    grads_other = swap(grads)
    squares, mlp = lax.optimization_barrier((norm_call(grads, grads_other, squares), mlp))
    norms = lax.all_to_all(squares, "dp", 0, 0)
    mixed = by_rows(mixed_kernel, bf16, 4, after, mlp, mlp_other, vec)
    norms, mixed = lax.optimization_barrier((norms, mixed))
    *updates, grad_norm, bias_proj_grad = adam_call(
        place,
        norms,
        grads,
        grads_other,
        g2,
        (w_qkv, w_proj, w_fc1, w_fc2, vectors),
        (m_qkv, m_proj, m_fc1, m_fc2, m_vectors),
        (v_qkv, v_proj, v_fc1, v_fc2, v_vectors),
    )
    return (
        mixed.reshape(1, 1, S, D),
        gt.reshape(1, 1, S, D),
        grad_norm[0, 0],
        *updates,
        bias_proj_grad.reshape(KR),
    )


def solution(mesh):
    frame = P("grp", "dp", None, None)
    ints = P("grp", "dp", None)
    rows = P("dp", None)
    cols = P(None, "dp")
    return jax.shard_map(
        local,
        mesh=mesh,
        in_specs=(frame, frame, ints, ints, ints, rows, rows, rows, rows, cols) + (rows,) * 8 + (cols,) * 2,
        out_specs=(frame, frame, P()) + (rows,) * 12 + (cols,) * 3 + (P("dp"),),
        check_vma=False,
    )
```

```python
import jax
import jax.numpy as jnp
from jax import lax
from jax.experimental import pallas as pl
from jax.experimental.pallas import tpu as pltpu
from jax.sharding import PartitionSpec as P

D = 768
H = 12
HD = 64
FF = 3072
STEP = 10
A = 196
S = 576

CORES = 2
HC = H // CORES
DC = D // CORES
FC = FF // CORES
PAIRS = HC // 2
T = CORES * S

WIN = 208
WINDOWS = (0, 192)

EPS_NORM = 1e-06
BETA_ONE = 0.9
BETA_TWO = 0.95
ADAM_EPS = 1e-08
DECAY_RATE = 0.05
RATE_VECTOR = 0.8
CLIP_LIMIT = 1.0
NEG = -1e30

bf16 = jnp.bfloat16
f32 = jnp.float32
VMEM_LIMIT = 56 * 1024 * 1024


SIDE = 4
CHIPS = SIDE**3
PLANE = SIDE * SIDE
KR = D // CHIPS
FR = FC // CHIPS
BLOCK = SIDE * KR
QUARTER = PLANE * KR
BOTH = ("grp", "dp")


def device(core, x, y, z):
    return ((core * SIDE + x) * SIDE + y) * SIDE + z


def lines():
    r = range(SIDE)
    return [[device(0, a, g, z) for a in r] for g in r for z in r] + [
        [device(1, g, a, z) for a in r] for g in r for z in r
    ]


def planes():
    r = range(SIDE)
    return [[device(0, a, g, z) for g in r for z in r] for a in r] + [
        [device(1, g, a, z) for g in r for z in r] for a in r
    ]


def shift(value, d):
    pairs = [(group[i], group[(i + d) % SIDE]) for group in lines() for i in range(SIDE)]
    return lax.ppermute(value, BOTH, pairs)


def plane_swap(value):
    return lax.all_to_all(value, BOTH, 0, 0, axis_index_groups=planes())


def natural(core, a, g):
    return jnp.where(core == 0, SIDE * a + g, SIDE * g + a)


def lay_out(place_ref, pieces, full_ref, cols=slice(None)):
    core, me = place_ref[0], place_ref[1]
    for d, piece in enumerate(pieces):
        a = (me + SIDE - d) & (SIDE - 1)
        for g in range(SIDE):
            at = pl.multiple_of(natural(core, a, g) * BLOCK, BLOCK)
            full_ref[pl.ds(at, BLOCK), :] = piece[g * BLOCK : (g + 1) * BLOCK, cols]


QKV = slice(0, 3 * DC)
PROJ = slice(3 * DC + 128, 3 * DC + 128 + D)
SHARE = 3 * DC + 128 + D


def usable_rows(place_ref, group, rows, base=0):
    slot = lax.broadcasted_iota(jnp.int32, (rows, 1), 0) + base
    first = ((slot < A) & (slot < place_ref[2])) | ((slot >= A) & (slot < 2 * A) & (slot - A < place_ref[3]))
    first = first.astype(f32)
    second = (slot < place_ref[4]).astype(f32)
    if isinstance(group, int):
        return second if group else first
    return jnp.where(group == 0, first, second)


def own_rows(win):
    row = lax.broadcasted_iota(jnp.int32, (WIN, 1), 0) + (WINDOWS[win] - win * A)
    return ((row >= 0) & (row < A)).astype(f32)


def key_bias(place_ref, win=None):
    if win is None:
        key = lax.broadcasted_iota(jnp.int32, (1, S), 1)
        return jnp.where(key < place_ref[4], 0.0, NEG)
    key = lax.broadcasted_iota(jnp.int32, (1, WIN), 1) + (WINDOWS[win] - win * A)
    return jnp.where((key >= 0) & (key < place_ref[2 + win]), 0.0, NEG)


def exact_dot(a, b):
    high = a.astype(bf16)
    rest = a - high.astype(f32)
    mid = rest.astype(bf16)
    low = (rest - mid.astype(f32)).astype(bf16)
    b = b.astype(bf16)
    return dot(high, b) + dot(mid, b) + dot(low, b)


def spots(core, shape, full, part):
    l = lax.broadcasted_iota(jnp.int32, shape, full)
    m = lax.broadcasted_iota(jnp.int32, shape, part)
    q = (m * 2731) >> 16
    return l == m + FR * (q + core)


def spots_t(core):
    return spots(core, (DC, D), 1, 0)


SMALL_LIMIT = 16 * 1024 * 1024


def params(limit=VMEM_LIMIT):
    return pltpu.CompilerParams(vmem_limit_bytes=limit)


def cost(flops, bytes_accessed, transcendentals=0):
    return pl.CostEstimate(
        flops=int(flops), bytes_accessed=int(bytes_accessed), transcendentals=int(transcendentals)
    )


def dot(a, b):
    return jnp.dot(a, b, preferred_element_type=f32)


def dot_t(a, b):
    return lax.dot_general(a, b, (((1,), (1,)), ((), ())), preferred_element_type=f32)


def t_dot(a, b):
    return lax.dot_general(a, b, (((0,), (0,)), ((), ())), preferred_element_type=f32)


def stats(z):
    mean_val = jnp.mean(z, axis=-1, keepdims=True)
    centred = z - mean_val
    variance = jnp.mean(centred * centred, axis=-1, keepdims=True)
    inv_std = lax.rsqrt(variance + EPS_NORM)
    return centred * inv_std, inv_std


def norm_back(grad, normed, inv_std, gain):
    e = grad * gain
    return inv_std * (
        e
        - jnp.mean(e, axis=-1, keepdims=True)
        - normed * jnp.mean(e * normed, axis=-1, keepdims=True)
    )


def swap_halves(u):
    lanes = u.shape[1]
    lane = lax.broadcasted_iota(jnp.int32, u.shape, 1)
    up = pltpu.roll(u, lanes - HD // 2, 1)
    down = pltpu.roll(u, HD // 2, 1)
    return jnp.where((lane & (HD - 1)) < HD // 2, up, down)


TURN = 1.5707963267948966


def sin_cos(a):
    k = jnp.floor(a * (1.0 / TURN) + 0.5)
    r = ((a - k * 1.5703125) - k * 4.837512969970703125e-4) - k * 7.54978995489188216e-8
    z = r * r
    s = ((-1.9515295891e-4 * z + 8.3321608736e-3) * z - 1.6666654611e-1) * z * r + r
    c = ((2.443315711809948e-5 * z - 1.388731625493765e-3) * z + 4.166664568298827e-2) * z * z - 0.5 * z + 1.0
    quarter = k.astype(jnp.int32)
    odd = (quarter & 1) == 1
    sine = jnp.where(odd, c, s)
    cosine = jnp.where(odd, s, c)
    sine = jnp.where((quarter & 2) == 0, sine, -sine)
    cosine = jnp.where(((quarter + 1) & 2) == 0, cosine, -cosine)
    return sine, cosine


def share_kernel(place_ref, w_ref, v_ref, p_ref, f_ref, out_ref, fc2_ref):
    core = place_ref[0]
    w = w_ref[...].astype(bf16)
    cols = []
    for p in range(PAIRS):
        for i in range(3):
            at = i * D + p * 128
            cols.append(jnp.where(core == 0, w[:, at : at + 128], w[:, at + DC : at + DC + 128]))
    v = jnp.concatenate([v_ref[...], jnp.zeros((128 - v_ref.shape[0], KR), f32)], axis=0)
    v = jnp.concatenate([v, jnp.zeros((128, 128 - KR), f32)], axis=1)
    cols.append(v.T[:KR, :].astype(bf16))
    cols.append(p_ref[...].astype(bf16))
    share = jnp.concatenate(cols, axis=1)
    for n in range(PLANE):
        out_ref[n] = share
    fc2_ref[...] = jnp.where(core == 0, f_ref[:FR, :], f_ref[FR:, :]).astype(bf16)


def share_call(place, w, vectors, w_proj, w_fc2):
    whole = lambda a: pl.BlockSpec(a.shape, lambda i, c: (0, 0))
    return pl.pallas_call(
        share_kernel,
        grid_spec=pltpu.PrefetchScalarGridSpec(
            num_scalar_prefetch=1,
            grid=(1,),
            in_specs=[whole(a) for a in (w, vectors, w_proj, w_fc2)],
            out_specs=[
                pl.BlockSpec((PLANE, KR, SHARE), lambda i, c: (0, 0, 0)),
                pl.BlockSpec((FR, D), lambda i, c: (0, 0)),
            ],
        ),
        out_shape=[
            jax.ShapeDtypeStruct((PLANE, KR, SHARE), bf16),
            jax.ShapeDtypeStruct((FR, D), bf16),
        ],
        compiler_params=params(),
        cost_estimate=cost(KR * D * 3, 1e6),
    )(place, w, vectors, w_proj, w_fc2)


def gy_kernel(place_ref, c_ref, co_ref, gy_ref):
    i = pl.program_id(0)
    keep = usable_rows(place_ref, i ^ place_ref[0], S)
    gy_ref[...] = (jnp.where(i == 0, c_ref[...], co_ref[...]).astype(f32) * keep).astype(bf16)


def gy_call(place, c, co):
    whole = pl.BlockSpec((S, D), lambda i, c: (0, 0))
    return pl.pallas_call(
        gy_kernel,
        grid_spec=pltpu.PrefetchScalarGridSpec(
            num_scalar_prefetch=1,
            grid=(CORES,),
            in_specs=[whole, whole],
            out_specs=pl.BlockSpec((S, D), lambda i, c: (i, 0)),
        ),
        out_shape=jax.ShapeDtypeStruct((T, D), bf16),
        compiler_params=params(),
        cost_estimate=cost(4 * T * D, T * D * 4),
    )(place, c, co)


def qkv_kernel(
    place_ref, x_ref, xo_ref, ints_ref, w0, w1, w2, w3, v0, v1, v2, v3,
    vec_ref, ht_ref, cos_ref, sin_ref, q_out, k_out, v_out, b1_ref, pos_ref,
    w_s, full_s, rows_s, freq_s,
):
    core = place_ref[0]

    @pl.when(pl.program_id(0) == 0)
    def _():
        lay_out(place_ref, (w0, w1, w2, w3), w_s)
        lay_out(place_ref, (v0, v1, v2, v3), full_s)
        rows_s[...] = full_s[...].astype(f32).T[:16, :]
        vec_ref[...] = rows_s[...]
        late = rows_s[8:16, :].astype(bf16)
        units = dot(late, spots(core, (D, DC), 0, 1).astype(bf16))
        for r in range(FC // DC):
            b1_ref[:, r * DC : (r + 1) * DC] = units[2 + r : 3 + r, :]
        src = lax.broadcasted_iota(jnp.int32, (D, DC), 0)
        dst = lax.broadcasted_iota(jnp.int32, (D, DC), 1)
        want = core * (DC // 2) + (dst // HD) * (HD // 2) + (dst & (HD // 2 - 1))
        freq_s[0:8, :] = dot(late, (src == want).astype(bf16))
        freq_s[8:16, :] = dot(late, (src == want + D // 2).astype(bf16))

    i = pl.program_id(0)
    x = jnp.where(i < pl.num_programs(0) // CORES, x_ref[...], xo_ref[...])
    h = stats(x.astype(f32))[0] * rows_s[0:1, :] + rows_s[1:2, :]
    pos = ints_ref[...].astype(f32).T
    pos_ref[...] = pos
    ht_ref[...] = h.T.astype(bf16)
    acc = dot(h.astype(bf16), w_s[...])
    angle = pos[:, 1:2] * freq_s[1:2, :] + pos[:, 0:1] * freq_s[9:10, :]
    lane = lax.broadcasted_iota(jnp.int32, (1, DC), 1)
    sign = jnp.where((lane & (HD - 1)) < HD // 2, -1.0, 1.0)
    small = jnp.max(jnp.abs(angle)) < 8000.0

    @pl.when(small)
    def _():
        sine, cosine = sin_cos(angle)
        cos_ref[...] = cosine
        sin_ref[...] = sine * sign

    @pl.when(jnp.logical_not(small))
    def _():
        cos_ref[...] = jnp.cos(angle)
        sin_ref[...] = jnp.sin(angle) * sign

    cosine, sine = cos_ref[...], sin_ref[...]
    at = pl.ds(pl.multiple_of(core * DC, DC), DC)
    part = lambda i: jnp.concatenate([acc[:, (3 * p + i) * 128 : (3 * p + i + 1) * 128] for p in range(PAIRS)], axis=1)
    q = part(0) + rows_s[4:5, at]
    k = part(1) + rows_s[5:6, at]
    q_out[...] = ((q * cosine + swap_halves(q) * sine) * HD ** (-0.5)).astype(bf16)
    k_out[...] = (k * cosine + swap_halves(k) * sine).astype(bf16)
    v_out[...] = (part(2) + rows_s[6:7, at]).astype(bf16)


def qkv_call(place, x, xo, ints, pieces):
    rows = S
    tile = lambda n: pl.BlockSpec((rows, n), lambda i, c: (i, 0))
    keep = lambda *n: pl.BlockSpec(n, lambda i, c: (0,) * len(n))
    return pl.pallas_call(
        qkv_kernel,
        grid_spec=pltpu.PrefetchScalarGridSpec(
            num_scalar_prefetch=1,
            grid=(CORES,),
            in_specs=[keep(S, D), keep(S, D), pl.BlockSpec((None, 8, S), lambda i, c: (i, 0, 0))]
            + [keep(QUARTER, 3 * DC)] * 4
            + [pl.BlockSpec((QUARTER, 128), lambda i, c: (0, 3 * DC // 128))] * 4,
            out_specs=[keep(16, D), pl.BlockSpec((None, D, rows), lambda i, c: (i, 0, 0))]
            + [tile(DC)] * 5
            + [keep(1, FC), tile(8)],
            scratch_shapes=[
                pltpu.VMEM((D, 3 * DC), bf16),
                pltpu.VMEM((D, 128), bf16),
                pltpu.VMEM((16, D), f32),
                pltpu.VMEM((16, DC), f32),
            ],
        ),
        out_shape=[
            jax.ShapeDtypeStruct((16, D), f32),
            jax.ShapeDtypeStruct((CORES, D, S), bf16),
            jax.ShapeDtypeStruct((T, DC), f32),
            jax.ShapeDtypeStruct((T, DC), f32),
            *[jax.ShapeDtypeStruct((T, DC), bf16)] * 3,
            jax.ShapeDtypeStruct((1, FC), f32),
            jax.ShapeDtypeStruct((T, 8), f32),
        ],
        compiler_params=params(),
        cost_estimate=cost(2 * T * D * 3 * DC + 60 * T * DC, T * D * 6 + D * 3 * DC * 2 + T * DC * 14),
    )(place, x, xo, ints, *pieces, *pieces)


def softmax_head(q, k, v, mine, bias):
    s = dot_t(jnp.where(mine, q, jnp.zeros_like(q)), k) + bias
    e = jnp.exp(s - jnp.max(s, axis=-1, keepdims=True))
    p = e * (1.0 / jnp.sum(e, axis=-1, keepdims=True))
    return p


def attn_fwd_kernel(
    place_ref, q0, k0, v0, q1, k1, v1, o_ref, p0_ref, p1_ref
):
    lane = lax.broadcasted_iota(jnp.int32, (1, 2 * HD), 1)
    low = lane < HD
    q, k, v = q1[0], k1[0], v1[0]
    mixes = []
    bias = key_bias(place_ref)
    for head, mine in ((0, low), (1, ~low)):
        p = softmax_head(q, k, v, mine, bias).astype(bf16)
        p1_ref[head] = p
        mixes.append(dot(p, v))
    mix = jnp.where(low, mixes[0], mixes[1])
    o_ref[1] = jnp.where(usable_rows(place_ref, 1, S) > 0, mix, v.astype(f32)).astype(bf16)
    o_ref[0] = v0[0]
    for win, base in enumerate(WINDOWS):
        q, k, v = (r[0, base : base + WIN, :] for r in (q0, k0, v0))
        own = own_rows(win)
        bias = key_bias(place_ref, win)
        mixes = []
        for head, mine in ((0, low), (1, ~low)):
            p = softmax_head(q, k, v, mine, bias)
            p = (p * own).astype(bf16)
            p0_ref[head, win] = p
            mixes.append(dot(p, v))
        mix = jnp.where(low, mixes[0], mixes[1])
        use = (own * usable_rows(place_ref, 0, WIN, base)) > 0
        before = o_ref[0, base : base + WIN, :].astype(f32)
        o_ref[0, base : base + WIN, :] = jnp.where(use, mix, before).astype(bf16)


def attn_fwd_call(place, q, k, v):
    block = lambda g: pl.BlockSpec((1, S, 2 * HD), lambda p, c: (g ^ c[0], 0, p))
    q, k, v = (a.reshape(CORES, S, DC) for a in (q, k, v))
    return pl.pallas_call(
        attn_fwd_kernel,
        grid_spec=pltpu.PrefetchScalarGridSpec(
            num_scalar_prefetch=1,
            grid=(PAIRS,),
            in_specs=[block(0)] * 3 + [block(1)] * 3,
            out_specs=[
                pl.BlockSpec((CORES, S, 2 * HD), lambda p, c: (0, 0, p)),
                pl.BlockSpec((2, 2, WIN, WIN), lambda p, c: (p, 0, 0, 0)),
                pl.BlockSpec((2, S, S), lambda p, c: (p, 0, 0)),
            ],
        ),
        out_shape=[
            jax.ShapeDtypeStruct((CORES, S, DC), bf16),
            jax.ShapeDtypeStruct((HC, 2, WIN, WIN), bf16),
            jax.ShapeDtypeStruct((HC, S, S), bf16),
        ],
        compiler_params=params(),
        cost_estimate=cost(4 * HC * (S * S + 2 * WIN * WIN) * 128, 12e6, HC * S * S),
    )(place, q, k, v, q, k, v)


def proj_kernel(place_ref, mine_ref, other_ref, x_ref, xo_ref, w0, w1, w2, w3, v_ref, after_ref, n2_ref, r2_ref, h2_ref, w_s):
    @pl.when(pl.program_id(0) == 0)
    def _():
        lay_out(place_ref, (w0, w1, w2, w3), w_s, PROJ)

    core = place_ref[0]
    at = lambda c: pl.ds(pl.multiple_of(c * DC, DC), DC)
    branch = dot(mine_ref[0], w_s[at(core), :]) + dot(other_ref[0], w_s[at(1 - core), :])
    x = jnp.where(pl.program_id(0) < pl.num_programs(0) // CORES, x_ref[...], xo_ref[...])
    after = x.astype(f32) + (branch + v_ref[7:8, :])
    normed, inv_std = stats(after)
    n2_ref[...] = normed
    r2_ref[...] = jnp.broadcast_to(inv_std, r2_ref.shape)

    @pl.when(pl.program_id(0) < pl.num_programs(0) // CORES)
    def _():
        after_ref[...] = after

    h2_ref[...] = (normed * v_ref[2:3, :] + v_ref[3:4, :]).astype(bf16)


def proj_call(place, mine, other, x, xo, pieces, vec):
    rows = 288
    half = S // rows
    tile = lambda n: pl.BlockSpec((rows, n), lambda i, c: (i, 0))
    whole = lambda a: pl.BlockSpec(a.shape, lambda i, c: (0,) * a.ndim)
    return pl.pallas_call(
        proj_kernel,
        grid_spec=pltpu.PrefetchScalarGridSpec(
            num_scalar_prefetch=1,
            grid=(T // rows,),
            in_specs=[
                pl.BlockSpec((1, rows, DC), lambda i, c: ((i // half) ^ c[0], i % half, 0)),
                pl.BlockSpec((1, rows, DC), lambda i, c: ((i // half) ^ c[0], i % half, 0)),
                pl.BlockSpec((rows, D), lambda i, c: (jnp.minimum(i, half - 1), 0)),
                pl.BlockSpec((rows, D), lambda i, c: (jnp.maximum(i - half, 0), 0)),
            ]
            + [whole(a) for a in pieces]
            + [whole(vec)],
            out_specs=[pl.BlockSpec((rows, D), lambda i, c: (jnp.minimum(i, half - 1), 0)), tile(D), tile(8), tile(D)],
            scratch_shapes=[pltpu.VMEM((D, D), bf16)],
        ),
        out_shape=[
            jax.ShapeDtypeStruct((S, D), f32),
            jax.ShapeDtypeStruct((T, D), f32),
            jax.ShapeDtypeStruct((T, 8), f32),
            jax.ShapeDtypeStruct((T, D), bf16),
        ],
        compiler_params=params(),
        cost_estimate=cost(2 * T * D * D, T * D * 10 + D * D * 2),
    )(place, mine, other, x, xo, *pieces, vec)


PACK = 4 * DC + 128
K0 = (2.0 / 3.141592653589793) ** 0.5
FT = 768


def gelu_slope(u):
    sq = u * u
    th = jnp.tanh(u * (K0 + (K0 * 0.044715) * sq))
    half = 0.5 + 0.5 * th
    return u * half, half + (u * (half - half * half)) * (2 * K0 + (6 * K0 * 0.044715) * sq)


def mlp_kernel(
    place_ref, h2_ref, gy_ref, w10, w11, w12, w13, w2_ref, b1_ref, mlp_ref, mlpo_ref, gh2b_ref, act_ref, gup_ref, gb1_ref, w1_s
):
    i = pl.program_id(0)

    @pl.when(i == 0)
    def _():
        lay_out(place_ref, (w10, w11, w12, w13), w1_s)
        gb1_ref[...] = jnp.zeros_like(gb1_ref)

    for f in range(FC // FT):
        c = slice(f * FT, (f + 1) * FT)
        act, slope = gelu_slope(dot(h2_ref[...], w1_s[:, c]) + b1_ref[:, c])
        act_ref[:, c] = act.astype(bf16)
        gup = (dot_t(gy_ref[...], w2_ref[c, :]) * slope).astype(bf16)
        gup_ref[:, c] = gup
        gb1_ref[:, c] += jnp.sum(gup.astype(f32), axis=0, keepdims=True)
    gh2b_ref[...] = dot_t(gup_ref[...], w1_s[...]).astype(bf16)
    mlp = dot(act_ref[...], w2_ref[...])
    half = pl.num_programs(0) // CORES

    @pl.when(i < half)
    def _():
        mlp_ref[...] = mlp

    @pl.when(i >= half)
    def _():
        mlpo_ref[...] = mlp


def mlp_call(place, h2, gy, pieces, w2, b1):
    rows = 288
    half = S // rows
    tile = lambda n: pl.BlockSpec((rows, n), lambda i, c: (i, 0))
    whole = lambda a: pl.BlockSpec(a.shape, lambda i, c: (0,) * a.ndim)
    return pl.pallas_call(
        mlp_kernel,
        grid_spec=pltpu.PrefetchScalarGridSpec(
            num_scalar_prefetch=1,
            grid=(T // rows,),
            in_specs=[tile(D), tile(D)]
            + [pl.BlockSpec((QUARTER, FC), lambda i, c: (0, 0))] * 4
            + [whole(w2), whole(b1)],
            out_specs=[
                pl.BlockSpec((rows, D), lambda i, c: (jnp.minimum(i, half - 1), 0)),
                pl.BlockSpec((rows, D), lambda i, c: (jnp.maximum(i - half, 0), 0)),
                tile(D),
                tile(FC),
                tile(FC),
                pl.BlockSpec((1, FC), lambda i, c: (0, 0)),
            ],
            scratch_shapes=[pltpu.VMEM((D, FC), bf16)],
        ),
        out_shape=[
            jax.ShapeDtypeStruct((S, D), f32),
            jax.ShapeDtypeStruct((S, D), f32),
            jax.ShapeDtypeStruct((T, D), bf16),
            jax.ShapeDtypeStruct((T, FC), bf16),
            jax.ShapeDtypeStruct((T, FC), bf16),
            jax.ShapeDtypeStruct((1, FC), f32),
        ],
        compiler_params=params(),
        cost_estimate=cost(8 * T * D * FC, 30e6, T * FC),
    )(place, h2, gy, *pieces, w2, b1)


def by_line(place_ref, value, block, out_ref):
    core = place_ref[0]
    for n in range(PLANE):
        to = jnp.where(core == 0, n, (n % SIDE) * SIDE + n // SIDE)
        out_ref[pl.ds(pl.multiple_of(to * block, block), block), :] = value[n * block : (n + 1) * block, :].astype(bf16)


def fc2_grad_kernel(place_ref, act_ref, gy_ref, out_ref):
    value = t_dot(act_ref[...], gy_ref[...])
    block = SIDE * FR
    for n in range(FT // block):
        m = pl.program_id(0) * (FT // block) + n
        to = jnp.where(place_ref[0] == 0, m, (m & (SIDE - 1)) * SIDE + m // SIDE)
        out_ref[pl.ds(pl.multiple_of(to * block, block), block), :] = value[n * block : (n + 1) * block, :].astype(bf16)


def fc2_grad_call(place, act, gy):
    return pl.pallas_call(
        fc2_grad_kernel,
        grid_spec=pltpu.PrefetchScalarGridSpec(
            num_scalar_prefetch=1,
            grid=(FC // FT,),
            in_specs=[pl.BlockSpec((T, FT), lambda i, c: (0, i)), pl.BlockSpec((T, D), lambda i, c: (0, 0))],
            out_specs=pl.BlockSpec((FC, D), lambda i, c: (0, 0)),
        ),
        out_shape=jax.ShapeDtypeStruct((FC, D), bf16),
        compiler_params=params(),
        cost_estimate=cost(2 * T * D * FC, T * (D + FC) * 2 + D * FC * 2),
    )(place, act, gy)


def mid_kernel(
    place_ref, h2_ref, gup_ref, n2_ref, r2_ref, gy_ref, gh2_ref, other_ref, v_ref, gw_ref, ga_ref, gab_ref, sums_ref
):
    i = pl.program_id(0)
    by_line(place_ref, t_dot(h2_ref[...], gup_ref[...]), BLOCK, gw_ref)
    normed, inv_std = n2_ref[...], r2_ref[:, 0:1]
    gh2 = gh2_ref[...].astype(f32) + other_ref[...].astype(f32)
    gy = gy_ref[...].astype(f32)
    ga = gy + norm_back(gh2, normed, inv_std, v_ref[2:3, :])
    gab = ga.astype(bf16)
    gab_ref[...] = gab
    mine = (i < pl.num_programs(0) // CORES).astype(f32)
    sums = [
        mine * jnp.sum(a, axis=0, keepdims=True) for a in (gh2 * normed, gh2, gab.astype(f32), gy)
    ] + [jnp.zeros((4, D), f32)]
    sums = jnp.concatenate(sums, axis=0)

    @pl.when(i == 0)
    def _():
        sums_ref[...] = sums

    @pl.when(i > 0)
    def _():
        sums_ref[...] += sums

    @pl.when(i < pl.num_programs(0) // CORES)
    def _():
        ga_ref[...] = ga


def mid_call(place, h2, gup, n2, r2, gy, gh2, other, vec):
    rows = 288
    half = S // rows
    cols = FC * rows // T
    tile = lambda n: pl.BlockSpec((rows, n), lambda i, c: (i, 0))
    flipped = pl.BlockSpec((rows, D), lambda i, c: ((i + half) % (2 * half), 0))
    whole = lambda a: pl.BlockSpec(a.shape, lambda i, c: (0,) * a.ndim)
    return pl.pallas_call(
        mid_kernel,
        grid_spec=pltpu.PrefetchScalarGridSpec(
            num_scalar_prefetch=1,
            grid=(T // rows,),
            in_specs=[whole(h2), pl.BlockSpec((T, cols), lambda i, c: (0, i))]
            + [tile(D), tile(8), tile(D), tile(D), flipped, whole(vec)],
            out_specs=[
                pl.BlockSpec((D, cols), lambda i, c: (0, i)),
                pl.BlockSpec((rows, D), lambda i, c: (jnp.minimum(i, half - 1), 0)),
                tile(D),
                pl.BlockSpec((8, D), lambda i, c: (0, 0)),
            ],
        ),
        out_shape=[
            jax.ShapeDtypeStruct((D, FC), bf16),
            jax.ShapeDtypeStruct((S, D), f32),
            jax.ShapeDtypeStruct((T, D), bf16),
            jax.ShapeDtypeStruct((8, D), f32),
        ],
        compiler_params=params(),
        cost_estimate=cost(2 * T * D * FC, T * D * 18 + T * FC * 2 + D * FC * 2),
    )(place, h2, gup, n2, r2, gy, gh2, other, vec)


def back_head(q_t, k, v, do, do_t, delta, p, mine, head):
    gp = dot_t(jnp.where(mine, do, jnp.zeros_like(do)), v)
    gs = (p.astype(f32) * (gp - delta)).astype(bf16)
    at = slice(head * HD, (head + 1) * HD)
    return dot(gs, k), dot(q_t[at, :], gs), dot(do_t[at, :], p)


def deltas(do, o, low):
    prod = do.astype(f32) * o.astype(f32)
    d0 = jnp.sum(jnp.where(low, prod, 0.0), axis=-1, keepdims=True)
    d1 = jnp.sum(jnp.where(low, 0.0, prod), axis=-1, keepdims=True)
    return d0, d1


def attn_bwd_kernel(
    place_ref,
    q0, k0, v0, o0, p0, cos0, sin0, pos0,
    q1, k1, v1, o1, p1, cos1, sin1, pos1,
    h1t_ref, ga_ref, cols_ref, mine_ref, other_ref, w0, w1, w2, w3,
    x_ref, xo_ref, mid_ref, gb1_ref,
    gw0, gw1, gw2, gw3, gh_ref, gho_ref,
    gq_s, gk_s, gv_s, gw_s, y_s, do_s, gqkv_s, att_s, rows_s, full_s, w_s,
):
    lane = lax.broadcasted_iota(jnp.int32, (1, 2 * HD), 1)
    low = lane < HD
    pair = pl.program_id(0)
    core = place_ref[0]

    @pl.when(pair == 0)
    def _():
        lay_out(place_ref, (w0, w1, w2, w3), y_s, PROJ)

    wy = y_s[pl.ds(pl.multiple_of(core * DC + pair * 2 * HD, 2 * HD), 2 * HD), :]
    for frame in range(CORES):
        do_s[frame] = dot_t(ga_ref[frame], wy).astype(bf16)

    def finish(frame, q, k, cos_ref, sin_ref, pos_ref):
        cosine, sine = cos_ref[0], sin_ref[0]
        gq = gq_s[...] * HD ** (-0.5)
        gk = gk_s[...]
        sq, sk = swap_halves(gq), swap_halves(gk)
        turn = (q.astype(f32) * HD**0.5) * sq + k.astype(f32) * sk
        gq = (gq * cosine - sq * sine).astype(bf16)
        gk = (gk * cosine - sk * sine).astype(bf16)
        gv = gv_s[...].astype(bf16)
        for i, g in enumerate((gq, gk, gv)):
            gqkv_s[frame ^ core, :, pl.ds(pl.multiple_of(pair * 6 * HD + i * 2 * HD, 2 * HD), 2 * HD)] = g
        pos = pos_ref[0]
        col = jnp.sum(turn * pos[:, 1:2], axis=0, keepdims=True)
        row = jnp.sum(turn * pos[:, 0:1], axis=0, keepdims=True)
        bias = [jnp.sum(g.astype(f32), axis=0, keepdims=True) for g in (gq, gk, gv)]
        return jnp.concatenate([col, row] + bias, axis=0)

    q, k, v, do = q1[0], k1[0], v1[0], do_s[1 ^ core]
    d = deltas(do, o1[0], low)
    q_t, do_t = q.astype(f32).T.astype(bf16), do.astype(f32).T.astype(bf16)
    out = [
        back_head(q_t, k, v, do, do_t, d[head], p1[head], mine, head)
        for head, mine in ((0, low), (1, ~low))
    ]
    gq_s[...] = jnp.where(low, out[0][0], out[1][0])
    gk_s[...] = jnp.concatenate([out[0][1], out[1][1]], axis=0).T
    gv_s[...] = jnp.concatenate([out[0][2], out[1][2]], axis=0).T
    sums1 = finish(1, q, k, cos1, sin1, pos1)
    gq_s[...] = jnp.zeros_like(gq_s)
    gk_s[...] = jnp.zeros_like(gk_s)
    gv_s[...] = jnp.zeros_like(gv_s)
    for win, base in enumerate(WINDOWS):
        at = pl.ds(base, WIN)
        q, k, v, o = (r[0, at, :] for r in (q0, k0, v0, o0))
        do = do_s[core, at, :]
        d = deltas(do, o, low)
        q_t, do_t = q.astype(f32).T.astype(bf16), do.astype(f32).T.astype(bf16)
        out = [
            back_head(q_t, k, v, do, do_t, d[head], p0[head, win], mine, head)
            for head, mine in ((0, low), (1, ~low))
        ]
        gq_s[at, :] += jnp.where(low, out[0][0], out[1][0])
        gk_s[at, :] += jnp.concatenate([out[0][1], out[1][1]], axis=0).T
        gv_s[at, :] += jnp.concatenate([out[0][2], out[1][2]], axis=0).T
    sums0 = finish(0, q0[0], k0[0], cos0, sin0, pos0)
    att_s[pair, 0:5, :] = sums0 + sums1

    gw = jnp.zeros((D, 6 * HD), f32)
    gw_mine = jnp.zeros((2 * HD, DC), f32)
    gw_other = jnp.zeros((2 * HD, DC), f32)
    for frame in range(CORES):
        cols = cols_ref[frame].astype(f32).T.astype(bf16)
        gw_mine += dot(cols, mine_ref[frame ^ core])
        gw_other += dot(cols, other_ref[frame ^ core])
        gw += dot(h1t_ref[frame], gqkv_s[frame, :, pl.ds(pl.multiple_of(pair * 6 * HD, 6 * HD), 6 * HD)])
    gw_s[:, : 6 * HD] = gw.astype(bf16)
    at = lambda c: pl.ds(pl.multiple_of(c * DC, DC), DC)
    gw_s[at(core), 6 * HD :] = gw_mine.T.astype(bf16)
    gw_s[at(1 - core), 6 * HD :] = gw_other.T.astype(bf16)
    to_chips(place_ref, gw_s, (gw0, gw1, gw2, gw3), pl.ds(pl.multiple_of(pair * 8 * HD, 8 * HD), 8 * HD))

    @pl.when(pair == PAIRS - 1)
    def _():
        lay_out(place_ref, (w0, w1, w2, w3), w_s, QKV)
        rows_s[...] = jnp.zeros_like(rows_s)
        for frame, x, out in ((0, x_ref, gh_ref), (1, xo_ref, gho_ref)):
            for half in range(2):
                at = slice(half * (S // 2), (half + 1) * (S // 2))
                gh = dot_t(gqkv_s[frame, at, :], w_s[...])
                out[at, :] = gh
                normed, _ = stats(x[at, :].astype(f32))
                rows_s[0:1, :] += jnp.sum(gh * normed, axis=0, keepdims=True)
                rows_s[1:2, :] += jnp.sum(gh, axis=0, keepdims=True)
        rows_s[2:4, :] = mid_ref[0:2, :]
        rows_s[7:9, :] = mid_ref[2:4, :]
        att = jnp.concatenate([att_s[p] for p in range(PAIRS)], axis=1)
        rows_s[4:7, pl.ds(pl.multiple_of(core * DC, DC), DC)] = att[2:5, :]
        src = lax.broadcasted_iota(jnp.int32, (DC, D), 0)
        dst = lax.broadcasted_iota(jnp.int32, (DC, D), 1)
        want = core * (DC // 2) + (src // HD) * (HD // 2) + (src & (HD // 2 - 1))
        side = lax.broadcasted_iota(jnp.int32, (1, DC), 1)
        turn = jnp.where((side & (HD - 1)) < HD // 2, att, -att)
        rows_s[9:10, :] = exact_dot(turn, dst == want)[0:1, :] + exact_dot(turn, dst == want + D // 2)[1:2, :]
        gb1 = jnp.concatenate([gb1_ref[:, r * DC : (r + 1) * DC] for r in range(FC // DC)] * 2, axis=0)
        rows_s[10:14, :] = exact_dot(gb1, spots_t(core))[:4, :]
        full_s[...] = rows_s[...].T.astype(bf16)
        to_chips(place_ref, full_s, (gw0, gw1, gw2, gw3), slice(4 * DC, PACK))


def to_chips(place_ref, full_ref, outs, cols):
    for d, out in enumerate(outs):
        a = (place_ref[1] + d) & (SIDE - 1)
        for g in range(SIDE):
            at = pl.multiple_of(natural(place_ref[0], a, g) * BLOCK, BLOCK)
            out[g * BLOCK : (g + 1) * BLOCK, cols] = full_ref[pl.ds(at, BLOCK), :]


def attn_bwd_call(
    place, q, k, v, ga, mine, other, p0, p1, cosine, sine, pos, h1t, pieces, x, xo, mid, gb1
):
    q, k, v, cosine, sine, pos, ga = (a.reshape(CORES, S, -1) for a in (q, k, v, cosine, sine, pos, ga))
    block = lambda g: pl.BlockSpec((1, S, 2 * HD), lambda p, c: (g ^ c[0], 0, p))
    own = lambda g: pl.BlockSpec((1, S, 2 * HD), lambda p, c: (g, 0, p))
    at = lambda g: pl.BlockSpec((1, S, 8), lambda p, c: (g ^ c[0], 0, 0))
    whole = lambda a: pl.BlockSpec(a.shape, lambda p, c: (0,) * a.ndim)
    keep = lambda *n: pl.BlockSpec(n, lambda p, c: (0,) * len(n))
    return pl.pallas_call(
        attn_bwd_kernel,
        grid_spec=pltpu.PrefetchScalarGridSpec(
            num_scalar_prefetch=1,
            grid=(PAIRS,),
            in_specs=[block(0)] * 3
            + [own(0), pl.BlockSpec((2, 2, WIN, WIN), lambda p, c: (p, 0, 0, 0))]
            + [block(0)] * 2
            + [at(0)]
            + [block(1)] * 3
            + [own(1), pl.BlockSpec((2, S, S), lambda p, c: (p, 0, 0))]
            + [block(1)] * 2
            + [at(1)]
            + [whole(h1t), whole(ga)]
            + [pl.BlockSpec((CORES, S, 2 * HD), lambda p, c: (0, 0, PAIRS * c[0] + p))]
            + [whole(mine), whole(other)]
            + [whole(a) for a in pieces]
            + [whole(a) for a in (x, xo, mid, gb1)],
            out_specs=[keep(QUARTER, PACK)] * 4 + [keep(S, D)] * 2,
            scratch_shapes=[pltpu.VMEM((S, 2 * HD), f32)] * 3
            + [pltpu.VMEM((D, 8 * HD), bf16), pltpu.VMEM((D, D), bf16), pltpu.VMEM((CORES, S, 2 * HD), bf16)]
            + [pltpu.VMEM((CORES, S, 3 * DC), bf16), pltpu.VMEM((PAIRS, 8, 2 * HD), f32)]
            + [pltpu.VMEM((128, D), f32), pltpu.VMEM((D, 128), bf16), pltpu.VMEM((D, 3 * DC), bf16)],
        ),
        out_shape=[
            *[jax.ShapeDtypeStruct((QUARTER, PACK), bf16)] * 4,
            *[jax.ShapeDtypeStruct((S, D), f32)] * 2,
        ],
        compiler_params=params(),
        cost_estimate=cost(10 * HC * S * S * 128 + 4 * T * D * 4 * DC, 36e6),
    )(
        place,
        q, k, v, mine, p0, cosine, sine, pos,
        q, k, v, mine, p1, cosine, sine, pos,
        h1t, ga, ga, mine, other, *pieces, x, xo, mid, gb1,
    )


def last_kernel(x_ref, ga_ref, gh_ref, other_ref, v_ref, gt_ref):
    normed, inv_std = stats(x_ref[...].astype(f32))
    gt_ref[...] = ga_ref[...] + norm_back(gh_ref[...] + other_ref[...], normed, inv_std, v_ref[0:1, :])


def mixed_kernel(after_ref, mlp_ref, mlpo_ref, v_ref, out_ref):
    out_ref[...] = (after_ref[...] + (mlp_ref[...] + mlpo_ref[...] + v_ref[8:9, :])).astype(bf16)


def by_rows(kernel, out_type, flops, *args):
    rows = 288
    tile = pl.BlockSpec((rows, D), lambda i: (i, 0))
    return pl.pallas_call(
        kernel,
        grid=(S // rows,),
        in_specs=[tile] * (len(args) - 1) + [pl.BlockSpec(args[-1].shape, lambda i: (0, 0))],
        out_specs=tile,
        out_shape=jax.ShapeDtypeStruct((S, D), out_type),
        compiler_params=params(),
        cost_estimate=cost(flops * S * D, S * D * 16),
    )(*args)


WIDE = PACK + FC


def pack_kernel(q0, q1, q2, q3, f_ref, out_ref):
    total = q0[...].astype(f32) + q1[...].astype(f32) + q2[...].astype(f32) + q3[...].astype(f32)
    fc1 = f_ref[...].astype(f32)
    for n in range(PLANE):
        at = slice(n * KR, (n + 1) * KR)
        out_ref[n, :, :PACK] = total[at, :].astype(bf16)
        out_ref[n, :, PACK:] = fc1[at, :].astype(bf16)


def pack_call(parts, fc1):
    return pl.pallas_call(
        pack_kernel,
        out_shape=jax.ShapeDtypeStruct((PLANE, KR, WIDE), bf16),
        compiler_params=params(),
        cost_estimate=cost(QUARTER * PACK * 4, QUARTER * PACK * 10),
    )(*parts, fc1)


def sum_kernel(in_ref, out_ref):
    total = in_ref[0].astype(f32)
    for n in range(1, PLANE):
        total += in_ref[n].astype(f32)
    out_ref[...] = total


def sum_call(packed):
    return pl.pallas_call(
        sum_kernel,
        out_shape=jax.ShapeDtypeStruct(packed.shape[1:], f32),
        compiler_params=params(SMALL_LIMIT),
        cost_estimate=cost(packed.size, packed.size * 2),
    )(packed)


def fc2_kernel(place_ref, mine_ref, other_ref, out_ref, sq_ref):
    first = place_ref[0] == 0
    a, b = mine_ref[...], other_ref[...]
    out_ref[:FR, :] = jnp.where(first, a, b)
    out_ref[FR:, :] = jnp.where(first, b, a)
    total = jnp.sum(a * a + b * b, axis=(0, 1), keepdims=True)
    sq_ref[...] = jnp.broadcast_to(total, sq_ref.shape)


def fc2_call(place, mine, other):
    whole = lambda a: pl.BlockSpec(a.shape, lambda i, c: (0,) * len(a.shape))
    shapes = [jax.ShapeDtypeStruct(s, f32) for s in ((2 * FR, D), (8, 128))]
    return pl.pallas_call(
        fc2_kernel,
        grid_spec=pltpu.PrefetchScalarGridSpec(
            num_scalar_prefetch=1,
            grid=(1,),
            in_specs=[whole(mine), whole(other)],
            out_specs=[whole(a) for a in shapes],
        ),
        out_shape=shapes,
        compiler_params=params(SMALL_LIMIT),
        cost_estimate=cost(6 * FR * D, FR * D * 16),
    )(place, mine, other)


def norm_kernel(g_ref, o_ref, sq_ref, out_ref):
    g, o = g_ref[...], o_ref[...]
    part = jnp.sum(g * g + o * o, axis=(0, 1), keepdims=True)
    cross = g[:, 4 * DC : PACK] * o[:, 4 * DC : PACK]
    part += 2.0 * jnp.sum(cross, axis=(0, 1), keepdims=True)
    out_ref[...] = jnp.broadcast_to((part + sq_ref[0:1, 0:1])[None], out_ref.shape)


def norm_call(g, o, squares):
    return pl.pallas_call(
        norm_kernel,
        out_shape=jax.ShapeDtypeStruct((CHIPS, 8, 128), f32),
        compiler_params=params(SMALL_LIMIT),
        cost_estimate=cost(4 * KR * PACK, 1e6),
    )(g, o, squares)


RATES = (D ** (-0.5), max(1, 2 * D // S) ** (-0.5), D ** (-0.5), FF ** (-0.5), RATE_VECTOR)


def adam_kernel(place_ref, norm_ref, mine_ref, other_ref, g2_ref, *refs):
    masters, firsts, seconds = refs[0:5], refs[5:10], refs[10:15]
    outs = refs[15:30]
    norm_out, bias_out = refs[30:32]
    core = place_ref[0]
    mine, other = mine_ref[...], other_ref[...]
    g0 = jnp.where(core == 0, mine, other)
    g1 = jnp.where(core == 0, other, mine)
    total = jnp.sum(jnp.sum(norm_ref[...], axis=0)[0:1, 0:1], axis=(0, 1), keepdims=True)
    grad_norm = jnp.sqrt(total)
    norm_out[...] = jnp.broadcast_to(grad_norm, norm_out.shape)
    clip = jnp.minimum(1.0, CLIP_LIMIT / (grad_norm + 1e-06))

    def update(i, at, grad):
        clipped = grad * clip
        master = masters[i][at]
        first = BETA_ONE * firsts[i][at] + (1.0 - BETA_ONE) * clipped
        second = BETA_TWO * seconds[i][at] + (1.0 - BETA_TWO) * clipped * clipped
        first_hat = first / (1.0 - BETA_ONE**STEP)
        second_hat = second / (1.0 - BETA_TWO**STEP)
        decay = 0.0 if i == 4 else DECAY_RATE
        outs[3 * i][at] = master - RATES[i] * (first_hat / (jnp.sqrt(second_hat) + ADAM_EPS) + decay * master)
        outs[3 * i + 1][at] = first
        outs[3 * i + 2][at] = second

    rows = slice(None)
    for c, g in ((0, g0), (1, g1)):
        for p in range(PAIRS):
            for i in range(3):
                col = i * D + c * DC + p * 128
                update(0, (rows, slice(col, col + 128)), g[:, (4 * p + i) * 128 : (4 * p + i + 1) * 128])
            col = c * DC + p * 128
            update(1, (rows, slice(col, col + 128)), g[:, (4 * p + 3) * 128 : (4 * p + 4) * 128])
    for r in range(FC // DC):
        at = slice(PACK + r * DC, PACK + (r + 1) * DC)
        part = exact_dot(g0[:, at], spots_t(0)) + exact_dot(g1[:, at], spots_t(1))
        update(2, (rows, slice(r * D, (r + 1) * D)), part)
    update(3, (rows, rows), g2_ref[...])
    vec = (g0 + g1)[:, 4 * DC : 4 * DC + 128]
    vec = jnp.concatenate([vec, jnp.zeros((16 - KR, 128), f32)], axis=0).T[:16, :KR]
    update(4, (rows, rows), vec[: masters[4].shape[0], :])
    bias_out[...] = vec[7:8, :] * clip


def adam_call(place, norm, mine, other, g2, masters, firsts, seconds):
    whole = lambda a: pl.BlockSpec(a.shape, lambda i, c: (0,) * len(a.shape))
    args = [norm, mine, other, g2, *masters, *firsts, *seconds]
    shapes = [jax.ShapeDtypeStruct(m.shape, f32) for m in masters for _ in range(3)]
    shapes += [jax.ShapeDtypeStruct((1, 128), f32), jax.ShapeDtypeStruct((1, KR), f32)]
    return pl.pallas_call(
        adam_kernel,
        grid_spec=pltpu.PrefetchScalarGridSpec(
            num_scalar_prefetch=1,
            grid=(1,),
            in_specs=[whole(a) for a in args],
            out_specs=[whole(a) for a in shapes],
        ),
        out_shape=shapes,
        compiler_params=params(SMALL_LIMIT),
        cost_estimate=cost(20 * KR * FF * 3, 3e6),
    )(place, *args)


def local(
    tokens,
    cotangent,
    counts,
    patch_row,
    patch_col,
    w_qkv,
    w_proj,
    w_fc1,
    w_fc2,
    vectors,
    m_qkv,
    v_qkv,
    m_proj,
    v_proj,
    m_fc1,
    v_fc1,
    m_fc2,
    v_fc2,
    m_vectors,
    v_vectors,
):
    core = lax.axis_index("grp")
    chip = lax.axis_index("dp")
    first_core = core == 0
    along = jnp.where(first_core, chip // PLANE, (chip // SIDE) % SIDE)
    vr = vectors.shape[0]

    def swap(a):
        return lax.ppermute(a, "grp", [(0, 1), (1, 0)])

    def along_line(quarter):
        return [quarter] + [shift(quarter, d) for d in range(1, SIDE)]

    def line_sum(whole):
        return lax.psum_scatter(whole, BOTH, scatter_dimension=0, axis_index_groups=lines(), tiled=True)

    me = jnp.stack([core, along]).astype(jnp.int32)
    shares, share_fc2 = share_call(me, w_qkv, vectors, w_proj, w_fc2)
    full_fc2 = lax.all_gather(share_fc2, "dp", axis=0, tiled=True)
    quarter = plane_swap(shares).reshape(QUARTER, SHARE)
    qkv_pieces = along_line(quarter)
    fc1_b = w_fc1.astype(bf16).reshape(KR, CHIPS, CORES, FR)
    share_fc1 = jnp.where(first_core, fc1_b[:, :, 0], fc1_b[:, :, 1]).reshape(KR, FC)
    share = jnp.broadcast_to(share_fc1[None], (PLANE, KR, FC))
    share, qkv_pieces[1] = lax.optimization_barrier((share, qkv_pieces[1]))
    quarter = plane_swap(share).reshape(QUARTER, FC)

    x_own = tokens.reshape(S, D)
    cot_own = cotangent.reshape(S, D)
    x_other, cot_other = swap(x_own), swap(cot_own)
    ints = jnp.concatenate(
        [
            patch_row.reshape(1, S),
            patch_col.reshape(1, S),
            jnp.pad(counts.reshape(1, 2), ((0, 0), (0, S - 2))),
            jnp.zeros((5, S), jnp.int32),
        ]
    )
    ints = jnp.stack([ints, swap(ints)])
    counts0 = jnp.where(first_core, ints[0, 2, :2], ints[1, 2, :2])
    counts1 = jnp.where(first_core, ints[1, 2, :1], ints[0, 2, :1])
    place = jnp.concatenate([jnp.stack([core, along]).astype(jnp.int32), counts0, counts1])

    vec, h1t, cosine, sine, q, k, v, b1, pos = qkv_call(place, x_own, x_other, ints, qkv_pieces)
    q, quarter = lax.optimization_barrier((q, quarter))
    pieces = along_line(quarter)
    mine, p0, p1 = attn_fwd_call(place, q, k, v)
    mine, pieces[1], cot_other = lax.optimization_barrier((mine, pieces[1], cot_other))
    other = swap(mine)
    gy = gy_call(place, cot_own, cot_other)
    other, gy = lax.optimization_barrier((other, gy))
    after, n2, r2, h2 = proj_call(place, mine, other, x_own, x_other, qkv_pieces, vec)
    mlp, mlp_part, gh2, act, gup, gb1 = mlp_call(place, h2, gy, pieces, full_fc2, b1)
    other_gh2 = swap(gh2)
    mlp_other = swap(mlp_part)

    gw2 = fc2_grad_call(place, act, gy)
    gw2, other_gh2 = lax.optimization_barrier((gw2, other_gh2))
    sum_fc2 = line_sum(gw2)
    gw1, ga, gab, sums_mid = mid_call(place, h2, gup, n2, r2, gy, gh2, other_gh2, vec)
    sum_fc1 = line_sum(gw1)
    *gw, gh1, gh1_part = attn_bwd_call(
        place, q, k, v, gab, mine, other, p0, p1, cosine, sine, pos, h1t, qkv_pieces,
        x_own, x_other, sums_mid, gb1,
    )

    got_fc2 = plane_swap(sum_fc2.reshape(PLANE, FR, D))
    parts = [gw[0]] + [shift(gw[d], d) for d in range(1, SIDE)]
    got_fc2, sum_fc1 = lax.optimization_barrier((got_fc2, sum_fc1))
    g_fc2 = sum_call(got_fc2)
    g2, squares = fc2_call(place, g_fc2, swap(g_fc2))
    packed, gh1, gh1_part = lax.optimization_barrier((pack_call(parts, sum_fc1), gh1, gh1_part))
    gh1_other = swap(gh1_part)
    got = plane_swap(packed)
    gt = by_rows(last_kernel, f32, 25, x_own, ga, gh1, gh1_other, vec)
    got, g2, squares, gt = lax.optimization_barrier((got, g2, squares, gt))
    grads = sum_call(got)

    grads_other = swap(grads)
    squares, mlp = lax.optimization_barrier((norm_call(grads, grads_other, squares), mlp))
    norms = lax.all_to_all(squares, "dp", 0, 0)
    mixed = by_rows(mixed_kernel, bf16, 4, after, mlp, mlp_other, vec)
    norms, mixed = lax.optimization_barrier((norms, mixed))
    *updates, grad_norm, bias_proj_grad = adam_call(
        place,
        norms,
        grads,
        grads_other,
        g2,
        (w_qkv, w_proj, w_fc1, w_fc2, vectors),
        (m_qkv, m_proj, m_fc1, m_fc2, m_vectors),
        (v_qkv, v_proj, v_fc1, v_fc2, v_vectors),
    )
    return (
        mixed.reshape(1, 1, S, D),
        gt.reshape(1, 1, S, D),
        grad_norm[0, 0],
        *updates,
        bias_proj_grad.reshape(KR),
    )


def solution(mesh):
    frame = P("grp", "dp", None, None)
    ints = P("grp", "dp", None)
    rows = P("dp", None)
    cols = P(None, "dp")
    return jax.shard_map(
        local,
        mesh=mesh,
        in_specs=(frame, frame, ints, ints, ints, rows, rows, rows, rows, cols) + (rows,) * 8 + (cols,) * 2,
        out_specs=(frame, frame, P()) + (rows,) * 12 + (cols,) * 3 + (P("dp"),),
        check_vma=False,
    )
```
